32 devices in a mesh: grp: 1, row: 32 (over z, y, x, core), col: 1.
Axes of the slice: x: 2, y: 2, z: 4, core: 2. Of those that a mesh axis runs over, the one named last changes fastest.
Arguments:
- alignment_rows: bfloat16 [64, 128, 256], P(('grp', 'row'), 'col'), may hold values from -40 to 40
- pair_state: bfloat16 [128, 128, 128], P(('grp', 'row'), 'col'), may hold values from -4 to 4
- update_cotangent: bfloat16 [64, 128, 256], P(('grp', 'row'), 'col'), may hold values from -96 to 96
- sequence_mask: int32 [64], P('grp'), may hold values 0 or 1
- residue_mask: int32 [128], P('grp'), may hold values 0 or 1
- left_weight: bfloat16 [256, 32], replicated, may hold values from -0.375 to 0.375
- right_weight: bfloat16 [256, 32], replicated, may hold values from -0.375 to 0.375
- outer_weight: bfloat16 [32, 32, 128], replicated, may hold values from -1 to 1
- bias_weight: bfloat16 [128, 8], replicated, may hold values from -1.5 to 1.5
- query_weight: bfloat16 [256, 256], replicated, may hold values from -13 to 13
- key_weight: bfloat16 [256, 256], replicated, may hold values from -0.375 to 0.375
- value_weight: bfloat16 [256, 256], replicated, may hold values from -0.375 to 0.375
- gate_weight: bfloat16 [256, 256], replicated, may hold values from -0.375 to 0.375
- output_weight: bfloat16 [256, 256], replicated, may hold values from -0.375 to 0.375
Outputs:
- alignment_update: bfloat16 [64, 128, 256], P(('grp', 'row'), 'col')
- pair_updated: bfloat16 [128, 128, 128], P(('grp', 'row'), 'col')
- pair_gradient: float32 [128, 128, 128], P(('grp', 'row'), 'col')
The draws below stay inside these ranges and needn't reach their ends.
All inputs are finite; a program needn't handle non-finite values.
Results may differ from the reference program's by a relative error of at most 0.034.
Values may be sent and summed in bfloat16 or wider, within the bound.
No kernel may reach another device: no remote copies, remote signals or barrier semaphores. Data moves between devices by JAX's collectives and lax.ppermute only.
A program may use at most 64 MiB of HBM per device.

```python
import math
import jax
import jax.numpy as jnp
from jax import lax

C_M = 256
C_Z = 128
HEADS = 8
HEAD_DIM = 32
OPM_C = 32
RES_DEV = 4
NSEQ = 64
NRES = 128
N_ROW = 32


def shared_direction(key):
    return jnp.clip(jax.random.normal(key, (C_M, C_M), jnp.float32), -6.0, 6.0)


def draw_key_weight(key, part):
    base = shared_direction(key)
    return (base / 16.0).astype(jnp.bfloat16)


def draw_query_weight(key, part):
    key = jax.random.fold_in(key, 6)
    own_part = jnp.clip(jax.random.normal(key, (C_M, C_M), jnp.float32), -6.0, 6.0)
    return (own_part / 16.0).astype(jnp.bfloat16)


def scaled_field(key, array_shape, divide_by):
    first_key, second_key, third_key = jax.random.split(key, 3)
    row_scale = jnp.exp(jax.random.uniform(second_key, array_shape[:-1] + (1,), jnp.float32) * math.log(10.0))
    col_scale = jnp.exp(jax.random.uniform(third_key, (1,) * (len(array_shape) - 1) + (array_shape[-1],), jnp.float32) * math.log(10.0))
    central = jnp.clip(jax.random.normal(first_key, array_shape, jnp.float32), -4.0, 4.0)
    return central * row_scale * col_scale / divide_by


def draw_alignment_rows(key, part):
    key = jax.random.fold_in(key, 1)
    return scaled_field(key, (NSEQ, NRES, C_M), 10.0).astype(jnp.bfloat16)


def draw_pair_state(key, part):
    key = jax.random.fold_in(key, 2)
    return scaled_field(key, (NRES, NRES, C_Z), 100.0).astype(jnp.bfloat16)


def place_ends(array, key, low, high):
    index_at = [jax.random.randint(jax.random.fold_in(key, axis), (), 0, length) for axis, length in enumerate(array.shape)]
    longest = array.shape.index(max(array.shape))
    next_to = index_at[:longest] + [(index_at[longest] + 1) % array.shape[longest]] + index_at[longest + 1:]
    return array.at[tuple(index_at)].set(low).at[tuple(next_to)].set(high)


def shard_levels(stream_key, dims, cuts, least, high):
    factor_of = 1.0
    for axis_at, blocks in cuts:
        heights = jax.random.uniform(jax.random.fold_in(jax.random.fold_in(stream_key, 6), axis_at), (blocks,), jnp.float32, least / len(cuts), high / len(cuts))
        factor_of = factor_of * jnp.repeat(jnp.exp(heights), dims[axis_at] // blocks).reshape((-1,) + (1,) * (len(dims) - 1 - axis_at))
    return factor_of


def gaussian(key, dims, scale, reach, pieces=(), kind=jnp.bfloat16):
    entries = jax.random.normal(key, dims, jnp.float32) * scale
    if len(pieces) > 0:
        entries = shard_levels(key, dims, pieces, -0.22, 0.18) * entries
    return jnp.clip(entries, min=-reach, max=reach).astype(kind)


def setup_inputs(seed: int = 0, part: int = 0) -> dict:
    splits = jax.random.split(jax.random.key(seed), 15)
    part_keys = jax.random.split(jax.random.fold_in(splits[14], part), 15)
    alignment_rows = draw_alignment_rows(jax.random.fold_in(jax.random.fold_in(splits[14], part), 71), part)
    pair_state = draw_pair_state(jax.random.fold_in(jax.random.fold_in(splits[14], part), 71), part)
    update_cotangent = gaussian(part_keys[2], (NSEQ, NRES, C_M), 16.0, 96.0, ((0, 32),))
    sequence_mask = place_ends((jax.random.randint(part_keys[3], (NSEQ,), 0, 4) < 3).astype(jnp.int32), jax.random.fold_in(part_keys[3], 1), 0, 1)
    residue_mask = place_ends((jax.random.randint(part_keys[4], (NRES,), 0, 8) < 7).astype(jnp.int32), jax.random.fold_in(part_keys[4], 1), 0, 1)
    left_weight = gaussian(splits[5], (C_M, OPM_C), C_M ** -0.5, 0.375)
    right_weight = gaussian(splits[6], (C_M, OPM_C), C_M ** -0.5, 0.375)
    outer_weight = gaussian(splits[7], (OPM_C, OPM_C, C_Z), OPM_C ** -0.5, 1.0)
    bias_weight = gaussian(splits[8], (C_Z, HEADS), (C_Z // 8) ** -0.5, 1.5)
    query_weight = draw_query_weight(jax.random.fold_in(splits[14], 71), part)
    key_weight = draw_key_weight(jax.random.fold_in(splits[14], 71), part)
    value_weight = gaussian(splits[11], (C_M, C_M), C_M ** -0.5, 0.375)
    gate_weight = gaussian(splits[12], (C_M, C_M), C_M ** -0.5, 0.375)
    output_weight = gaussian(splits[13], (C_M, C_M), C_M ** -0.5, 0.375)
    return dict(alignment_rows=alignment_rows, pair_state=pair_state, update_cotangent=update_cotangent, sequence_mask=sequence_mask, residue_mask=residue_mask, left_weight=left_weight, right_weight=right_weight, outer_weight=outer_weight, bias_weight=bias_weight, query_weight=query_weight, key_weight=key_weight, value_weight=value_weight, gate_weight=gate_weight, output_weight=output_weight)


norm_eps = 1e-05
mask_fill = 1000000000.0

def layer_normalize(values):
    values = values.astype(jnp.float32)
    center = values - lax.optimization_barrier(jnp.mean(values, axis=-1, keepdims=True))
    spread = lax.optimization_barrier(jnp.mean(center * center, axis=-1, keepdims=True))
    return center * lax.rsqrt(spread + norm_eps)

def norm_backward(values, upstream):
    values = values.astype(jnp.float32)
    center = values - lax.optimization_barrier(jnp.mean(values, axis=-1, keepdims=True))
    inverse = lax.rsqrt(lax.optimization_barrier(jnp.mean(center * center, axis=-1, keepdims=True)) + norm_eps)
    normal_part = center * inverse
    return inverse * (upstream - lax.optimization_barrier(jnp.mean(upstream, axis=-1, keepdims=True)) - normal_part * lax.optimization_barrier(jnp.mean(upstream * normal_part, axis=-1, keepdims=True)))

def rounded_values(values):
    return lax.optimization_barrier(values.astype(jnp.bfloat16))

def reference(alignment_rows, pair_state, update_cotangent, sequence_mask, residue_mask, left_weight, right_weight, outer_weight, bias_weight, query_weight, key_weight, value_weight, gate_weight, output_weight):
    score_scale = HEAD_DIM ** (-0.5)
    seq_live = sequence_mask.astype(jnp.float32)
    res_live = residue_mask.astype(jnp.float32)
    normalized_input = rounded_values(layer_normalize(alignment_rows))
    flat_rows = normalized_input.reshape(-1, C_M)
    live_grid = (seq_live[:, None] * res_live[None, :])[..., None]
    left_proj = rounded_values(jnp.dot(flat_rows, left_weight, preferred_element_type=jnp.float32).reshape(NSEQ, NRES, OPM_C) * live_grid)
    right_proj = rounded_values(jnp.dot(flat_rows, right_weight, preferred_element_type=jnp.float32).reshape(NSEQ, NRES, OPM_C) * live_grid)
    divisor = jnp.maximum(jnp.sum(seq_live) * res_live[:, None] * res_live[None, :], 1.0)
    row_blocks = left_proj.reshape(NSEQ, N_ROW, RES_DEV, OPM_C).transpose(1, 0, 2, 3)

    def outer_rows(row_block):
        outer_sum = jnp.einsum('sip,sjq->ipjq', row_block.astype(jnp.float32), right_proj.astype(jnp.float32))
        return jnp.einsum('ipjq,pqz->ijz', rounded_values(outer_sum).astype(jnp.float32), outer_weight.astype(jnp.float32))
    opm_update = lax.map(outer_rows, row_blocks).reshape(NRES, NRES, C_Z)
    pair_updated = rounded_values(pair_state.astype(jnp.float32) + opm_update / divisor[..., None])
    pair_normed = rounded_values(layer_normalize(pair_updated))
    bias_all = rounded_values(jnp.einsum('ijz,zh->ihj', pair_normed.astype(jnp.float32), bias_weight.astype(jnp.float32)))
    projected_queries = rounded_values(jnp.dot(flat_rows, query_weight, preferred_element_type=jnp.float32)).reshape(NSEQ, NRES, HEADS, HEAD_DIM)
    projected_keys = rounded_values(jnp.dot(flat_rows, key_weight, preferred_element_type=jnp.float32)).reshape(NSEQ, NRES, HEADS, HEAD_DIM)
    projected_values = rounded_values(jnp.dot(flat_rows, value_weight, preferred_element_type=jnp.float32)).reshape(NSEQ, NRES, HEADS, HEAD_DIM)
    gate_activations = jax.nn.sigmoid(jnp.dot(flat_rows, gate_weight, preferred_element_type=jnp.float32)).reshape(NSEQ, NRES, C_M)
    key_mask = (res_live - 1.0) * mask_fill

    def single_sequence(running, sequence_items):
        query_one, keys_one, values_one, gate_one, cot_one = sequence_items
        scores = jnp.einsum('ihd,jhd->ihj', query_one.astype(jnp.float32), keys_one.astype(jnp.float32)) * score_scale
        scores = scores + bias_all.astype(jnp.float32) + key_mask
        maxima = lax.optimization_barrier(jnp.max(scores, axis=-1))
        weights = jnp.exp(scores - maxima[..., None])
        totals = lax.optimization_barrier(jnp.sum(weights, axis=-1))
        summed = jnp.einsum('ihj,jhd->ihd', rounded_values(weights).astype(jnp.float32), values_one.astype(jnp.float32))
        attended = (summed / totals[..., None]).reshape(NRES, C_M)
        gated = rounded_values(gate_one * attended)
        update = jnp.dot(gated, output_weight, preferred_element_type=jnp.float32).astype(jnp.bfloat16)
        d_gated = jnp.dot(cot_one, output_weight.T, preferred_element_type=jnp.float32)
        d_attended = d_gated * gate_one
        delta_sum = lax.optimization_barrier(jnp.sum((d_attended * attended).reshape(NRES, HEADS, HEAD_DIM), axis=-1))
        probs = jnp.exp(scores - (maxima + jnp.log(totals))[..., None])
        d_rounded = rounded_values(d_attended).astype(jnp.float32).reshape(NRES, HEADS, HEAD_DIM)
        d_weights = jnp.einsum('ihd,jhd->ihj', d_rounded, values_one.astype(jnp.float32))
        return (running + probs * (d_weights - delta_sum[..., None]), update)
    initial_value = jnp.zeros((NRES, HEADS, NRES), jnp.float32)
    bias_gradient, alignment_update = lax.scan(single_sequence, initial_value, (projected_queries, projected_keys, projected_values, gate_activations, update_cotangent))
    d_normed = jnp.einsum('ihj,zh->ijz', bias_gradient, bias_weight.astype(jnp.float32), precision=lax.Precision.HIGHEST)
    pair_gradient = norm_backward(pair_updated, d_normed)
    return (alignment_update, pair_updated, pair_gradient)
```

```python
import jax
import jax.numpy as jnp
from jax import lax
from jax.sharding import PartitionSpec as P

norm_eps = 1e-05
mask_fill = 1000000000.0


def layer_normalize(values):
    values = values.astype(jnp.float32)
    center = values - jnp.mean(values, axis=-1, keepdims=True)
    spread = jnp.mean(center * center, axis=-1, keepdims=True)
    return center * lax.rsqrt(spread + norm_eps)


def norm_backward(values, upstream):
    values = values.astype(jnp.float32)
    center = values - jnp.mean(values, axis=-1, keepdims=True)
    inverse = lax.rsqrt(jnp.mean(center * center, axis=-1, keepdims=True) + norm_eps)
    normal_part = center * inverse
    return inverse * (
        upstream
        - jnp.mean(upstream, axis=-1, keepdims=True)
        - normal_part * jnp.mean(upstream * normal_part, axis=-1, keepdims=True)
    )


def spread_all(shard):
    copies = jnp.broadcast_to(shard[None], (lax.axis_size("row"),) + shard.shape)
    gathered = lax.all_to_all(copies, "row", split_axis=0, concat_axis=0, tiled=True)
    return gathered.reshape((-1,) + shard.shape[1:])


def attend_partial(
    projected_queries, projected_keys, projected_values, bias_all, key_mask, score_scale
):
    scores = jnp.einsum(
        "ihd,jhd->ihj", projected_queries, projected_keys, preferred_element_type=jnp.float32
    )
    scores = scores * score_scale + bias_all.astype(jnp.float32) + key_mask
    maxima = jnp.max(scores, axis=-1)
    weights = jnp.exp(scores - maxima[..., None])
    totals = jnp.sum(weights, axis=-1)
    summed = jnp.einsum(
        "ihj,jhd->ihd",
        weights.astype(jnp.bfloat16),
        projected_values,
        preferred_element_type=jnp.float32,
    )
    return (maxima, totals, summed.reshape(summed.shape[0], -1))


def on_device(
    alignment_rows,
    pair_state,
    update_cotangent,
    sequence_mask,
    residue_mask,
    left_weight,
    right_weight,
    outer_weight,
    bias_weight,
    query_weight,
    key_weight,
    value_weight,
    gate_weight,
    output_weight,
):
    sequence_wise, residue_half, channel_count = alignment_rows.shape
    rows_here = pair_state.shape[0]
    residues = residue_mask.shape[0]
    head_count = bias_weight.shape[1]
    head_dim = channel_count // head_count
    score_scale = head_dim ** (-0.5)
    row_index = lax.axis_index("row")
    col_index = lax.axis_index("col")
    complete_alignment, complete_cotangent = (
        lax.all_gather(alignment_rows, "col", axis=1, tiled=True),
        lax.all_gather(update_cotangent, "col", axis=1, tiled=True),
    )
    seq_live = sequence_mask.astype(jnp.float32)
    res_live = residue_mask.astype(jnp.float32)
    own_seq = lax.dynamic_slice_in_dim(seq_live, row_index * sequence_wise, sequence_wise)
    own_cols = lax.dynamic_slice_in_dim(res_live, col_index * residue_half, residue_half)
    own_rows = lax.dynamic_slice_in_dim(res_live, row_index * rows_here, rows_here)
    normalized_input = layer_normalize(complete_alignment).astype(jnp.bfloat16)
    flat_rows = normalized_input.reshape(-1, channel_count)
    normed_half = lax.dynamic_slice_in_dim(
        normalized_input, col_index * residue_half, residue_half, 1
    )
    half_rows = normed_half.reshape(-1, channel_count)
    left_proj = jnp.dot(flat_rows, left_weight, preferred_element_type=jnp.float32).reshape(
        sequence_wise, residues, -1
    )
    left_proj = (left_proj * (own_seq[:, None] * res_live[None, :])[..., None]).astype(jnp.bfloat16)
    right_proj = jnp.dot(half_rows, right_weight, preferred_element_type=jnp.float32).reshape(
        sequence_wise, residue_half, -1
    )
    right_proj = (right_proj * (own_seq[:, None] * own_cols[None, :])[..., None]).astype(
        jnp.bfloat16
    )
    left_tile = lax.all_to_all(left_proj, "row", split_axis=1, concat_axis=0, tiled=True)
    right_all = spread_all(right_proj)
    outer_width = left_tile.shape[2]
    outer_sum = lax.dot_general(
        left_tile.reshape(left_tile.shape[0], -1),
        right_all.reshape(right_all.shape[0], -1),
        (((0,), (0,)), ((), ())),
        preferred_element_type=jnp.float32,
    )
    outer_half = outer_sum.astype(jnp.bfloat16).reshape(
        rows_here, outer_width, residue_half, outer_width
    )
    opm_update = jnp.einsum(
        "ipjq,pqz->ijz", outer_half, outer_weight, preferred_element_type=jnp.float32
    )
    divisor = jnp.maximum(jnp.sum(seq_live) * own_rows[:, None] * own_cols[None, :], 1.0)
    pair_updated = (pair_state.astype(jnp.float32) + opm_update / divisor[..., None]).astype(
        jnp.bfloat16
    )
    pair_normed = layer_normalize(pair_updated).astype(jnp.bfloat16)
    bias_tile = jnp.einsum(
        "ijz,zh->ihj", pair_normed, bias_weight, preferred_element_type=jnp.float32
    ).astype(jnp.bfloat16)
    projected_queries = (
        jnp.dot(flat_rows, query_weight, preferred_element_type=jnp.float32)
        .astype(jnp.bfloat16)
        .reshape(sequence_wise, residues, head_count, head_dim)
    )
    gate_activations = jax.nn.sigmoid(
        jnp.dot(flat_rows, gate_weight, preferred_element_type=jnp.float32)
    ).reshape(sequence_wise, residues, channel_count)
    key_live = (res_live - 1.0) * mask_fill
    half_live = lax.dynamic_slice_in_dim(key_live, col_index * residue_half, residue_half)
    bias_cols = lax.all_gather(bias_tile, "col", axis=2, tiled=True)
    bias_all = spread_all(bias_cols)
    key_count = bias_all.shape[2]
    projected_keys = (
        jnp.dot(flat_rows, key_weight, preferred_element_type=jnp.float32)
        .astype(jnp.bfloat16)
        .reshape(sequence_wise, key_count, head_count, head_dim)
    )
    projected_values = (
        jnp.dot(flat_rows, value_weight, preferred_element_type=jnp.float32)
        .astype(jnp.bfloat16)
        .reshape(sequence_wise, key_count, head_count, head_dim)
    )
    maxima, totals, summed = lax.map(
        lambda inputs: attend_partial(
            inputs[0], inputs[1], inputs[2], bias_all, key_live, score_scale
        ),
        (projected_queries, projected_keys, projected_values),
    )
    attended = summed / jnp.repeat(totals, head_dim, axis=-1)
    gated = gate_activations * attended
    gated_own = lax.dynamic_slice_in_dim(gated, col_index * residue_half, residue_half, 1).astype(
        jnp.bfloat16
    )
    alignment_update = (
        jnp.dot(
            gated_own.reshape(-1, channel_count), output_weight, preferred_element_type=jnp.float32
        )
        .astype(jnp.bfloat16)
        .reshape(sequence_wise, residue_half, channel_count)
    )
    d_gated = lax.dot_general(
        complete_cotangent.reshape(-1, channel_count),
        output_weight,
        (((1,), (1,)), ((), ())),
        preferred_element_type=jnp.float32,
    ).reshape(sequence_wise, residues, channel_count)
    d_attended = d_gated * gate_activations
    delta_sum = jnp.sum(
        (d_attended * attended).reshape(sequence_wise, residues, head_count, head_dim), axis=-1
    )
    d_rounded = d_attended.astype(jnp.bfloat16).reshape(
        sequence_wise, residues, head_count, head_dim
    )
    log_total = maxima + jnp.log(totals)
    keys_half = lax.dynamic_slice_in_dim(projected_keys, col_index * residue_half, residue_half, 1)
    values_half = lax.dynamic_slice_in_dim(
        projected_values, col_index * residue_half, residue_half, 1
    )
    bias_half = lax.dynamic_slice_in_dim(bias_all, col_index * residue_half, residue_half, 2)
    bias_rows = bias_half.astype(jnp.float32)

    def single_sequence(running, sequence_items):
        query_rows, d_rows, total_rows, delta_rows, keys_one, values_one = sequence_items
        scores = jnp.einsum(
            "ihd,jhd->ihj", query_rows, keys_one, preferred_element_type=jnp.float32
        )
        scores = scores * score_scale + bias_rows + half_live
        probs = jnp.exp(scores - total_rows[..., None])
        d_weights = jnp.einsum(
            "ihd,jhd->ihj", d_rows, values_one, preferred_element_type=jnp.float32
        )
        return (running + probs * (d_weights - delta_rows[..., None]), None)

    sequence_items = (projected_queries, d_rounded, log_total, delta_sum, keys_half, values_half)
    initial_value = jnp.zeros(
        (rows_here * lax.axis_size("row"), head_count, residue_half), jnp.float32
    )
    result, unused = lax.scan(single_sequence, initial_value, sequence_items)
    shares = lax.all_to_all(
        result.astype(jnp.bfloat16).reshape((-1,) + (rows_here,) + result.shape[1:]),
        "row",
        split_axis=0,
        concat_axis=0,
        tiled=True,
    )
    bias_gradient = jnp.sum(shares.astype(jnp.float32), axis=0)
    d_normed = jnp.einsum(
        "ihj,zh->ijz",
        bias_gradient,
        bias_weight.astype(jnp.float32),
        precision=lax.Precision.HIGHEST,
    )
    pair_gradient = norm_backward(pair_updated, d_normed)
    return (alignment_update, pair_updated, pair_gradient)


def solution(mesh):
    placed = (
        P(("grp", "row"), "col", None),
        P(("grp", "row"), "col", None),
        P(("grp", "row"), "col", None),
        P("grp"),
        P("grp"),
        P(),
        P(),
        P(),
        P(),
        P(),
        P(),
        P(),
        P(),
        P(),
    )
    return jax.shard_map(
        on_device,
        mesh=mesh,
        in_specs=placed,
        out_specs=(
            P(("grp", "row"), "col", None),
            P(("grp", "row"), "col", None),
            P(("grp", "row"), "col", None),
        ),
        check_vma=False,
    )
```

```python
import jax
import jax.numpy as jnp
from jax import lax
from jax.experimental import pallas as pl
from jax.experimental.pallas import tpu as pltpu
from jax.sharding import PartitionSpec as P

norm_eps = 1e-05
mask_fill = 1000000000.0


def layer_normalize(values):
    values = values.astype(jnp.float32)
    center = values - jnp.mean(values, axis=-1, keepdims=True)
    spread = jnp.mean(center * center, axis=-1, keepdims=True)
    return center * lax.rsqrt(spread + norm_eps)


def norm_backward(values, upstream):
    values = values.astype(jnp.float32)
    center = values - jnp.mean(values, axis=-1, keepdims=True)
    inverse = lax.rsqrt(jnp.mean(center * center, axis=-1, keepdims=True) + norm_eps)
    normal_part = center * inverse
    return inverse * (
        upstream
        - jnp.mean(upstream, axis=-1, keepdims=True)
        - normal_part * jnp.mean(upstream * normal_part, axis=-1, keepdims=True)
    )


def spread_all(shard):
    copies = jnp.broadcast_to(shard[None], (lax.axis_size("row"),) + shard.shape)
    gathered = lax.all_to_all(copies, "row", split_axis=0, concat_axis=0, tiled=True)
    return gathered.reshape((-1,) + shard.shape[1:])


def attend_partial(
    projected_queries, projected_keys, projected_values, bias_all, key_mask, score_scale
):
    scores = jnp.einsum(
        "ihd,jhd->ihj", projected_queries, projected_keys, preferred_element_type=jnp.float32
    )
    scores = scores * score_scale + bias_all.astype(jnp.float32) + key_mask
    maxima = jnp.max(scores, axis=-1)
    weights = jnp.exp(scores - maxima[..., None])
    totals = jnp.sum(weights, axis=-1)
    summed = jnp.einsum(
        "ihj,jhd->ihd",
        weights.astype(jnp.bfloat16),
        projected_values,
        preferred_element_type=jnp.float32,
    )
    return (maxima, totals, summed.reshape(summed.shape[0], -1))


def on_device_general(
    alignment_rows,
    pair_state,
    update_cotangent,
    sequence_mask,
    residue_mask,
    left_weight,
    right_weight,
    outer_weight,
    bias_weight,
    query_weight,
    key_weight,
    value_weight,
    gate_weight,
    output_weight,
):
    sequence_wise, residue_half, channel_count = alignment_rows.shape
    rows_here = pair_state.shape[0]
    residues = residue_mask.shape[0]
    head_count = bias_weight.shape[1]
    head_dim = channel_count // head_count
    score_scale = head_dim ** (-0.5)
    row_index = lax.axis_index("row")
    col_index = lax.axis_index("col")
    complete_alignment, complete_cotangent = (
        lax.all_gather(alignment_rows, "col", axis=1, tiled=True),
        lax.all_gather(update_cotangent, "col", axis=1, tiled=True),
    )
    seq_live = sequence_mask.astype(jnp.float32)
    res_live = residue_mask.astype(jnp.float32)
    own_seq = lax.dynamic_slice_in_dim(seq_live, row_index * sequence_wise, sequence_wise)
    own_cols = lax.dynamic_slice_in_dim(res_live, col_index * residue_half, residue_half)
    own_rows = lax.dynamic_slice_in_dim(res_live, row_index * rows_here, rows_here)
    normalized_input = layer_normalize(complete_alignment).astype(jnp.bfloat16)
    flat_rows = normalized_input.reshape(-1, channel_count)
    normed_half = lax.dynamic_slice_in_dim(
        normalized_input, col_index * residue_half, residue_half, 1
    )
    half_rows = normed_half.reshape(-1, channel_count)
    left_proj = jnp.dot(flat_rows, left_weight, preferred_element_type=jnp.float32).reshape(
        sequence_wise, residues, -1
    )
    left_proj = (left_proj * (own_seq[:, None] * res_live[None, :])[..., None]).astype(jnp.bfloat16)
    right_proj = jnp.dot(half_rows, right_weight, preferred_element_type=jnp.float32).reshape(
        sequence_wise, residue_half, -1
    )
    right_proj = (right_proj * (own_seq[:, None] * own_cols[None, :])[..., None]).astype(
        jnp.bfloat16
    )
    left_tile = lax.all_to_all(left_proj, "row", split_axis=1, concat_axis=0, tiled=True)
    right_all = spread_all(right_proj)
    outer_width = left_tile.shape[2]
    outer_sum = lax.dot_general(
        left_tile.reshape(left_tile.shape[0], -1),
        right_all.reshape(right_all.shape[0], -1),
        (((0,), (0,)), ((), ())),
        preferred_element_type=jnp.float32,
    )
    outer_half = outer_sum.astype(jnp.bfloat16).reshape(
        rows_here, outer_width, residue_half, outer_width
    )
    opm_update = jnp.einsum(
        "ipjq,pqz->ijz", outer_half, outer_weight, preferred_element_type=jnp.float32
    )
    divisor = jnp.maximum(jnp.sum(seq_live) * own_rows[:, None] * own_cols[None, :], 1.0)
    pair_updated = (pair_state.astype(jnp.float32) + opm_update / divisor[..., None]).astype(
        jnp.bfloat16
    )
    pair_normed = layer_normalize(pair_updated).astype(jnp.bfloat16)
    bias_tile = jnp.einsum(
        "ijz,zh->ihj", pair_normed, bias_weight, preferred_element_type=jnp.float32
    ).astype(jnp.bfloat16)
    projected_queries = (
        jnp.dot(flat_rows, query_weight, preferred_element_type=jnp.float32)
        .astype(jnp.bfloat16)
        .reshape(sequence_wise, residues, head_count, head_dim)
    )
    gate_activations = jax.nn.sigmoid(
        jnp.dot(flat_rows, gate_weight, preferred_element_type=jnp.float32)
    ).reshape(sequence_wise, residues, channel_count)
    key_live = (res_live - 1.0) * mask_fill
    half_live = lax.dynamic_slice_in_dim(key_live, col_index * residue_half, residue_half)
    bias_cols = lax.all_gather(bias_tile, "col", axis=2, tiled=True)
    bias_all = spread_all(bias_cols)
    key_count = bias_all.shape[2]
    projected_keys = (
        jnp.dot(flat_rows, key_weight, preferred_element_type=jnp.float32)
        .astype(jnp.bfloat16)
        .reshape(sequence_wise, key_count, head_count, head_dim)
    )
    projected_values = (
        jnp.dot(flat_rows, value_weight, preferred_element_type=jnp.float32)
        .astype(jnp.bfloat16)
        .reshape(sequence_wise, key_count, head_count, head_dim)
    )
    maxima, totals, summed = lax.map(
        lambda inputs: attend_partial(
            inputs[0], inputs[1], inputs[2], bias_all, key_live, score_scale
        ),
        (projected_queries, projected_keys, projected_values),
    )
    attended = summed / jnp.repeat(totals, head_dim, axis=-1)
    gated = gate_activations * attended
    gated_own = lax.dynamic_slice_in_dim(gated, col_index * residue_half, residue_half, 1).astype(
        jnp.bfloat16
    )
    alignment_update = (
        jnp.dot(
            gated_own.reshape(-1, channel_count), output_weight, preferred_element_type=jnp.float32
        )
        .astype(jnp.bfloat16)
        .reshape(sequence_wise, residue_half, channel_count)
    )
    d_gated = lax.dot_general(
        complete_cotangent.reshape(-1, channel_count),
        output_weight,
        (((1,), (1,)), ((), ())),
        preferred_element_type=jnp.float32,
    ).reshape(sequence_wise, residues, channel_count)
    d_attended = d_gated * gate_activations
    delta_sum = jnp.sum(
        (d_attended * attended).reshape(sequence_wise, residues, head_count, head_dim), axis=-1
    )
    d_rounded = d_attended.astype(jnp.bfloat16).reshape(
        sequence_wise, residues, head_count, head_dim
    )
    log_total = maxima + jnp.log(totals)
    keys_half = lax.dynamic_slice_in_dim(projected_keys, col_index * residue_half, residue_half, 1)
    values_half = lax.dynamic_slice_in_dim(
        projected_values, col_index * residue_half, residue_half, 1
    )
    bias_half = lax.dynamic_slice_in_dim(bias_all, col_index * residue_half, residue_half, 2)
    bias_rows = bias_half.astype(jnp.float32)

    def single_sequence(running, sequence_items):
        query_rows, d_rows, total_rows, delta_rows, keys_one, values_one = sequence_items
        scores = jnp.einsum(
            "ihd,jhd->ihj", query_rows, keys_one, preferred_element_type=jnp.float32
        )
        scores = scores * score_scale + bias_rows + half_live
        probs = jnp.exp(scores - total_rows[..., None])
        d_weights = jnp.einsum(
            "ihd,jhd->ihj", d_rows, values_one, preferred_element_type=jnp.float32
        )
        return (running + probs * (d_weights - delta_rows[..., None]), None)

    sequence_items = (projected_queries, d_rounded, log_total, delta_sum, keys_half, values_half)
    initial_value = jnp.zeros(
        (rows_here * lax.axis_size("row"), head_count, residue_half), jnp.float32
    )
    result, unused = lax.scan(single_sequence, initial_value, sequence_items)
    shares = lax.all_to_all(
        result.astype(jnp.bfloat16).reshape((-1,) + (rows_here,) + result.shape[1:]),
        "row",
        split_axis=0,
        concat_axis=0,
        tiled=True,
    )
    bias_gradient = jnp.sum(shares.astype(jnp.float32), axis=0)
    d_normed = jnp.einsum(
        "ihj,zh->ijz",
        bias_gradient,
        bias_weight.astype(jnp.float32),
        precision=lax.Precision.HIGHEST,
    )
    pair_gradient = norm_backward(pair_updated, d_normed)
    return (alignment_update, pair_updated, pair_gradient)


LANES = 128
LEFT_ROWS = 4
STRIDE = 40
f32 = jnp.float32
bf16 = jnp.bfloat16


def dot_nn(a, b):
    return lax.dot_general(a, b, (((1,), (0,)), ((), ())), preferred_element_type=f32)


def dot_nt(a, b):
    return lax.dot_general(a, b, (((1,), (1,)), ((), ())), preferred_element_type=f32)


def dot_tn(a, b):
    return lax.dot_general(a, b, (((0,), (0,)), ((), ())), preferred_element_type=f32)


def lane_index(rows):
    return lax.broadcasted_iota(jnp.int32, (rows, LANES), 1)


def factors_kernel(seq_ref, res_ref, rows_ref, left_ref, right_ref, send_ref, normed_ref, left_scr):
    seqs = send_ref.shape[2] // 18
    residues = res_ref.shape[1]
    chips = send_ref.shape[0]
    me = lax.axis_index("row")
    normed = layer_normalize(rows_ref[...]).astype(bf16)
    normed_ref[...] = normed
    live = res_ref[...].astype(f32)
    live_rows = jnp.broadcast_to(live, (residues, residues)).T
    right_t = right_ref[...].astype(f32).T.astype(bf16)
    left_wide = jnp.concatenate([left_ref[...]] * 4, axis=1)
    low = lane_index(16) < 64
    lane_group = lane_index(chips) // 32
    halves = ([], [])
    tail = []
    for s in range(seqs):
        seq_live = seq_ref[me * seqs + s].astype(f32)
        own = normed[s * residues : (s + 1) * residues]
        factor = dot_nt(right_t, own) * (live * seq_live)
        first, second = factor[:16], factor[16:]
        halves[0].append(jnp.where(low, first, pltpu.roll(second, 64, 1)))
        halves[1].append(jnp.where(low, pltpu.roll(first, 64, 1), second))
        left_scr[...] = dot_nn(own, left_wide) * (live_rows * seq_live)
        for a in range(2):
            row = jnp.zeros((chips, LANES), f32)
            for b in range(4):
                part = left_scr[pl.ds(4 * a + b, chips, stride=8), :]
                row = jnp.where(lane_group == b, part, row)
            tail.append(row)
    tail = jnp.stack(tail, axis=1).astype(bf16)
    right_rows = 16 * seqs
    for core in range(2):
        block = jnp.concatenate(halves[core], axis=0).astype(bf16)
        send_ref[:, core, :right_rows, :] = jnp.broadcast_to(block[None], (chips, right_rows, LANES))
        send_ref[:, core, right_rows:, :] = tail


def projections_kernel(
    normed_ref, cot_ref, wq_ref, wk_ref, wv_ref, wg_ref, wo_ref, q_ref, k_ref, v_ref, gate_ref, d_ref
):
    normed = normed_ref[...]
    q_ref[...] = dot_nn(normed, wq_ref[...]).astype(bf16)
    k_ref[...] = dot_nn(normed, wk_ref[...]).astype(bf16)
    v_ref[...] = dot_nn(normed, wv_ref[...]).astype(bf16)
    gate = jax.nn.sigmoid(dot_nn(normed, wg_ref[...]))
    gate_ref[...] = gate
    d_ref[...] = (dot_nt(cot_ref[...], wo_ref[...]) * gate).astype(bf16)


def pair_kernel(recv_ref, weight_ref, pair_ref, div_ref, bias_w_ref, send_ref, updated_ref, flat, rbuf, lbuf, obuf):
    peers, block_rows, _ = recv_ref.shape
    seqs = block_rows // 18
    for p in range(peers):
        flat[p * STRIDE : p * STRIDE + block_rows, :] = recv_ref[p].astype(f32)
    for s in range(seqs):
        for g in range(16):
            part = flat[pl.ds(s * 16 + g, peers, stride=STRIDE), :]
            rbuf[s * peers : (s + 1) * peers, g * LANES : (g + 1) * LANES] = part.astype(bf16)
        for a in range(2):
            part = flat[pl.ds(16 * seqs + 2 * s + a, peers, stride=STRIDE), :]
            lbuf[s * peers : (s + 1) * peers, a * LANES : (a + 1) * LANES] = part.astype(bf16)
    left_t = lbuf[...].astype(f32).T.astype(bf16)
    for g in range(16):
        outer = dot_nn(left_t, rbuf[:, g * LANES : (g + 1) * LANES]).astype(bf16)
        for i in range(8):
            obuf[g * 32 : (g + 1) * 32, i * LANES : (i + 1) * LANES] = outer[i * 32 : (i + 1) * 32]
    sums = dot_nn(weight_ref[...], obuf[...])
    low = lane_index(LANES) < 64

    def piece(a, i):
        return sums[a * LANES : (a + 1) * LANES, i * LANES : (i + 1) * LANES]

    blocks = []
    bias_w = bias_w_ref[...]
    for b in range(4):
        straight = jnp.where(low, piece(0, b), piece(1, b + 4))
        crossed = jnp.where(low, piece(0, b + 4), piece(1, b))
        update = (straight + pltpu.roll(crossed, 64, 1)) / div_ref[b : b + 1, :]
        state = jnp.concatenate([pair_ref[b], pair_ref[b + 4]], axis=0).astype(f32)
        updated = (state + update.T).astype(bf16)
        updated_ref[b] = updated[:64]
        updated_ref[b + 4] = updated[64:]
        pair_normed = layer_normalize(updated).astype(bf16)
        blocks.append(dot_nt(bias_w, pair_normed))
    block = jnp.concatenate(blocks, axis=0).astype(bf16)
    send_ref[...] = jnp.broadcast_to(block[None], send_ref.shape)


def attention_kernel(
    scale, bias_ref, res_ref, q_ref, k_ref, v_ref, gate_ref, d_ref, send_ref, gated_ref, flat, grads
):
    residues = res_ref.shape[1]
    channels = q_ref.shape[1]
    seqs = q_ref.shape[0] // residues
    heads = flat.shape[0] // residues
    flat[...] = bias_ref[...].reshape(flat.shape).astype(f32)
    key_mask = (res_ref[...].astype(f32) - 1.0) * mask_fill
    sub = lax.broadcasted_iota(jnp.int32, (residues, LANES), 0) % 8
    keep = (sub < 4) == (lane_index(residues) < 64)
    head_of = lax.broadcasted_iota(jnp.int32, (1, channels), 1) // (channels // heads)
    attended = [jnp.zeros((residues, channels), f32) for _ in range(seqs)]
    for h in range(heads):
        raw = flat[pl.ds(h, residues, stride=heads), :]
        up, down = pltpu.roll(raw, residues - 4, 0), pltpu.roll(raw, 4, 0)
        moved = pltpu.roll(jnp.where(sub < 4, up, down), 64, 1)
        bias = jnp.where(keep, raw, moved) + key_mask
        of_head = head_of == h
        total = jnp.zeros((residues, residues), f32)
        for s in range(seqs):
            at = slice(s * residues, (s + 1) * residues)
            q = jnp.where(of_head, q_ref[at, :], jnp.zeros((), bf16))
            d = jnp.where(of_head, d_ref[at, :], jnp.zeros((), bf16))
            scores = dot_nt(q, k_ref[at, :]) * scale + bias
            weights = jnp.exp(scores - jnp.max(scores, axis=-1, keepdims=True))
            inverse = 1.0 / jnp.sum(weights, axis=-1, keepdims=True)
            mixed = dot_nn(weights.astype(bf16), v_ref[at, :]) * inverse
            attended[s] = jnp.where(of_head, mixed, attended[s])
            probs = weights * inverse
            flow = probs * dot_nt(d, v_ref[at, :])
            total = total + (flow - probs * jnp.sum(flow, axis=-1, keepdims=True))
        grads[pl.ds(h, residues, stride=heads), :] = total
    send_ref[...] = grads[...].astype(bf16).reshape(send_ref.shape)
    for s in range(seqs):
        at = slice(s * residues, (s + 1) * residues)
        gated_ref[at, :] = (gate_ref[at, :] * attended[s]).astype(bf16)


def output_kernel(gated_ref, wo_ref, out_ref):
    out_ref[...] = dot_nn(gated_ref[...], wo_ref[...]).astype(bf16)


def gradient_kernel(shares_ref, bias_w_ref, pair_ref, out_ref):
    total = jnp.sum(shares_ref[...].astype(f32), axis=0)
    rows = pair_ref.shape[0]
    heads = total.shape[0] // rows
    bias_w = bias_w_ref[...].astype(f32)
    for i in range(rows):
        own = total[i * heads : (i + 1) * heads]
        upstream = lax.dot_general(
            own, bias_w, (((0,), (0,)), ((), ())), precision=lax.Precision.HIGHEST, preferred_element_type=f32
        )
        out_ref[i] = norm_backward(pair_ref[i], upstream)


def kernel_call(body, out_shape, in_specs=None, scratch=(), flops=0, moved=0):
    vmem = pl.BlockSpec(memory_space=pltpu.VMEM)
    many = isinstance(out_shape, (list, tuple))
    return pl.pallas_call(
        body,
        out_shape=out_shape,
        in_specs=in_specs,
        out_specs=[vmem] * len(out_shape) if many else vmem,
        scratch_shapes=list(scratch),
        compiler_params=pltpu.CompilerParams(vmem_limit_bytes=24 * 1024 * 1024),
        cost_estimate=pl.CostEstimate(flops=flops, bytes_accessed=moved, transcendentals=0),
    )


def on_device_paired(
    alignment_rows,
    pair_state,
    update_cotangent,
    sequence_mask,
    residue_mask,
    left_weight,
    right_weight,
    outer_weight,
    bias_weight,
    query_weight,
    key_weight,
    value_weight,
    gate_weight,
    output_weight,
):
    sequence_wise, residues, channel_count = alignment_rows.shape
    rows_here, _, pair_channels = pair_state.shape
    head_count = bias_weight.shape[1]
    peers = lax.axis_size("row")
    factor = left_weight.shape[1]
    chips = peers // 2
    vmem = pl.BlockSpec(memory_space=pltpu.VMEM)
    smem = pl.BlockSpec(memory_space=pltpu.SMEM)
    me = lax.axis_index("row")
    core = me % 2
    sibling = [(i, i ^ 1) for i in range(peers)]
    token_rows = sequence_wise * residues
    half = residues // 2
    block_rows = sequence_wise * 18
    res_row = residue_mask.reshape(1, residues)
    flat_rows = alignment_rows.reshape(token_rows, channel_count)
    shape = jax.ShapeDtypeStruct

    send, normed = kernel_call(
        factors_kernel,
        [shape((chips, 2, block_rows, LANES), bf16), shape((token_rows, channel_count), bf16)],
        [smem, vmem, vmem, vmem, vmem],
        [pltpu.VMEM((residues, LANES), f32)],
        flops=2 * token_rows * channel_count * LANES,
        moved=1 << 19,
    )(sequence_mask, res_row, flat_rows, left_weight, right_weight)
    received = lax.all_to_all(
        send.reshape(peers, block_rows, LANES), "row", split_axis=0, concat_axis=0, tiled=True
    )

    queries, keys, values, gate, d_rounded = kernel_call(
        projections_kernel,
        [shape((token_rows, channel_count), t) for t in (bf16, bf16, bf16, f32, bf16)],
        [vmem] * 7,
        flops=10 * token_rows * channel_count * channel_count,
        moved=1 << 21,
    )(
        normed,
        update_cotangent.reshape(token_rows, channel_count),
        query_weight,
        key_weight,
        value_weight,
        gate_weight,
        output_weight,
    )

    def trade_columns(tile):
        kept = lax.dynamic_slice_in_dim(tile, core * half, half, 1)
        got = lax.ppermute(lax.dynamic_slice_in_dim(tile, (1 - core) * half, half, 1), "row", sibling)
        return jnp.where(core == 0, jnp.concatenate([kept, got]), jnp.concatenate([got, kept]))

    def trade_rows(tile):
        kept = lax.dynamic_slice_in_dim(tile, core * rows_here, rows_here, 0)
        got = lax.ppermute(
            lax.dynamic_slice_in_dim(tile, (1 - core) * rows_here, rows_here, 0), "row", sibling
        )
        return jnp.where(
            core == 0, jnp.concatenate([kept, got], axis=1), jnp.concatenate([got, kept], axis=1)
        )

    pair_tile = trade_columns(pair_state)
    weight_t = (
        outer_weight.reshape(factor, 2, 16, pair_channels)
        .transpose(1, 3, 2, 0)
        .reshape(2 * pair_channels, 16 * factor)
    )
    seq_live = sequence_mask.astype(f32)
    res_live = residue_mask.astype(f32)
    tile_rows = lax.dynamic_slice_in_dim(res_live, (me // 2) * 8, 8).reshape(2, 4)
    tile_cols = lax.dynamic_slice_in_dim(res_live, core * half, half)
    divisor = jnp.maximum(
        jnp.sum(seq_live) * tile_rows.T[:, :, None] * tile_cols[None, None, :], 1.0
    ).reshape(4, 2 * half)
    bias_rows = 4 * head_count
    send_bias, updated_tile = kernel_call(
        pair_kernel,
        [shape((peers, bias_rows, LANES), bf16), shape((8, half, pair_channels), bf16)],
        [vmem] * 5,
        [
            pltpu.VMEM((peers * STRIDE, LANES), f32),
            pltpu.VMEM((peers * sequence_wise, 16 * LANES), bf16),
            pltpu.VMEM((peers * sequence_wise, 2 * LANES), bf16),
            pltpu.VMEM((16 * factor, 8 * LANES), bf16),
        ],
        flops=1 << 29,
        moved=1 << 20,
    )(received, weight_t, pair_tile, divisor, bias_weight.T)
    bias_all = lax.all_to_all(send_bias, "row", split_axis=0, concat_axis=0, tiled=True)
    pair_updated = trade_rows(updated_tile)

    send_grad, gated = kernel_call(
        lambda *refs: attention_kernel((channel_count // head_count) ** (-0.5), *refs),
        [shape((peers, rows_here * head_count, LANES), bf16), shape((token_rows, channel_count), bf16)],
        [vmem] * 7,
        [pltpu.VMEM((residues * head_count, LANES), f32), pltpu.VMEM((residues * head_count, LANES), f32)],
        flops=1 << 29,
        moved=1 << 21,
    )(bias_all, res_row, queries, keys, values, gate, d_rounded)
    shares = lax.all_to_all(send_grad, "row", split_axis=0, concat_axis=0, tiled=True)
    update = kernel_call(
        output_kernel,
        shape((token_rows, channel_count), bf16),
        [vmem] * 2,
        flops=2 * token_rows * channel_count * channel_count,
        moved=1 << 19,
    )(gated, output_weight)
    pair_gradient = kernel_call(
        gradient_kernel,
        shape((rows_here, residues, pair_channels), f32),
        [vmem] * 3,
        flops=1 << 24,
        moved=1 << 20,
    )(shares, bias_weight.T, pair_updated)
    return (update.reshape(alignment_rows.shape), pair_updated, pair_gradient)


def solution(mesh):
    placed = (
        P(("grp", "row"), "col", None),
        P(("grp", "row"), "col", None),
        P(("grp", "row"), "col", None),
        P("grp"),
        P("grp"),
        P(),
        P(),
        P(),
        P(),
        P(),
        P(),
        P(),
        P(),
        P(),
    )
    one_column = mesh.shape["col"] == 1 and mesh.shape["row"] % 2 == 0
    return jax.shard_map(
        on_device_paired if one_column else on_device_general,
        mesh=mesh,
        in_specs=placed,
        out_specs=(
            P(("grp", "row"), "col", None),
            P(("grp", "row"), "col", None),
            P(("grp", "row"), "col", None),
        ),
        check_vma=False,
    )
```

```python
import jax
import jax.numpy as jnp
from jax import lax
from jax.experimental import pallas as pl
from jax.experimental.pallas import tpu as pltpu
from jax.sharding import PartitionSpec as P

norm_eps = 1e-05
mask_fill = 1000000000.0


def layer_normalize(values):
    values = values.astype(jnp.float32)
    center = values - jnp.mean(values, axis=-1, keepdims=True)
    spread = jnp.mean(center * center, axis=-1, keepdims=True)
    return center * lax.rsqrt(spread + norm_eps)


def norm_backward(values, upstream):
    values = values.astype(jnp.float32)
    center = values - jnp.mean(values, axis=-1, keepdims=True)
    inverse = lax.rsqrt(jnp.mean(center * center, axis=-1, keepdims=True) + norm_eps)
    normal_part = center * inverse
    return inverse * (
        upstream
        - jnp.mean(upstream, axis=-1, keepdims=True)
        - normal_part * jnp.mean(upstream * normal_part, axis=-1, keepdims=True)
    )


def spread_all(shard):
    copies = jnp.broadcast_to(shard[None], (lax.axis_size("row"),) + shard.shape)
    gathered = lax.all_to_all(copies, "row", split_axis=0, concat_axis=0, tiled=True)
    return gathered.reshape((-1,) + shard.shape[1:])


def attend_partial(
    projected_queries, projected_keys, projected_values, bias_all, key_mask, score_scale
):
    scores = jnp.einsum(
        "ihd,jhd->ihj", projected_queries, projected_keys, preferred_element_type=jnp.float32
    )
    scores = scores * score_scale + bias_all.astype(jnp.float32) + key_mask
    maxima = jnp.max(scores, axis=-1)
    weights = jnp.exp(scores - maxima[..., None])
    totals = jnp.sum(weights, axis=-1)
    summed = jnp.einsum(
        "ihj,jhd->ihd",
        weights.astype(jnp.bfloat16),
        projected_values,
        preferred_element_type=jnp.float32,
    )
    return (maxima, totals, summed.reshape(summed.shape[0], -1))


def on_device_general(
    alignment_rows,
    pair_state,
    update_cotangent,
    sequence_mask,
    residue_mask,
    left_weight,
    right_weight,
    outer_weight,
    bias_weight,
    query_weight,
    key_weight,
    value_weight,
    gate_weight,
    output_weight,
):
    sequence_wise, residue_half, channel_count = alignment_rows.shape
    rows_here = pair_state.shape[0]
    residues = residue_mask.shape[0]
    head_count = bias_weight.shape[1]
    head_dim = channel_count // head_count
    score_scale = head_dim ** (-0.5)
    row_index = lax.axis_index("row")
    col_index = lax.axis_index("col")
    complete_alignment, complete_cotangent = (
        lax.all_gather(alignment_rows, "col", axis=1, tiled=True),
        lax.all_gather(update_cotangent, "col", axis=1, tiled=True),
    )
    seq_live = sequence_mask.astype(jnp.float32)
    res_live = residue_mask.astype(jnp.float32)
    own_seq = lax.dynamic_slice_in_dim(seq_live, row_index * sequence_wise, sequence_wise)
    own_cols = lax.dynamic_slice_in_dim(res_live, col_index * residue_half, residue_half)
    own_rows = lax.dynamic_slice_in_dim(res_live, row_index * rows_here, rows_here)
    normalized_input = layer_normalize(complete_alignment).astype(jnp.bfloat16)
    flat_rows = normalized_input.reshape(-1, channel_count)
    normed_half = lax.dynamic_slice_in_dim(
        normalized_input, col_index * residue_half, residue_half, 1
    )
    half_rows = normed_half.reshape(-1, channel_count)
    left_proj = jnp.dot(flat_rows, left_weight, preferred_element_type=jnp.float32).reshape(
        sequence_wise, residues, -1
    )
    left_proj = (left_proj * (own_seq[:, None] * res_live[None, :])[..., None]).astype(jnp.bfloat16)
    right_proj = jnp.dot(half_rows, right_weight, preferred_element_type=jnp.float32).reshape(
        sequence_wise, residue_half, -1
    )
    right_proj = (right_proj * (own_seq[:, None] * own_cols[None, :])[..., None]).astype(
        jnp.bfloat16
    )
    left_tile = lax.all_to_all(left_proj, "row", split_axis=1, concat_axis=0, tiled=True)
    right_all = spread_all(right_proj)
    outer_width = left_tile.shape[2]
    outer_sum = lax.dot_general(
        left_tile.reshape(left_tile.shape[0], -1),
        right_all.reshape(right_all.shape[0], -1),
        (((0,), (0,)), ((), ())),
        preferred_element_type=jnp.float32,
    )
    outer_half = outer_sum.astype(jnp.bfloat16).reshape(
        rows_here, outer_width, residue_half, outer_width
    )
    opm_update = jnp.einsum(
        "ipjq,pqz->ijz", outer_half, outer_weight, preferred_element_type=jnp.float32
    )
    divisor = jnp.maximum(jnp.sum(seq_live) * own_rows[:, None] * own_cols[None, :], 1.0)
    pair_updated = (pair_state.astype(jnp.float32) + opm_update / divisor[..., None]).astype(
        jnp.bfloat16
    )
    pair_normed = layer_normalize(pair_updated).astype(jnp.bfloat16)
    bias_tile = jnp.einsum(
        "ijz,zh->ihj", pair_normed, bias_weight, preferred_element_type=jnp.float32
    ).astype(jnp.bfloat16)
    projected_queries = (
        jnp.dot(flat_rows, query_weight, preferred_element_type=jnp.float32)
        .astype(jnp.bfloat16)
        .reshape(sequence_wise, residues, head_count, head_dim)
    )
    gate_activations = jax.nn.sigmoid(
        jnp.dot(flat_rows, gate_weight, preferred_element_type=jnp.float32)
    ).reshape(sequence_wise, residues, channel_count)
    key_live = (res_live - 1.0) * mask_fill
    half_live = lax.dynamic_slice_in_dim(key_live, col_index * residue_half, residue_half)
    bias_cols = lax.all_gather(bias_tile, "col", axis=2, tiled=True)
    bias_all = spread_all(bias_cols)
    key_count = bias_all.shape[2]
    projected_keys = (
        jnp.dot(flat_rows, key_weight, preferred_element_type=jnp.float32)
        .astype(jnp.bfloat16)
        .reshape(sequence_wise, key_count, head_count, head_dim)
    )
    projected_values = (
        jnp.dot(flat_rows, value_weight, preferred_element_type=jnp.float32)
        .astype(jnp.bfloat16)
        .reshape(sequence_wise, key_count, head_count, head_dim)
    )
    maxima, totals, summed = lax.map(
        lambda inputs: attend_partial(
            inputs[0], inputs[1], inputs[2], bias_all, key_live, score_scale
        ),
        (projected_queries, projected_keys, projected_values),
    )
    attended = summed / jnp.repeat(totals, head_dim, axis=-1)
    gated = gate_activations * attended
    gated_own = lax.dynamic_slice_in_dim(gated, col_index * residue_half, residue_half, 1).astype(
        jnp.bfloat16
    )
    alignment_update = (
        jnp.dot(
            gated_own.reshape(-1, channel_count), output_weight, preferred_element_type=jnp.float32
        )
        .astype(jnp.bfloat16)
        .reshape(sequence_wise, residue_half, channel_count)
    )
    d_gated = lax.dot_general(
        complete_cotangent.reshape(-1, channel_count),
        output_weight,
        (((1,), (1,)), ((), ())),
        preferred_element_type=jnp.float32,
    ).reshape(sequence_wise, residues, channel_count)
    d_attended = d_gated * gate_activations
    delta_sum = jnp.sum(
        (d_attended * attended).reshape(sequence_wise, residues, head_count, head_dim), axis=-1
    )
    d_rounded = d_attended.astype(jnp.bfloat16).reshape(
        sequence_wise, residues, head_count, head_dim
    )
    log_total = maxima + jnp.log(totals)
    keys_half = lax.dynamic_slice_in_dim(projected_keys, col_index * residue_half, residue_half, 1)
    values_half = lax.dynamic_slice_in_dim(
        projected_values, col_index * residue_half, residue_half, 1
    )
    bias_half = lax.dynamic_slice_in_dim(bias_all, col_index * residue_half, residue_half, 2)
    bias_rows = bias_half.astype(jnp.float32)

    def single_sequence(running, sequence_items):
        query_rows, d_rows, total_rows, delta_rows, keys_one, values_one = sequence_items
        scores = jnp.einsum(
            "ihd,jhd->ihj", query_rows, keys_one, preferred_element_type=jnp.float32
        )
        scores = scores * score_scale + bias_rows + half_live
        probs = jnp.exp(scores - total_rows[..., None])
        d_weights = jnp.einsum(
            "ihd,jhd->ihj", d_rows, values_one, preferred_element_type=jnp.float32
        )
        return (running + probs * (d_weights - delta_rows[..., None]), None)

    sequence_items = (projected_queries, d_rounded, log_total, delta_sum, keys_half, values_half)
    initial_value = jnp.zeros(
        (rows_here * lax.axis_size("row"), head_count, residue_half), jnp.float32
    )
    result, unused = lax.scan(single_sequence, initial_value, sequence_items)
    shares = lax.all_to_all(
        result.astype(jnp.bfloat16).reshape((-1,) + (rows_here,) + result.shape[1:]),
        "row",
        split_axis=0,
        concat_axis=0,
        tiled=True,
    )
    bias_gradient = jnp.sum(shares.astype(jnp.float32), axis=0)
    d_normed = jnp.einsum(
        "ihj,zh->ijz",
        bias_gradient,
        bias_weight.astype(jnp.float32),
        precision=lax.Precision.HIGHEST,
    )
    pair_gradient = norm_backward(pair_updated, d_normed)
    return (alignment_update, pair_updated, pair_gradient)


LANES = 128
LEFT_ROWS = 4
STRIDE = 40
f32 = jnp.float32
bf16 = jnp.bfloat16


def dot_nn(a, b):
    return lax.dot_general(a, b, (((1,), (0,)), ((), ())), preferred_element_type=f32)


def dot_nt(a, b):
    return lax.dot_general(a, b, (((1,), (1,)), ((), ())), preferred_element_type=f32)


def dot_tn(a, b):
    return lax.dot_general(a, b, (((0,), (0,)), ((), ())), preferred_element_type=f32)


def lane_index(rows):
    return lax.broadcasted_iota(jnp.int32, (rows, LANES), 1)


def factors_kernel(seq_ref, res_ref, rows_ref, left_ref, right_ref, send_ref, normed_ref, left_scr):
    seqs = send_ref.shape[2] // 18
    residues = res_ref.shape[1]
    chips = send_ref.shape[0]
    me = lax.axis_index("row")
    normed = layer_normalize(rows_ref[...]).astype(bf16)
    normed_ref[...] = normed
    live = res_ref[...].astype(f32)
    live_rows = jnp.broadcast_to(live, (residues, residues)).T
    right_t = right_ref[...]
    left_wide = jnp.concatenate([left_ref[...]] * 4, axis=0)
    low = lane_index(16) < 64
    lane_group = lane_index(chips) // 32
    halves = ([], [])
    tail = []
    for s in range(seqs):
        seq_live = seq_ref[me * seqs + s].astype(f32)
        own = normed[s * residues : (s + 1) * residues]
        factor = dot_nt(right_t, own) * (live * seq_live)
        first, second = factor[:16], factor[16:]
        halves[0].append(jnp.where(low, first, pltpu.roll(second, 64, 1)))
        halves[1].append(jnp.where(low, pltpu.roll(first, 64, 1), second))
        left_scr[...] = dot_nt(own, left_wide) * (live_rows * seq_live)
        for a in range(2):
            row = jnp.zeros((chips, LANES), f32)
            for b in range(4):
                part = left_scr[pl.ds(4 * a + b, chips, stride=8), :]
                row = jnp.where(lane_group == b, part, row)
            tail.append(row)
    tail = jnp.stack(tail, axis=1).astype(bf16)
    right_rows = 16 * seqs
    for core in range(2):
        block = jnp.concatenate(halves[core], axis=0).astype(bf16)
        send_ref[:, core, :right_rows, :] = jnp.broadcast_to(block[None], (chips, right_rows, LANES))
        send_ref[:, core, right_rows:, :] = tail


def by_head(rows, heads):
    channels = rows.shape[1]
    head_of = lax.broadcasted_iota(jnp.int32, (1, channels), 1) // (channels // heads)
    return jnp.concatenate(
        [jnp.where(head_of == h, rows, jnp.zeros((), rows.dtype)) for h in range(heads)], axis=0
    )


def projections_kernel(
    heads, scale, normed_ref, cot_ref, wq_ref, wk_ref, wv_ref, wg_ref, wo_ref, score_ref, flow_ref, v_ref, gate_ref
):
    seqs, _, residues = score_ref.shape
    normed = normed_ref[...]
    queries = dot_nn(normed, wq_ref[...]).astype(bf16)
    keys = dot_nn(normed, wk_ref[...]).astype(bf16)
    values = dot_nn(normed, wv_ref[...]).astype(bf16)
    gate = jax.nn.sigmoid(dot_nn(normed, wg_ref[...]))
    d_rounded = (dot_nt(cot_ref[...], wo_ref[...]) * gate).astype(bf16)
    v_ref[...] = values
    gate_ref[...] = gate
    for s in range(seqs):
        at = slice(s * residues, (s + 1) * residues)
        score_ref[s] = dot_nt(by_head(queries[at], heads), keys[at]) * scale
        flow_ref[s] = dot_nt(by_head(d_rounded[at], heads), values[at])


def pair_kernel(recv_ref, weight_ref, pair_ref, div_ref, bias_w_ref, send_ref, updated_ref, flat, rbuf, lbuf, obuf):
    peers, block_rows, _ = recv_ref.shape
    seqs = block_rows // 18
    for p in range(peers):
        flat[p * STRIDE : p * STRIDE + block_rows, :] = recv_ref[p].astype(f32)
    for s in range(seqs):
        for g in range(16):
            part = flat[pl.ds(s * 16 + g, peers, stride=STRIDE), :]
            rbuf[s * peers : (s + 1) * peers, g * LANES : (g + 1) * LANES] = part.astype(bf16)
        for a in range(2):
            part = flat[pl.ds(16 * seqs + 2 * s + a, peers, stride=STRIDE), :]
            lbuf[s * peers : (s + 1) * peers, a * LANES : (a + 1) * LANES] = part.astype(bf16)
    left_t = lbuf[...].astype(f32).T.astype(bf16)
    for g in range(16):
        outer = dot_nn(left_t, rbuf[:, g * LANES : (g + 1) * LANES]).astype(bf16)
        for i in range(8):
            obuf[g * 32 : (g + 1) * 32, i * LANES : (i + 1) * LANES] = outer[i * 32 : (i + 1) * 32]
    sums = dot_nn(weight_ref[...], obuf[...])
    low = lane_index(LANES) < 64

    def piece(a, i):
        return sums[a * LANES : (a + 1) * LANES, i * LANES : (i + 1) * LANES]

    blocks = []
    bias_w = bias_w_ref[...]
    for b in range(4):
        straight = jnp.where(low, piece(0, b), piece(1, b + 4))
        crossed = jnp.where(low, piece(0, b + 4), piece(1, b))
        update = (straight + pltpu.roll(crossed, 64, 1)) / div_ref[b : b + 1, :]
        state = jnp.concatenate([pair_ref[b], pair_ref[b + 4]], axis=0).astype(f32)
        updated = (state + update.T).astype(bf16)
        updated_ref[b] = updated[:64]
        updated_ref[b + 4] = updated[64:]
        pair_normed = layer_normalize(updated).astype(bf16)
        blocks.append(dot_nt(bias_w, pair_normed))
    block = jnp.concatenate(blocks, axis=0).astype(bf16)
    send_ref[...] = jnp.broadcast_to(block[None], send_ref.shape)


def placed_bias(flat, res_ref, heads, h):
    residues = res_ref.shape[1]
    sub = lax.broadcasted_iota(jnp.int32, (residues, LANES), 0) % 8
    keep = (sub < 4) == (lane_index(residues) < 64)
    raw = flat[pl.ds(h, residues, stride=heads), :]
    moved = jnp.where(sub < 4, pltpu.roll(raw, residues - 4, 0), pltpu.roll(raw, 4, 0))
    key_mask = (res_ref[...].astype(f32) - 1.0) * mask_fill
    return jnp.where(keep, raw, pltpu.roll(moved, 64, 1)) + key_mask


def bias_gradient_kernel(bias_ref, res_ref, score_ref, flow_ref, send_ref, full_ref, flat, grads):
    seqs, rows, residues = score_ref.shape
    heads = rows // residues
    flat[...] = bias_ref[...].reshape(flat.shape).astype(f32)
    ones = jnp.ones((residues, LANES), bf16)
    for h in range(heads):
        at = slice(h * residues, (h + 1) * residues)
        bias = placed_bias(flat, res_ref, heads, h)
        full_ref[at, :] = bias
        total = jnp.zeros((residues, residues), f32)
        for s in range(seqs):
            scores = score_ref[s, at, :] + bias
            weights = jnp.exp(scores - jnp.max(scores, axis=-1, keepdims=True))
            flow = flow_ref[s, at, :]
            inverse = 1.0 / dot_nn(weights.astype(bf16), ones)
            delta = dot_nn((weights * flow).astype(bf16), ones) * inverse
            total = total + weights * inverse * (flow - delta)
        grads[pl.ds(h, residues, stride=heads), :] = total
    send_ref[...] = grads[...].astype(bf16).reshape(send_ref.shape)


def output_kernel(score_ref, full_ref, v_ref, gate_ref, wo_ref, out_ref):
    seqs, rows, residues = score_ref.shape
    heads = rows // residues
    channels = v_ref.shape[1]
    head_of = lax.broadcasted_iota(jnp.int32, (1, channels), 1) // (channels // heads)
    ones = jnp.ones((residues, LANES), bf16)
    for s in range(seqs):
        own = slice(s * residues, (s + 1) * residues)
        attended = jnp.zeros((residues, channels), f32)
        for h in range(heads):
            at = slice(h * residues, (h + 1) * residues)
            scores = score_ref[s, at, :] + full_ref[at, :]
            weights = jnp.exp(scores - jnp.max(scores, axis=-1, keepdims=True))
            total = jnp.sum(weights, axis=-1, keepdims=True)
            mixed = dot_nn(weights.astype(bf16), v_ref[own, :]) / total
            attended = jnp.where(head_of == h, mixed, attended)
        gated = (gate_ref[own, :] * attended).astype(bf16)
        out_ref[own, :] = dot_nn(gated, wo_ref[...]).astype(bf16)


def gradient_kernel(shares_ref, bias_w_ref, pair_ref, out_ref):
    total = jnp.sum(shares_ref[...].astype(f32), axis=0)
    rows = pair_ref.shape[0]
    heads = total.shape[0] // rows
    bias_w = bias_w_ref[...].astype(f32)
    for i in range(rows):
        own = total[i * heads : (i + 1) * heads]
        upstream = lax.dot_general(
            own, bias_w, (((0,), (0,)), ((), ())), precision=lax.Precision.HIGHEST, preferred_element_type=f32
        )
        out_ref[i] = norm_backward(pair_ref[i], upstream)


def kernel_call(body, out_shape, in_specs=None, scratch=(), flops=0, moved=0):
    vmem = pl.BlockSpec(memory_space=pltpu.VMEM)
    many = isinstance(out_shape, (list, tuple))
    return pl.pallas_call(
        body,
        out_shape=out_shape,
        in_specs=in_specs,
        out_specs=[vmem] * len(out_shape) if many else vmem,
        scratch_shapes=list(scratch),
        compiler_params=pltpu.CompilerParams(vmem_limit_bytes=24 * 1024 * 1024),
        cost_estimate=pl.CostEstimate(flops=flops, bytes_accessed=moved, transcendentals=0),
    )


def on_device_paired(
    alignment_rows,
    pair_state,
    update_cotangent,
    sequence_mask,
    residue_mask,
    left_weight,
    right_weight,
    outer_weight,
    bias_weight,
    query_weight,
    key_weight,
    value_weight,
    gate_weight,
    output_weight,
):
    sequence_wise, residues, channel_count = alignment_rows.shape
    rows_here, _, pair_channels = pair_state.shape
    head_count = bias_weight.shape[1]
    peers = lax.axis_size("row")
    factor = left_weight.shape[1]
    chips = peers // 2
    vmem = pl.BlockSpec(memory_space=pltpu.VMEM)
    smem = pl.BlockSpec(memory_space=pltpu.SMEM)
    me = lax.axis_index("row")
    core = me % 2
    sibling = [(i, i ^ 1) for i in range(peers)]
    token_rows = sequence_wise * residues
    half = residues // 2
    block_rows = sequence_wise * 18
    res_row = residue_mask.reshape(1, residues)
    flat_rows = alignment_rows.reshape(token_rows, channel_count)
    shape = jax.ShapeDtypeStruct

    send, normed = kernel_call(
        factors_kernel,
        [shape((chips, 2, block_rows, LANES), bf16), shape((token_rows, channel_count), bf16)],
        [smem, vmem, vmem, vmem, vmem],
        [pltpu.VMEM((residues, LANES), f32)],
        flops=2 * token_rows * channel_count * LANES,
        moved=1 << 19,
    )(sequence_mask, res_row, flat_rows, left_weight.T, right_weight.T)
    received = lax.all_to_all(
        send.reshape(peers, block_rows, LANES), "row", split_axis=0, concat_axis=0, tiled=True
    )

    head_rows = head_count * residues
    scale = (channel_count // head_count) ** (-0.5)
    scores, flow, values, gate = kernel_call(
        lambda *refs: projections_kernel(head_count, scale, *refs),
        [
            shape((sequence_wise, head_rows, residues), f32),
            shape((sequence_wise, head_rows, residues), f32),
            shape((token_rows, channel_count), bf16),
            shape((token_rows, channel_count), f32),
        ],
        [vmem] * 7,
        flops=10 * token_rows * channel_count * channel_count,
        moved=1 << 22,
    )(
        normed,
        update_cotangent.reshape(token_rows, channel_count),
        query_weight,
        key_weight,
        value_weight,
        gate_weight,
        output_weight,
    )

    def trade_columns(tile):
        kept = lax.dynamic_slice_in_dim(tile, core * half, half, 1)
        got = lax.ppermute(lax.dynamic_slice_in_dim(tile, (1 - core) * half, half, 1), "row", sibling)
        return jnp.where(core == 0, jnp.concatenate([kept, got]), jnp.concatenate([got, kept]))

    def trade_rows(tile):
        kept = lax.dynamic_slice_in_dim(tile, core * rows_here, rows_here, 0)
        got = lax.ppermute(
            lax.dynamic_slice_in_dim(tile, (1 - core) * rows_here, rows_here, 0), "row", sibling
        )
        return jnp.where(
            core == 0, jnp.concatenate([kept, got], axis=1), jnp.concatenate([got, kept], axis=1)
        )

    pair_tile = trade_columns(pair_state)
    weight_t = (
        outer_weight.reshape(factor, 2, 16, pair_channels)
        .transpose(1, 3, 2, 0)
        .reshape(2 * pair_channels, 16 * factor)
    )
    seq_live = sequence_mask.astype(f32)
    res_live = residue_mask.astype(f32)
    tile_rows = lax.dynamic_slice_in_dim(res_live, (me // 2) * 8, 8).reshape(2, 4)
    tile_cols = lax.dynamic_slice_in_dim(res_live, core * half, half)
    divisor = jnp.maximum(
        jnp.sum(seq_live) * tile_rows.T[:, :, None] * tile_cols[None, None, :], 1.0
    ).reshape(4, 2 * half)
    bias_rows = 4 * head_count
    send_bias, updated_tile = kernel_call(
        pair_kernel,
        [shape((peers, bias_rows, LANES), bf16), shape((8, half, pair_channels), bf16)],
        [vmem] * 5,
        [
            pltpu.VMEM((peers * STRIDE, LANES), f32),
            pltpu.VMEM((peers * sequence_wise, 16 * LANES), bf16),
            pltpu.VMEM((peers * sequence_wise, 2 * LANES), bf16),
            pltpu.VMEM((16 * factor, 8 * LANES), bf16),
        ],
        flops=1 << 29,
        moved=1 << 20,
    )(received, weight_t, pair_tile, divisor, bias_weight.T)
    bias_all = lax.all_to_all(send_bias, "row", split_axis=0, concat_axis=0, tiled=True)
    pair_updated = trade_rows(updated_tile)

    send_grad, full_bias = kernel_call(
        bias_gradient_kernel,
        [shape((peers, rows_here * head_count, LANES), bf16), shape((head_rows, residues), f32)],
        [vmem] * 4,
        [pltpu.VMEM((head_rows, LANES), f32), pltpu.VMEM((head_rows, LANES), f32)],
        flops=1 << 28,
        moved=1 << 22,
    )(bias_all, res_row, scores, flow)
    shares = lax.all_to_all(send_grad, "row", split_axis=0, concat_axis=0, tiled=True)
    update = kernel_call(
        output_kernel,
        shape((token_rows, channel_count), bf16),
        [vmem] * 5,
        flops=1 << 29,
        moved=1 << 22,
    )(scores, full_bias, values, gate, output_weight)
    pair_gradient = kernel_call(
        gradient_kernel,
        shape((rows_here, residues, pair_channels), f32),
        [vmem] * 3,
        flops=1 << 24,
        moved=1 << 20,
    )(shares, bias_weight.T, pair_updated)
    return (update.reshape(alignment_rows.shape), pair_updated, pair_gradient)


def solution(mesh):
    placed = (
        P(("grp", "row"), "col", None),
        P(("grp", "row"), "col", None),
        P(("grp", "row"), "col", None),
        P("grp"),
        P("grp"),
        P(),
        P(),
        P(),
        P(),
        P(),
        P(),
        P(),
        P(),
        P(),
    )
    one_column = mesh.shape["col"] == 1 and mesh.shape["row"] % 2 == 0
    return jax.shard_map(
        on_device_paired if one_column else on_device_general,
        mesh=mesh,
        in_specs=placed,
        out_specs=(
            P(("grp", "row"), "col", None),
            P(("grp", "row"), "col", None),
            P(("grp", "row"), "col", None),
        ),
        check_vma=False,
    )
```

```python
import jax
import jax.numpy as jnp
from jax import lax
from jax.experimental import pallas as pl
from jax.experimental.pallas import tpu as pltpu
from jax.sharding import PartitionSpec as P

norm_eps = 1e-05
mask_fill = 1000000000.0


def layer_normalize(values):
    values = values.astype(jnp.float32)
    center = values - jnp.mean(values, axis=-1, keepdims=True)
    spread = jnp.mean(center * center, axis=-1, keepdims=True)
    return center * lax.rsqrt(spread + norm_eps)


def norm_backward(values, upstream):
    values = values.astype(jnp.float32)
    center = values - jnp.mean(values, axis=-1, keepdims=True)
    inverse = lax.rsqrt(jnp.mean(center * center, axis=-1, keepdims=True) + norm_eps)
    normal_part = center * inverse
    return inverse * (
        upstream
        - jnp.mean(upstream, axis=-1, keepdims=True)
        - normal_part * jnp.mean(upstream * normal_part, axis=-1, keepdims=True)
    )


def spread_all(shard):
    copies = jnp.broadcast_to(shard[None], (lax.axis_size("row"),) + shard.shape)
    gathered = lax.all_to_all(copies, "row", split_axis=0, concat_axis=0, tiled=True)
    return gathered.reshape((-1,) + shard.shape[1:])


def attend_partial(
    projected_queries, projected_keys, projected_values, bias_all, key_mask, score_scale
):
    scores = jnp.einsum(
        "ihd,jhd->ihj", projected_queries, projected_keys, preferred_element_type=jnp.float32
    )
    scores = scores * score_scale + bias_all.astype(jnp.float32) + key_mask
    maxima = jnp.max(scores, axis=-1)
    weights = jnp.exp(scores - maxima[..., None])
    totals = jnp.sum(weights, axis=-1)
    summed = jnp.einsum(
        "ihj,jhd->ihd",
        weights.astype(jnp.bfloat16),
        projected_values,
        preferred_element_type=jnp.float32,
    )
    return (maxima, totals, summed.reshape(summed.shape[0], -1))


def on_device_general(
    alignment_rows,
    pair_state,
    update_cotangent,
    sequence_mask,
    residue_mask,
    left_weight,
    right_weight,
    outer_weight,
    bias_weight,
    query_weight,
    key_weight,
    value_weight,
    gate_weight,
    output_weight,
):
    sequence_wise, residue_half, channel_count = alignment_rows.shape
    rows_here = pair_state.shape[0]
    residues = residue_mask.shape[0]
    head_count = bias_weight.shape[1]
    head_dim = channel_count // head_count
    score_scale = head_dim ** (-0.5)
    row_index = lax.axis_index("row")
    col_index = lax.axis_index("col")
    complete_alignment, complete_cotangent = (
        lax.all_gather(alignment_rows, "col", axis=1, tiled=True),
        lax.all_gather(update_cotangent, "col", axis=1, tiled=True),
    )
    seq_live = sequence_mask.astype(jnp.float32)
    res_live = residue_mask.astype(jnp.float32)
    own_seq = lax.dynamic_slice_in_dim(seq_live, row_index * sequence_wise, sequence_wise)
    own_cols = lax.dynamic_slice_in_dim(res_live, col_index * residue_half, residue_half)
    own_rows = lax.dynamic_slice_in_dim(res_live, row_index * rows_here, rows_here)
    normalized_input = layer_normalize(complete_alignment).astype(jnp.bfloat16)
    flat_rows = normalized_input.reshape(-1, channel_count)
    normed_half = lax.dynamic_slice_in_dim(
        normalized_input, col_index * residue_half, residue_half, 1
    )
    half_rows = normed_half.reshape(-1, channel_count)
    left_proj = jnp.dot(flat_rows, left_weight, preferred_element_type=jnp.float32).reshape(
        sequence_wise, residues, -1
    )
    left_proj = (left_proj * (own_seq[:, None] * res_live[None, :])[..., None]).astype(jnp.bfloat16)
    right_proj = jnp.dot(half_rows, right_weight, preferred_element_type=jnp.float32).reshape(
        sequence_wise, residue_half, -1
    )
    right_proj = (right_proj * (own_seq[:, None] * own_cols[None, :])[..., None]).astype(
        jnp.bfloat16
    )
    left_tile = lax.all_to_all(left_proj, "row", split_axis=1, concat_axis=0, tiled=True)
    right_all = spread_all(right_proj)
    outer_width = left_tile.shape[2]
    outer_sum = lax.dot_general(
        left_tile.reshape(left_tile.shape[0], -1),
        right_all.reshape(right_all.shape[0], -1),
        (((0,), (0,)), ((), ())),
        preferred_element_type=jnp.float32,
    )
    outer_half = outer_sum.astype(jnp.bfloat16).reshape(
        rows_here, outer_width, residue_half, outer_width
    )
    opm_update = jnp.einsum(
        "ipjq,pqz->ijz", outer_half, outer_weight, preferred_element_type=jnp.float32
    )
    divisor = jnp.maximum(jnp.sum(seq_live) * own_rows[:, None] * own_cols[None, :], 1.0)
    pair_updated = (pair_state.astype(jnp.float32) + opm_update / divisor[..., None]).astype(
        jnp.bfloat16
    )
    pair_normed = layer_normalize(pair_updated).astype(jnp.bfloat16)
    bias_tile = jnp.einsum(
        "ijz,zh->ihj", pair_normed, bias_weight, preferred_element_type=jnp.float32
    ).astype(jnp.bfloat16)
    projected_queries = (
        jnp.dot(flat_rows, query_weight, preferred_element_type=jnp.float32)
        .astype(jnp.bfloat16)
        .reshape(sequence_wise, residues, head_count, head_dim)
    )
    gate_activations = jax.nn.sigmoid(
        jnp.dot(flat_rows, gate_weight, preferred_element_type=jnp.float32)
    ).reshape(sequence_wise, residues, channel_count)
    key_live = (res_live - 1.0) * mask_fill
    half_live = lax.dynamic_slice_in_dim(key_live, col_index * residue_half, residue_half)
    bias_cols = lax.all_gather(bias_tile, "col", axis=2, tiled=True)
    bias_all = spread_all(bias_cols)
    key_count = bias_all.shape[2]
    projected_keys = (
        jnp.dot(flat_rows, key_weight, preferred_element_type=jnp.float32)
        .astype(jnp.bfloat16)
        .reshape(sequence_wise, key_count, head_count, head_dim)
    )
    projected_values = (
        jnp.dot(flat_rows, value_weight, preferred_element_type=jnp.float32)
        .astype(jnp.bfloat16)
        .reshape(sequence_wise, key_count, head_count, head_dim)
    )
    maxima, totals, summed = lax.map(
        lambda inputs: attend_partial(
            inputs[0], inputs[1], inputs[2], bias_all, key_live, score_scale
        ),
        (projected_queries, projected_keys, projected_values),
    )
    attended = summed / jnp.repeat(totals, head_dim, axis=-1)
    gated = gate_activations * attended
    gated_own = lax.dynamic_slice_in_dim(gated, col_index * residue_half, residue_half, 1).astype(
        jnp.bfloat16
    )
    alignment_update = (
        jnp.dot(
            gated_own.reshape(-1, channel_count), output_weight, preferred_element_type=jnp.float32
        )
        .astype(jnp.bfloat16)
        .reshape(sequence_wise, residue_half, channel_count)
    )
    d_gated = lax.dot_general(
        complete_cotangent.reshape(-1, channel_count),
        output_weight,
        (((1,), (1,)), ((), ())),
        preferred_element_type=jnp.float32,
    ).reshape(sequence_wise, residues, channel_count)
    d_attended = d_gated * gate_activations
    delta_sum = jnp.sum(
        (d_attended * attended).reshape(sequence_wise, residues, head_count, head_dim), axis=-1
    )
    d_rounded = d_attended.astype(jnp.bfloat16).reshape(
        sequence_wise, residues, head_count, head_dim
    )
    log_total = maxima + jnp.log(totals)
    keys_half = lax.dynamic_slice_in_dim(projected_keys, col_index * residue_half, residue_half, 1)
    values_half = lax.dynamic_slice_in_dim(
        projected_values, col_index * residue_half, residue_half, 1
    )
    bias_half = lax.dynamic_slice_in_dim(bias_all, col_index * residue_half, residue_half, 2)
    bias_rows = bias_half.astype(jnp.float32)

    def single_sequence(running, sequence_items):
        query_rows, d_rows, total_rows, delta_rows, keys_one, values_one = sequence_items
        scores = jnp.einsum(
            "ihd,jhd->ihj", query_rows, keys_one, preferred_element_type=jnp.float32
        )
        scores = scores * score_scale + bias_rows + half_live
        probs = jnp.exp(scores - total_rows[..., None])
        d_weights = jnp.einsum(
            "ihd,jhd->ihj", d_rows, values_one, preferred_element_type=jnp.float32
        )
        return (running + probs * (d_weights - delta_rows[..., None]), None)

    sequence_items = (projected_queries, d_rounded, log_total, delta_sum, keys_half, values_half)
    initial_value = jnp.zeros(
        (rows_here * lax.axis_size("row"), head_count, residue_half), jnp.float32
    )
    result, unused = lax.scan(single_sequence, initial_value, sequence_items)
    shares = lax.all_to_all(
        result.astype(jnp.bfloat16).reshape((-1,) + (rows_here,) + result.shape[1:]),
        "row",
        split_axis=0,
        concat_axis=0,
        tiled=True,
    )
    bias_gradient = jnp.sum(shares.astype(jnp.float32), axis=0)
    d_normed = jnp.einsum(
        "ihj,zh->ijz",
        bias_gradient,
        bias_weight.astype(jnp.float32),
        precision=lax.Precision.HIGHEST,
    )
    pair_gradient = norm_backward(pair_updated, d_normed)
    return (alignment_update, pair_updated, pair_gradient)


LANES = 128
LEFT_ROWS = 4
STRIDE = 40
f32 = jnp.float32
bf16 = jnp.bfloat16


def dot_nn(a, b):
    return lax.dot_general(a, b, (((1,), (0,)), ((), ())), preferred_element_type=f32)


def dot_nt(a, b):
    return lax.dot_general(a, b, (((1,), (1,)), ((), ())), preferred_element_type=f32)


def dot_tn(a, b):
    return lax.dot_general(a, b, (((0,), (0,)), ((), ())), preferred_element_type=f32)


def lane_index(rows):
    return lax.broadcasted_iota(jnp.int32, (rows, LANES), 1)


def factors_kernel(seq_ref, res_ref, rows_ref, left_ref, right_ref, send_ref, normed_ref, left_scr):
    seqs = send_ref.shape[2] // 18
    residues = res_ref.shape[1]
    chips = send_ref.shape[0]
    me = lax.axis_index("row")
    normed = layer_normalize(rows_ref[...]).astype(bf16)
    normed_ref[...] = normed
    live = res_ref[...].astype(f32)
    live_rows = jnp.broadcast_to(live, (residues, residues)).T
    right_t = right_ref[...]
    left_wide = jnp.concatenate([left_ref[...]] * 4, axis=0)
    low = lane_index(16) < 64
    lane_group = lane_index(chips) // 32
    halves = ([], [])
    tail = []
    for s in range(seqs):
        seq_live = seq_ref[me * seqs + s].astype(f32)
        own = normed[s * residues : (s + 1) * residues]
        factor = dot_nt(right_t, own) * (live * seq_live)
        first, second = factor[:16], factor[16:]
        halves[0].append(jnp.where(low, first, pltpu.roll(second, 64, 1)))
        halves[1].append(jnp.where(low, pltpu.roll(first, 64, 1), second))
        left_scr[...] = dot_nt(own, left_wide) * (live_rows * seq_live)
        for a in range(2):
            row = jnp.zeros((chips, LANES), f32)
            for b in range(4):
                part = left_scr[pl.ds(4 * a + b, chips, stride=8), :]
                row = jnp.where(lane_group == b, part, row)
            tail.append(row)
    tail = jnp.stack(tail, axis=1).astype(bf16)
    right_rows = 16 * seqs
    for core in range(2):
        block = jnp.concatenate(halves[core], axis=0).astype(bf16)
        send_ref[:, core, :right_rows, :] = jnp.broadcast_to(block[None], (chips, right_rows, LANES))
        send_ref[:, core, right_rows:, :] = tail


def by_head(rows, heads):
    channels = rows.shape[1]
    head_of = lax.broadcasted_iota(jnp.int32, (1, channels), 1) // (channels // heads)
    return jnp.concatenate(
        [jnp.where(head_of == h, rows, jnp.zeros((), rows.dtype)) for h in range(heads)], axis=0
    )


def projections_kernel(
    heads, scale, normed_ref, cot_ref, wq_ref, wk_ref, wv_ref, wg_ref, wo_ref, score_ref, flow_ref, v_ref, gate_ref
):
    seqs, _, residues = score_ref.shape
    normed = normed_ref[...]
    queries = dot_nn(normed, wq_ref[...]).astype(bf16)
    keys = dot_nn(normed, wk_ref[...]).astype(bf16)
    values = dot_nn(normed, wv_ref[...]).astype(bf16)
    gate = jax.nn.sigmoid(dot_nn(normed, wg_ref[...]))
    d_rounded = (dot_nt(cot_ref[...], wo_ref[...]) * gate).astype(bf16)
    v_ref[...] = values
    gate_ref[...] = gate
    for s in range(seqs):
        at = slice(s * residues, (s + 1) * residues)
        score_ref[s] = dot_nt(by_head(queries[at], heads), keys[at]) * scale
        flow_ref[s] = dot_nt(by_head(d_rounded[at], heads), values[at])


def pair_kernel(recv_ref, weight_ref, pair_ref, div_ref, bias_w_ref, send_ref, updated_ref, flat, rbuf, lbuf, obuf):
    peers, block_rows, _ = recv_ref.shape
    seqs = block_rows // 18
    for p in range(peers):
        flat[p * STRIDE : p * STRIDE + block_rows, :] = recv_ref[p].astype(f32)
    for s in range(seqs):
        for g in range(16):
            part = flat[pl.ds(s * 16 + g, peers, stride=STRIDE), :]
            rbuf[s * peers : (s + 1) * peers, g * LANES : (g + 1) * LANES] = part.astype(bf16)
        for a in range(2):
            part = flat[pl.ds(16 * seqs + 2 * s + a, peers, stride=STRIDE), :]
            lbuf[s * peers : (s + 1) * peers, a * LANES : (a + 1) * LANES] = part.astype(bf16)
    left_t = lbuf[...].astype(f32).T.astype(bf16)
    for g in range(16):
        outer = dot_nn(left_t, rbuf[:, g * LANES : (g + 1) * LANES]).astype(bf16)
        for i in range(8):
            obuf[g * 32 : (g + 1) * 32, i * LANES : (i + 1) * LANES] = outer[i * 32 : (i + 1) * 32]
    sums = dot_nn(weight_ref[...], obuf[...])
    low = lane_index(LANES) < 64

    def piece(a, i):
        return sums[a * LANES : (a + 1) * LANES, i * LANES : (i + 1) * LANES]

    blocks = []
    bias_w = bias_w_ref[...]
    for b in range(4):
        straight = jnp.where(low, piece(0, b), piece(1, b + 4))
        crossed = jnp.where(low, piece(0, b + 4), piece(1, b))
        update = (straight + pltpu.roll(crossed, 64, 1)) / div_ref[b : b + 1, :]
        state = jnp.concatenate([pair_ref[b], pair_ref[b + 4]], axis=0).astype(f32)
        updated = (state + update.T).astype(bf16)
        updated_ref[b] = updated[:64]
        updated_ref[b + 4] = updated[64:]
        pair_normed = layer_normalize(updated).astype(bf16)
        blocks.append(dot_nt(bias_w, pair_normed))
    block = jnp.concatenate(blocks, axis=0).astype(bf16)
    send_ref[...] = jnp.broadcast_to(block[None], send_ref.shape)


def placed_bias(flat, res_ref, heads, h):
    residues = res_ref.shape[1]
    sub = lax.broadcasted_iota(jnp.int32, (residues, LANES), 0) % 8
    keep = (sub < 4) == (lane_index(residues) < 64)
    raw = flat[pl.ds(h, residues, stride=heads), :]
    moved = jnp.where(sub < 4, pltpu.roll(raw, residues - 4, 0), pltpu.roll(raw, 4, 0))
    key_mask = (res_ref[...].astype(f32) - 1.0) * mask_fill
    return jnp.where(keep, raw, pltpu.roll(moved, 64, 1)) + key_mask


def bias_gradient_kernel(bias_ref, res_ref, score_ref, flow_ref, send_ref, full_ref, flat, grads):
    seqs, rows, residues = score_ref.shape
    heads = rows // residues
    flat[...] = bias_ref[...].reshape(flat.shape).astype(f32)
    ones = jnp.ones((residues, LANES), bf16)
    for h in range(heads):
        at = slice(h * residues, (h + 1) * residues)
        bias = placed_bias(flat, res_ref, heads, h)
        full_ref[at, :] = bias
        total = jnp.zeros((residues, residues), f32)
        for s in range(seqs):
            scores = score_ref[s, at, :] + bias
            weights = jnp.exp(scores - jnp.max(scores, axis=-1, keepdims=True))
            flow = flow_ref[s, at, :]
            inverse = 1.0 / dot_nn(weights.astype(bf16), ones)
            delta = dot_nn((weights * flow).astype(bf16), ones) * inverse
            total = total + weights * inverse * (flow - delta)
        grads[pl.ds(h, residues, stride=heads), :] = total
    send_ref[...] = grads[...].astype(bf16).reshape(send_ref.shape)


def output_kernel(score_ref, full_ref, v_ref, gate_ref, wo_ref, out_ref):
    seqs, rows, residues = score_ref.shape
    heads = rows // residues
    channels = v_ref.shape[1]
    head_of = lax.broadcasted_iota(jnp.int32, (1, channels), 1) // (channels // heads)
    ones = jnp.ones((residues, LANES), bf16)
    for s in range(seqs):
        own = slice(s * residues, (s + 1) * residues)
        attended = jnp.zeros((residues, channels), f32)
        for h in range(heads):
            at = slice(h * residues, (h + 1) * residues)
            scores = score_ref[s, at, :] + full_ref[at, :]
            weights = jnp.exp(scores - jnp.max(scores, axis=-1, keepdims=True))
            total = jnp.sum(weights, axis=-1, keepdims=True)
            mixed = dot_nn(weights.astype(bf16), v_ref[own, :]) / total
            attended = jnp.where(head_of == h, mixed, attended)
        gated = (gate_ref[own, :] * attended).astype(bf16)
        out_ref[own, :] = dot_nn(gated, wo_ref[...]).astype(bf16)


def gradient_kernel(shares_ref, bias_w_ref, pair_ref, out_ref):
    total = jnp.sum(shares_ref[...].astype(f32), axis=0)
    rows = pair_ref.shape[0]
    heads = total.shape[0] // rows
    bias_w = bias_w_ref[...].astype(f32)
    for i in range(rows):
        own = total[i * heads : (i + 1) * heads]
        upstream = lax.dot_general(
            own, bias_w, (((0,), (0,)), ((), ())), precision=lax.Precision.HIGHEST, preferred_element_type=f32
        )
        out_ref[i] = norm_backward(pair_ref[i], upstream)


def kernel_call(body, out_shape, in_specs=None, scratch=(), flops=0, moved=0, vmem_mib=24):
    vmem = pl.BlockSpec(memory_space=pltpu.VMEM)
    many = isinstance(out_shape, (list, tuple))
    return pl.pallas_call(
        body,
        out_shape=out_shape,
        in_specs=in_specs,
        out_specs=[vmem] * len(out_shape) if many else vmem,
        scratch_shapes=list(scratch),
        compiler_params=pltpu.CompilerParams(vmem_limit_bytes=vmem_mib * 1024 * 1024),
        cost_estimate=pl.CostEstimate(flops=flops, bytes_accessed=moved, transcendentals=0),
    )


def on_device_paired(
    alignment_rows,
    pair_state,
    update_cotangent,
    sequence_mask,
    residue_mask,
    left_weight,
    right_weight,
    outer_weight,
    bias_weight,
    query_weight,
    key_weight,
    value_weight,
    gate_weight,
    output_weight,
):
    sequence_wise, residues, channel_count = alignment_rows.shape
    rows_here, _, pair_channels = pair_state.shape
    head_count = bias_weight.shape[1]
    peers = lax.axis_size("row")
    factor = left_weight.shape[1]
    chips = peers // 2
    vmem = pl.BlockSpec(memory_space=pltpu.VMEM)
    smem = pl.BlockSpec(memory_space=pltpu.SMEM)
    me = lax.axis_index("row")
    core = me % 2
    sibling = [(i, i ^ 1) for i in range(peers)]
    token_rows = sequence_wise * residues
    half = residues // 2
    block_rows = sequence_wise * 18
    res_row = residue_mask.reshape(1, residues)
    flat_rows = alignment_rows.reshape(token_rows, channel_count)
    shape = jax.ShapeDtypeStruct

    send, normed = kernel_call(
        factors_kernel,
        [shape((chips, 2, block_rows, LANES), bf16), shape((token_rows, channel_count), bf16)],
        [smem, vmem, vmem, vmem, vmem],
        [pltpu.VMEM((residues, LANES), f32)],
        flops=2 * token_rows * channel_count * LANES,
        moved=1 << 19,
        vmem_mib=60,
    )(sequence_mask, res_row, flat_rows, left_weight.T, right_weight.T)
    received = lax.all_to_all(
        send.reshape(peers, block_rows, LANES), "row", split_axis=0, concat_axis=0, tiled=True
    )

    head_rows = head_count * residues
    scale = (channel_count // head_count) ** (-0.5)
    scores, flow, values, gate = kernel_call(
        lambda *refs: projections_kernel(head_count, scale, *refs),
        [
            shape((sequence_wise, head_rows, residues), f32),
            shape((sequence_wise, head_rows, residues), f32),
            shape((token_rows, channel_count), bf16),
            shape((token_rows, channel_count), f32),
        ],
        [vmem] * 7,
        flops=10 * token_rows * channel_count * channel_count,
        moved=1 << 22,
    )(
        normed,
        update_cotangent.reshape(token_rows, channel_count),
        query_weight,
        key_weight,
        value_weight,
        gate_weight,
        output_weight,
    )

    def trade_columns(tile):
        kept = lax.dynamic_slice_in_dim(tile, core * half, half, 1)
        got = lax.ppermute(lax.dynamic_slice_in_dim(tile, (1 - core) * half, half, 1), "row", sibling)
        return jnp.where(core == 0, jnp.concatenate([kept, got]), jnp.concatenate([got, kept]))

    def trade_rows(tile):
        kept = lax.dynamic_slice_in_dim(tile, core * rows_here, rows_here, 0)
        got = lax.ppermute(
            lax.dynamic_slice_in_dim(tile, (1 - core) * rows_here, rows_here, 0), "row", sibling
        )
        return jnp.where(
            core == 0, jnp.concatenate([kept, got], axis=1), jnp.concatenate([got, kept], axis=1)
        )

    pair_tile = trade_columns(pair_state)
    weight_t = (
        outer_weight.reshape(factor, 2, 16, pair_channels)
        .transpose(1, 3, 2, 0)
        .reshape(2 * pair_channels, 16 * factor)
    )
    seq_live = sequence_mask.astype(f32)
    res_live = residue_mask.astype(f32)
    tile_rows = lax.dynamic_slice_in_dim(res_live, (me // 2) * 8, 8).reshape(2, 4)
    tile_cols = lax.dynamic_slice_in_dim(res_live, core * half, half)
    divisor = jnp.maximum(
        jnp.sum(seq_live) * tile_rows.T[:, :, None] * tile_cols[None, None, :], 1.0
    ).reshape(4, 2 * half)
    bias_rows = 4 * head_count
    send_bias, updated_tile = kernel_call(
        pair_kernel,
        [shape((peers, bias_rows, LANES), bf16), shape((8, half, pair_channels), bf16)],
        [vmem] * 5,
        [
            pltpu.VMEM((peers * STRIDE, LANES), f32),
            pltpu.VMEM((peers * sequence_wise, 16 * LANES), bf16),
            pltpu.VMEM((peers * sequence_wise, 2 * LANES), bf16),
            pltpu.VMEM((16 * factor, 8 * LANES), bf16),
        ],
        flops=1 << 29,
        moved=1 << 20,
    )(received, weight_t, pair_tile, divisor, bias_weight.T)
    bias_all = lax.all_to_all(send_bias, "row", split_axis=0, concat_axis=0, tiled=True)
    pair_updated = trade_rows(updated_tile)

    send_grad, full_bias = kernel_call(
        bias_gradient_kernel,
        [shape((peers, rows_here * head_count, LANES), bf16), shape((head_rows, residues), f32)],
        [vmem] * 4,
        [pltpu.VMEM((head_rows, LANES), f32), pltpu.VMEM((head_rows, LANES), f32)],
        flops=1 << 28,
        moved=1 << 22,
    )(bias_all, res_row, scores, flow)
    shares = lax.all_to_all(send_grad, "row", split_axis=0, concat_axis=0, tiled=True)
    update = kernel_call(
        output_kernel,
        shape((token_rows, channel_count), bf16),
        [vmem] * 5,
        flops=1 << 29,
        moved=1 << 22,
    )(scores, full_bias, values, gate, output_weight)
    pair_gradient = kernel_call(
        gradient_kernel,
        shape((rows_here, residues, pair_channels), f32),
        [vmem] * 3,
        flops=1 << 24,
        moved=1 << 20,
    )(shares, bias_weight.T, pair_updated)
    return (update.reshape(alignment_rows.shape), pair_updated, pair_gradient)


def solution(mesh):
    placed = (
        P(("grp", "row"), "col", None),
        P(("grp", "row"), "col", None),
        P(("grp", "row"), "col", None),
        P("grp"),
        P("grp"),
        P(),
        P(),
        P(),
        P(),
        P(),
        P(),
        P(),
        P(),
        P(),
    )
    one_column = mesh.shape["col"] == 1 and mesh.shape["row"] % 2 == 0
    return jax.shard_map(
        on_device_paired if one_column else on_device_general,
        mesh=mesh,
        in_specs=placed,
        out_specs=(
            P(("grp", "row"), "col", None),
            P(("grp", "row"), "col", None),
            P(("grp", "row"), "col", None),
        ),
        check_vma=False,
    )
```

```python
import jax
import jax.numpy as jnp
from jax import lax
from jax.experimental import pallas as pl
from jax.experimental.pallas import tpu as pltpu
from jax.sharding import PartitionSpec as P

norm_eps = 1e-05
mask_fill = 1000000000.0


def layer_normalize(values):
    values = values.astype(jnp.float32)
    center = values - jnp.mean(values, axis=-1, keepdims=True)
    spread = jnp.mean(center * center, axis=-1, keepdims=True)
    return center * lax.rsqrt(spread + norm_eps)


def norm_backward(values, upstream):
    values = values.astype(jnp.float32)
    center = values - jnp.mean(values, axis=-1, keepdims=True)
    inverse = lax.rsqrt(jnp.mean(center * center, axis=-1, keepdims=True) + norm_eps)
    normal_part = center * inverse
    return inverse * (
        upstream
        - jnp.mean(upstream, axis=-1, keepdims=True)
        - normal_part * jnp.mean(upstream * normal_part, axis=-1, keepdims=True)
    )


def spread_all(shard):
    copies = jnp.broadcast_to(shard[None], (lax.axis_size("row"),) + shard.shape)
    gathered = lax.all_to_all(copies, "row", split_axis=0, concat_axis=0, tiled=True)
    return gathered.reshape((-1,) + shard.shape[1:])


def attend_partial(
    projected_queries, projected_keys, projected_values, bias_all, key_mask, score_scale
):
    scores = jnp.einsum(
        "ihd,jhd->ihj", projected_queries, projected_keys, preferred_element_type=jnp.float32
    )
    scores = scores * score_scale + bias_all.astype(jnp.float32) + key_mask
    maxima = jnp.max(scores, axis=-1)
    weights = jnp.exp(scores - maxima[..., None])
    totals = jnp.sum(weights, axis=-1)
    summed = jnp.einsum(
        "ihj,jhd->ihd",
        weights.astype(jnp.bfloat16),
        projected_values,
        preferred_element_type=jnp.float32,
    )
    return (maxima, totals, summed.reshape(summed.shape[0], -1))


def on_device_general(
    alignment_rows,
    pair_state,
    update_cotangent,
    sequence_mask,
    residue_mask,
    left_weight,
    right_weight,
    outer_weight,
    bias_weight,
    query_weight,
    key_weight,
    value_weight,
    gate_weight,
    output_weight,
):
    sequence_wise, residue_half, channel_count = alignment_rows.shape
    rows_here = pair_state.shape[0]
    residues = residue_mask.shape[0]
    head_count = bias_weight.shape[1]
    head_dim = channel_count // head_count
    score_scale = head_dim ** (-0.5)
    row_index = lax.axis_index("row")
    col_index = lax.axis_index("col")
    complete_alignment, complete_cotangent = (
        lax.all_gather(alignment_rows, "col", axis=1, tiled=True),
        lax.all_gather(update_cotangent, "col", axis=1, tiled=True),
    )
    seq_live = sequence_mask.astype(jnp.float32)
    res_live = residue_mask.astype(jnp.float32)
    own_seq = lax.dynamic_slice_in_dim(seq_live, row_index * sequence_wise, sequence_wise)
    own_cols = lax.dynamic_slice_in_dim(res_live, col_index * residue_half, residue_half)
    own_rows = lax.dynamic_slice_in_dim(res_live, row_index * rows_here, rows_here)
    normalized_input = layer_normalize(complete_alignment).astype(jnp.bfloat16)
    flat_rows = normalized_input.reshape(-1, channel_count)
    normed_half = lax.dynamic_slice_in_dim(
        normalized_input, col_index * residue_half, residue_half, 1
    )
    half_rows = normed_half.reshape(-1, channel_count)
    left_proj = jnp.dot(flat_rows, left_weight, preferred_element_type=jnp.float32).reshape(
        sequence_wise, residues, -1
    )
    left_proj = (left_proj * (own_seq[:, None] * res_live[None, :])[..., None]).astype(jnp.bfloat16)
    right_proj = jnp.dot(half_rows, right_weight, preferred_element_type=jnp.float32).reshape(
        sequence_wise, residue_half, -1
    )
    right_proj = (right_proj * (own_seq[:, None] * own_cols[None, :])[..., None]).astype(
        jnp.bfloat16
    )
    left_tile = lax.all_to_all(left_proj, "row", split_axis=1, concat_axis=0, tiled=True)
    right_all = spread_all(right_proj)
    outer_width = left_tile.shape[2]
    outer_sum = lax.dot_general(
        left_tile.reshape(left_tile.shape[0], -1),
        right_all.reshape(right_all.shape[0], -1),
        (((0,), (0,)), ((), ())),
        preferred_element_type=jnp.float32,
    )
    outer_half = outer_sum.astype(jnp.bfloat16).reshape(
        rows_here, outer_width, residue_half, outer_width
    )
    opm_update = jnp.einsum(
        "ipjq,pqz->ijz", outer_half, outer_weight, preferred_element_type=jnp.float32
    )
    divisor = jnp.maximum(jnp.sum(seq_live) * own_rows[:, None] * own_cols[None, :], 1.0)
    pair_updated = (pair_state.astype(jnp.float32) + opm_update / divisor[..., None]).astype(
        jnp.bfloat16
    )
    pair_normed = layer_normalize(pair_updated).astype(jnp.bfloat16)
    bias_tile = jnp.einsum(
        "ijz,zh->ihj", pair_normed, bias_weight, preferred_element_type=jnp.float32
    ).astype(jnp.bfloat16)
    projected_queries = (
        jnp.dot(flat_rows, query_weight, preferred_element_type=jnp.float32)
        .astype(jnp.bfloat16)
        .reshape(sequence_wise, residues, head_count, head_dim)
    )
    gate_activations = jax.nn.sigmoid(
        jnp.dot(flat_rows, gate_weight, preferred_element_type=jnp.float32)
    ).reshape(sequence_wise, residues, channel_count)
    key_live = (res_live - 1.0) * mask_fill
    half_live = lax.dynamic_slice_in_dim(key_live, col_index * residue_half, residue_half)
    bias_cols = lax.all_gather(bias_tile, "col", axis=2, tiled=True)
    bias_all = spread_all(bias_cols)
    key_count = bias_all.shape[2]
    projected_keys = (
        jnp.dot(flat_rows, key_weight, preferred_element_type=jnp.float32)
        .astype(jnp.bfloat16)
        .reshape(sequence_wise, key_count, head_count, head_dim)
    )
    projected_values = (
        jnp.dot(flat_rows, value_weight, preferred_element_type=jnp.float32)
        .astype(jnp.bfloat16)
        .reshape(sequence_wise, key_count, head_count, head_dim)
    )
    maxima, totals, summed = lax.map(
        lambda inputs: attend_partial(
            inputs[0], inputs[1], inputs[2], bias_all, key_live, score_scale
        ),
        (projected_queries, projected_keys, projected_values),
    )
    attended = summed / jnp.repeat(totals, head_dim, axis=-1)
    gated = gate_activations * attended
    gated_own = lax.dynamic_slice_in_dim(gated, col_index * residue_half, residue_half, 1).astype(
        jnp.bfloat16
    )
    alignment_update = (
        jnp.dot(
            gated_own.reshape(-1, channel_count), output_weight, preferred_element_type=jnp.float32
        )
        .astype(jnp.bfloat16)
        .reshape(sequence_wise, residue_half, channel_count)
    )
    d_gated = lax.dot_general(
        complete_cotangent.reshape(-1, channel_count),
        output_weight,
        (((1,), (1,)), ((), ())),
        preferred_element_type=jnp.float32,
    ).reshape(sequence_wise, residues, channel_count)
    d_attended = d_gated * gate_activations
    delta_sum = jnp.sum(
        (d_attended * attended).reshape(sequence_wise, residues, head_count, head_dim), axis=-1
    )
    d_rounded = d_attended.astype(jnp.bfloat16).reshape(
        sequence_wise, residues, head_count, head_dim
    )
    log_total = maxima + jnp.log(totals)
    keys_half = lax.dynamic_slice_in_dim(projected_keys, col_index * residue_half, residue_half, 1)
    values_half = lax.dynamic_slice_in_dim(
        projected_values, col_index * residue_half, residue_half, 1
    )
    bias_half = lax.dynamic_slice_in_dim(bias_all, col_index * residue_half, residue_half, 2)
    bias_rows = bias_half.astype(jnp.float32)

    def single_sequence(running, sequence_items):
        query_rows, d_rows, total_rows, delta_rows, keys_one, values_one = sequence_items
        scores = jnp.einsum(
            "ihd,jhd->ihj", query_rows, keys_one, preferred_element_type=jnp.float32
        )
        scores = scores * score_scale + bias_rows + half_live
        probs = jnp.exp(scores - total_rows[..., None])
        d_weights = jnp.einsum(
            "ihd,jhd->ihj", d_rows, values_one, preferred_element_type=jnp.float32
        )
        return (running + probs * (d_weights - delta_rows[..., None]), None)

    sequence_items = (projected_queries, d_rounded, log_total, delta_sum, keys_half, values_half)
    initial_value = jnp.zeros(
        (rows_here * lax.axis_size("row"), head_count, residue_half), jnp.float32
    )
    result, unused = lax.scan(single_sequence, initial_value, sequence_items)
    shares = lax.all_to_all(
        result.astype(jnp.bfloat16).reshape((-1,) + (rows_here,) + result.shape[1:]),
        "row",
        split_axis=0,
        concat_axis=0,
        tiled=True,
    )
    bias_gradient = jnp.sum(shares.astype(jnp.float32), axis=0)
    d_normed = jnp.einsum(
        "ihj,zh->ijz",
        bias_gradient,
        bias_weight.astype(jnp.float32),
        precision=lax.Precision.HIGHEST,
    )
    pair_gradient = norm_backward(pair_updated, d_normed)
    return (alignment_update, pair_updated, pair_gradient)


LANES = 128
STRIDE = 40
GROUP = 4
f32 = jnp.float32
bf16 = jnp.bfloat16


def dot_nn(a, b):
    return lax.dot_general(a, b, (((1,), (0,)), ((), ())), preferred_element_type=f32)


def dot_nt(a, b):
    return lax.dot_general(a, b, (((1,), (1,)), ((), ())), preferred_element_type=f32)


def dot_tn(a, b):
    return lax.dot_general(a, b, (((0,), (0,)), ((), ())), preferred_element_type=f32)


def lane_index(rows):
    return lax.broadcasted_iota(jnp.int32, (rows, LANES), 1)


def factors_kernel(seq_ref, res_ref, rows_ref, left_ref, right_ref, send_ref, normed_ref, left_scr):
    seqs = send_ref.shape[2] // 18
    residues = res_ref.shape[1]
    chips = send_ref.shape[0]
    me = lax.axis_index("row")
    normed = layer_normalize(rows_ref[...]).astype(bf16)
    normed_ref[...] = normed
    live = res_ref[...].astype(f32)
    live_rows = jnp.broadcast_to(live, (residues, residues)).T
    right_t = right_ref[...]
    left_wide = jnp.concatenate([left_ref[...]] * 4, axis=0)
    low = lane_index(16) < 64
    lane_group = lane_index(chips) // 32
    halves = ([], [])
    tail = []
    for s in range(seqs):
        seq_live = seq_ref[me * seqs + s].astype(f32)
        own = normed[s * residues : (s + 1) * residues]
        factor = dot_nt(right_t, own) * (live * seq_live)
        first, second = factor[:16], factor[16:]
        halves[0].append(jnp.where(low, first, pltpu.roll(second, 64, 1)))
        halves[1].append(jnp.where(low, pltpu.roll(first, 64, 1), second))
        left_scr[...] = dot_nt(own, left_wide) * (live_rows * seq_live)
        for a in range(2):
            row = jnp.zeros((chips, LANES), f32)
            for b in range(4):
                part = left_scr[pl.ds(4 * a + b, chips, stride=8), :]
                row = jnp.where(lane_group == b, part, row)
            tail.append(row)
    tail = jnp.stack(tail, axis=1).astype(bf16)
    right_rows = 16 * seqs
    for core in range(2):
        block = jnp.concatenate(halves[core], axis=0).astype(bf16)
        send_ref[:, core, :right_rows, :] = jnp.broadcast_to(block[None], (chips, right_rows, LANES))
        send_ref[:, core, right_rows:, :] = tail


def side_by_side(first, second, at):
    low = lane_index(first.shape[0]) < 64
    span = slice(at // 2 * LANES, at // 2 * LANES + LANES)
    first, second = first[:, span], second[:, span]
    if at % 2 == 0:
        return jnp.where(low, first, pltpu.roll(second, 64, 1))
    return jnp.where(low, pltpu.roll(first, 64, 1), second)


def partner(step):
    return lax.bitwise_xor(lax.rem(lax.axis_index("row"), GROUP), step)


def projections_kernel(
    normed_ref, cot_ref, wq_ref, wk_ref, wv_ref, wg_ref, wo_ref, gate_ref, *rest
):
    block_refs, every = rest[:GROUP], rest[GROUP]
    residues = gate_ref.shape[1]
    seqs = normed_ref.shape[0] // residues
    normed = normed_ref[...]
    queries = dot_nn(normed, wq_ref[...])
    keys = dot_nn(normed, wk_ref[...])
    values = dot_nn(normed, wv_ref[...])
    gate = jax.nn.sigmoid(dot_nn(normed, wg_ref[...]))
    d_attended = dot_nt(cot_ref[...], wo_ref[...]) * gate
    for t in range(GROUP):
        rows = side_by_side(queries, d_attended, t).astype(bf16)
        columns = side_by_side(keys, values, t).astype(bf16)
        gate_ref[t] = side_by_side(gate[:residues], gate[residues:], t)
        for s in range(seqs):
            every[t, s] = rows[s * residues : (s + 1) * residues]
            every[t, seqs + s] = columns[s * residues : (s + 1) * residues]
    for step in range(GROUP):
        block_refs[step][...] = every[partner(step)]


def products_kernel(scale, *refs):
    block_refs, score_ref, flow_ref = refs[:GROUP], refs[GROUP], refs[GROUP + 1]
    rows = score_ref.shape[1]
    residues = score_ref.shape[2]
    part_of = lane_index(residues) // 32
    seqs = block_refs[0].shape[0] // 2
    for step, block in enumerate(block_refs):
        for s in range(seqs):
            wide = jnp.concatenate(
                [jnp.where(part_of == g, block[s], jnp.zeros((), bf16)) for g in range(4)], axis=0
            )
            both = dot_nt(wide, block[seqs + s])
            score_ref[step * seqs + s] = both[:rows] * scale
            flow_ref[step * seqs + s] = both[rows:]


def pair_kernel(recv_ref, weight_ref, pair_ref, div_ref, bias_w_ref, send_ref, updated_ref, flat, rbuf, lbuf, obuf):
    peers, block_rows, _ = recv_ref.shape
    seqs = block_rows // 18
    for p in range(peers):
        flat[p * STRIDE : p * STRIDE + block_rows, :] = recv_ref[p].astype(f32)
    for s in range(seqs):
        for g in range(16):
            part = flat[pl.ds(s * 16 + g, peers, stride=STRIDE), :]
            rbuf[s * peers : (s + 1) * peers, g * LANES : (g + 1) * LANES] = part.astype(bf16)
        for a in range(2):
            part = flat[pl.ds(16 * seqs + 2 * s + a, peers, stride=STRIDE), :]
            lbuf[s * peers : (s + 1) * peers, a * LANES : (a + 1) * LANES] = part.astype(bf16)
    left_t = lbuf[...].astype(f32).T.astype(bf16)
    for g in range(16):
        outer = dot_nn(left_t, rbuf[:, g * LANES : (g + 1) * LANES]).astype(bf16)
        for i in range(8):
            obuf[g * 32 : (g + 1) * 32, i * LANES : (i + 1) * LANES] = outer[i * 32 : (i + 1) * 32]
    sums = dot_nn(weight_ref[...], obuf[...])
    low = lane_index(LANES) < 64

    def piece(a, i):
        return sums[a * LANES : (a + 1) * LANES, i * LANES : (i + 1) * LANES]

    blocks = []
    bias_w = bias_w_ref[...]
    for b in range(4):
        straight = jnp.where(low, piece(0, b), piece(1, b + 4))
        crossed = jnp.where(low, piece(0, b + 4), piece(1, b))
        update = (straight + pltpu.roll(crossed, 64, 1)) / div_ref[b : b + 1, :]
        state = jnp.concatenate([pair_ref[b], pair_ref[b + 4]], axis=0).astype(f32)
        updated = (state + update.T).astype(bf16)
        updated_ref[b] = updated[:64]
        updated_ref[b + 4] = updated[64:]
        pair_normed = layer_normalize(updated).astype(bf16)
        blocks.append(dot_nt(bias_w, pair_normed))
    lines, _, share, _ = send_ref.shape
    heads = share // 4
    for t in range(GROUP):
        block = jnp.concatenate([rows[t * heads : (t + 1) * heads] for rows in blocks], axis=0).astype(bf16)
        send_ref[:, t] = jnp.broadcast_to(block[None], (lines, share, LANES))


def placed_bias(flat, res_ref, heads, h):
    residues = res_ref.shape[1]
    sub = lax.broadcasted_iota(jnp.int32, (residues, LANES), 0) % 8
    keep = (sub < 4) == (lane_index(residues) < 64)
    raw = flat[pl.ds(h, residues, stride=heads), :]
    moved = jnp.where(sub < 4, pltpu.roll(raw, residues - 4, 0), pltpu.roll(raw, 4, 0))
    key_mask = (res_ref[...].astype(f32) - 1.0) * mask_fill
    return jnp.where(keep, raw, pltpu.roll(moved, 64, 1)) + key_mask


def bias_gradient_kernel(bias_ref, res_ref, score_ref, flow_ref, send_ref, full_ref, flat, grads):
    seqs, rows, residues = score_ref.shape
    heads = rows // residues
    flat[...] = bias_ref[...].reshape(flat.shape).astype(f32)
    ones = jnp.ones((residues, LANES), bf16)
    for h in range(heads):
        at = slice(h * residues, (h + 1) * residues)
        bias = placed_bias(flat, res_ref, heads, h)
        full_ref[at, :] = bias
        total = jnp.zeros((residues, residues), f32)
        for s in range(seqs):
            scores = score_ref[s, at, :] + bias
            weights = jnp.exp(scores - jnp.max(scores, axis=-1, keepdims=True))
            flow = flow_ref[s, at, :]
            inverse = 1.0 / dot_nn(weights.astype(bf16), ones)
            delta = dot_nn((weights * flow).astype(bf16), ones) * inverse
            total = total + weights * inverse * (flow - delta)
        grads[pl.ds(h, residues, stride=heads), :] = total
    send_ref[...] = grads[...].astype(bf16).reshape(send_ref.shape)


def attended_kernel(score_ref, full_ref, *refs):
    block_refs, out_refs = refs[:GROUP], refs[GROUP:]
    _, rows, residues = score_ref.shape
    heads = rows // residues
    seqs = block_refs[0].shape[0] // 2
    part_of = lane_index(residues) // 32
    for step in range(GROUP):
        attended = []
        for s in range(seqs):
            own = jnp.zeros((residues, LANES), f32)
            for h in range(heads):
                at = slice(h * residues, (h + 1) * residues)
                scores = score_ref[step * seqs + s, at, :] + full_ref[at, :]
                weights = jnp.exp(scores - jnp.max(scores, axis=-1, keepdims=True))
                total = jnp.sum(weights, axis=-1, keepdims=True)
                mixed = dot_nn(weights.astype(bf16), block_refs[step][seqs + s]) / total
                own = jnp.where(part_of == heads + h, mixed, own)
            attended.append(own)
        out_refs[step][...] = jnp.where(
            part_of < heads, pltpu.roll(attended[0], 64, 1), attended[1]
        ).astype(bf16)


def output_kernel(gate_ref, wo_ref, *refs):
    in_refs, out_ref = refs[:GROUP], refs[GROUP]
    residues = gate_ref.shape[1]
    low = lane_index(residues) < 64
    zero = jnp.zeros((), bf16)
    sums = [jnp.zeros((residues, out_ref.shape[1]), f32) for _ in range(2)]
    for step in range(GROUP):
        at = partner(step)
        gated = (gate_ref[at] * in_refs[step][...].astype(f32)).astype(bf16)
        weight = wo_ref[pl.ds(pl.multiple_of(at * 64, 64), 64), :]
        weight = jnp.concatenate([weight, weight], axis=0)
        sums[0] = sums[0] + dot_nn(jnp.where(low, gated, zero), weight)
        sums[1] = sums[1] + dot_nn(jnp.where(low, zero, gated), weight)
    for s in range(2):
        out_ref[s * residues : (s + 1) * residues, :] = sums[s].astype(bf16)


def gradient_kernel(shares_ref, bias_w_ref, pair_ref, out_ref):
    peers, share, _ = shares_ref.shape
    total = jnp.sum(shares_ref[...].astype(f32).reshape(peers // GROUP, GROUP, share, LANES), axis=0)
    rows = pair_ref.shape[0]
    heads = share // rows
    bias_w = bias_w_ref[...].astype(f32)
    for i in range(rows):
        own = jnp.concatenate([total[t, i * heads : (i + 1) * heads] for t in range(GROUP)], axis=0)
        upstream = lax.dot_general(
            own, bias_w, (((0,), (0,)), ((), ())), precision=lax.Precision.HIGHEST, preferred_element_type=f32
        )
        out_ref[i] = norm_backward(pair_ref[i], upstream)


def kernel_call(body, out_shape, in_specs=None, scratch=(), flops=0, moved=0, vmem_mib=24):
    vmem = pl.BlockSpec(memory_space=pltpu.VMEM)
    many = isinstance(out_shape, (list, tuple))
    return pl.pallas_call(
        body,
        out_shape=out_shape,
        in_specs=in_specs,
        out_specs=[vmem] * len(out_shape) if many else vmem,
        scratch_shapes=list(scratch),
        compiler_params=pltpu.CompilerParams(vmem_limit_bytes=vmem_mib * 1024 * 1024),
        cost_estimate=pl.CostEstimate(flops=flops, bytes_accessed=moved, transcendentals=0),
    )


def on_device_paired(
    alignment_rows,
    pair_state,
    update_cotangent,
    sequence_mask,
    residue_mask,
    left_weight,
    right_weight,
    outer_weight,
    bias_weight,
    query_weight,
    key_weight,
    value_weight,
    gate_weight,
    output_weight,
):
    sequence_wise, residues, channel_count = alignment_rows.shape
    rows_here, _, pair_channels = pair_state.shape
    head_count = bias_weight.shape[1]
    peers = lax.axis_size("row")
    factor = left_weight.shape[1]
    chips = peers // 2
    vmem = pl.BlockSpec(memory_space=pltpu.VMEM)
    smem = pl.BlockSpec(memory_space=pltpu.SMEM)
    me = lax.axis_index("row")
    core = me % 2
    sibling = [(i, i ^ 1) for i in range(peers)]
    token_rows = sequence_wise * residues
    half = residues // 2
    block_rows = sequence_wise * 18
    res_row = residue_mask.reshape(1, residues)
    flat_rows = alignment_rows.reshape(token_rows, channel_count)
    shape = jax.ShapeDtypeStruct

    send, normed = kernel_call(
        factors_kernel,
        [shape((chips, 2, block_rows, LANES), bf16), shape((token_rows, channel_count), bf16)],
        [smem, vmem, vmem, vmem, vmem],
        [pltpu.VMEM((residues, LANES), f32)],
        flops=2 * token_rows * channel_count * LANES,
        moved=1 << 19,
        vmem_mib=60,
    )(sequence_mask, res_row, flat_rows, left_weight.T, right_weight.T)
    received = lax.all_to_all(
        send.reshape(peers, block_rows, LANES), "row", split_axis=0, concat_axis=0, tiled=True
    )

    group_heads = head_count // GROUP
    head_rows = group_heads * residues
    scale = (channel_count // head_count) ** (-0.5)
    gate, *blocks = kernel_call(
        projections_kernel,
        [shape((GROUP, residues, LANES), f32)]
        + [shape((2 * sequence_wise, residues, LANES), bf16)] * GROUP,
        [vmem] * 7,
        [pltpu.VMEM((GROUP, 2 * sequence_wise, residues, LANES), bf16)],
        flops=10 * token_rows * channel_count * channel_count,
        moved=1 << 21,
    )(
        normed,
        update_cotangent.reshape(token_rows, channel_count),
        query_weight,
        key_weight,
        value_weight,
        gate_weight,
        output_weight,
    )

    def trade(parts):
        return parts[:1] + [
            lax.ppermute(parts[d], "row", [(i, i ^ d) for i in range(peers)]) for d in range(1, GROUP)
        ]

    blocks = trade(blocks)
    scores, flow = kernel_call(
        lambda *refs: products_kernel(scale, *refs),
        [shape((GROUP * sequence_wise, head_rows, residues), f32)] * 2,
        [vmem] * GROUP,
        flops=1 << 28,
        moved=1 << 21,
    )(*blocks)

    def trade_columns(tile):
        kept = lax.dynamic_slice_in_dim(tile, core * half, half, 1)
        got = lax.ppermute(lax.dynamic_slice_in_dim(tile, (1 - core) * half, half, 1), "row", sibling)
        return jnp.where(core == 0, jnp.concatenate([kept, got]), jnp.concatenate([got, kept]))

    def trade_rows(tile):
        kept = lax.dynamic_slice_in_dim(tile, core * rows_here, rows_here, 0)
        got = lax.ppermute(
            lax.dynamic_slice_in_dim(tile, (1 - core) * rows_here, rows_here, 0), "row", sibling
        )
        return jnp.where(
            core == 0, jnp.concatenate([kept, got], axis=1), jnp.concatenate([got, kept], axis=1)
        )

    pair_tile = trade_columns(pair_state)
    weight_t = (
        outer_weight.reshape(factor, 2, 16, pair_channels)
        .transpose(1, 3, 2, 0)
        .reshape(2 * pair_channels, 16 * factor)
    )
    seq_live = sequence_mask.astype(f32)
    res_live = residue_mask.astype(f32)
    tile_rows = lax.dynamic_slice_in_dim(res_live, (me // 2) * 8, 8).reshape(2, 4)
    tile_cols = lax.dynamic_slice_in_dim(res_live, core * half, half)
    divisor = jnp.maximum(
        jnp.sum(seq_live) * tile_rows.T[:, :, None] * tile_cols[None, None, :], 1.0
    ).reshape(4, 2 * half)
    share_rows = 4 * group_heads
    send_bias, updated_tile = kernel_call(
        pair_kernel,
        [shape((peers // GROUP, GROUP, share_rows, LANES), bf16), shape((8, half, pair_channels), bf16)],
        [vmem] * 5,
        [
            pltpu.VMEM((peers * STRIDE, LANES), f32),
            pltpu.VMEM((peers * sequence_wise, 16 * LANES), bf16),
            pltpu.VMEM((peers * sequence_wise, 2 * LANES), bf16),
            pltpu.VMEM((16 * factor, 8 * LANES), bf16),
        ],
        flops=1 << 29,
        moved=1 << 20,
    )(received, weight_t, pair_tile, divisor, bias_weight.T)
    bias_all = lax.all_to_all(
        send_bias.reshape(peers, share_rows, LANES), "row", split_axis=0, concat_axis=0, tiled=True
    )
    pair_updated = trade_rows(updated_tile)

    send_grad, full_bias = kernel_call(
        bias_gradient_kernel,
        [shape((peers, rows_here * group_heads, LANES), bf16), shape((head_rows, residues), f32)],
        [vmem] * 4,
        [pltpu.VMEM((head_rows, LANES), f32), pltpu.VMEM((head_rows, LANES), f32)],
        flops=1 << 28,
        moved=1 << 22,
    )(bias_all, res_row, scores, flow)
    shares = lax.all_to_all(send_grad, "row", split_axis=0, concat_axis=0, tiled=True)
    attended = kernel_call(
        attended_kernel,
        [shape((residues, LANES), bf16)] * GROUP,
        [vmem] * (2 + GROUP),
        flops=1 << 28,
        moved=1 << 21,
    )(scores, full_bias, *blocks)
    update = kernel_call(
        output_kernel,
        shape((token_rows, channel_count), bf16),
        [vmem] * (2 + GROUP),
        flops=2 * token_rows * channel_count * channel_count,
        moved=1 << 20,
    )(gate, output_weight, *trade(list(attended)))
    pair_gradient = kernel_call(
        gradient_kernel,
        shape((rows_here, residues, pair_channels), f32),
        [vmem] * 3,
        flops=1 << 24,
        moved=1 << 20,
    )(shares, bias_weight.T, pair_updated)
    return (update.reshape(alignment_rows.shape), pair_updated, pair_gradient)


def on_device(*arguments):
    rows, pair, left, bias = arguments[0], arguments[1], arguments[5], arguments[8]
    peers = lax.axis_size("row")
    fits = (
        lax.axis_size("col") == 1
        and peers == 32
        and rows.shape == (2, 128, 256)
        and pair.shape == (4, 128, 128)
        and left.shape[1] == 32
        and bias.shape[1] == 8
    )
    return (on_device_paired if fits else on_device_general)(*arguments)


def solution(mesh):
    placed = (
        P(("grp", "row"), "col", None),
        P(("grp", "row"), "col", None),
        P(("grp", "row"), "col", None),
        P("grp"),
        P("grp"),
        P(),
        P(),
        P(),
        P(),
        P(),
        P(),
        P(),
        P(),
        P(),
    )
    return jax.shard_map(
        on_device,
        mesh=mesh,
        in_specs=placed,
        out_specs=(
            P(("grp", "row"), "col", None),
            P(("grp", "row"), "col", None),
            P(("grp", "row"), "col", None),
        ),
        check_vma=False,
    )
```

```python
import jax
import jax.numpy as jnp
from jax import lax
from jax.experimental import pallas as pl
from jax.experimental.pallas import tpu as pltpu
from jax.sharding import PartitionSpec as P

norm_eps = 1e-05
mask_fill = 1000000000.0


def layer_normalize(values):
    values = values.astype(jnp.float32)
    center = values - jnp.mean(values, axis=-1, keepdims=True)
    spread = jnp.mean(center * center, axis=-1, keepdims=True)
    return center * lax.rsqrt(spread + norm_eps)


def norm_backward(values, upstream):
    values = values.astype(jnp.float32)
    center = values - jnp.mean(values, axis=-1, keepdims=True)
    inverse = lax.rsqrt(jnp.mean(center * center, axis=-1, keepdims=True) + norm_eps)
    normal_part = center * inverse
    return inverse * (
        upstream
        - jnp.mean(upstream, axis=-1, keepdims=True)
        - normal_part * jnp.mean(upstream * normal_part, axis=-1, keepdims=True)
    )


def spread_all(shard):
    copies = jnp.broadcast_to(shard[None], (lax.axis_size("row"),) + shard.shape)
    gathered = lax.all_to_all(copies, "row", split_axis=0, concat_axis=0, tiled=True)
    return gathered.reshape((-1,) + shard.shape[1:])


def attend_partial(
    projected_queries, projected_keys, projected_values, bias_all, key_mask, score_scale
):
    scores = jnp.einsum(
        "ihd,jhd->ihj", projected_queries, projected_keys, preferred_element_type=jnp.float32
    )
    scores = scores * score_scale + bias_all.astype(jnp.float32) + key_mask
    maxima = jnp.max(scores, axis=-1)
    weights = jnp.exp(scores - maxima[..., None])
    totals = jnp.sum(weights, axis=-1)
    summed = jnp.einsum(
        "ihj,jhd->ihd",
        weights.astype(jnp.bfloat16),
        projected_values,
        preferred_element_type=jnp.float32,
    )
    return (maxima, totals, summed.reshape(summed.shape[0], -1))


def on_device_general(
    alignment_rows,
    pair_state,
    update_cotangent,
    sequence_mask,
    residue_mask,
    left_weight,
    right_weight,
    outer_weight,
    bias_weight,
    query_weight,
    key_weight,
    value_weight,
    gate_weight,
    output_weight,
):
    sequence_wise, residue_half, channel_count = alignment_rows.shape
    rows_here = pair_state.shape[0]
    residues = residue_mask.shape[0]
    head_count = bias_weight.shape[1]
    head_dim = channel_count // head_count
    score_scale = head_dim ** (-0.5)
    row_index = lax.axis_index("row")
    col_index = lax.axis_index("col")
    complete_alignment, complete_cotangent = (
        lax.all_gather(alignment_rows, "col", axis=1, tiled=True),
        lax.all_gather(update_cotangent, "col", axis=1, tiled=True),
    )
    seq_live = sequence_mask.astype(jnp.float32)
    res_live = residue_mask.astype(jnp.float32)
    own_seq = lax.dynamic_slice_in_dim(seq_live, row_index * sequence_wise, sequence_wise)
    own_cols = lax.dynamic_slice_in_dim(res_live, col_index * residue_half, residue_half)
    own_rows = lax.dynamic_slice_in_dim(res_live, row_index * rows_here, rows_here)
    normalized_input = layer_normalize(complete_alignment).astype(jnp.bfloat16)
    flat_rows = normalized_input.reshape(-1, channel_count)
    normed_half = lax.dynamic_slice_in_dim(
        normalized_input, col_index * residue_half, residue_half, 1
    )
    half_rows = normed_half.reshape(-1, channel_count)
    left_proj = jnp.dot(flat_rows, left_weight, preferred_element_type=jnp.float32).reshape(
        sequence_wise, residues, -1
    )
    left_proj = (left_proj * (own_seq[:, None] * res_live[None, :])[..., None]).astype(jnp.bfloat16)
    right_proj = jnp.dot(half_rows, right_weight, preferred_element_type=jnp.float32).reshape(
        sequence_wise, residue_half, -1
    )
    right_proj = (right_proj * (own_seq[:, None] * own_cols[None, :])[..., None]).astype(
        jnp.bfloat16
    )
    left_tile = lax.all_to_all(left_proj, "row", split_axis=1, concat_axis=0, tiled=True)
    right_all = spread_all(right_proj)
    outer_width = left_tile.shape[2]
    outer_sum = lax.dot_general(
        left_tile.reshape(left_tile.shape[0], -1),
        right_all.reshape(right_all.shape[0], -1),
        (((0,), (0,)), ((), ())),
        preferred_element_type=jnp.float32,
    )
    outer_half = outer_sum.astype(jnp.bfloat16).reshape(
        rows_here, outer_width, residue_half, outer_width
    )
    opm_update = jnp.einsum(
        "ipjq,pqz->ijz", outer_half, outer_weight, preferred_element_type=jnp.float32
    )
    divisor = jnp.maximum(jnp.sum(seq_live) * own_rows[:, None] * own_cols[None, :], 1.0)
    pair_updated = (pair_state.astype(jnp.float32) + opm_update / divisor[..., None]).astype(
        jnp.bfloat16
    )
    pair_normed = layer_normalize(pair_updated).astype(jnp.bfloat16)
    bias_tile = jnp.einsum(
        "ijz,zh->ihj", pair_normed, bias_weight, preferred_element_type=jnp.float32
    ).astype(jnp.bfloat16)
    projected_queries = (
        jnp.dot(flat_rows, query_weight, preferred_element_type=jnp.float32)
        .astype(jnp.bfloat16)
        .reshape(sequence_wise, residues, head_count, head_dim)
    )
    gate_activations = jax.nn.sigmoid(
        jnp.dot(flat_rows, gate_weight, preferred_element_type=jnp.float32)
    ).reshape(sequence_wise, residues, channel_count)
    key_live = (res_live - 1.0) * mask_fill
    half_live = lax.dynamic_slice_in_dim(key_live, col_index * residue_half, residue_half)
    bias_cols = lax.all_gather(bias_tile, "col", axis=2, tiled=True)
    bias_all = spread_all(bias_cols)
    key_count = bias_all.shape[2]
    projected_keys = (
        jnp.dot(flat_rows, key_weight, preferred_element_type=jnp.float32)
        .astype(jnp.bfloat16)
        .reshape(sequence_wise, key_count, head_count, head_dim)
    )
    projected_values = (
        jnp.dot(flat_rows, value_weight, preferred_element_type=jnp.float32)
        .astype(jnp.bfloat16)
        .reshape(sequence_wise, key_count, head_count, head_dim)
    )
    maxima, totals, summed = lax.map(
        lambda inputs: attend_partial(
            inputs[0], inputs[1], inputs[2], bias_all, key_live, score_scale
        ),
        (projected_queries, projected_keys, projected_values),
    )
    attended = summed / jnp.repeat(totals, head_dim, axis=-1)
    gated = gate_activations * attended
    gated_own = lax.dynamic_slice_in_dim(gated, col_index * residue_half, residue_half, 1).astype(
        jnp.bfloat16
    )
    alignment_update = (
        jnp.dot(
            gated_own.reshape(-1, channel_count), output_weight, preferred_element_type=jnp.float32
        )
        .astype(jnp.bfloat16)
        .reshape(sequence_wise, residue_half, channel_count)
    )
    d_gated = lax.dot_general(
        complete_cotangent.reshape(-1, channel_count),
        output_weight,
        (((1,), (1,)), ((), ())),
        preferred_element_type=jnp.float32,
    ).reshape(sequence_wise, residues, channel_count)
    d_attended = d_gated * gate_activations
    delta_sum = jnp.sum(
        (d_attended * attended).reshape(sequence_wise, residues, head_count, head_dim), axis=-1
    )
    d_rounded = d_attended.astype(jnp.bfloat16).reshape(
        sequence_wise, residues, head_count, head_dim
    )
    log_total = maxima + jnp.log(totals)
    keys_half = lax.dynamic_slice_in_dim(projected_keys, col_index * residue_half, residue_half, 1)
    values_half = lax.dynamic_slice_in_dim(
        projected_values, col_index * residue_half, residue_half, 1
    )
    bias_half = lax.dynamic_slice_in_dim(bias_all, col_index * residue_half, residue_half, 2)
    bias_rows = bias_half.astype(jnp.float32)

    def single_sequence(running, sequence_items):
        query_rows, d_rows, total_rows, delta_rows, keys_one, values_one = sequence_items
        scores = jnp.einsum(
            "ihd,jhd->ihj", query_rows, keys_one, preferred_element_type=jnp.float32
        )
        scores = scores * score_scale + bias_rows + half_live
        probs = jnp.exp(scores - total_rows[..., None])
        d_weights = jnp.einsum(
            "ihd,jhd->ihj", d_rows, values_one, preferred_element_type=jnp.float32
        )
        return (running + probs * (d_weights - delta_rows[..., None]), None)

    sequence_items = (projected_queries, d_rounded, log_total, delta_sum, keys_half, values_half)
    initial_value = jnp.zeros(
        (rows_here * lax.axis_size("row"), head_count, residue_half), jnp.float32
    )
    result, unused = lax.scan(single_sequence, initial_value, sequence_items)
    shares = lax.all_to_all(
        result.astype(jnp.bfloat16).reshape((-1,) + (rows_here,) + result.shape[1:]),
        "row",
        split_axis=0,
        concat_axis=0,
        tiled=True,
    )
    bias_gradient = jnp.sum(shares.astype(jnp.float32), axis=0)
    d_normed = jnp.einsum(
        "ihj,zh->ijz",
        bias_gradient,
        bias_weight.astype(jnp.float32),
        precision=lax.Precision.HIGHEST,
    )
    pair_gradient = norm_backward(pair_updated, d_normed)
    return (alignment_update, pair_updated, pair_gradient)


LANES = 128
GROUP = 4
f32 = jnp.float32
bf16 = jnp.bfloat16


def dot_nn(a, b):
    return lax.dot_general(a, b, (((1,), (0,)), ((), ())), preferred_element_type=f32)


def dot_nt(a, b):
    return lax.dot_general(a, b, (((1,), (1,)), ((), ())), preferred_element_type=f32)


def dot_tn(a, b):
    return lax.dot_general(a, b, (((0,), (0,)), ((), ())), preferred_element_type=f32)


def lane_index(rows):
    return lax.broadcasted_iota(jnp.int32, (rows, LANES), 1)


def swap_groups(parts):
    lane = lane_index(parts[0].shape[0])
    low, even = lane < 64, lane % 64 < 32
    parts = [
        jnp.where(low, parts[0], pltpu.roll(parts[2], 64, 1)),
        jnp.where(low, parts[1], pltpu.roll(parts[3], 64, 1)),
        jnp.where(low, pltpu.roll(parts[0], 64, 1), parts[2]),
        jnp.where(low, pltpu.roll(parts[1], 64, 1), parts[3]),
    ]
    return [
        jnp.where(even, parts[0], pltpu.roll(parts[1], 32, 1)),
        jnp.where(even, pltpu.roll(parts[0], 96, 1), parts[1]),
        jnp.where(even, parts[2], pltpu.roll(parts[3], 32, 1)),
        jnp.where(even, pltpu.roll(parts[2], 96, 1), parts[3]),
    ]


def factors_kernel(
    seq_smem_ref, res_smem_ref, seq_ref, res_ref, bias_w_ref, rows_ref, left_ref, right_ref, pair_ref,
    send_ref, aux_ref, normed_ref, *refs
):
    pair_refs, left_scr = refs[:GROUP], refs[GROUP]
    columns_each = pair_refs[0].shape[1]
    for step in range(GROUP):
        first = pl.multiple_of(partner(step) * columns_each, columns_each)
        pair_refs[step][...] = pair_ref[:, pl.ds(first, columns_each), :]
    lines = send_ref.shape[0]
    seqs = send_ref.shape[2] // 12
    residues = res_ref.shape[1]
    me = lax.axis_index("row")
    normed = layer_normalize(rows_ref[...]).astype(bf16)
    normed_ref[...] = normed
    live = res_ref[...].astype(f32)
    live_rows = jnp.broadcast_to(live, (residues, residues)).T
    right_t = right_ref[...]
    left_wide = jnp.concatenate([left_ref[...]] * 4, axis=0)
    lane_group = lane_index(lines) // 32
    quarters = []
    tail = []
    for s in range(seqs):
        seq_live = seq_smem_ref[me * seqs + s].astype(f32)
        own = normed[s * residues : (s + 1) * residues]
        factor = dot_nt(right_t, own) * (live * seq_live)
        quarters.append(swap_groups([factor[a * 8 : (a + 1) * 8] for a in range(4)]))
        left_scr[...] = dot_nt(own, left_wide) * (live_rows * seq_live)
        for a in range(4):
            row = jnp.zeros((lines, LANES), f32)
            for b in range(4):
                part = left_scr[pl.ds(4 * a + b, lines, stride=4 * GROUP), :]
                row = jnp.where(lane_group == b, part, row)
            tail.append(row)
    tail = jnp.stack(tail, axis=1).astype(bf16)
    right_rows = 8 * seqs
    for t in range(GROUP):
        block = jnp.concatenate([own[t] for own in quarters], axis=0).astype(bf16)
        send_ref[:, t, :right_rows, :] = jnp.broadcast_to(block[None], (lines, right_rows, LANES))
        send_ref[:, t, right_rows:, :] = tail
    aux_ref[0:4] = tile_divisor(res_smem_ref, res_ref, seq_ref)
    aux_ref[4:8] = jnp.broadcast_to((live - 1.0) * mask_fill, (4, LANES))
    aux_ref[8:16] = bias_w_ref[...].astype(f32)


def side_by_side(first, second, at):
    low = lane_index(first.shape[0]) < 64
    span = slice(at // 2 * LANES, at // 2 * LANES + LANES)
    first, second = first[:, span], second[:, span]
    if at % 2 == 0:
        return jnp.where(low, first, pltpu.roll(second, 64, 1))
    return jnp.where(low, pltpu.roll(first, 64, 1), second)


def partner(step):
    return lax.bitwise_xor(lax.rem(lax.axis_index("row"), GROUP), step)


def tile_divisor(res_smem_ref, res_ref, seq_ref):
    own = partner(0)
    rows = lax.div(lax.axis_index("row"), GROUP) * 16
    lane = lane_index(1)
    live = res_ref[...].astype(f32)
    columns = jnp.zeros((1, LANES), f32)
    for t in range(GROUP):
        turned = live if t == 0 else pltpu.roll(live, LANES - 32 * t, 1)
        columns = jnp.where(own == t, turned, columns)
    columns = jnp.where(lane < 32, columns, 0.0)
    columns = columns + pltpu.roll(columns, 32, 1)
    columns = columns + pltpu.roll(columns, 64, 1)
    total = jnp.sum(seq_ref[...].astype(f32), axis=-1, keepdims=True)
    lines = []
    for b in range(4):
        line = jnp.zeros((1, LANES), f32)
        for a in range(4):
            line = jnp.where(lane // 32 == a, res_smem_ref[rows + 4 * a + b].astype(f32), line)
        lines.append(jnp.maximum(total * line * columns, 1.0))
    return jnp.concatenate(lines, axis=0)


def projections_kernel(normed_ref, cot_ref, weights_ref, wo_ref, gate_ref, *rest):
    block_refs, every = rest[:GROUP], rest[GROUP]
    normed = normed_ref[...]
    tokens = normed.shape[0]
    residues = gate_ref.shape[1]
    seqs = tokens // residues
    channels = normed.shape[1]
    queries, keys, values, gate = [
        dot_nn(normed, weights_ref[:, at * channels : (at + 1) * channels]) for at in range(4)
    ]
    gate = jax.nn.sigmoid(gate)
    d_attended = dot_nt(cot_ref[...], wo_ref[...]) * gate
    for t in range(GROUP):
        rows = side_by_side(queries, d_attended, t).astype(bf16)
        columns = side_by_side(keys, values, t).astype(bf16)
        gate_ref[t] = side_by_side(gate[:residues], gate[residues:], t)
        for s in range(seqs):
            every[t, s] = rows[s * residues : (s + 1) * residues]
            every[t, seqs + s] = columns[s * residues : (s + 1) * residues]
    for step in range(GROUP):
        block_refs[step][...] = every[partner(step)]


def products_kernel(scale, *refs):
    block_refs, (score_ref, flow_ref, value_ref) = refs[:GROUP], refs[GROUP:]
    rows = score_ref.shape[1]
    residues = score_ref.shape[2]
    part_of = lane_index(residues) // 32
    seqs = block_refs[0].shape[0] // 2
    for step, block in enumerate(block_refs):
        for s in range(seqs):
            wide = jnp.concatenate(
                [jnp.where(part_of == g, block[s], jnp.zeros((), bf16)) for g in range(4)], axis=0
            )
            both = dot_nt(wide, block[seqs + s])
            score_ref[step * seqs + s] = both[:rows] * scale
            flow_ref[step * seqs + s] = both[rows:]
            value_ref[step * seqs + s] = jnp.where(part_of < 2, jnp.ones((), bf16), block[seqs + s])


def pair_kernel(recv_ref, weight_ref, aux_ref, *refs):
    pair_refs, send_ref, updated_refs = refs[:GROUP], refs[GROUP], refs[GROUP + 1 : 2 * GROUP + 1]
    flat, rbuf, lbuf, obuf, state, after = refs[2 * GROUP + 1 :]
    peers, block_rows, _ = recv_ref.shape
    seqs = block_rows // 12
    for step in range(GROUP):
        state[partner(step)] = pair_refs[step][...]
    flat[...] = recv_ref[...].astype(f32).reshape(flat.shape)
    for s in range(seqs):
        for g in range(8):
            part = flat[pl.ds(s * 8 + g, peers, stride=block_rows), :]
            rbuf[s * peers : (s + 1) * peers, g * LANES : (g + 1) * LANES] = part.astype(bf16)
        for a in range(4):
            part = flat[pl.ds(8 * seqs + 4 * s + a, peers, stride=block_rows), :]
            lbuf[s * peers : (s + 1) * peers, a * LANES : (a + 1) * LANES] = part
    left_t = lbuf[...].T.astype(bf16)
    for g in range(8):
        outer = dot_nn(left_t, rbuf[:, g * LANES : (g + 1) * LANES])
        for b in range(4):
            turned = swap_groups([outer[(4 * a + b) * 32 : (4 * a + b + 1) * 32] for a in range(4)])
            for a in range(4):
                obuf[(g * 4 + a) * 32 : (g * 4 + a + 1) * 32, b * LANES : (b + 1) * LANES] = turned[a].astype(bf16)
    sums = dot_nn(weight_ref[...], obuf[...])
    bias_w = aux_ref[8:16].astype(bf16)
    blocks = []
    for b in range(4):
        update = sums[:, b * LANES : (b + 1) * LANES] / aux_ref[b : b + 1, :]
        before = jnp.concatenate([state[a, b] for a in range(GROUP)], axis=0).astype(f32)
        updated = (before + update.T).astype(bf16)
        for a in range(GROUP):
            after[a, b] = updated[a * 32 : (a + 1) * 32]
        blocks.append(dot_nt(bias_w, layer_normalize(updated).astype(bf16)))
    lines, _, share, _ = send_ref.shape
    heads = share // 4
    for t in range(GROUP):
        block = jnp.concatenate([rows[t * heads : (t + 1) * heads] for rows in blocks], axis=0).astype(bf16)
        send_ref[:, t] = jnp.broadcast_to(block[None], (lines, share, LANES))
    for step in range(GROUP):
        updated_refs[step][...] = after[partner(step)]


def placed_bias(flat, mask_ref, heads, h):
    residues = mask_ref.shape[1]
    row = lax.broadcasted_iota(jnp.int32, (residues, LANES), 0)
    lane = lane_index(residues)
    bias = flat[pl.ds(h, residues, stride=heads), :]
    for rows, lanes in ((8, 64), (4, 32)):
        first = row % (2 * rows) < rows
        low = lane % (2 * lanes) < lanes
        moved = jnp.where(first, pltpu.roll(bias, residues - rows, 0), pltpu.roll(bias, rows, 0))
        moved = jnp.where(low, pltpu.roll(moved, LANES - lanes, 1), pltpu.roll(moved, lanes, 1))
        bias = jnp.where(first == low, bias, moved)
    return bias + mask_ref[4:5, :]


def bias_gradient_kernel(bias_ref, mask_ref, score_ref, flow_ref, *refs):
    part_refs, (pair_ref, send_ref, weights_ref, flat, grads) = refs[:GROUP], refs[GROUP:]
    columns_each = part_refs[0].shape[1]
    for step in range(GROUP):
        first = pl.multiple_of(partner(step) * columns_each, columns_each)
        pair_ref[:, pl.ds(first, columns_each), :] = part_refs[step][...]
    seqs, rows, residues = score_ref.shape
    heads = rows // residues
    flat[...] = bias_ref[...].reshape(flat.shape).astype(f32)
    ones = jnp.ones((residues, LANES), bf16)
    for h in range(heads):
        at = slice(h * residues, (h + 1) * residues)
        bias = placed_bias(flat, mask_ref, heads, h)
        total = jnp.zeros((residues, residues), f32)
        for s in range(seqs):
            scores = score_ref[s, at, :] + bias
            weights = jnp.exp(scores - jnp.max(scores, axis=-1, keepdims=True))
            rounded = weights.astype(bf16)
            weights_ref[s, at, :] = rounded
            flow = flow_ref[s, at, :]
            inverse = 1.0 / dot_nn(rounded, ones)
            delta = dot_nn((weights * flow).astype(bf16), ones) * inverse
            total = total + weights * inverse * (flow - delta)
        grads[pl.ds(h, residues, stride=heads), :] = total
    send_ref[...] = grads[...].astype(bf16).reshape(send_ref.shape)


def attended_kernel(weights_ref, value_ref, *out_refs):
    sequences, _, residues = weights_ref.shape
    seqs = sequences // GROUP
    lane = lane_index(residues)
    for step in range(GROUP):
        attended = []
        for s in range(seqs):
            mixed = dot_nn(weights_ref[step * seqs + s], value_ref[step * seqs + s])
            picked = jnp.where(lane < 96, mixed[:residues], mixed[residues:])
            totals = jnp.where(lane < 32, mixed[:residues], mixed[residues:])
            attended.append(picked / pltpu.roll(totals, 64, 1))
        out_refs[step][...] = jnp.where(lane < 64, pltpu.roll(attended[0], 64, 1), attended[1]).astype(bf16)


def output_kernel(gate_ref, wo_ref, *refs):
    in_refs, out_ref = refs[:GROUP], refs[GROUP]
    residues = gate_ref.shape[1]
    low = lane_index(residues) < 64
    zero = jnp.zeros((), bf16)
    sums = [jnp.zeros((residues, out_ref.shape[1]), f32) for _ in range(2)]
    for step in range(GROUP):
        at = partner(step)
        gated = (gate_ref[at] * in_refs[step][...].astype(f32)).astype(bf16)
        weight = wo_ref[pl.ds(pl.multiple_of(at * 64, 64), 64), :]
        weight = jnp.concatenate([weight, weight], axis=0)
        sums[0] = sums[0] + dot_nn(jnp.where(low, gated, zero), weight)
        sums[1] = sums[1] + dot_nn(jnp.where(low, zero, gated), weight)
    for s in range(2):
        out_ref[s * residues : (s + 1) * residues, :] = sums[s].astype(bf16)


def gradient_kernel(shares_ref, aux_ref, pair_ref, out_ref):
    peers, share, _ = shares_ref.shape
    total = jnp.sum(shares_ref[...].astype(f32).reshape(peers // GROUP, GROUP, share, LANES), axis=0)
    rows = pair_ref.shape[0]
    heads = share // rows
    bias_w = aux_ref[8:16]
    for i in range(rows):
        own = jnp.concatenate([total[t, i * heads : (i + 1) * heads] for t in range(GROUP)], axis=0)
        upstream = lax.dot_general(
            own, bias_w, (((0,), (0,)), ((), ())), precision=lax.Precision.HIGHEST, preferred_element_type=f32
        )
        out_ref[i] = norm_backward(pair_ref[i], upstream)


def kernel_call(body, out_shape, in_specs=None, scratch=(), flops=0, moved=0, vmem_mib=12):
    vmem = pl.BlockSpec(memory_space=pltpu.VMEM)
    many = isinstance(out_shape, (list, tuple))
    return pl.pallas_call(
        body,
        out_shape=out_shape,
        in_specs=in_specs,
        out_specs=[vmem] * len(out_shape) if many else vmem,
        scratch_shapes=list(scratch),
        compiler_params=pltpu.CompilerParams(vmem_limit_bytes=vmem_mib * 1024 * 1024),
        cost_estimate=pl.CostEstimate(flops=flops, bytes_accessed=moved, transcendentals=0),
    )


def on_device_paired(
    alignment_rows,
    pair_state,
    update_cotangent,
    sequence_mask,
    residue_mask,
    left_weight,
    right_weight,
    outer_weight,
    bias_weight,
    query_weight,
    key_weight,
    value_weight,
    gate_weight,
    output_weight,
):
    sequence_wise, residues, channel_count = alignment_rows.shape
    rows_here, _, pair_channels = pair_state.shape
    head_count = bias_weight.shape[1]
    peers = lax.axis_size("row")
    factor = left_weight.shape[1]
    lines = peers // GROUP
    vmem = pl.BlockSpec(memory_space=pltpu.VMEM)
    smem = pl.BlockSpec(memory_space=pltpu.SMEM)
    token_rows = sequence_wise * residues
    columns_each = residues // GROUP
    block_rows = sequence_wise * 12
    flat_rows = alignment_rows.reshape(token_rows, channel_count)
    shape = jax.ShapeDtypeStruct

    send, aux, normed, *pair_blocks = kernel_call(
        factors_kernel,
        [
            shape((lines, GROUP, block_rows, LANES), bf16),
            shape((16, LANES), f32),
            shape((token_rows, channel_count), bf16),
        ]
        + [shape((rows_here, columns_each, pair_channels), bf16)] * GROUP,
        [smem] * 2 + [vmem] * 7,
        [pltpu.VMEM((residues, LANES), f32)],
        flops=2 * token_rows * channel_count * LANES,
        moved=1 << 20,
        vmem_mib=60,
    )(
        sequence_mask,
        residue_mask,
        sequence_mask.reshape(1, -1),
        residue_mask.reshape(1, -1),
        bias_weight.T,
        flat_rows,
        left_weight.T,
        right_weight.T,
        pair_state,
    )
    received = lax.all_to_all(
        send.reshape(peers, block_rows, LANES), "row", split_axis=0, concat_axis=0, tiled=True
    )

    group_heads = head_count // GROUP
    head_rows = group_heads * residues
    scale = (channel_count // head_count) ** (-0.5)
    normed, *weights = lax.optimization_barrier((normed, query_weight, key_weight, value_weight, gate_weight))
    gate, *blocks = kernel_call(
        projections_kernel,
        [shape((GROUP, residues, LANES), f32)]
        + [shape((2 * sequence_wise, residues, LANES), bf16)] * GROUP,
        [vmem] * 4,
        [pltpu.VMEM((GROUP, 2 * sequence_wise, residues, LANES), bf16)],
        flops=10 * token_rows * channel_count * channel_count,
        moved=1 << 21,
    )(
        normed,
        update_cotangent.reshape(token_rows, channel_count),
        jnp.concatenate(weights, axis=1),
        output_weight,
    )

    def trade(parts):
        return parts[:1] + [
            lax.ppermute(parts[d], "row", [(i, i ^ d) for i in range(peers)]) for d in range(1, GROUP)
        ]

    pair_blocks = trade(pair_blocks)
    blocks = trade(blocks)
    scores, flow, values = kernel_call(
        lambda *refs: products_kernel(scale, *refs),
        [shape((GROUP * sequence_wise, head_rows, residues), f32)] * 2
        + [shape((GROUP * sequence_wise, residues, LANES), bf16)],
        [vmem] * GROUP,
        flops=1 << 28,
        moved=1 << 21,
    )(*blocks)

    weight_t = (
        outer_weight.reshape(factor, 4, 8, pair_channels)
        .transpose(3, 2, 1, 0)
        .reshape(pair_channels, 32 * factor)
    )
    share_rows = 4 * group_heads
    part_shape = shape((rows_here, columns_each, pair_channels), bf16)
    send_bias, *updated = kernel_call(
        pair_kernel,
        [shape((lines, GROUP, share_rows, LANES), bf16)] + [part_shape] * GROUP,
        [vmem] * (3 + GROUP),
        [
            pltpu.VMEM((peers * block_rows, LANES), f32),
            pltpu.VMEM((peers * sequence_wise, 8 * LANES), bf16),
            pltpu.VMEM((peers * sequence_wise, 4 * LANES), f32),
            pltpu.VMEM((32 * factor, 4 * LANES), bf16),
            pltpu.VMEM((GROUP, rows_here, columns_each, pair_channels), bf16),
            pltpu.VMEM((GROUP, rows_here, columns_each, pair_channels), bf16),
        ],
        flops=1 << 28,
        moved=1 << 20,
    )(received, weight_t, aux, *pair_blocks)
    bias_all = lax.all_to_all(
        send_bias.reshape(peers, share_rows, LANES), "row", split_axis=0, concat_axis=0, tiled=True
    )
    updated = trade(updated)

    pair_updated, send_grad, weights = kernel_call(
        bias_gradient_kernel,
        [
            shape((rows_here, residues, pair_channels), bf16),
            shape((peers, rows_here * group_heads, LANES), bf16),
            shape((GROUP * sequence_wise, head_rows, residues), bf16),
        ],
        [vmem] * (4 + GROUP),
        [pltpu.VMEM((head_rows, LANES), f32), pltpu.VMEM((head_rows, LANES), f32)],
        flops=1 << 28,
        moved=1 << 22,
    )(bias_all, aux, scores, flow, *updated)
    shares = lax.all_to_all(send_grad, "row", split_axis=0, concat_axis=0, tiled=True)
    attended = kernel_call(
        attended_kernel,
        [shape((residues, LANES), bf16)] * GROUP,
        [vmem] * 2,
        flops=1 << 28,
        moved=1 << 21,
    )(weights, values)
    update = kernel_call(
        output_kernel,
        shape((token_rows, channel_count), bf16),
        [vmem] * (2 + GROUP),
        flops=2 * token_rows * channel_count * channel_count,
        moved=1 << 20,
    )(gate, output_weight, *trade(list(attended)))
    pair_gradient = kernel_call(
        gradient_kernel,
        shape((rows_here, residues, pair_channels), f32),
        [vmem] * 3,
        flops=1 << 24,
        moved=1 << 20,
    )(shares, aux, pair_updated)
    return (update.reshape(alignment_rows.shape), pair_updated, pair_gradient)


def on_device(*arguments):
    rows, pair, left, bias = arguments[0], arguments[1], arguments[5], arguments[8]
    peers = lax.axis_size("row")
    fits = (
        lax.axis_size("col") == 1
        and peers == 32
        and rows.shape == (2, 128, 256)
        and pair.shape == (4, 128, 128)
        and left.shape[1] == 32
        and bias.shape[1] == 8
    )
    return (on_device_paired if fits else on_device_general)(*arguments)


def solution(mesh):
    placed = (
        P(("grp", "row"), "col", None),
        P(("grp", "row"), "col", None),
        P(("grp", "row"), "col", None),
        P("grp"),
        P("grp"),
        P(),
        P(),
        P(),
        P(),
        P(),
        P(),
        P(),
        P(),
        P(),
    )
    return jax.shard_map(
        on_device,
        mesh=mesh,
        in_specs=placed,
        out_specs=(
            P(("grp", "row"), "col", None),
            P(("grp", "row"), "col", None),
            P(("grp", "row"), "col", None),
        ),
        check_vma=False,
    )
```

```python
import jax
import jax.numpy as jnp
from jax import lax
from jax.experimental import pallas as pl
from jax.experimental.pallas import tpu as pltpu
from jax.sharding import PartitionSpec as P

norm_eps = 1e-05
mask_fill = 1000000000.0


def layer_normalize(values):
    values = values.astype(jnp.float32)
    center = values - jnp.mean(values, axis=-1, keepdims=True)
    spread = jnp.mean(center * center, axis=-1, keepdims=True)
    return center * lax.rsqrt(spread + norm_eps)


def norm_backward(values, upstream):
    values = values.astype(jnp.float32)
    center = values - jnp.mean(values, axis=-1, keepdims=True)
    inverse = lax.rsqrt(jnp.mean(center * center, axis=-1, keepdims=True) + norm_eps)
    normal_part = center * inverse
    return inverse * (
        upstream
        - jnp.mean(upstream, axis=-1, keepdims=True)
        - normal_part * jnp.mean(upstream * normal_part, axis=-1, keepdims=True)
    )


def spread_all(shard):
    copies = jnp.broadcast_to(shard[None], (lax.axis_size("row"),) + shard.shape)
    gathered = lax.all_to_all(copies, "row", split_axis=0, concat_axis=0, tiled=True)
    return gathered.reshape((-1,) + shard.shape[1:])


def attend_partial(
    projected_queries, projected_keys, projected_values, bias_all, key_mask, score_scale
):
    scores = jnp.einsum(
        "ihd,jhd->ihj", projected_queries, projected_keys, preferred_element_type=jnp.float32
    )
    scores = scores * score_scale + bias_all.astype(jnp.float32) + key_mask
    maxima = jnp.max(scores, axis=-1)
    weights = jnp.exp(scores - maxima[..., None])
    totals = jnp.sum(weights, axis=-1)
    summed = jnp.einsum(
        "ihj,jhd->ihd",
        weights.astype(jnp.bfloat16),
        projected_values,
        preferred_element_type=jnp.float32,
    )
    return (maxima, totals, summed.reshape(summed.shape[0], -1))


def on_device_general(
    alignment_rows,
    pair_state,
    update_cotangent,
    sequence_mask,
    residue_mask,
    left_weight,
    right_weight,
    outer_weight,
    bias_weight,
    query_weight,
    key_weight,
    value_weight,
    gate_weight,
    output_weight,
):
    sequence_wise, residue_half, channel_count = alignment_rows.shape
    rows_here = pair_state.shape[0]
    residues = residue_mask.shape[0]
    head_count = bias_weight.shape[1]
    head_dim = channel_count // head_count
    score_scale = head_dim ** (-0.5)
    row_index = lax.axis_index("row")
    col_index = lax.axis_index("col")
    complete_alignment, complete_cotangent = (
        lax.all_gather(alignment_rows, "col", axis=1, tiled=True),
        lax.all_gather(update_cotangent, "col", axis=1, tiled=True),
    )
    seq_live = sequence_mask.astype(jnp.float32)
    res_live = residue_mask.astype(jnp.float32)
    own_seq = lax.dynamic_slice_in_dim(seq_live, row_index * sequence_wise, sequence_wise)
    own_cols = lax.dynamic_slice_in_dim(res_live, col_index * residue_half, residue_half)
    own_rows = lax.dynamic_slice_in_dim(res_live, row_index * rows_here, rows_here)
    normalized_input = layer_normalize(complete_alignment).astype(jnp.bfloat16)
    flat_rows = normalized_input.reshape(-1, channel_count)
    normed_half = lax.dynamic_slice_in_dim(
        normalized_input, col_index * residue_half, residue_half, 1
    )
    half_rows = normed_half.reshape(-1, channel_count)
    left_proj = jnp.dot(flat_rows, left_weight, preferred_element_type=jnp.float32).reshape(
        sequence_wise, residues, -1
    )
    left_proj = (left_proj * (own_seq[:, None] * res_live[None, :])[..., None]).astype(jnp.bfloat16)
    right_proj = jnp.dot(half_rows, right_weight, preferred_element_type=jnp.float32).reshape(
        sequence_wise, residue_half, -1
    )
    right_proj = (right_proj * (own_seq[:, None] * own_cols[None, :])[..., None]).astype(
        jnp.bfloat16
    )
    left_tile = lax.all_to_all(left_proj, "row", split_axis=1, concat_axis=0, tiled=True)
    right_all = spread_all(right_proj)
    outer_width = left_tile.shape[2]
    outer_sum = lax.dot_general(
        left_tile.reshape(left_tile.shape[0], -1),
        right_all.reshape(right_all.shape[0], -1),
        (((0,), (0,)), ((), ())),
        preferred_element_type=jnp.float32,
    )
    outer_half = outer_sum.astype(jnp.bfloat16).reshape(
        rows_here, outer_width, residue_half, outer_width
    )
    opm_update = jnp.einsum(
        "ipjq,pqz->ijz", outer_half, outer_weight, preferred_element_type=jnp.float32
    )
    divisor = jnp.maximum(jnp.sum(seq_live) * own_rows[:, None] * own_cols[None, :], 1.0)
    pair_updated = (pair_state.astype(jnp.float32) + opm_update / divisor[..., None]).astype(
        jnp.bfloat16
    )
    pair_normed = layer_normalize(pair_updated).astype(jnp.bfloat16)
    bias_tile = jnp.einsum(
        "ijz,zh->ihj", pair_normed, bias_weight, preferred_element_type=jnp.float32
    ).astype(jnp.bfloat16)
    projected_queries = (
        jnp.dot(flat_rows, query_weight, preferred_element_type=jnp.float32)
        .astype(jnp.bfloat16)
        .reshape(sequence_wise, residues, head_count, head_dim)
    )
    gate_activations = jax.nn.sigmoid(
        jnp.dot(flat_rows, gate_weight, preferred_element_type=jnp.float32)
    ).reshape(sequence_wise, residues, channel_count)
    key_live = (res_live - 1.0) * mask_fill
    half_live = lax.dynamic_slice_in_dim(key_live, col_index * residue_half, residue_half)
    bias_cols = lax.all_gather(bias_tile, "col", axis=2, tiled=True)
    bias_all = spread_all(bias_cols)
    key_count = bias_all.shape[2]
    projected_keys = (
        jnp.dot(flat_rows, key_weight, preferred_element_type=jnp.float32)
        .astype(jnp.bfloat16)
        .reshape(sequence_wise, key_count, head_count, head_dim)
    )
    projected_values = (
        jnp.dot(flat_rows, value_weight, preferred_element_type=jnp.float32)
        .astype(jnp.bfloat16)
        .reshape(sequence_wise, key_count, head_count, head_dim)
    )
    maxima, totals, summed = lax.map(
        lambda inputs: attend_partial(
            inputs[0], inputs[1], inputs[2], bias_all, key_live, score_scale
        ),
        (projected_queries, projected_keys, projected_values),
    )
    attended = summed / jnp.repeat(totals, head_dim, axis=-1)
    gated = gate_activations * attended
    gated_own = lax.dynamic_slice_in_dim(gated, col_index * residue_half, residue_half, 1).astype(
        jnp.bfloat16
    )
    alignment_update = (
        jnp.dot(
            gated_own.reshape(-1, channel_count), output_weight, preferred_element_type=jnp.float32
        )
        .astype(jnp.bfloat16)
        .reshape(sequence_wise, residue_half, channel_count)
    )
    d_gated = lax.dot_general(
        complete_cotangent.reshape(-1, channel_count),
        output_weight,
        (((1,), (1,)), ((), ())),
        preferred_element_type=jnp.float32,
    ).reshape(sequence_wise, residues, channel_count)
    d_attended = d_gated * gate_activations
    delta_sum = jnp.sum(
        (d_attended * attended).reshape(sequence_wise, residues, head_count, head_dim), axis=-1
    )
    d_rounded = d_attended.astype(jnp.bfloat16).reshape(
        sequence_wise, residues, head_count, head_dim
    )
    log_total = maxima + jnp.log(totals)
    keys_half = lax.dynamic_slice_in_dim(projected_keys, col_index * residue_half, residue_half, 1)
    values_half = lax.dynamic_slice_in_dim(
        projected_values, col_index * residue_half, residue_half, 1
    )
    bias_half = lax.dynamic_slice_in_dim(bias_all, col_index * residue_half, residue_half, 2)
    bias_rows = bias_half.astype(jnp.float32)

    def single_sequence(running, sequence_items):
        query_rows, d_rows, total_rows, delta_rows, keys_one, values_one = sequence_items
        scores = jnp.einsum(
            "ihd,jhd->ihj", query_rows, keys_one, preferred_element_type=jnp.float32
        )
        scores = scores * score_scale + bias_rows + half_live
        probs = jnp.exp(scores - total_rows[..., None])
        d_weights = jnp.einsum(
            "ihd,jhd->ihj", d_rows, values_one, preferred_element_type=jnp.float32
        )
        return (running + probs * (d_weights - delta_rows[..., None]), None)

    sequence_items = (projected_queries, d_rounded, log_total, delta_sum, keys_half, values_half)
    initial_value = jnp.zeros(
        (rows_here * lax.axis_size("row"), head_count, residue_half), jnp.float32
    )
    result, unused = lax.scan(single_sequence, initial_value, sequence_items)
    shares = lax.all_to_all(
        result.astype(jnp.bfloat16).reshape((-1,) + (rows_here,) + result.shape[1:]),
        "row",
        split_axis=0,
        concat_axis=0,
        tiled=True,
    )
    bias_gradient = jnp.sum(shares.astype(jnp.float32), axis=0)
    d_normed = jnp.einsum(
        "ihj,zh->ijz",
        bias_gradient,
        bias_weight.astype(jnp.float32),
        precision=lax.Precision.HIGHEST,
    )
    pair_gradient = norm_backward(pair_updated, d_normed)
    return (alignment_update, pair_updated, pair_gradient)


LANES = 128
GROUP = 4
PIECES = 4
f32 = jnp.float32
bf16 = jnp.bfloat16


def dot_nn(a, b):
    return lax.dot_general(a, b, (((1,), (0,)), ((), ())), preferred_element_type=f32)


def dot_nt(a, b):
    return lax.dot_general(a, b, (((1,), (1,)), ((), ())), preferred_element_type=f32)


def dot_tn(a, b):
    return lax.dot_general(a, b, (((0,), (0,)), ((), ())), preferred_element_type=f32)


def lane_index(rows):
    return lax.broadcasted_iota(jnp.int32, (rows, LANES), 1)


def swap_groups(parts):
    lane = lane_index(parts[0].shape[0])
    low, even = lane < 64, lane % 64 < 32
    parts = [
        jnp.where(low, parts[0], pltpu.roll(parts[2], 64, 1)),
        jnp.where(low, parts[1], pltpu.roll(parts[3], 64, 1)),
        jnp.where(low, pltpu.roll(parts[0], 64, 1), parts[2]),
        jnp.where(low, pltpu.roll(parts[1], 64, 1), parts[3]),
    ]
    return [
        jnp.where(even, parts[0], pltpu.roll(parts[1], 32, 1)),
        jnp.where(even, pltpu.roll(parts[0], 96, 1), parts[1]),
        jnp.where(even, parts[2], pltpu.roll(parts[3], 32, 1)),
        jnp.where(even, pltpu.roll(parts[2], 96, 1), parts[3]),
    ]


def factors_kernel(
    seq_smem_ref, res_smem_ref, seq_ref, res_ref, bias_w_ref, left_ref, right_ref, pair_ref, *refs
):
    row_refs, (send_ref, aux_ref, normed_ref, *pair_refs, left_scr) = refs[:PIECES], refs[PIECES:]
    columns_each = pair_refs[0].shape[1]
    for step in range(GROUP):
        first = pl.multiple_of(partner(step) * columns_each, columns_each)
        pair_refs[step][...] = pair_ref[:, pl.ds(first, columns_each), :]
    lines = send_ref.shape[0]
    seqs = send_ref.shape[2] // 12
    residues = res_ref.shape[1]
    me = lax.axis_index("row")
    normed = jnp.concatenate([layer_normalize(rows[...]).astype(bf16) for rows in row_refs], axis=0)
    normed_ref[...] = normed
    live = res_ref[...].astype(f32)
    live_rows = jnp.broadcast_to(live, (residues, residues)).T
    right_t = right_ref[...]
    left_wide = jnp.concatenate([left_ref[...]] * 4, axis=0)
    lane_group = lane_index(lines) // 32
    quarters = []
    tail = []
    for s in range(seqs):
        seq_live = seq_smem_ref[me * seqs + s].astype(f32)
        own = normed[s * residues : (s + 1) * residues]
        factor = dot_nt(right_t, own) * (live * seq_live)
        quarters.append(swap_groups([factor[a * 8 : (a + 1) * 8] for a in range(4)]))
        left_scr[...] = dot_nt(own, left_wide) * (live_rows * seq_live)
        for a in range(4):
            row = jnp.zeros((lines, LANES), f32)
            for b in range(4):
                part = left_scr[pl.ds(4 * a + b, lines, stride=4 * GROUP), :]
                row = jnp.where(lane_group == b, part, row)
            tail.append(row)
    tail = jnp.stack(tail, axis=1).astype(bf16)
    right_rows = 8 * seqs
    for t in range(GROUP):
        block = jnp.concatenate([own[t] for own in quarters], axis=0).astype(bf16)
        send_ref[:, t, :right_rows, :] = jnp.broadcast_to(block[None], (lines, right_rows, LANES))
        send_ref[:, t, right_rows:, :] = tail
    aux_ref[0:4] = tile_divisor(res_smem_ref, res_ref, seq_ref)
    aux_ref[4:8] = jnp.broadcast_to((live - 1.0) * mask_fill, (4, LANES))
    aux_ref[8:16] = bias_w_ref[...].astype(f32)


def side_by_side(first, second, at):
    low = lane_index(first.shape[0]) < 64
    span = slice(at // 2 * LANES, at // 2 * LANES + LANES)
    first, second = first[:, span], second[:, span]
    if at % 2 == 0:
        return jnp.where(low, first, pltpu.roll(second, 64, 1))
    return jnp.where(low, pltpu.roll(first, 64, 1), second)


def partner(step):
    return lax.bitwise_xor(lax.rem(lax.axis_index("row"), GROUP), step)


def tile_divisor(res_smem_ref, res_ref, seq_ref):
    own = partner(0)
    rows = lax.div(lax.axis_index("row"), GROUP) * 16
    lane = lane_index(1)
    live = res_ref[...].astype(f32)
    columns = jnp.zeros((1, LANES), f32)
    for t in range(GROUP):
        turned = live if t == 0 else pltpu.roll(live, LANES - 32 * t, 1)
        columns = jnp.where(own == t, turned, columns)
    columns = jnp.where(lane < 32, columns, 0.0)
    columns = columns + pltpu.roll(columns, 32, 1)
    columns = columns + pltpu.roll(columns, 64, 1)
    total = jnp.sum(seq_ref[...].astype(f32), axis=-1, keepdims=True)
    lines = []
    for b in range(4):
        line = jnp.zeros((1, LANES), f32)
        for a in range(4):
            line = jnp.where(lane // 32 == a, res_smem_ref[rows + 4 * a + b].astype(f32), line)
        lines.append(jnp.maximum(total * line * columns, 1.0))
    return jnp.concatenate(lines, axis=0)


def projections_kernel(
    normed_ref, cot_ref, weights_ref, wo_ref, aux_ref, pair_ref, gate_ref, aux_out_ref, pair_out_ref, *rest
):
    block_refs, every = rest[:GROUP], rest[GROUP]
    aux_out_ref[...] = aux_ref[...]
    pair_out_ref[...] = pair_ref[...]
    normed = normed_ref[...]
    tokens = normed.shape[0]
    residues = gate_ref.shape[1]
    seqs = tokens // residues
    channels = normed.shape[1]
    queries, keys, values, gate = [
        dot_nn(normed, weights_ref[:, at * channels : (at + 1) * channels]) for at in range(4)
    ]
    gate = jax.nn.sigmoid(gate)
    d_attended = dot_nt(cot_ref[...], wo_ref[...]) * gate
    for t in range(GROUP):
        rows = side_by_side(queries, d_attended, t).astype(bf16)
        columns = side_by_side(keys, values, t).astype(bf16)
        gate_ref[t] = side_by_side(gate[:residues], gate[residues:], t)
        for s in range(seqs):
            every[t, s] = rows[s * residues : (s + 1) * residues]
            every[t, seqs + s] = columns[s * residues : (s + 1) * residues]
    for step in range(GROUP):
        block_refs[step][...] = every[partner(step)]


def products_kernel(scale, *refs):
    block_refs, (score_ref, flow_ref, value_ref) = refs[:GROUP], refs[GROUP:]
    rows = score_ref.shape[1]
    residues = score_ref.shape[2]
    part_of = lane_index(residues) // 32
    seqs = block_refs[0].shape[0] // 2
    for step, block in enumerate(block_refs):
        for s in range(seqs):
            wide = jnp.concatenate(
                [jnp.where(part_of == g, block[s], jnp.zeros((), bf16)) for g in range(4)], axis=0
            )
            both = dot_nt(wide, block[seqs + s])
            score_ref[step * seqs + s] = both[:rows] * scale
            flow_ref[step * seqs + s] = both[rows:]
            value_ref[step * seqs + s] = jnp.where(part_of < 2, jnp.ones((), bf16), block[seqs + s])


def pair_kernel(recv_ref, weight_ref, aux_ref, *refs):
    pair_refs, send_ref, updated_refs = refs[:GROUP], refs[GROUP], refs[GROUP + 1 : 2 * GROUP + 1]
    flat, rbuf, lbuf, obuf, state, after = refs[2 * GROUP + 1 :]
    peers, block_rows, _ = recv_ref.shape
    seqs = block_rows // 12
    for step in range(GROUP):
        state[partner(step)] = pair_refs[step][...]
    flat[...] = recv_ref[...].astype(f32).reshape(flat.shape)
    for s in range(seqs):
        for g in range(8):
            part = flat[pl.ds(s * 8 + g, peers, stride=block_rows), :]
            for a in range(4):
                turned = part if a == 0 else pltpu.roll(part, 32 * a, 1)
                rbuf[a, s * peers : (s + 1) * peers, g * LANES : (g + 1) * LANES] = turned.astype(bf16)
        for a in range(4):
            part = flat[pl.ds(8 * seqs + 4 * s + a, peers, stride=block_rows), :]
            lbuf[s * peers : (s + 1) * peers, a * LANES : (a + 1) * LANES] = part
    left_t = lbuf[...].T.astype(bf16)
    outer = [dot_nn(left_t[a * LANES : (a + 1) * LANES], rbuf[a]).astype(bf16) for a in range(4)]
    lane_group = lane_index(LANES) // 32
    sums = None
    for q in range(4):
        for g in range(8):
            span = slice(g * LANES, (g + 1) * LANES)
            picked = outer[3][:, span]
            for a in range(3):
                picked = jnp.where(lane_group == (q + a) % 4, outer[a][:, span], picked)
            for b in range(4):
                obuf[q, g * 32 : (g + 1) * 32, b * LANES : (b + 1) * LANES] = picked[b * 32 : (b + 1) * 32]
        part = dot_nn(weight_ref[q], obuf[q])
        if q:
            part = jnp.concatenate(
                [pltpu.roll(part[:, b * LANES : (b + 1) * LANES], LANES - 32 * q, 1) for b in range(4)], axis=1
            )
        sums = part if sums is None else sums + part
    bias_w = aux_ref[8:16].astype(bf16)
    blocks = []
    for b in range(4):
        update = sums[:, b * LANES : (b + 1) * LANES] / aux_ref[b : b + 1, :]
        before = jnp.concatenate([state[a, b] for a in range(GROUP)], axis=0).astype(f32)
        updated = (before + update.T).astype(bf16)
        for a in range(GROUP):
            after[a, b] = updated[a * 32 : (a + 1) * 32]
        line = dot_nt(bias_w, layer_normalize(updated).astype(bf16))
        blocks.append(pltpu.roll(line, partner(0) * 32, 1))
    lines, _, share, _ = send_ref.shape
    heads = share // 4
    for t in range(GROUP):
        block = jnp.concatenate([rows[t * heads : (t + 1) * heads] for rows in blocks], axis=0).astype(bf16)
        send_ref[:, t] = jnp.broadcast_to(block[None], (lines, share, LANES))
    for step in range(GROUP):
        updated_refs[step][...] = after[partner(step)]


def place_bias(flat, mask_ref, heads, h, bias):
    lines = bias.shape[0] // 16
    lane_group = lane_index(lines) // 32
    mask = mask_ref[4:5, :]
    for b in range(4):
        rows = [flat[pl.ds((4 * t + b) * heads + h, lines, stride=16 * heads), :] for t in range(GROUP)]
        for a in range(4):
            picked = rows[3]
            for t in range(3):
                picked = jnp.where(lane_group == (a + t) % 4, rows[t], picked)
            if a:
                picked = pltpu.roll(picked, LANES - 32 * a, 1)
            bias[pl.ds(4 * a + b, lines, stride=16), :] = picked + mask


def bias_gradient_kernel(bias_ref, mask_ref, score_ref, flow_ref, *refs):
    part_refs, (pair_ref, send_ref, weights_ref, flat, grads, placed) = refs[:GROUP], refs[GROUP:]
    columns_each = part_refs[0].shape[1]
    for step in range(GROUP):
        first = pl.multiple_of(partner(step) * columns_each, columns_each)
        pair_ref[:, pl.ds(first, columns_each), :] = part_refs[step][...]
    seqs, rows, residues = score_ref.shape
    heads = rows // residues
    flat[...] = bias_ref[...].reshape(flat.shape).astype(f32)
    ones = jnp.ones((residues, LANES), bf16)
    for h in range(heads):
        at = slice(h * residues, (h + 1) * residues)
        place_bias(flat, mask_ref, heads, h, placed.at[h])
        bias = placed[h]
        total = jnp.zeros((residues, residues), f32)
        for s in range(seqs):
            scores = score_ref[s, at, :] + bias
            weights = jnp.exp(scores - jnp.max(scores, axis=-1, keepdims=True))
            rounded = weights.astype(bf16)
            weights_ref[s, at, :] = rounded
            flow = flow_ref[s, at, :]
            inverse = 1.0 / dot_nn(rounded, ones)
            delta = dot_nn((weights * flow).astype(bf16), ones) * inverse
            total = total + weights * inverse * (flow - delta)
        grads[pl.ds(h, residues, stride=heads), :] = total
    send_ref[...] = grads[...].astype(bf16).reshape(send_ref.shape)


def attended_kernel(weights_ref, value_ref, *out_refs):
    sequences, _, residues = weights_ref.shape
    seqs = sequences // GROUP
    lane = lane_index(residues)
    for step in range(GROUP):
        attended = []
        for s in range(seqs):
            mixed = dot_nn(weights_ref[step * seqs + s], value_ref[step * seqs + s])
            picked = jnp.where(lane < 96, mixed[:residues], mixed[residues:])
            totals = jnp.where(lane < 32, mixed[:residues], mixed[residues:])
            attended.append(picked / pltpu.roll(totals, 64, 1))
        out_refs[step][...] = jnp.where(lane < 64, pltpu.roll(attended[0], 64, 1), attended[1]).astype(bf16)


def output_kernel(gate_ref, wo_ref, *refs):
    in_refs, out_ref = refs[:GROUP], refs[GROUP]
    residues = gate_ref.shape[1]
    low = lane_index(residues) < 64
    zero = jnp.zeros((), bf16)
    sums = [jnp.zeros((residues, out_ref.shape[1]), f32) for _ in range(2)]
    for step in range(GROUP):
        at = partner(step)
        gated = (gate_ref[at] * in_refs[step][...].astype(f32)).astype(bf16)
        weight = wo_ref[pl.ds(pl.multiple_of(at * 64, 64), 64), :]
        weight = jnp.concatenate([weight, weight], axis=0)
        sums[0] = sums[0] + dot_nn(jnp.where(low, gated, zero), weight)
        sums[1] = sums[1] + dot_nn(jnp.where(low, zero, gated), weight)
    for s in range(2):
        out_ref[s * residues : (s + 1) * residues, :] = sums[s].astype(bf16)


def split_sum(values):
    high = values.astype(bf16)
    return high, (values - high.astype(f32)).astype(bf16)


def gradient_kernel(shares_ref, aux_ref, pair_ref, out_hbm, result, left_for):
    peers, share, _ = shares_ref.shape
    rows, _, channels = pair_ref.shape
    heads = share // rows
    total = jnp.sum(shares_ref[...].astype(f32).reshape(peers // GROUP, GROUP, share, LANES), axis=0)
    bias_w = aux_ref[8:16]
    mean_high, mean_low = split_sum(
        jnp.broadcast_to(jnp.mean(bias_w, axis=-1, keepdims=True), bias_w.shape)
    )
    exact = bias_w.astype(bf16)
    none = jnp.zeros(exact.shape, bf16)
    weights = jnp.concatenate(
        [
            jnp.concatenate([exact, mean_high], axis=1),
            jnp.concatenate([exact, mean_high], axis=1),
            jnp.concatenate([none, mean_low], axis=1),
        ],
        axis=0,
    )
    moves = []
    for i in range(rows):
        own = jnp.concatenate([total[t, i * heads : (i + 1) * heads] for t in range(GROUP)], axis=0)
        high, low = split_sum(own)
        both = dot_tn(jnp.concatenate([high, low, high], axis=0), weights)
        upstream, mean = both[:, :channels], both[:, channels:]
        values = pair_ref[i].astype(f32)
        center = values - jnp.mean(values, axis=-1, keepdims=True)
        inverse = lax.rsqrt(jnp.mean(center * center, axis=-1, keepdims=True) + norm_eps)
        normal = center * inverse
        result[i] = inverse * (
            upstream - mean - normal * jnp.mean(upstream * normal, axis=-1, keepdims=True)
        )
        moves.append(pltpu.make_async_copy(result.at[i], out_hbm.at[i], left_for.at[i]))
        moves[-1].start()
    for move in moves:
        move.wait()


def kernel_call(body, out_shape, in_specs=None, scratch=(), flops=0, moved=0, vmem_mib=12, out_specs=None, grid=()):
    vmem = pl.BlockSpec(memory_space=pltpu.VMEM)
    many = isinstance(out_shape, (list, tuple))
    return pl.pallas_call(
        body,
        grid=grid,
        out_shape=out_shape,
        in_specs=in_specs,
        out_specs=out_specs or ([vmem] * len(out_shape) if many else vmem),
        scratch_shapes=list(scratch),
        compiler_params=pltpu.CompilerParams(vmem_limit_bytes=vmem_mib * 1024 * 1024),
        cost_estimate=pl.CostEstimate(flops=flops, bytes_accessed=moved, transcendentals=0),
    )


def on_device_paired(
    alignment_rows,
    pair_state,
    update_cotangent,
    sequence_mask,
    residue_mask,
    left_weight,
    right_weight,
    outer_weight,
    bias_weight,
    query_weight,
    key_weight,
    value_weight,
    gate_weight,
    output_weight,
):
    sequence_wise, residues, channel_count = alignment_rows.shape
    rows_here, _, pair_channels = pair_state.shape
    head_count = bias_weight.shape[1]
    peers = lax.axis_size("row")
    factor = left_weight.shape[1]
    lines = peers // GROUP
    vmem = pl.BlockSpec(memory_space=pltpu.VMEM)
    smem = pl.BlockSpec(memory_space=pltpu.SMEM)
    token_rows = sequence_wise * residues
    columns_each = residues // GROUP
    block_rows = sequence_wise * 12
    flat_rows = alignment_rows.reshape(token_rows, channel_count)
    shape = jax.ShapeDtypeStruct

    pieces = [
        pl.BlockSpec((token_rows // PIECES, channel_count), lambda step, at=at: (at, 0)) for at in range(PIECES)
    ]
    send, aux, normed, *pair_blocks = kernel_call(
        factors_kernel,
        [
            shape((lines, GROUP, block_rows, LANES), bf16),
            shape((16, LANES), f32),
            shape((token_rows, channel_count), bf16),
        ]
        + [shape((rows_here, columns_each, pair_channels), bf16)] * GROUP,
        [smem] * 2 + [vmem] * 6 + pieces,
        [pltpu.VMEM((residues, LANES), f32)],
        flops=2 * token_rows * channel_count * LANES,
        moved=1 << 20,
        vmem_mib=60,
        grid=(1,),
    )(
        sequence_mask,
        residue_mask,
        sequence_mask.reshape(1, -1),
        residue_mask.reshape(1, -1),
        bias_weight.T,
        left_weight.T,
        right_weight.T,
        pair_state,
        *[flat_rows] * PIECES,
    )
    received = lax.all_to_all(
        send.reshape(peers, block_rows, LANES), "row", split_axis=0, concat_axis=0, tiled=True
    )

    group_heads = head_count // GROUP
    head_rows = group_heads * residues
    scale = (channel_count // head_count) ** (-0.5)
    normed, *weights = lax.optimization_barrier((normed, query_weight, key_weight, value_weight, gate_weight))
    part_shape = shape((rows_here, columns_each, pair_channels), bf16)
    gate, aux, own_block, *blocks = kernel_call(
        projections_kernel,
        [shape((GROUP, residues, LANES), f32), shape((16, LANES), f32), part_shape]
        + [shape((2 * sequence_wise, residues, LANES), bf16)] * GROUP,
        [vmem] * 6,
        [pltpu.VMEM((GROUP, 2 * sequence_wise, residues, LANES), bf16)],
        flops=10 * token_rows * channel_count * channel_count,
        moved=1 << 21,
    )(
        normed,
        update_cotangent.reshape(token_rows, channel_count),
        jnp.concatenate(weights, axis=1),
        output_weight,
        aux,
        pair_blocks[0],
    )

    def trade(parts):
        return parts[:1] + [
            lax.ppermute(parts[d], "row", [(i, i ^ d) for i in range(peers)]) for d in range(1, GROUP)
        ]

    pair_blocks = [own_block] + trade(pair_blocks)[1:]
    blocks = trade(blocks)
    scores, flow, values = kernel_call(
        lambda *refs: products_kernel(scale, *refs),
        [shape((GROUP * sequence_wise, head_rows, residues), f32)] * 2
        + [shape((GROUP * sequence_wise, residues, LANES), bf16)],
        [vmem] * GROUP,
        flops=1 << 28,
        moved=1 << 21,
    )(*blocks)

    weight_t = (
        outer_weight.reshape(factor, 4, 8, pair_channels)
        .transpose(1, 3, 2, 0)
        .reshape(4, pair_channels, 8 * factor)
    )
    share_rows = 4 * group_heads
    send_bias, *updated = kernel_call(
        pair_kernel,
        [shape((lines, GROUP, share_rows, LANES), bf16)] + [part_shape] * GROUP,
        [vmem] * (3 + GROUP),
        [
            pltpu.VMEM((peers * block_rows, LANES), f32),
            pltpu.VMEM((4, peers * sequence_wise, 8 * LANES), bf16),
            pltpu.VMEM((peers * sequence_wise, 4 * LANES), f32),
            pltpu.VMEM((4, 8 * factor, 4 * LANES), bf16),
            pltpu.VMEM((GROUP, rows_here, columns_each, pair_channels), bf16),
            pltpu.VMEM((GROUP, rows_here, columns_each, pair_channels), bf16),
        ],
        flops=1 << 28,
        moved=1 << 20,
    )(received, weight_t, aux, *pair_blocks)
    bias_all = lax.all_to_all(
        send_bias.reshape(peers, share_rows, LANES), "row", split_axis=0, concat_axis=0, tiled=True
    )
    updated = trade(updated)

    pair_updated, send_grad, weights = kernel_call(
        bias_gradient_kernel,
        [
            shape((rows_here, residues, pair_channels), bf16),
            shape((peers, rows_here * group_heads, LANES), bf16),
            shape((GROUP * sequence_wise, head_rows, residues), bf16),
        ],
        [vmem] * (4 + GROUP),
        [pltpu.VMEM((head_rows, LANES), f32)] * 2 + [pltpu.VMEM((group_heads, residues, LANES), f32)],
        flops=1 << 28,
        moved=1 << 22,
    )(bias_all, aux, scores, flow, *updated)
    shares = lax.all_to_all(send_grad, "row", split_axis=0, concat_axis=0, tiled=True)
    attended = kernel_call(
        attended_kernel,
        [shape((residues, LANES), bf16)] * GROUP,
        [vmem] * 2,
        flops=1 << 28,
        moved=1 << 21,
    )(weights, values)
    update = kernel_call(
        output_kernel,
        shape((token_rows, channel_count), bf16),
        [vmem] * (2 + GROUP),
        flops=2 * token_rows * channel_count * channel_count,
        moved=1 << 20,
    )(gate, output_weight, *trade(list(attended)))
    pair_gradient = kernel_call(
        gradient_kernel,
        shape((rows_here, residues, pair_channels), f32),
        [vmem] * 3,
        [pltpu.VMEM((rows_here, residues, pair_channels), f32), pltpu.SemaphoreType.DMA((rows_here,))],
        flops=1 << 24,
        moved=1 << 20,
        out_specs=pl.BlockSpec(memory_space=pltpu.HBM),
    )(shares, aux, pair_updated)
    return (update.reshape(alignment_rows.shape), pair_updated, pair_gradient)


def on_device(*arguments):
    rows, pair, left, bias = arguments[0], arguments[1], arguments[5], arguments[8]
    peers = lax.axis_size("row")
    fits = (
        lax.axis_size("col") == 1
        and peers == 32
        and rows.shape == (2, 128, 256)
        and pair.shape == (4, 128, 128)
        and left.shape[1] == 32
        and bias.shape[1] == 8
    )
    return (on_device_paired if fits else on_device_general)(*arguments)


def solution(mesh):
    placed = (
        P(("grp", "row"), "col", None),
        P(("grp", "row"), "col", None),
        P(("grp", "row"), "col", None),
        P("grp"),
        P("grp"),
        P(),
        P(),
        P(),
        P(),
        P(),
        P(),
        P(),
        P(),
        P(),
    )
    return jax.shard_map(
        on_device,
        mesh=mesh,
        in_specs=placed,
        out_specs=(
            P(("grp", "row"), "col", None),
            P(("grp", "row"), "col", None),
            P(("grp", "row"), "col", None),
        ),
        check_vma=False,
    )
```

```python
import jax
import jax.numpy as jnp
from jax import lax
from jax.experimental import pallas as pl
from jax.experimental.pallas import tpu as pltpu
from jax.sharding import PartitionSpec as P

norm_eps = 1e-05
mask_fill = 1000000000.0


def layer_normalize(values):
    values = values.astype(jnp.float32)
    center = values - jnp.mean(values, axis=-1, keepdims=True)
    spread = jnp.mean(center * center, axis=-1, keepdims=True)
    return center * lax.rsqrt(spread + norm_eps)


def norm_backward(values, upstream):
    values = values.astype(jnp.float32)
    center = values - jnp.mean(values, axis=-1, keepdims=True)
    inverse = lax.rsqrt(jnp.mean(center * center, axis=-1, keepdims=True) + norm_eps)
    normal_part = center * inverse
    return inverse * (
        upstream
        - jnp.mean(upstream, axis=-1, keepdims=True)
        - normal_part * jnp.mean(upstream * normal_part, axis=-1, keepdims=True)
    )


def spread_all(shard):
    copies = jnp.broadcast_to(shard[None], (lax.axis_size("row"),) + shard.shape)
    gathered = lax.all_to_all(copies, "row", split_axis=0, concat_axis=0, tiled=True)
    return gathered.reshape((-1,) + shard.shape[1:])


def attend_partial(
    projected_queries, projected_keys, projected_values, bias_all, key_mask, score_scale
):
    scores = jnp.einsum(
        "ihd,jhd->ihj", projected_queries, projected_keys, preferred_element_type=jnp.float32
    )
    scores = scores * score_scale + bias_all.astype(jnp.float32) + key_mask
    maxima = jnp.max(scores, axis=-1)
    weights = jnp.exp(scores - maxima[..., None])
    totals = jnp.sum(weights, axis=-1)
    summed = jnp.einsum(
        "ihj,jhd->ihd",
        weights.astype(jnp.bfloat16),
        projected_values,
        preferred_element_type=jnp.float32,
    )
    return (maxima, totals, summed.reshape(summed.shape[0], -1))


def on_device_general(
    alignment_rows,
    pair_state,
    update_cotangent,
    sequence_mask,
    residue_mask,
    left_weight,
    right_weight,
    outer_weight,
    bias_weight,
    query_weight,
    key_weight,
    value_weight,
    gate_weight,
    output_weight,
):
    sequence_wise, residue_half, channel_count = alignment_rows.shape
    rows_here = pair_state.shape[0]
    residues = residue_mask.shape[0]
    head_count = bias_weight.shape[1]
    head_dim = channel_count // head_count
    score_scale = head_dim ** (-0.5)
    row_index = lax.axis_index("row")
    col_index = lax.axis_index("col")
    complete_alignment, complete_cotangent = (
        lax.all_gather(alignment_rows, "col", axis=1, tiled=True),
        lax.all_gather(update_cotangent, "col", axis=1, tiled=True),
    )
    seq_live = sequence_mask.astype(jnp.float32)
    res_live = residue_mask.astype(jnp.float32)
    own_seq = lax.dynamic_slice_in_dim(seq_live, row_index * sequence_wise, sequence_wise)
    own_cols = lax.dynamic_slice_in_dim(res_live, col_index * residue_half, residue_half)
    own_rows = lax.dynamic_slice_in_dim(res_live, row_index * rows_here, rows_here)
    normalized_input = layer_normalize(complete_alignment).astype(jnp.bfloat16)
    flat_rows = normalized_input.reshape(-1, channel_count)
    normed_half = lax.dynamic_slice_in_dim(
        normalized_input, col_index * residue_half, residue_half, 1
    )
    half_rows = normed_half.reshape(-1, channel_count)
    left_proj = jnp.dot(flat_rows, left_weight, preferred_element_type=jnp.float32).reshape(
        sequence_wise, residues, -1
    )
    left_proj = (left_proj * (own_seq[:, None] * res_live[None, :])[..., None]).astype(jnp.bfloat16)
    right_proj = jnp.dot(half_rows, right_weight, preferred_element_type=jnp.float32).reshape(
        sequence_wise, residue_half, -1
    )
    right_proj = (right_proj * (own_seq[:, None] * own_cols[None, :])[..., None]).astype(
        jnp.bfloat16
    )
    left_tile = lax.all_to_all(left_proj, "row", split_axis=1, concat_axis=0, tiled=True)
    right_all = spread_all(right_proj)
    outer_width = left_tile.shape[2]
    outer_sum = lax.dot_general(
        left_tile.reshape(left_tile.shape[0], -1),
        right_all.reshape(right_all.shape[0], -1),
        (((0,), (0,)), ((), ())),
        preferred_element_type=jnp.float32,
    )
    outer_half = outer_sum.astype(jnp.bfloat16).reshape(
        rows_here, outer_width, residue_half, outer_width
    )
    opm_update = jnp.einsum(
        "ipjq,pqz->ijz", outer_half, outer_weight, preferred_element_type=jnp.float32
    )
    divisor = jnp.maximum(jnp.sum(seq_live) * own_rows[:, None] * own_cols[None, :], 1.0)
    pair_updated = (pair_state.astype(jnp.float32) + opm_update / divisor[..., None]).astype(
        jnp.bfloat16
    )
    pair_normed = layer_normalize(pair_updated).astype(jnp.bfloat16)
    bias_tile = jnp.einsum(
        "ijz,zh->ihj", pair_normed, bias_weight, preferred_element_type=jnp.float32
    ).astype(jnp.bfloat16)
    projected_queries = (
        jnp.dot(flat_rows, query_weight, preferred_element_type=jnp.float32)
        .astype(jnp.bfloat16)
        .reshape(sequence_wise, residues, head_count, head_dim)
    )
    gate_activations = jax.nn.sigmoid(
        jnp.dot(flat_rows, gate_weight, preferred_element_type=jnp.float32)
    ).reshape(sequence_wise, residues, channel_count)
    key_live = (res_live - 1.0) * mask_fill
    half_live = lax.dynamic_slice_in_dim(key_live, col_index * residue_half, residue_half)
    bias_cols = lax.all_gather(bias_tile, "col", axis=2, tiled=True)
    bias_all = spread_all(bias_cols)
    key_count = bias_all.shape[2]
    projected_keys = (
        jnp.dot(flat_rows, key_weight, preferred_element_type=jnp.float32)
        .astype(jnp.bfloat16)
        .reshape(sequence_wise, key_count, head_count, head_dim)
    )
    projected_values = (
        jnp.dot(flat_rows, value_weight, preferred_element_type=jnp.float32)
        .astype(jnp.bfloat16)
        .reshape(sequence_wise, key_count, head_count, head_dim)
    )
    maxima, totals, summed = lax.map(
        lambda inputs: attend_partial(
            inputs[0], inputs[1], inputs[2], bias_all, key_live, score_scale
        ),
        (projected_queries, projected_keys, projected_values),
    )
    attended = summed / jnp.repeat(totals, head_dim, axis=-1)
    gated = gate_activations * attended
    gated_own = lax.dynamic_slice_in_dim(gated, col_index * residue_half, residue_half, 1).astype(
        jnp.bfloat16
    )
    alignment_update = (
        jnp.dot(
            gated_own.reshape(-1, channel_count), output_weight, preferred_element_type=jnp.float32
        )
        .astype(jnp.bfloat16)
        .reshape(sequence_wise, residue_half, channel_count)
    )
    d_gated = lax.dot_general(
        complete_cotangent.reshape(-1, channel_count),
        output_weight,
        (((1,), (1,)), ((), ())),
        preferred_element_type=jnp.float32,
    ).reshape(sequence_wise, residues, channel_count)
    d_attended = d_gated * gate_activations
    delta_sum = jnp.sum(
        (d_attended * attended).reshape(sequence_wise, residues, head_count, head_dim), axis=-1
    )
    d_rounded = d_attended.astype(jnp.bfloat16).reshape(
        sequence_wise, residues, head_count, head_dim
    )
    log_total = maxima + jnp.log(totals)
    keys_half = lax.dynamic_slice_in_dim(projected_keys, col_index * residue_half, residue_half, 1)
    values_half = lax.dynamic_slice_in_dim(
        projected_values, col_index * residue_half, residue_half, 1
    )
    bias_half = lax.dynamic_slice_in_dim(bias_all, col_index * residue_half, residue_half, 2)
    bias_rows = bias_half.astype(jnp.float32)

    def single_sequence(running, sequence_items):
        query_rows, d_rows, total_rows, delta_rows, keys_one, values_one = sequence_items
        scores = jnp.einsum(
            "ihd,jhd->ihj", query_rows, keys_one, preferred_element_type=jnp.float32
        )
        scores = scores * score_scale + bias_rows + half_live
        probs = jnp.exp(scores - total_rows[..., None])
        d_weights = jnp.einsum(
            "ihd,jhd->ihj", d_rows, values_one, preferred_element_type=jnp.float32
        )
        return (running + probs * (d_weights - delta_rows[..., None]), None)

    sequence_items = (projected_queries, d_rounded, log_total, delta_sum, keys_half, values_half)
    initial_value = jnp.zeros(
        (rows_here * lax.axis_size("row"), head_count, residue_half), jnp.float32
    )
    result, unused = lax.scan(single_sequence, initial_value, sequence_items)
    shares = lax.all_to_all(
        result.astype(jnp.bfloat16).reshape((-1,) + (rows_here,) + result.shape[1:]),
        "row",
        split_axis=0,
        concat_axis=0,
        tiled=True,
    )
    bias_gradient = jnp.sum(shares.astype(jnp.float32), axis=0)
    d_normed = jnp.einsum(
        "ihj,zh->ijz",
        bias_gradient,
        bias_weight.astype(jnp.float32),
        precision=lax.Precision.HIGHEST,
    )
    pair_gradient = norm_backward(pair_updated, d_normed)
    return (alignment_update, pair_updated, pair_gradient)


LANES = 128
GROUP = 4
PIECES = 4
f32 = jnp.float32
bf16 = jnp.bfloat16


def dot_nn(a, b):
    return lax.dot_general(a, b, (((1,), (0,)), ((), ())), preferred_element_type=f32)


def dot_nt(a, b):
    return lax.dot_general(a, b, (((1,), (1,)), ((), ())), preferred_element_type=f32)


def dot_tn(a, b):
    return lax.dot_general(a, b, (((0,), (0,)), ((), ())), preferred_element_type=f32)


def lane_index(rows):
    return lax.broadcasted_iota(jnp.int32, (rows, LANES), 1)


def swap_groups(parts):
    lane = lane_index(parts[0].shape[0])
    low, even = lane < 64, lane % 64 < 32
    parts = [
        jnp.where(low, parts[0], pltpu.roll(parts[2], 64, 1)),
        jnp.where(low, parts[1], pltpu.roll(parts[3], 64, 1)),
        jnp.where(low, pltpu.roll(parts[0], 64, 1), parts[2]),
        jnp.where(low, pltpu.roll(parts[1], 64, 1), parts[3]),
    ]
    return [
        jnp.where(even, parts[0], pltpu.roll(parts[1], 32, 1)),
        jnp.where(even, pltpu.roll(parts[0], 96, 1), parts[1]),
        jnp.where(even, parts[2], pltpu.roll(parts[3], 32, 1)),
        jnp.where(even, pltpu.roll(parts[2], 96, 1), parts[3]),
    ]


def factors_kernel(
    seq_smem_ref, res_smem_ref, seq_ref, res_ref, bias_w_ref, left_ref, right_ref, pair_ref, *refs
):
    row_refs, (send_ref, aux_ref, normed_ref, *pair_refs, left_scr) = refs[:PIECES], refs[PIECES:]
    columns_each = pair_refs[0].shape[1]
    for step in range(GROUP):
        first = pl.multiple_of(partner(step) * columns_each, columns_each)
        pair_refs[step][...] = pair_ref[:, pl.ds(first, columns_each), :]
    lines = send_ref.shape[0]
    seqs = send_ref.shape[2] // 12
    residues = res_ref.shape[1]
    me = lax.axis_index("row")
    normed = jnp.concatenate([layer_normalize(rows[...]).astype(bf16) for rows in row_refs], axis=0)
    normed_ref[...] = normed
    live = res_ref[...].astype(f32)
    live_rows = jnp.broadcast_to(live, (residues, residues)).T
    right_t = right_ref[...]
    left_wide = jnp.concatenate([left_ref[...]] * 4, axis=0)
    lane_group = lane_index(lines) // 32
    quarters = []
    tail = []
    for s in range(seqs):
        seq_live = seq_smem_ref[me * seqs + s].astype(f32)
        own = normed[s * residues : (s + 1) * residues]
        factor = dot_nt(right_t, own) * (live * seq_live)
        quarters.append(swap_groups([factor[a * 8 : (a + 1) * 8] for a in range(4)]))
        left_scr[:residues] = dot_nt(own, left_wide) * (live_rows * seq_live)
        for a in range(4):
            row = jnp.zeros((lines, LANES), f32)
            for b in range(4):
                part = left_scr[pl.ds(4 * a + b, lines, stride=4 * GROUP), :]
                row = jnp.where(lane_group == b, part, row)
            tail.append(row)
    tail = jnp.stack(tail, axis=1).astype(bf16)
    right_rows = 8 * seqs
    for t in range(GROUP):
        block = jnp.concatenate([own[t] for own in quarters], axis=0).astype(bf16)
        send_ref[:, t, :right_rows, :] = jnp.broadcast_to(block[None], (lines, right_rows, LANES))
        send_ref[:, t, right_rows:, :] = tail
    aux_ref[0:4] = tile_divisor(res_smem_ref, res_ref, seq_ref)
    aux_ref[4:8] = jnp.broadcast_to((live - 1.0) * mask_fill, (4, LANES))
    aux_ref[8:16] = bias_w_ref[...].astype(f32)


def side_by_side(first, second, at):
    low = lane_index(first.shape[0]) < 64
    span = slice(at // 2 * LANES, at // 2 * LANES + LANES)
    first, second = first[:, span], second[:, span]
    if at % 2 == 0:
        return jnp.where(low, first, pltpu.roll(second, 64, 1))
    return jnp.where(low, pltpu.roll(first, 64, 1), second)


def partner(step):
    return lax.bitwise_xor(lax.rem(lax.axis_index("row"), GROUP), step)


def tile_divisor(res_smem_ref, res_ref, seq_ref):
    own = partner(0)
    rows = lax.div(lax.axis_index("row"), GROUP) * 16
    lane = lane_index(1)
    live = res_ref[...].astype(f32)
    columns = jnp.zeros((1, LANES), f32)
    for t in range(GROUP):
        turned = live if t == 0 else pltpu.roll(live, LANES - 32 * t, 1)
        columns = jnp.where(own == t, turned, columns)
    columns = jnp.where(lane < 32, columns, 0.0)
    columns = columns + pltpu.roll(columns, 32, 1)
    columns = columns + pltpu.roll(columns, 64, 1)
    total = jnp.sum(seq_ref[...].astype(f32), axis=-1, keepdims=True)
    lines = []
    for b in range(4):
        line = jnp.zeros((1, LANES), f32)
        for a in range(4):
            line = jnp.where(lane // 32 == a, res_smem_ref[rows + 4 * a + b].astype(f32), line)
        lines.append(jnp.maximum(total * line * columns, 1.0))
    return jnp.concatenate(lines, axis=0)


def projections_kernel(
    normed_ref, cot_ref, weights_ref, wo_ref, aux_ref, pair_ref, gate_ref, aux_out_ref, pair_out_ref, *rest
):
    block_refs, every = rest[:GROUP], rest[GROUP]
    aux_out_ref[...] = aux_ref[...]
    pair_out_ref[...] = pair_ref[...]
    normed = normed_ref[...]
    tokens = normed.shape[0]
    residues = gate_ref.shape[1]
    seqs = tokens // residues
    channels = normed.shape[1]
    queries, keys, values, gate = [
        dot_nn(normed, weights_ref[:, at * channels : (at + 1) * channels]) for at in range(4)
    ]
    gate = jax.nn.sigmoid(gate)
    d_attended = dot_nt(cot_ref[...], wo_ref[...]) * gate
    for t in range(GROUP):
        rows = side_by_side(queries, d_attended, t).astype(bf16)
        columns = side_by_side(keys, values, t).astype(bf16)
        gate_ref[t] = side_by_side(gate[:residues], gate[residues:], t)
        for s in range(seqs):
            every[t, s] = rows[s * residues : (s + 1) * residues]
            every[t, seqs + s] = columns[s * residues : (s + 1) * residues]
    for step in range(GROUP):
        block_refs[step][...] = every[partner(step)]


def products_kernel(scale, *refs):
    block_refs, (score_ref, flow_ref, value_ref) = refs[:GROUP], refs[GROUP:]
    rows = score_ref.shape[1]
    residues = score_ref.shape[2]
    part_of = lane_index(residues) // 32
    seqs = block_refs[0].shape[0] // 2
    for step, block in enumerate(block_refs):
        for s in range(seqs):
            wide = jnp.concatenate(
                [jnp.where(part_of == g, block[s], jnp.zeros((), bf16)) for g in range(4)], axis=0
            )
            both = dot_nt(wide, block[seqs + s])
            score_ref[step * seqs + s] = both[:rows] * scale
            flow_ref[step * seqs + s] = both[rows:]
            value_ref[step * seqs + s] = jnp.where(part_of < 2, jnp.ones((), bf16), block[seqs + s])


def pair_kernel(recv_ref, weight_ref, aux_ref, *refs):
    pair_refs, send_ref, updated_refs = refs[:GROUP], refs[GROUP], refs[GROUP + 1 : 2 * GROUP + 1]
    flat, rbuf, lbuf, obuf, state, after = refs[2 * GROUP + 1 :]
    peers, block_rows, _ = recv_ref.shape
    seqs = block_rows // 12
    for step in range(GROUP):
        state[partner(step)] = pair_refs[step][...]
    before = [
        jnp.concatenate([state[a, b] for a in range(GROUP)], axis=0).astype(f32).T for b in range(4)
    ]
    flat[: peers * block_rows] = recv_ref[...].astype(f32).reshape(peers * block_rows, LANES)
    for s in range(seqs):
        for g in range(8):
            part = flat[pl.ds(s * 8 + g, peers, stride=block_rows), :]
            for a in range(4):
                turned = part if a == 0 else pltpu.roll(part, 32 * a, 1)
                rbuf[a, s * peers : (s + 1) * peers, g * LANES : (g + 1) * LANES] = turned.astype(bf16)
        for a in range(4):
            part = flat[pl.ds(8 * seqs + 4 * s + a, peers, stride=block_rows), :]
            lbuf[s * peers : (s + 1) * peers, a * LANES : (a + 1) * LANES] = part
    left_t = lbuf[...].T.astype(bf16)
    outer = [dot_nn(left_t[a * LANES : (a + 1) * LANES], rbuf[a]).astype(bf16) for a in range(4)]
    lane_group = lane_index(LANES) // 32
    sums = None
    for q in range(4):
        for g in range(8):
            span = slice(g * LANES, (g + 1) * LANES)
            picked = outer[3][:, span]
            for a in range(3):
                picked = jnp.where(lane_group == (q + a) % 4, outer[a][:, span], picked)
            for b in range(4):
                obuf[q, g * 32 : (g + 1) * 32, b * LANES : (b + 1) * LANES] = picked[b * 32 : (b + 1) * 32]
        part = dot_nn(weight_ref[q], obuf[q])
        if q:
            part = jnp.concatenate(
                [pltpu.roll(part[:, b * LANES : (b + 1) * LANES], LANES - 32 * q, 1) for b in range(4)], axis=1
            )
        sums = part if sums is None else sums + part
    bias_w = aux_ref[8:16].astype(bf16)
    blocks = []
    for b in range(4):
        update = sums[:, b * LANES : (b + 1) * LANES] / aux_ref[b : b + 1, :]
        updated = (before[b] + update).astype(bf16)
        values = updated.astype(f32)
        center = values - jnp.mean(values, axis=0, keepdims=True)
        spread = jnp.mean(center * center, axis=0, keepdims=True)
        line = dot_nn(bias_w, (center * lax.rsqrt(spread + norm_eps)).astype(bf16))
        blocks.append(pltpu.roll(line, partner(0) * 32, 1))
        values = values.T.astype(bf16)
        for a in range(GROUP):
            after[a, b] = values[a * 32 : (a + 1) * 32]
    lines, _, share, _ = send_ref.shape
    heads = share // 4
    for t in range(GROUP):
        block = jnp.concatenate([rows[t * heads : (t + 1) * heads] for rows in blocks], axis=0).astype(bf16)
        send_ref[:, t] = jnp.broadcast_to(block[None], (lines, share, LANES))
    for step in range(GROUP):
        updated_refs[step][...] = after[partner(step)]


def place_bias(flat, mask_ref, heads, h, bias):
    lines = bias.shape[0] // 16 - 1
    lane_group = lane_index(lines) // 32
    mask = mask_ref[4:5, :]
    for b in range(4):
        rows = [flat[pl.ds((4 * t + b) * heads + h, lines, stride=16 * heads), :] for t in range(GROUP)]
        for a in range(4):
            picked = rows[3]
            for t in range(3):
                picked = jnp.where(lane_group == (a + t) % 4, rows[t], picked)
            if a:
                picked = pltpu.roll(picked, LANES - 32 * a, 1)
            bias[pl.ds(4 * a + b, lines, stride=16), :] = picked + mask


def bias_gradient_kernel(bias_ref, mask_ref, score_ref, flow_ref, *refs):
    part_refs, (pair_ref, send_ref, weights_ref, flat, grads, placed) = refs[:GROUP], refs[GROUP:]
    columns_each = part_refs[0].shape[1]
    for step in range(GROUP):
        first = pl.multiple_of(partner(step) * columns_each, columns_each)
        pair_ref[:, pl.ds(first, columns_each), :] = part_refs[step][...]
    seqs, rows, residues = score_ref.shape
    heads = rows // residues
    flat[:rows] = bias_ref[...].reshape(rows, LANES).astype(f32)
    ones = jnp.ones((residues, LANES), bf16)
    for h in range(heads):
        at = slice(h * residues, (h + 1) * residues)
        place_bias(flat, mask_ref, heads, h, placed.at[h])
        bias = placed[h, :residues]
        total = jnp.zeros((residues, residues), f32)
        for s in range(seqs):
            scores = score_ref[s, at, :] + bias
            weights = jnp.exp(scores - jnp.max(scores, axis=-1, keepdims=True))
            rounded = weights.astype(bf16)
            weights_ref[s, at, :] = rounded
            flow = flow_ref[s, at, :]
            inverse = 1.0 / dot_nn(rounded, ones)
            delta = dot_nn((weights * flow).astype(bf16), ones) * inverse
            total = total + weights * inverse * (flow - delta)
        grads[pl.ds(h, residues, stride=heads), :] = total
    send_ref[...] = grads[:rows].astype(bf16).reshape(send_ref.shape)


def attended_kernel(weights_ref, value_ref, *out_refs):
    sequences, _, residues = weights_ref.shape
    seqs = sequences // GROUP
    lane = lane_index(residues)
    for step in range(GROUP):
        attended = []
        for s in range(seqs):
            mixed = dot_nn(weights_ref[step * seqs + s], value_ref[step * seqs + s])
            picked = jnp.where(lane < 96, mixed[:residues], mixed[residues:])
            totals = jnp.where(lane < 32, mixed[:residues], mixed[residues:])
            attended.append(picked / pltpu.roll(totals, 64, 1))
        out_refs[step][...] = jnp.where(lane < 64, pltpu.roll(attended[0], 64, 1), attended[1]).astype(bf16)


def output_kernel(gate_ref, wo_ref, *refs):
    in_refs, out_ref = refs[:GROUP], refs[GROUP]
    residues = gate_ref.shape[1]
    low = lane_index(residues) < 64
    zero = jnp.zeros((), bf16)
    sums = [jnp.zeros((residues, out_ref.shape[1]), f32) for _ in range(2)]
    for step in range(GROUP):
        at = partner(step)
        gated = (gate_ref[at] * in_refs[step][...].astype(f32)).astype(bf16)
        weight = wo_ref[pl.ds(pl.multiple_of(at * 64, 64), 64), :]
        weight = jnp.concatenate([weight, weight], axis=0)
        sums[0] = sums[0] + dot_nn(jnp.where(low, gated, zero), weight)
        sums[1] = sums[1] + dot_nn(jnp.where(low, zero, gated), weight)
    for s in range(2):
        out_ref[s * residues : (s + 1) * residues, :] = sums[s].astype(bf16)


def split_sum(values):
    high = values.astype(bf16)
    return high, (values - high.astype(f32)).astype(bf16)


def normal_kernel(pair_ref, normal_ref, inverse_ref):
    values = pair_ref[...].astype(f32)
    center = values - jnp.mean(values, axis=-1, keepdims=True)
    inverse = lax.rsqrt(jnp.mean(center * center, axis=-1, keepdims=True) + norm_eps)
    normal_ref[...] = center * inverse
    inverse_ref[...] = jnp.broadcast_to(inverse, values.shape)


def gradient_kernel(shares_ref, aux_ref, normal_ref, inverse_ref, out_hbm, result, left_for):
    peers, share, _ = shares_ref.shape
    rows, _, channels = normal_ref.shape
    heads = share // rows
    total = jnp.sum(shares_ref[...].astype(f32).reshape(peers // GROUP, GROUP, share, LANES), axis=0)
    bias_w = aux_ref[8:16]
    mean_high, mean_low = split_sum(
        jnp.broadcast_to(jnp.mean(bias_w, axis=-1, keepdims=True), bias_w.shape)
    )
    exact = bias_w.astype(bf16)
    none = jnp.zeros(exact.shape, bf16)
    weights = jnp.concatenate(
        [
            jnp.concatenate([exact, mean_high], axis=1),
            jnp.concatenate([exact, mean_high], axis=1),
            jnp.concatenate([none, mean_low], axis=1),
        ],
        axis=0,
    )
    moves = []
    for i in range(rows):
        own = jnp.concatenate([total[t, i * heads : (i + 1) * heads] for t in range(GROUP)], axis=0)
        high, low = split_sum(own)
        both = dot_tn(jnp.concatenate([high, low, high], axis=0), weights)
        upstream, mean = both[:, :channels], both[:, channels:]
        normal = normal_ref[i]
        result[i] = inverse_ref[i] * (
            upstream - mean - normal * jnp.mean(upstream * normal, axis=-1, keepdims=True)
        )
        moves.append(pltpu.make_async_copy(result.at[i], out_hbm.at[i], left_for.at[i]))
        moves[-1].start()
    for move in moves:
        move.wait()


def kernel_call(body, out_shape, in_specs=None, scratch=(), flops=0, moved=0, vmem_mib=12, out_specs=None, grid=()):
    vmem = pl.BlockSpec(memory_space=pltpu.VMEM)
    many = isinstance(out_shape, (list, tuple))
    return pl.pallas_call(
        body,
        grid=grid,
        out_shape=out_shape,
        in_specs=in_specs,
        out_specs=out_specs or ([vmem] * len(out_shape) if many else vmem),
        scratch_shapes=list(scratch),
        compiler_params=pltpu.CompilerParams(vmem_limit_bytes=vmem_mib * 1024 * 1024),
        cost_estimate=pl.CostEstimate(flops=flops, bytes_accessed=moved, transcendentals=0),
    )


def on_device_paired(
    alignment_rows,
    pair_state,
    update_cotangent,
    sequence_mask,
    residue_mask,
    left_weight,
    right_weight,
    outer_weight,
    bias_weight,
    query_weight,
    key_weight,
    value_weight,
    gate_weight,
    output_weight,
):
    sequence_wise, residues, channel_count = alignment_rows.shape
    rows_here, _, pair_channels = pair_state.shape
    head_count = bias_weight.shape[1]
    peers = lax.axis_size("row")
    factor = left_weight.shape[1]
    lines = peers // GROUP
    vmem = pl.BlockSpec(memory_space=pltpu.VMEM)
    smem = pl.BlockSpec(memory_space=pltpu.SMEM)
    token_rows = sequence_wise * residues
    columns_each = residues // GROUP
    block_rows = sequence_wise * 12
    flat_rows = alignment_rows.reshape(token_rows, channel_count)
    shape = jax.ShapeDtypeStruct

    pieces = [
        pl.BlockSpec((token_rows // PIECES, channel_count), lambda step, at=at: (at, 0)) for at in range(PIECES)
    ]
    send, aux, normed, *pair_blocks = kernel_call(
        factors_kernel,
        [
            shape((lines, GROUP, block_rows, LANES), bf16),
            shape((16, LANES), f32),
            shape((token_rows, channel_count), bf16),
        ]
        + [shape((rows_here, columns_each, pair_channels), bf16)] * GROUP,
        [smem] * 2 + [vmem] * 6 + pieces,
        [pltpu.VMEM((residues + 4 * GROUP, LANES), f32)],
        flops=2 * token_rows * channel_count * LANES,
        moved=1 << 20,
        vmem_mib=60,
        grid=(1,),
    )(
        sequence_mask,
        residue_mask,
        sequence_mask.reshape(1, -1),
        residue_mask.reshape(1, -1),
        bias_weight.T,
        left_weight.T,
        right_weight.T,
        pair_state,
        *[flat_rows] * PIECES,
    )
    received = lax.all_to_all(
        send.reshape(peers, block_rows, LANES), "row", split_axis=0, concat_axis=0, tiled=True
    )

    group_heads = head_count // GROUP
    head_rows = group_heads * residues
    scale = (channel_count // head_count) ** (-0.5)
    normed, *weights = lax.optimization_barrier((normed, query_weight, key_weight, value_weight, gate_weight))
    part_shape = shape((rows_here, columns_each, pair_channels), bf16)
    gate, aux, own_block, *blocks = kernel_call(
        projections_kernel,
        [shape((GROUP, residues, LANES), f32), shape((16, LANES), f32), part_shape]
        + [shape((2 * sequence_wise, residues, LANES), bf16)] * GROUP,
        [vmem] * 6,
        [pltpu.VMEM((GROUP, 2 * sequence_wise, residues, LANES), bf16)],
        flops=10 * token_rows * channel_count * channel_count,
        moved=1 << 21,
    )(
        normed,
        update_cotangent.reshape(token_rows, channel_count),
        jnp.concatenate(weights, axis=1),
        output_weight,
        aux,
        pair_blocks[0],
    )

    def trade(parts):
        return parts[:1] + [
            lax.ppermute(parts[d], "row", [(i, i ^ d) for i in range(peers)]) for d in range(1, GROUP)
        ]

    pair_blocks = [own_block] + trade(pair_blocks)[1:]
    blocks = trade(blocks)
    scores, flow, values = kernel_call(
        lambda *refs: products_kernel(scale, *refs),
        [shape((GROUP * sequence_wise, head_rows, residues), f32)] * 2
        + [shape((GROUP * sequence_wise, residues, LANES), bf16)],
        [vmem] * GROUP,
        flops=1 << 28,
        moved=1 << 21,
    )(*blocks)

    weight_t = (
        outer_weight.reshape(factor, 4, 8, pair_channels)
        .transpose(1, 3, 2, 0)
        .reshape(4, pair_channels, 8 * factor)
    )
    share_rows = 4 * group_heads
    send_bias, *updated = kernel_call(
        pair_kernel,
        [shape((lines, GROUP, share_rows, LANES), bf16)] + [part_shape] * GROUP,
        [vmem] * (3 + GROUP),
        [
            pltpu.VMEM(((peers + 1) * block_rows, LANES), f32),
            pltpu.VMEM((4, peers * sequence_wise, 8 * LANES), bf16),
            pltpu.VMEM((peers * sequence_wise, 4 * LANES), f32),
            pltpu.VMEM((4, 8 * factor, 4 * LANES), bf16),
            pltpu.VMEM((GROUP, rows_here, columns_each, pair_channels), bf16),
            pltpu.VMEM((GROUP, rows_here, columns_each, pair_channels), bf16),
        ],
        flops=1 << 28,
        moved=1 << 20,
    )(received, weight_t, aux, *pair_blocks)
    bias_all = lax.all_to_all(
        send_bias.reshape(peers, share_rows, LANES), "row", split_axis=0, concat_axis=0, tiled=True
    )
    updated = trade(updated)

    pair_updated, send_grad, weights = kernel_call(
        bias_gradient_kernel,
        [
            shape((rows_here, residues, pair_channels), bf16),
            shape((peers, rows_here * group_heads, LANES), bf16),
            shape((GROUP * sequence_wise, head_rows, residues), bf16),
        ],
        [vmem] * (4 + GROUP),
        [pltpu.VMEM((head_rows + 16 * group_heads, LANES), f32)] * 2
        + [pltpu.VMEM((group_heads, residues + 16, LANES), f32)],
        flops=1 << 28,
        moved=1 << 22,
    )(bias_all, aux, scores, flow, *updated)
    shares = lax.all_to_all(send_grad, "row", split_axis=0, concat_axis=0, tiled=True)
    attended = kernel_call(
        attended_kernel,
        [shape((residues, LANES), bf16)] * GROUP,
        [vmem] * 2,
        flops=1 << 28,
        moved=1 << 21,
    )(weights, values)
    update = kernel_call(
        output_kernel,
        shape((token_rows, channel_count), bf16),
        [vmem] * (2 + GROUP),
        flops=2 * token_rows * channel_count * channel_count,
        moved=1 << 20,
    )(gate, output_weight, *trade(list(attended)))
    normal, inverse = kernel_call(
        normal_kernel,
        [shape((rows_here, residues, pair_channels), f32)] * 2,
        [vmem],
        flops=1 << 22,
        moved=1 << 20,
    )(pair_updated)
    pair_gradient = kernel_call(
        gradient_kernel,
        shape((rows_here, residues, pair_channels), f32),
        [vmem] * 4,
        [pltpu.VMEM((rows_here, residues, pair_channels), f32), pltpu.SemaphoreType.DMA((rows_here,))],
        flops=1 << 24,
        moved=1 << 20,
        out_specs=pl.BlockSpec(memory_space=pltpu.HBM),
    )(shares, aux, normal, inverse)
    return (update.reshape(alignment_rows.shape), pair_updated, pair_gradient)


def on_device(*arguments):
    rows, pair, left, bias = arguments[0], arguments[1], arguments[5], arguments[8]
    peers = lax.axis_size("row")
    fits = (
        lax.axis_size("col") == 1
        and peers == 32
        and rows.shape == (2, 128, 256)
        and pair.shape == (4, 128, 128)
        and left.shape[1] == 32
        and bias.shape[1] == 8
    )
    return (on_device_paired if fits else on_device_general)(*arguments)


def solution(mesh):
    placed = (
        P(("grp", "row"), "col", None),
        P(("grp", "row"), "col", None),
        P(("grp", "row"), "col", None),
        P("grp"),
        P("grp"),
        P(),
        P(),
        P(),
        P(),
        P(),
        P(),
        P(),
        P(),
        P(),
    )
    return jax.shard_map(
        on_device,
        mesh=mesh,
        in_specs=placed,
        out_specs=(
            P(("grp", "row"), "col", None),
            P(("grp", "row"), "col", None),
            P(("grp", "row"), "col", None),
        ),
        check_vma=False,
    )
```

```python
import jax
import jax.numpy as jnp
from jax import lax
from jax.experimental import pallas as pl
from jax.experimental.pallas import tpu as pltpu
from jax.sharding import PartitionSpec as P

norm_eps = 1e-05
mask_fill = 1000000000.0


def layer_normalize(values):
    values = values.astype(jnp.float32)
    center = values - jnp.mean(values, axis=-1, keepdims=True)
    spread = jnp.mean(center * center, axis=-1, keepdims=True)
    return center * lax.rsqrt(spread + norm_eps)


def norm_backward(values, upstream):
    values = values.astype(jnp.float32)
    center = values - jnp.mean(values, axis=-1, keepdims=True)
    inverse = lax.rsqrt(jnp.mean(center * center, axis=-1, keepdims=True) + norm_eps)
    normal_part = center * inverse
    return inverse * (
        upstream
        - jnp.mean(upstream, axis=-1, keepdims=True)
        - normal_part * jnp.mean(upstream * normal_part, axis=-1, keepdims=True)
    )


def spread_all(shard):
    copies = jnp.broadcast_to(shard[None], (lax.axis_size("row"),) + shard.shape)
    gathered = lax.all_to_all(copies, "row", split_axis=0, concat_axis=0, tiled=True)
    return gathered.reshape((-1,) + shard.shape[1:])


def attend_partial(
    projected_queries, projected_keys, projected_values, bias_all, key_mask, score_scale
):
    scores = jnp.einsum(
        "ihd,jhd->ihj", projected_queries, projected_keys, preferred_element_type=jnp.float32
    )
    scores = scores * score_scale + bias_all.astype(jnp.float32) + key_mask
    maxima = jnp.max(scores, axis=-1)
    weights = jnp.exp(scores - maxima[..., None])
    totals = jnp.sum(weights, axis=-1)
    summed = jnp.einsum(
        "ihj,jhd->ihd",
        weights.astype(jnp.bfloat16),
        projected_values,
        preferred_element_type=jnp.float32,
    )
    return (maxima, totals, summed.reshape(summed.shape[0], -1))


def on_device_general(
    alignment_rows,
    pair_state,
    update_cotangent,
    sequence_mask,
    residue_mask,
    left_weight,
    right_weight,
    outer_weight,
    bias_weight,
    query_weight,
    key_weight,
    value_weight,
    gate_weight,
    output_weight,
):
    sequence_wise, residue_half, channel_count = alignment_rows.shape
    rows_here = pair_state.shape[0]
    residues = residue_mask.shape[0]
    head_count = bias_weight.shape[1]
    head_dim = channel_count // head_count
    score_scale = head_dim ** (-0.5)
    row_index = lax.axis_index("row")
    col_index = lax.axis_index("col")
    complete_alignment, complete_cotangent = (
        lax.all_gather(alignment_rows, "col", axis=1, tiled=True),
        lax.all_gather(update_cotangent, "col", axis=1, tiled=True),
    )
    seq_live = sequence_mask.astype(jnp.float32)
    res_live = residue_mask.astype(jnp.float32)
    own_seq = lax.dynamic_slice_in_dim(seq_live, row_index * sequence_wise, sequence_wise)
    own_cols = lax.dynamic_slice_in_dim(res_live, col_index * residue_half, residue_half)
    own_rows = lax.dynamic_slice_in_dim(res_live, row_index * rows_here, rows_here)
    normalized_input = layer_normalize(complete_alignment).astype(jnp.bfloat16)
    flat_rows = normalized_input.reshape(-1, channel_count)
    normed_half = lax.dynamic_slice_in_dim(
        normalized_input, col_index * residue_half, residue_half, 1
    )
    half_rows = normed_half.reshape(-1, channel_count)
    left_proj = jnp.dot(flat_rows, left_weight, preferred_element_type=jnp.float32).reshape(
        sequence_wise, residues, -1
    )
    left_proj = (left_proj * (own_seq[:, None] * res_live[None, :])[..., None]).astype(jnp.bfloat16)
    right_proj = jnp.dot(half_rows, right_weight, preferred_element_type=jnp.float32).reshape(
        sequence_wise, residue_half, -1
    )
    right_proj = (right_proj * (own_seq[:, None] * own_cols[None, :])[..., None]).astype(
        jnp.bfloat16
    )
    left_tile = lax.all_to_all(left_proj, "row", split_axis=1, concat_axis=0, tiled=True)
    right_all = spread_all(right_proj)
    outer_width = left_tile.shape[2]
    outer_sum = lax.dot_general(
        left_tile.reshape(left_tile.shape[0], -1),
        right_all.reshape(right_all.shape[0], -1),
        (((0,), (0,)), ((), ())),
        preferred_element_type=jnp.float32,
    )
    outer_half = outer_sum.astype(jnp.bfloat16).reshape(
        rows_here, outer_width, residue_half, outer_width
    )
    opm_update = jnp.einsum(
        "ipjq,pqz->ijz", outer_half, outer_weight, preferred_element_type=jnp.float32
    )
    divisor = jnp.maximum(jnp.sum(seq_live) * own_rows[:, None] * own_cols[None, :], 1.0)
    pair_updated = (pair_state.astype(jnp.float32) + opm_update / divisor[..., None]).astype(
        jnp.bfloat16
    )
    pair_normed = layer_normalize(pair_updated).astype(jnp.bfloat16)
    bias_tile = jnp.einsum(
        "ijz,zh->ihj", pair_normed, bias_weight, preferred_element_type=jnp.float32
    ).astype(jnp.bfloat16)
    projected_queries = (
        jnp.dot(flat_rows, query_weight, preferred_element_type=jnp.float32)
        .astype(jnp.bfloat16)
        .reshape(sequence_wise, residues, head_count, head_dim)
    )
    gate_activations = jax.nn.sigmoid(
        jnp.dot(flat_rows, gate_weight, preferred_element_type=jnp.float32)
    ).reshape(sequence_wise, residues, channel_count)
    key_live = (res_live - 1.0) * mask_fill
    half_live = lax.dynamic_slice_in_dim(key_live, col_index * residue_half, residue_half)
    bias_cols = lax.all_gather(bias_tile, "col", axis=2, tiled=True)
    bias_all = spread_all(bias_cols)
    key_count = bias_all.shape[2]
    projected_keys = (
        jnp.dot(flat_rows, key_weight, preferred_element_type=jnp.float32)
        .astype(jnp.bfloat16)
        .reshape(sequence_wise, key_count, head_count, head_dim)
    )
    projected_values = (
        jnp.dot(flat_rows, value_weight, preferred_element_type=jnp.float32)
        .astype(jnp.bfloat16)
        .reshape(sequence_wise, key_count, head_count, head_dim)
    )
    maxima, totals, summed = lax.map(
        lambda inputs: attend_partial(
            inputs[0], inputs[1], inputs[2], bias_all, key_live, score_scale
        ),
        (projected_queries, projected_keys, projected_values),
    )
    attended = summed / jnp.repeat(totals, head_dim, axis=-1)
    gated = gate_activations * attended
    gated_own = lax.dynamic_slice_in_dim(gated, col_index * residue_half, residue_half, 1).astype(
        jnp.bfloat16
    )
    alignment_update = (
        jnp.dot(
            gated_own.reshape(-1, channel_count), output_weight, preferred_element_type=jnp.float32
        )
        .astype(jnp.bfloat16)
        .reshape(sequence_wise, residue_half, channel_count)
    )
    d_gated = lax.dot_general(
        complete_cotangent.reshape(-1, channel_count),
        output_weight,
        (((1,), (1,)), ((), ())),
        preferred_element_type=jnp.float32,
    ).reshape(sequence_wise, residues, channel_count)
    d_attended = d_gated * gate_activations
    delta_sum = jnp.sum(
        (d_attended * attended).reshape(sequence_wise, residues, head_count, head_dim), axis=-1
    )
    d_rounded = d_attended.astype(jnp.bfloat16).reshape(
        sequence_wise, residues, head_count, head_dim
    )
    log_total = maxima + jnp.log(totals)
    keys_half = lax.dynamic_slice_in_dim(projected_keys, col_index * residue_half, residue_half, 1)
    values_half = lax.dynamic_slice_in_dim(
        projected_values, col_index * residue_half, residue_half, 1
    )
    bias_half = lax.dynamic_slice_in_dim(bias_all, col_index * residue_half, residue_half, 2)
    bias_rows = bias_half.astype(jnp.float32)

    def single_sequence(running, sequence_items):
        query_rows, d_rows, total_rows, delta_rows, keys_one, values_one = sequence_items
        scores = jnp.einsum(
            "ihd,jhd->ihj", query_rows, keys_one, preferred_element_type=jnp.float32
        )
        scores = scores * score_scale + bias_rows + half_live
        probs = jnp.exp(scores - total_rows[..., None])
        d_weights = jnp.einsum(
            "ihd,jhd->ihj", d_rows, values_one, preferred_element_type=jnp.float32
        )
        return (running + probs * (d_weights - delta_rows[..., None]), None)

    sequence_items = (projected_queries, d_rounded, log_total, delta_sum, keys_half, values_half)
    initial_value = jnp.zeros(
        (rows_here * lax.axis_size("row"), head_count, residue_half), jnp.float32
    )
    result, unused = lax.scan(single_sequence, initial_value, sequence_items)
    shares = lax.all_to_all(
        result.astype(jnp.bfloat16).reshape((-1,) + (rows_here,) + result.shape[1:]),
        "row",
        split_axis=0,
        concat_axis=0,
        tiled=True,
    )
    bias_gradient = jnp.sum(shares.astype(jnp.float32), axis=0)
    d_normed = jnp.einsum(
        "ihj,zh->ijz",
        bias_gradient,
        bias_weight.astype(jnp.float32),
        precision=lax.Precision.HIGHEST,
    )
    pair_gradient = norm_backward(pair_updated, d_normed)
    return (alignment_update, pair_updated, pair_gradient)


LANES = 128
GROUP = 4
PIECES = 4
f32 = jnp.float32
bf16 = jnp.bfloat16


def dot_nn(a, b):
    return lax.dot_general(a, b, (((1,), (0,)), ((), ())), preferred_element_type=f32)


def dot_nt(a, b):
    return lax.dot_general(a, b, (((1,), (1,)), ((), ())), preferred_element_type=f32)


def dot_tn(a, b):
    return lax.dot_general(a, b, (((0,), (0,)), ((), ())), preferred_element_type=f32)


def lane_index(rows):
    return lax.broadcasted_iota(jnp.int32, (rows, LANES), 1)


def swap_groups(parts):
    lane = lane_index(parts[0].shape[0])
    low, even = lane < 64, lane % 64 < 32
    parts = [
        jnp.where(low, parts[0], pltpu.roll(parts[2], 64, 1)),
        jnp.where(low, parts[1], pltpu.roll(parts[3], 64, 1)),
        jnp.where(low, pltpu.roll(parts[0], 64, 1), parts[2]),
        jnp.where(low, pltpu.roll(parts[1], 64, 1), parts[3]),
    ]
    return [
        jnp.where(even, parts[0], pltpu.roll(parts[1], 32, 1)),
        jnp.where(even, pltpu.roll(parts[0], 96, 1), parts[1]),
        jnp.where(even, parts[2], pltpu.roll(parts[3], 32, 1)),
        jnp.where(even, pltpu.roll(parts[2], 96, 1), parts[3]),
    ]


def factors_kernel(
    seq_smem_ref, res_smem_ref, seq_ref, res_ref, bias_w_ref, left_ref, right_ref, pair_ref, *refs
):
    row_refs, (send_ref, aux_ref, normed_ref, *pair_refs, left_scr) = refs[:PIECES], refs[PIECES:]
    columns_each = pair_refs[0].shape[1]
    for step in range(GROUP):
        first = pl.multiple_of(partner(step) * columns_each, columns_each)
        pair_refs[step][...] = pair_ref[:, pl.ds(first, columns_each), :]
    lines = send_ref.shape[0]
    seqs = send_ref.shape[2] // 12
    residues = res_ref.shape[1]
    me = lax.axis_index("row")
    normed = jnp.concatenate([layer_normalize(rows[...]).astype(bf16) for rows in row_refs], axis=0)
    normed_ref[...] = normed
    live = res_ref[...].astype(f32)
    live_rows = jnp.broadcast_to(live, (residues, residues)).T
    right_t = right_ref[...]
    left_wide = jnp.concatenate([left_ref[...]] * 4, axis=0)
    lane_group = lane_index(lines) // 32
    quarters = []
    tail = []
    for s in range(seqs):
        seq_live = seq_smem_ref[me * seqs + s].astype(f32)
        own = normed[s * residues : (s + 1) * residues]
        factor = dot_nt(right_t, own) * (live * seq_live)
        quarters.append(swap_groups([factor[a * 8 : (a + 1) * 8] for a in range(4)]))
        left_scr[:residues] = dot_nt(own, left_wide) * (live_rows * seq_live)
        for a in range(4):
            row = jnp.zeros((lines, LANES), f32)
            for b in range(4):
                part = left_scr[pl.ds(4 * a + b, lines, stride=4 * GROUP), :]
                row = jnp.where(lane_group == b, part, row)
            tail.append(row)
    tail = jnp.stack(tail, axis=1).astype(bf16)
    right_rows = 8 * seqs
    for t in range(GROUP):
        block = jnp.concatenate([own[t] for own in quarters], axis=0).astype(bf16)
        send_ref[:, t, :right_rows, :] = jnp.broadcast_to(block[None], (lines, right_rows, LANES))
        send_ref[:, t, right_rows:, :] = tail
    aux_ref[0:4] = tile_divisor(res_smem_ref, res_ref, seq_ref)
    aux_ref[4:8] = jnp.broadcast_to((live - 1.0) * mask_fill, (4, LANES))
    aux_ref[8:16] = bias_w_ref[...].astype(f32)


def side_by_side(first, second, at):
    low = lane_index(first.shape[0]) < 64
    span = slice(at // 2 * LANES, at // 2 * LANES + LANES)
    first, second = first[:, span], second[:, span]
    if at % 2 == 0:
        return jnp.where(low, first, pltpu.roll(second, 64, 1))
    return jnp.where(low, pltpu.roll(first, 64, 1), second)


def partner(step):
    return lax.bitwise_xor(lax.rem(lax.axis_index("row"), GROUP), step)


def tile_divisor(res_smem_ref, res_ref, seq_ref):
    own = partner(0)
    rows = lax.div(lax.axis_index("row"), GROUP) * 16
    lane = lane_index(1)
    live = res_ref[...].astype(f32)
    columns = jnp.zeros((1, LANES), f32)
    for t in range(GROUP):
        turned = live if t == 0 else pltpu.roll(live, LANES - 32 * t, 1)
        columns = jnp.where(own == t, turned, columns)
    columns = jnp.where(lane < 32, columns, 0.0)
    columns = columns + pltpu.roll(columns, 32, 1)
    columns = columns + pltpu.roll(columns, 64, 1)
    total = jnp.sum(seq_ref[...].astype(f32), axis=-1, keepdims=True)
    lines = []
    for b in range(4):
        line = jnp.zeros((1, LANES), f32)
        for a in range(4):
            line = jnp.where(lane // 32 == a, res_smem_ref[rows + 4 * a + b].astype(f32), line)
        lines.append(jnp.maximum(total * line * columns, 1.0))
    return jnp.concatenate(lines, axis=0)


def projections_kernel(
    normed_ref, cot_ref, weights_ref, wo_ref, aux_ref, pair_ref, gate_ref, aux_out_ref, pair_out_ref, *rest
):
    block_refs, every = rest[:GROUP], rest[GROUP]
    aux_out_ref[...] = aux_ref[...]
    pair_out_ref[...] = pair_ref[...]
    normed = normed_ref[...]
    tokens = normed.shape[0]
    residues = gate_ref.shape[1]
    seqs = tokens // residues
    channels = normed.shape[1]
    queries, keys, values, gate = [
        dot_nn(normed, weights_ref[:, at * channels : (at + 1) * channels]) for at in range(4)
    ]
    gate = jax.nn.sigmoid(gate)
    d_attended = dot_nt(cot_ref[...], wo_ref[...]) * gate
    for t in range(GROUP):
        rows = side_by_side(queries, d_attended, t).astype(bf16)
        columns = side_by_side(keys, values, t).astype(bf16)
        gate_ref[t] = side_by_side(gate[:residues], gate[residues:], t)
        for s in range(seqs):
            every[t, s] = rows[s * residues : (s + 1) * residues]
            every[t, seqs + s] = columns[s * residues : (s + 1) * residues]
    for step in range(GROUP):
        block_refs[step][...] = every[partner(step)]


def pair_kernel(recv_ref, weight_ref, aux_ref, *refs):
    pair_refs, send_ref, updated_refs = refs[:GROUP], refs[GROUP], refs[GROUP + 1 : 2 * GROUP + 1]
    flat, rbuf, lbuf, obuf, state, after = refs[2 * GROUP + 1 :]
    peers, block_rows, _ = recv_ref.shape
    seqs = block_rows // 12
    for step in range(GROUP):
        state[partner(step)] = pair_refs[step][...]
    before = [
        jnp.concatenate([state[a, b] for a in range(GROUP)], axis=0).astype(f32).T for b in range(4)
    ]
    flat[: peers * block_rows] = recv_ref[...].astype(f32).reshape(peers * block_rows, LANES)
    for s in range(seqs):
        for g in range(8):
            part = flat[pl.ds(s * 8 + g, peers, stride=block_rows), :]
            for a in range(4):
                turned = part if a == 0 else pltpu.roll(part, 32 * a, 1)
                rbuf[a, s * peers : (s + 1) * peers, g * LANES : (g + 1) * LANES] = turned.astype(bf16)
        for a in range(4):
            part = flat[pl.ds(8 * seqs + 4 * s + a, peers, stride=block_rows), :]
            lbuf[s * peers : (s + 1) * peers, a * LANES : (a + 1) * LANES] = part
    left_t = lbuf[...].T.astype(bf16)
    outer = [dot_nn(left_t[a * LANES : (a + 1) * LANES], rbuf[a]).astype(bf16) for a in range(4)]
    lane_group = lane_index(LANES) // 32
    sums = None
    for q in range(4):
        for g in range(8):
            span = slice(g * LANES, (g + 1) * LANES)
            picked = outer[3][:, span]
            for a in range(3):
                picked = jnp.where(lane_group == (q + a) % 4, outer[a][:, span], picked)
            for b in range(4):
                obuf[q, g * 32 : (g + 1) * 32, b * LANES : (b + 1) * LANES] = picked[b * 32 : (b + 1) * 32]
        part = dot_nn(weight_ref[q], obuf[q])
        if q:
            part = jnp.concatenate(
                [pltpu.roll(part[:, b * LANES : (b + 1) * LANES], LANES - 32 * q, 1) for b in range(4)], axis=1
            )
        sums = part if sums is None else sums + part
    bias_w = aux_ref[8:16].astype(bf16)
    blocks = []
    for b in range(4):
        update = sums[:, b * LANES : (b + 1) * LANES] / aux_ref[b : b + 1, :]
        updated = (before[b] + update).astype(bf16)
        values = updated.astype(f32)
        center = values - jnp.mean(values, axis=0, keepdims=True)
        spread = jnp.mean(center * center, axis=0, keepdims=True)
        line = dot_nn(bias_w, (center * lax.rsqrt(spread + norm_eps)).astype(bf16))
        blocks.append(pltpu.roll(line, partner(0) * 32, 1))
        values = values.T.astype(bf16)
        for a in range(GROUP):
            after[a, b] = values[a * 32 : (a + 1) * 32]
    lines, _, share, _ = send_ref.shape
    heads = share // 4
    for t in range(GROUP):
        block = jnp.concatenate([rows[t * heads : (t + 1) * heads] for rows in blocks], axis=0).astype(bf16)
        send_ref[:, t] = jnp.broadcast_to(block[None], (lines, share, LANES))
    for step in range(GROUP):
        updated_refs[step][...] = after[partner(step)]


def place_bias(flat, mask_ref, heads, h, bias):
    lines = bias.shape[0] // 16 - 1
    lane_group = lane_index(lines) // 32
    mask = mask_ref[4:5, :]
    for b in range(4):
        rows = [flat[pl.ds((4 * t + b) * heads + h, lines, stride=16 * heads), :] for t in range(GROUP)]
        for a in range(4):
            picked = rows[3]
            for t in range(3):
                picked = jnp.where(lane_group == (a + t) % 4, rows[t], picked)
            if a:
                picked = pltpu.roll(picked, LANES - 32 * a, 1)
            bias[pl.ds(4 * a + b, lines, stride=16), :] = picked + mask


def place_kernel(bias_ref, mask_ref, placed, flat):
    heads = placed.shape[0]
    rows = bias_ref.shape[0] * bias_ref.shape[1]
    flat[:rows] = bias_ref[...].reshape(rows, LANES).astype(f32)
    for h in range(heads):
        place_bias(flat, mask_ref, heads, h, placed.at[h])


def bias_gradient_kernel(scale, *refs):
    block_refs, (placed, send_ref, weights_ref, value_ref, grads) = refs[:GROUP], refs[GROUP:]
    sequences, rows, residues = weights_ref.shape
    heads = rows // residues
    seqs = sequences // GROUP
    ones = jnp.ones((residues, LANES), bf16)
    part_of = lane_index(residues) // 32
    totals = [jnp.zeros((residues, residues), f32) for _ in range(heads)]
    for step, block in enumerate(block_refs):
        for s in range(seqs):
            at = step * seqs + s
            columns = block[seqs + s]
            value_ref[at] = jnp.where(part_of < heads, jnp.ones((), bf16), columns)
            wide = jnp.concatenate(
                [jnp.where(part_of == g, block[s], jnp.zeros((), bf16)) for g in range(2 * heads)], axis=0
            )
            both = dot_nt(wide, columns)
            for h in range(heads):
                own = slice(h * residues, (h + 1) * residues)
                scores = both[own] * scale + placed[h, :residues]
                weights = jnp.exp(scores - jnp.max(scores, axis=-1, keepdims=True))
                rounded = weights.astype(bf16)
                weights_ref[at, own, :] = rounded
                flow = both[(heads + h) * residues : (heads + h + 1) * residues]
                inverse = 1.0 / dot_nn(rounded, ones)
                delta = dot_nn((weights * flow).astype(bf16), ones) * inverse
                totals[h] = totals[h] + weights * inverse * (flow - delta)
    for h in range(heads):
        grads[pl.ds(h, residues, stride=heads), :] = totals[h]
    send_ref[...] = grads[:rows].astype(bf16).reshape(send_ref.shape)


def attended_kernel(weights_ref, value_ref, *refs):
    part_refs, out_refs = refs[:GROUP], refs[GROUP:]
    sequences, _, residues = weights_ref.shape
    seqs = sequences // GROUP
    lane = lane_index(residues)
    for step in range(GROUP):
        attended = []
        for s in range(seqs):
            mixed = dot_nn(weights_ref[step * seqs + s], value_ref[step * seqs + s])
            picked = jnp.where(lane < 96, mixed[:residues], mixed[residues:])
            totals = jnp.where(lane < 32, mixed[:residues], mixed[residues:])
            attended.append(picked / pltpu.roll(totals, 64, 1))
        out_refs[step][0] = jnp.where(lane < 64, pltpu.roll(attended[0], 64, 1), attended[1]).astype(bf16)
        out_refs[step][1] = part_refs[step][...].reshape(residues, LANES)


def output_kernel(gate_ref, wo_ref, *refs):
    in_refs, (out_ref, pair_ref, normal_ref, inverse_ref) = refs[:GROUP], refs[GROUP:]
    residues = gate_ref.shape[1]
    rows = pair_ref.shape[0]
    columns_each = residues // GROUP
    low = lane_index(residues) < 64
    zero = jnp.zeros((), bf16)
    sums = [jnp.zeros((residues, out_ref.shape[1]), f32) for _ in range(2)]
    for step in range(GROUP):
        at = partner(step)
        gated = (gate_ref[at] * in_refs[step][0].astype(f32)).astype(bf16)
        weight = wo_ref[pl.ds(pl.multiple_of(at * 64, 64), 64), :]
        weight = jnp.concatenate([weight, weight], axis=0)
        sums[0] = sums[0] + dot_nn(jnp.where(low, gated, zero), weight)
        sums[1] = sums[1] + dot_nn(jnp.where(low, zero, gated), weight)
        columns = pl.ds(pl.multiple_of(at * columns_each, columns_each), columns_each)
        pair_ref[:, columns, :] = in_refs[step][1].reshape(rows, columns_each, LANES)
        values = in_refs[step][1].astype(f32)
        center = values - jnp.mean(values, axis=-1, keepdims=True)
        inverse = lax.rsqrt(jnp.mean(center * center, axis=-1, keepdims=True) + norm_eps)
        normal_ref[:, columns, :] = (center * inverse).reshape(rows, columns_each, LANES)
        inverse_ref[:, columns, :] = jnp.broadcast_to(inverse, values.shape).reshape(rows, columns_each, LANES)
    for s in range(2):
        out_ref[s * residues : (s + 1) * residues, :] = sums[s].astype(bf16)


def split_sum(values):
    high = values.astype(bf16)
    return high, (values - high.astype(f32)).astype(bf16)


def gradient_kernel(
    shares_ref, aux_ref, normal_ref, inverse_ref, update_ref, pair_ref, update_hbm, pair_hbm, out_hbm, result, left_for
):
    moves = [
        pltpu.make_async_copy(update_ref, update_hbm, left_for.at[0]),
        pltpu.make_async_copy(pair_ref, pair_hbm, left_for.at[1]),
    ]
    for move in moves:
        move.start()
    peers, share, _ = shares_ref.shape
    rows, _, channels = normal_ref.shape
    heads = share // rows
    total = jnp.sum(shares_ref[...].astype(f32).reshape(peers // GROUP, GROUP, share, LANES), axis=0)
    bias_w = aux_ref[8:16]
    mean_high, mean_low = split_sum(
        jnp.broadcast_to(jnp.mean(bias_w, axis=-1, keepdims=True), bias_w.shape)
    )
    exact = bias_w.astype(bf16)
    none = jnp.zeros(exact.shape, bf16)
    weights = jnp.concatenate(
        [
            jnp.concatenate([exact, mean_high], axis=1),
            jnp.concatenate([exact, mean_high], axis=1),
            jnp.concatenate([none, mean_low], axis=1),
        ],
        axis=0,
    )
    for i in range(rows):
        own = jnp.concatenate([total[t, i * heads : (i + 1) * heads] for t in range(GROUP)], axis=0)
        high, low = split_sum(own)
        both = dot_tn(jnp.concatenate([high, low, high], axis=0), weights)
        upstream, mean = both[:, :channels], both[:, channels:]
        normal = normal_ref[i]
        result[i] = inverse_ref[i] * (
            upstream - mean - normal * jnp.mean(upstream * normal, axis=-1, keepdims=True)
        )
        moves.append(pltpu.make_async_copy(result.at[i], out_hbm.at[i], left_for.at[2 + i]))
        moves[-1].start()
    for move in moves:
        move.wait()


def kernel_call(body, out_shape, in_specs=None, scratch=(), flops=0, moved=0, vmem_mib=12, out_specs=None, grid=()):
    vmem = pl.BlockSpec(memory_space=pltpu.VMEM)
    many = isinstance(out_shape, (list, tuple))
    return pl.pallas_call(
        body,
        grid=grid,
        out_shape=out_shape,
        in_specs=in_specs,
        out_specs=out_specs or ([vmem] * len(out_shape) if many else vmem),
        scratch_shapes=list(scratch),
        compiler_params=pltpu.CompilerParams(vmem_limit_bytes=vmem_mib * 1024 * 1024),
        cost_estimate=pl.CostEstimate(flops=flops, bytes_accessed=moved, transcendentals=0),
    )


def on_device_paired(
    alignment_rows,
    pair_state,
    update_cotangent,
    sequence_mask,
    residue_mask,
    left_weight,
    right_weight,
    outer_weight,
    bias_weight,
    query_weight,
    key_weight,
    value_weight,
    gate_weight,
    output_weight,
):
    sequence_wise, residues, channel_count = alignment_rows.shape
    rows_here, _, pair_channels = pair_state.shape
    head_count = bias_weight.shape[1]
    peers = lax.axis_size("row")
    factor = left_weight.shape[1]
    lines = peers // GROUP
    vmem = pl.BlockSpec(memory_space=pltpu.VMEM)
    smem = pl.BlockSpec(memory_space=pltpu.SMEM)
    token_rows = sequence_wise * residues
    columns_each = residues // GROUP
    block_rows = sequence_wise * 12
    flat_rows = alignment_rows.reshape(token_rows, channel_count)
    shape = jax.ShapeDtypeStruct

    pieces = [
        pl.BlockSpec((token_rows // PIECES, channel_count), lambda step, at=at: (at, 0)) for at in range(PIECES)
    ]
    send, aux, normed, *pair_blocks = kernel_call(
        factors_kernel,
        [
            shape((lines, GROUP, block_rows, LANES), bf16),
            shape((16, LANES), f32),
            shape((token_rows, channel_count), bf16),
        ]
        + [shape((rows_here, columns_each, pair_channels), bf16)] * GROUP,
        [smem] * 2 + [vmem] * 6 + pieces,
        [pltpu.VMEM((residues + 4 * GROUP, LANES), f32)],
        flops=2 * token_rows * channel_count * LANES,
        moved=1 << 20,
        vmem_mib=60,
        grid=(1,),
    )(
        sequence_mask,
        residue_mask,
        sequence_mask.reshape(1, -1),
        residue_mask.reshape(1, -1),
        bias_weight.T,
        left_weight.T,
        right_weight.T,
        pair_state,
        *[flat_rows] * PIECES,
    )
    received = lax.all_to_all(
        send.reshape(peers, block_rows, LANES), "row", split_axis=0, concat_axis=0, tiled=True
    )

    group_heads = head_count // GROUP
    head_rows = group_heads * residues
    scale = (channel_count // head_count) ** (-0.5)
    normed, *weights = lax.optimization_barrier((normed, query_weight, key_weight, value_weight, gate_weight))
    joined = jnp.concatenate(weights, axis=1)
    joined, *pair_blocks = lax.optimization_barrier((joined, *pair_blocks))
    part_shape = shape((rows_here, columns_each, pair_channels), bf16)
    gate, aux, own_block, *blocks = kernel_call(
        projections_kernel,
        [shape((GROUP, residues, LANES), f32), shape((16, LANES), f32), part_shape]
        + [shape((2 * sequence_wise, residues, LANES), bf16)] * GROUP,
        [vmem] * 6,
        [pltpu.VMEM((GROUP, 2 * sequence_wise, residues, LANES), bf16)],
        flops=10 * token_rows * channel_count * channel_count,
        moved=1 << 21,
    )(
        normed,
        update_cotangent.reshape(token_rows, channel_count),
        joined,
        output_weight,
        aux,
        pair_blocks[0],
    )

    def trade(parts):
        return parts[:1] + [
            lax.ppermute(parts[d], "row", [(i, i ^ d) for i in range(peers)]) for d in range(1, GROUP)
        ]

    pair_blocks = [own_block] + trade(pair_blocks)[1:]
    blocks = trade(blocks)
    weight_t = (
        outer_weight.reshape(factor, 4, 8, pair_channels)
        .transpose(1, 3, 2, 0)
        .reshape(4, pair_channels, 8 * factor)
    )
    share_rows = 4 * group_heads
    send_bias, *updated = kernel_call(
        pair_kernel,
        [shape((lines, GROUP, share_rows, LANES), bf16)] + [part_shape] * GROUP,
        [vmem] * (3 + GROUP),
        [
            pltpu.VMEM(((peers + 1) * block_rows, LANES), f32),
            pltpu.VMEM((4, peers * sequence_wise, 8 * LANES), bf16),
            pltpu.VMEM((peers * sequence_wise, 4 * LANES), f32),
            pltpu.VMEM((4, 8 * factor, 4 * LANES), bf16),
            pltpu.VMEM((GROUP, rows_here, columns_each, pair_channels), bf16),
            pltpu.VMEM((GROUP, rows_here, columns_each, pair_channels), bf16),
        ],
        flops=1 << 28,
        moved=1 << 20,
    )(received, weight_t, aux, *pair_blocks)
    bias_all = lax.all_to_all(
        send_bias.reshape(peers, share_rows, LANES), "row", split_axis=0, concat_axis=0, tiled=True
    )

    placed = kernel_call(
        place_kernel,
        shape((group_heads, residues + 16, LANES), f32),
        [vmem] * 2,
        [pltpu.VMEM((head_rows + 16 * group_heads, LANES), f32)],
        flops=1 << 22,
        moved=1 << 18,
    )(bias_all, aux)
    send_grad, weights, values = kernel_call(
        lambda *refs: bias_gradient_kernel(scale, *refs),
        [
            shape((peers, rows_here * group_heads, LANES), bf16),
            shape((GROUP * sequence_wise, head_rows, residues), bf16),
            shape((GROUP * sequence_wise, residues, LANES), bf16),
        ],
        [vmem] * (1 + GROUP),
        [pltpu.VMEM((head_rows + 16 * group_heads, LANES), f32)],
        flops=1 << 28,
        moved=1 << 22,
    )(*blocks, placed)
    shares = lax.all_to_all(send_grad, "row", split_axis=0, concat_axis=0, tiled=True)
    attended = kernel_call(
        attended_kernel,
        [shape((2, residues, LANES), bf16)] * GROUP,
        [vmem] * (2 + GROUP),
        flops=1 << 28,
        moved=1 << 21,
    )(weights, values, *updated)
    update, pair_updated, normal, inverse = kernel_call(
        output_kernel,
        [
            shape((token_rows, channel_count), bf16),
            shape((rows_here, residues, pair_channels), bf16),
            shape((rows_here, residues, pair_channels), f32),
            shape((rows_here, residues, pair_channels), f32),
        ],
        [vmem] * (2 + GROUP),
        flops=2 * token_rows * channel_count * channel_count,
        moved=1 << 20,
    )(gate, output_weight, *trade(list(attended)))
    update, pair_updated, pair_gradient = kernel_call(
        gradient_kernel,
        [
            shape((token_rows, channel_count), bf16),
            shape((rows_here, residues, pair_channels), bf16),
            shape((rows_here, residues, pair_channels), f32),
        ],
        [vmem] * 6,
        [pltpu.VMEM((rows_here, residues, pair_channels), f32), pltpu.SemaphoreType.DMA((2 + rows_here,))],
        flops=1 << 24,
        moved=1 << 20,
        out_specs=[pl.BlockSpec(memory_space=pltpu.HBM)] * 3,
    )(shares, aux, normal, inverse, update, pair_updated)
    return (update.reshape(alignment_rows.shape), pair_updated, pair_gradient)


def on_device(*arguments):
    rows, pair, left, bias = arguments[0], arguments[1], arguments[5], arguments[8]
    peers = lax.axis_size("row")
    fits = (
        lax.axis_size("col") == 1
        and peers == 32
        and rows.shape == (2, 128, 256)
        and pair.shape == (4, 128, 128)
        and left.shape[1] == 32
        and bias.shape[1] == 8
    )
    return (on_device_paired if fits else on_device_general)(*arguments)


def solution(mesh):
    placed = (
        P(("grp", "row"), "col", None),
        P(("grp", "row"), "col", None),
        P(("grp", "row"), "col", None),
        P("grp"),
        P("grp"),
        P(),
        P(),
        P(),
        P(),
        P(),
        P(),
        P(),
        P(),
        P(),
    )
    return jax.shard_map(
        on_device,
        mesh=mesh,
        in_specs=placed,
        out_specs=(
            P(("grp", "row"), "col", None),
            P(("grp", "row"), "col", None),
            P(("grp", "row"), "col", None),
        ),
        check_vma=False,
    )
```

```python
import jax
import jax.numpy as jnp
from jax import lax
from jax.experimental import pallas as pl
from jax.experimental.pallas import tpu as pltpu
from jax.sharding import PartitionSpec as P

norm_eps = 1e-05
mask_fill = 1000000000.0


def layer_normalize(values):
    values = values.astype(jnp.float32)
    center = values - jnp.mean(values, axis=-1, keepdims=True)
    spread = jnp.mean(center * center, axis=-1, keepdims=True)
    return center * lax.rsqrt(spread + norm_eps)


def norm_backward(values, upstream):
    values = values.astype(jnp.float32)
    center = values - jnp.mean(values, axis=-1, keepdims=True)
    inverse = lax.rsqrt(jnp.mean(center * center, axis=-1, keepdims=True) + norm_eps)
    normal_part = center * inverse
    return inverse * (
        upstream
        - jnp.mean(upstream, axis=-1, keepdims=True)
        - normal_part * jnp.mean(upstream * normal_part, axis=-1, keepdims=True)
    )


def spread_all(shard):
    copies = jnp.broadcast_to(shard[None], (lax.axis_size("row"),) + shard.shape)
    gathered = lax.all_to_all(copies, "row", split_axis=0, concat_axis=0, tiled=True)
    return gathered.reshape((-1,) + shard.shape[1:])


def attend_partial(
    projected_queries, projected_keys, projected_values, bias_all, key_mask, score_scale
):
    scores = jnp.einsum(
        "ihd,jhd->ihj", projected_queries, projected_keys, preferred_element_type=jnp.float32
    )
    scores = scores * score_scale + bias_all.astype(jnp.float32) + key_mask
    maxima = jnp.max(scores, axis=-1)
    weights = jnp.exp(scores - maxima[..., None])
    totals = jnp.sum(weights, axis=-1)
    summed = jnp.einsum(
        "ihj,jhd->ihd",
        weights.astype(jnp.bfloat16),
        projected_values,
        preferred_element_type=jnp.float32,
    )
    return (maxima, totals, summed.reshape(summed.shape[0], -1))


def on_device_general(
    alignment_rows,
    pair_state,
    update_cotangent,
    sequence_mask,
    residue_mask,
    left_weight,
    right_weight,
    outer_weight,
    bias_weight,
    query_weight,
    key_weight,
    value_weight,
    gate_weight,
    output_weight,
):
    sequence_wise, residue_half, channel_count = alignment_rows.shape
    rows_here = pair_state.shape[0]
    residues = residue_mask.shape[0]
    head_count = bias_weight.shape[1]
    head_dim = channel_count // head_count
    score_scale = head_dim ** (-0.5)
    row_index = lax.axis_index("row")
    col_index = lax.axis_index("col")
    complete_alignment, complete_cotangent = (
        lax.all_gather(alignment_rows, "col", axis=1, tiled=True),
        lax.all_gather(update_cotangent, "col", axis=1, tiled=True),
    )
    seq_live = sequence_mask.astype(jnp.float32)
    res_live = residue_mask.astype(jnp.float32)
    own_seq = lax.dynamic_slice_in_dim(seq_live, row_index * sequence_wise, sequence_wise)
    own_cols = lax.dynamic_slice_in_dim(res_live, col_index * residue_half, residue_half)
    own_rows = lax.dynamic_slice_in_dim(res_live, row_index * rows_here, rows_here)
    normalized_input = layer_normalize(complete_alignment).astype(jnp.bfloat16)
    flat_rows = normalized_input.reshape(-1, channel_count)
    normed_half = lax.dynamic_slice_in_dim(
        normalized_input, col_index * residue_half, residue_half, 1
    )
    half_rows = normed_half.reshape(-1, channel_count)
    left_proj = jnp.dot(flat_rows, left_weight, preferred_element_type=jnp.float32).reshape(
        sequence_wise, residues, -1
    )
    left_proj = (left_proj * (own_seq[:, None] * res_live[None, :])[..., None]).astype(jnp.bfloat16)
    right_proj = jnp.dot(half_rows, right_weight, preferred_element_type=jnp.float32).reshape(
        sequence_wise, residue_half, -1
    )
    right_proj = (right_proj * (own_seq[:, None] * own_cols[None, :])[..., None]).astype(
        jnp.bfloat16
    )
    left_tile = lax.all_to_all(left_proj, "row", split_axis=1, concat_axis=0, tiled=True)
    right_all = spread_all(right_proj)
    outer_width = left_tile.shape[2]
    outer_sum = lax.dot_general(
        left_tile.reshape(left_tile.shape[0], -1),
        right_all.reshape(right_all.shape[0], -1),
        (((0,), (0,)), ((), ())),
        preferred_element_type=jnp.float32,
    )
    outer_half = outer_sum.astype(jnp.bfloat16).reshape(
        rows_here, outer_width, residue_half, outer_width
    )
    opm_update = jnp.einsum(
        "ipjq,pqz->ijz", outer_half, outer_weight, preferred_element_type=jnp.float32
    )
    divisor = jnp.maximum(jnp.sum(seq_live) * own_rows[:, None] * own_cols[None, :], 1.0)
    pair_updated = (pair_state.astype(jnp.float32) + opm_update / divisor[..., None]).astype(
        jnp.bfloat16
    )
    pair_normed = layer_normalize(pair_updated).astype(jnp.bfloat16)
    bias_tile = jnp.einsum(
        "ijz,zh->ihj", pair_normed, bias_weight, preferred_element_type=jnp.float32
    ).astype(jnp.bfloat16)
    projected_queries = (
        jnp.dot(flat_rows, query_weight, preferred_element_type=jnp.float32)
        .astype(jnp.bfloat16)
        .reshape(sequence_wise, residues, head_count, head_dim)
    )
    gate_activations = jax.nn.sigmoid(
        jnp.dot(flat_rows, gate_weight, preferred_element_type=jnp.float32)
    ).reshape(sequence_wise, residues, channel_count)
    key_live = (res_live - 1.0) * mask_fill
    half_live = lax.dynamic_slice_in_dim(key_live, col_index * residue_half, residue_half)
    bias_cols = lax.all_gather(bias_tile, "col", axis=2, tiled=True)
    bias_all = spread_all(bias_cols)
    key_count = bias_all.shape[2]
    projected_keys = (
        jnp.dot(flat_rows, key_weight, preferred_element_type=jnp.float32)
        .astype(jnp.bfloat16)
        .reshape(sequence_wise, key_count, head_count, head_dim)
    )
    projected_values = (
        jnp.dot(flat_rows, value_weight, preferred_element_type=jnp.float32)
        .astype(jnp.bfloat16)
        .reshape(sequence_wise, key_count, head_count, head_dim)
    )
    maxima, totals, summed = lax.map(
        lambda inputs: attend_partial(
            inputs[0], inputs[1], inputs[2], bias_all, key_live, score_scale
        ),
        (projected_queries, projected_keys, projected_values),
    )
    attended = summed / jnp.repeat(totals, head_dim, axis=-1)
    gated = gate_activations * attended
    gated_own = lax.dynamic_slice_in_dim(gated, col_index * residue_half, residue_half, 1).astype(
        jnp.bfloat16
    )
    alignment_update = (
        jnp.dot(
            gated_own.reshape(-1, channel_count), output_weight, preferred_element_type=jnp.float32
        )
        .astype(jnp.bfloat16)
        .reshape(sequence_wise, residue_half, channel_count)
    )
    d_gated = lax.dot_general(
        complete_cotangent.reshape(-1, channel_count),
        output_weight,
        (((1,), (1,)), ((), ())),
        preferred_element_type=jnp.float32,
    ).reshape(sequence_wise, residues, channel_count)
    d_attended = d_gated * gate_activations
    delta_sum = jnp.sum(
        (d_attended * attended).reshape(sequence_wise, residues, head_count, head_dim), axis=-1
    )
    d_rounded = d_attended.astype(jnp.bfloat16).reshape(
        sequence_wise, residues, head_count, head_dim
    )
    log_total = maxima + jnp.log(totals)
    keys_half = lax.dynamic_slice_in_dim(projected_keys, col_index * residue_half, residue_half, 1)
    values_half = lax.dynamic_slice_in_dim(
        projected_values, col_index * residue_half, residue_half, 1
    )
    bias_half = lax.dynamic_slice_in_dim(bias_all, col_index * residue_half, residue_half, 2)
    bias_rows = bias_half.astype(jnp.float32)

    def single_sequence(running, sequence_items):
        query_rows, d_rows, total_rows, delta_rows, keys_one, values_one = sequence_items
        scores = jnp.einsum(
            "ihd,jhd->ihj", query_rows, keys_one, preferred_element_type=jnp.float32
        )
        scores = scores * score_scale + bias_rows + half_live
        probs = jnp.exp(scores - total_rows[..., None])
        d_weights = jnp.einsum(
            "ihd,jhd->ihj", d_rows, values_one, preferred_element_type=jnp.float32
        )
        return (running + probs * (d_weights - delta_rows[..., None]), None)

    sequence_items = (projected_queries, d_rounded, log_total, delta_sum, keys_half, values_half)
    initial_value = jnp.zeros(
        (rows_here * lax.axis_size("row"), head_count, residue_half), jnp.float32
    )
    result, unused = lax.scan(single_sequence, initial_value, sequence_items)
    shares = lax.all_to_all(
        result.astype(jnp.bfloat16).reshape((-1,) + (rows_here,) + result.shape[1:]),
        "row",
        split_axis=0,
        concat_axis=0,
        tiled=True,
    )
    bias_gradient = jnp.sum(shares.astype(jnp.float32), axis=0)
    d_normed = jnp.einsum(
        "ihj,zh->ijz",
        bias_gradient,
        bias_weight.astype(jnp.float32),
        precision=lax.Precision.HIGHEST,
    )
    pair_gradient = norm_backward(pair_updated, d_normed)
    return (alignment_update, pair_updated, pair_gradient)


LANES = 128
GROUP = 4
PIECES = 4
f32 = jnp.float32
bf16 = jnp.bfloat16


def dot_nn(a, b):
    return lax.dot_general(a, b, (((1,), (0,)), ((), ())), preferred_element_type=f32)


def dot_nt(a, b):
    return lax.dot_general(a, b, (((1,), (1,)), ((), ())), preferred_element_type=f32)


def dot_tn(a, b):
    return lax.dot_general(a, b, (((0,), (0,)), ((), ())), preferred_element_type=f32)


def lane_index(rows):
    return lax.broadcasted_iota(jnp.int32, (rows, LANES), 1)


def swap_groups(parts):
    lane = lane_index(parts[0].shape[0])
    low, even = lane < 64, lane % 64 < 32
    parts = [
        jnp.where(low, parts[0], pltpu.roll(parts[2], 64, 1)),
        jnp.where(low, parts[1], pltpu.roll(parts[3], 64, 1)),
        jnp.where(low, pltpu.roll(parts[0], 64, 1), parts[2]),
        jnp.where(low, pltpu.roll(parts[1], 64, 1), parts[3]),
    ]
    return [
        jnp.where(even, parts[0], pltpu.roll(parts[1], 32, 1)),
        jnp.where(even, pltpu.roll(parts[0], 96, 1), parts[1]),
        jnp.where(even, parts[2], pltpu.roll(parts[3], 32, 1)),
        jnp.where(even, pltpu.roll(parts[2], 96, 1), parts[3]),
    ]


def factors_kernel(
    seq_smem_ref, res_smem_ref, seq_ref, res_ref, bias_w_ref, left_ref, right_ref, *refs
):
    row_refs, (send_ref, aux_ref, normed_ref, left_scr) = refs[:PIECES], refs[PIECES:]
    lines = send_ref.shape[0]
    seqs = send_ref.shape[2] // 12
    residues = res_ref.shape[1]
    me = lax.axis_index("row")
    normed = jnp.concatenate([layer_normalize(rows[...]).astype(bf16) for rows in row_refs], axis=0)
    normed_ref[...] = normed
    live = res_ref[...].astype(f32)
    live_rows = jnp.broadcast_to(live, (residues, residues)).T
    right_t = right_ref[...]
    left_wide = jnp.concatenate([left_ref[...]] * 4, axis=0)
    lane_group = lane_index(lines) // 32
    quarters = []
    tail = []
    for s in range(seqs):
        seq_live = seq_smem_ref[me * seqs + s].astype(f32)
        own = normed[s * residues : (s + 1) * residues]
        factor = dot_nt(right_t, own) * (live * seq_live)
        quarters.append(swap_groups([factor[a * 8 : (a + 1) * 8] for a in range(4)]))
        left_scr[:residues] = dot_nt(own, left_wide) * (live_rows * seq_live)
        for a in range(4):
            row = jnp.zeros((lines, LANES), f32)
            for b in range(4):
                part = left_scr[pl.ds(4 * a + b, lines, stride=4 * GROUP), :]
                row = jnp.where(lane_group == b, part, row)
            tail.append(row)
    tail = jnp.stack(tail, axis=1).astype(bf16)
    right_rows = 8 * seqs
    for t in range(GROUP):
        block = jnp.concatenate([own[t] for own in quarters], axis=0).astype(bf16)
        send_ref[:, t, :right_rows, :] = jnp.broadcast_to(block[None], (lines, right_rows, LANES))
        send_ref[:, t, right_rows:, :] = tail
    aux_ref[0:4] = tile_divisor(res_smem_ref, res_ref, seq_ref)
    aux_ref[4:8] = jnp.broadcast_to((live - 1.0) * mask_fill, (4, LANES))
    aux_ref[8:16] = bias_w_ref[...].astype(f32)


def side_by_side(first, second, at):
    low = lane_index(first.shape[0]) < 64
    span = slice(at // 2 * LANES, at // 2 * LANES + LANES)
    first, second = first[:, span], second[:, span]
    if at % 2 == 0:
        return jnp.where(low, first, pltpu.roll(second, 64, 1))
    return jnp.where(low, pltpu.roll(first, 64, 1), second)


def partner(step):
    return lax.bitwise_xor(lax.rem(lax.axis_index("row"), GROUP), step)


def tile_divisor(res_smem_ref, res_ref, seq_ref):
    own = partner(0)
    rows = lax.div(lax.axis_index("row"), GROUP) * 16
    lane = lane_index(1)
    live = res_ref[...].astype(f32)
    columns = jnp.zeros((1, LANES), f32)
    for t in range(GROUP):
        turned = live if t == 0 else pltpu.roll(live, LANES - 32 * t, 1)
        columns = jnp.where(own == t, turned, columns)
    columns = jnp.where(lane < 32, columns, 0.0)
    columns = columns + pltpu.roll(columns, 32, 1)
    columns = columns + pltpu.roll(columns, 64, 1)
    total = jnp.sum(seq_ref[...].astype(f32), axis=-1, keepdims=True)
    lines = []
    for b in range(4):
        line = jnp.zeros((1, LANES), f32)
        for a in range(4):
            line = jnp.where(lane // 32 == a, res_smem_ref[rows + 4 * a + b].astype(f32), line)
        lines.append(jnp.maximum(total * line * columns, 1.0))
    return jnp.concatenate(lines, axis=0)


def projections_kernel(
    normed_ref, cot_ref, weights_ref, wo_ref, aux_ref, pair_ref, gate_ref, aux_out_ref, pair_out_ref, *rest
):
    block_refs, every = rest[:GROUP], rest[GROUP]
    aux_out_ref[...] = aux_ref[...]
    pair_out_ref[...] = pair_ref[...]
    normed = normed_ref[...]
    tokens = normed.shape[0]
    residues = gate_ref.shape[1]
    seqs = tokens // residues
    channels = normed.shape[1]
    queries, keys, values, gate = [
        dot_nn(normed, weights_ref[:, at * channels : (at + 1) * channels]) for at in range(4)
    ]
    gate = jax.nn.sigmoid(gate)
    d_attended = dot_nt(cot_ref[...], wo_ref[...]) * gate
    for t in range(GROUP):
        rows = side_by_side(queries, d_attended, t).astype(bf16)
        columns = side_by_side(keys, values, t).astype(bf16)
        gate_ref[t] = side_by_side(gate[:residues], gate[residues:], t)
        for s in range(seqs):
            every[t, s] = rows[s * residues : (s + 1) * residues]
            every[t, seqs + s] = columns[s * residues : (s + 1) * residues]
    for step in range(GROUP):
        block_refs[step][...] = every[partner(step)]


def pair_kernel(recv_ref, weight_ref, aux_ref, *refs):
    pair_refs, send_ref, updated_refs = refs[:GROUP], refs[GROUP], refs[GROUP + 1 : 2 * GROUP + 1]
    flat, rbuf, lbuf, obuf, state, after = refs[2 * GROUP + 1 :]
    peers, block_rows, _ = recv_ref.shape
    seqs = block_rows // 12
    for step in range(GROUP):
        state[partner(step)] = pair_refs[step][...]
    before = [
        jnp.concatenate([state[a, b] for a in range(GROUP)], axis=0).astype(f32).T for b in range(4)
    ]
    flat[: peers * block_rows] = recv_ref[...].astype(f32).reshape(peers * block_rows, LANES)
    for s in range(seqs):
        for g in range(8):
            part = flat[pl.ds(s * 8 + g, peers, stride=block_rows), :]
            for a in range(4):
                turned = part if a == 0 else pltpu.roll(part, 32 * a, 1)
                rbuf[a, s * peers : (s + 1) * peers, g * LANES : (g + 1) * LANES] = turned.astype(bf16)
        for a in range(4):
            part = flat[pl.ds(8 * seqs + 4 * s + a, peers, stride=block_rows), :]
            lbuf[s * peers : (s + 1) * peers, a * LANES : (a + 1) * LANES] = part
    left_t = lbuf[...].T.astype(bf16)
    outer = [dot_nn(left_t[a * LANES : (a + 1) * LANES], rbuf[a]).astype(bf16) for a in range(4)]
    lane_group = lane_index(LANES) // 32
    sums = None
    for q in range(4):
        for g in range(8):
            span = slice(g * LANES, (g + 1) * LANES)
            picked = outer[3][:, span]
            for a in range(3):
                picked = jnp.where(lane_group == (q + a) % 4, outer[a][:, span], picked)
            for b in range(4):
                obuf[q, g * 32 : (g + 1) * 32, b * LANES : (b + 1) * LANES] = picked[b * 32 : (b + 1) * 32]
        part = dot_nn(weight_ref[q], obuf[q])
        if q:
            part = jnp.concatenate(
                [pltpu.roll(part[:, b * LANES : (b + 1) * LANES], LANES - 32 * q, 1) for b in range(4)], axis=1
            )
        sums = part if sums is None else sums + part
    bias_w = aux_ref[8:16].astype(bf16)
    blocks = []
    for b in range(4):
        update = sums[:, b * LANES : (b + 1) * LANES] / aux_ref[b : b + 1, :]
        updated = (before[b] + update).astype(bf16)
        values = updated.astype(f32)
        center = values - jnp.mean(values, axis=0, keepdims=True)
        spread = jnp.mean(center * center, axis=0, keepdims=True)
        line = dot_nn(bias_w, (center * lax.rsqrt(spread + norm_eps)).astype(bf16))
        blocks.append(pltpu.roll(line, partner(0) * 32, 1))
        values = values.T.astype(bf16)
        for a in range(GROUP):
            after[a, b] = values[a * 32 : (a + 1) * 32]
    lines, _, share, _ = send_ref.shape
    heads = share // 4
    for t in range(GROUP):
        block = jnp.concatenate([rows[t * heads : (t + 1) * heads] for rows in blocks], axis=0).astype(bf16)
        send_ref[:, t] = jnp.broadcast_to(block[None], (lines, share, LANES))
    for step in range(GROUP):
        updated_refs[step][...] = after[partner(step)]


def place_bias(flat, heads, h, bias):
    lines = bias.shape[0] // 16 - 1
    lane_group = lane_index(lines) // 32
    for b in range(4):
        rows = [flat[pl.ds((4 * t + b) * heads + h, lines, stride=16 * heads), :] for t in range(GROUP)]
        for a in range(4):
            picked = rows[3]
            for t in range(3):
                picked = jnp.where(lane_group == (a + t) % 4, rows[t], picked)
            if a:
                picked = pltpu.roll(picked, LANES - 32 * a, 1)
            bias[pl.ds(4 * a + b, lines, stride=16), :] = picked


def place_kernel(bias_ref, mask_ref, placed, flat):
    heads = placed.shape[0]
    rows = bias_ref.shape[0] * bias_ref.shape[1]
    flat[:rows] = bias_ref[...].reshape(rows, LANES).astype(f32)
    for h in range(heads):
        place_bias(flat, heads, h, placed.at[h])
    placed[0, placed.shape[1] - 16 : placed.shape[1] - 12] = mask_ref[4:8]


def bias_gradient_kernel(scale, *refs):
    block_refs, (placed, send_ref, weights_ref, value_ref, grads) = refs[:GROUP], refs[GROUP:]
    sequences, rows, residues = weights_ref.shape
    heads = rows // residues
    seqs = sequences // GROUP
    ones = jnp.ones((residues, LANES), bf16)
    part_of = lane_index(residues) // 32
    key_mask = placed[0, residues : residues + 1]
    totals = [jnp.zeros((residues, residues), f32) for _ in range(heads)]
    for step, block in enumerate(block_refs):
        for s in range(seqs):
            at = step * seqs + s
            columns = block[seqs + s]
            value_ref[at] = jnp.where(part_of < heads, jnp.ones((), bf16), columns)
            wide = jnp.concatenate(
                [jnp.where(part_of == g, block[s], jnp.zeros((), bf16)) for g in range(2 * heads)], axis=0
            )
            both = dot_nt(wide, columns)
            for h in range(heads):
                own = slice(h * residues, (h + 1) * residues)
                scores = both[own] * scale + placed[h, :residues] + key_mask
                weights = jnp.exp(scores - jnp.max(scores, axis=-1, keepdims=True))
                rounded = weights.astype(bf16)
                weights_ref[at, own, :] = rounded
                flow = both[(heads + h) * residues : (heads + h + 1) * residues]
                inverse = 1.0 / dot_nn(rounded, ones)
                delta = dot_nn((weights * flow).astype(bf16), ones) * inverse
                totals[h] = totals[h] + weights * inverse * (flow - delta)
    for h in range(heads):
        grads[pl.ds(h, residues, stride=heads), :] = totals[h]
    send_ref[...] = grads[:rows].astype(bf16).reshape(send_ref.shape)


def attended_kernel(weights_ref, value_ref, *refs):
    part_refs, out_refs = refs[:GROUP], refs[GROUP:]
    sequences, _, residues = weights_ref.shape
    seqs = sequences // GROUP
    lane = lane_index(residues)
    for step in range(GROUP):
        attended = []
        for s in range(seqs):
            mixed = dot_nn(weights_ref[step * seqs + s], value_ref[step * seqs + s])
            picked = jnp.where(lane < 96, mixed[:residues], mixed[residues:])
            totals = jnp.where(lane < 32, mixed[:residues], mixed[residues:])
            attended.append(picked / pltpu.roll(totals, 64, 1))
        out_refs[step][0] = jnp.where(lane < 64, pltpu.roll(attended[0], 64, 1), attended[1]).astype(bf16)
        out_refs[step][1] = part_refs[step][...].reshape(residues, LANES)


def output_kernel(gate_ref, wo_ref, *refs):
    in_refs, (out_ref, pair_ref, normal_ref, inverse_ref) = refs[:GROUP], refs[GROUP:]
    residues = gate_ref.shape[1]
    rows = pair_ref.shape[0]
    columns_each = residues // GROUP
    low = lane_index(residues) < 64
    zero = jnp.zeros((), bf16)
    sums = [jnp.zeros((residues, out_ref.shape[1]), f32) for _ in range(2)]
    for step in range(GROUP):
        at = partner(step)
        gated = (gate_ref[at] * in_refs[step][0].astype(f32)).astype(bf16)
        weight = wo_ref[pl.ds(pl.multiple_of(at * 64, 64), 64), :]
        weight = jnp.concatenate([weight, weight], axis=0)
        sums[0] = sums[0] + dot_nn(jnp.where(low, gated, zero), weight)
        sums[1] = sums[1] + dot_nn(jnp.where(low, zero, gated), weight)
        columns = pl.ds(pl.multiple_of(at * columns_each, columns_each), columns_each)
        pair_ref[:, columns, :] = in_refs[step][1].reshape(rows, columns_each, LANES)
        values = in_refs[step][1].astype(f32)
        center = values - jnp.mean(values, axis=-1, keepdims=True)
        inverse = lax.rsqrt(jnp.mean(center * center, axis=-1, keepdims=True) + norm_eps)
        normal_ref[:, columns, :] = (center * inverse).reshape(rows, columns_each, LANES)
        inverse_ref[:, columns, :] = jnp.broadcast_to(inverse, values.shape).reshape(rows, columns_each, LANES)
    for s in range(2):
        out_ref[s * residues : (s + 1) * residues, :] = sums[s].astype(bf16)


def split_sum(values):
    high = values.astype(bf16)
    return high, (values - high.astype(f32)).astype(bf16)


def gradient_kernel(
    shares_ref, aux_ref, normal_ref, inverse_ref, update_ref, pair_ref, update_hbm, pair_hbm, out_hbm, result, left_for
):
    moves = [
        pltpu.make_async_copy(update_ref, update_hbm, left_for.at[0]),
        pltpu.make_async_copy(pair_ref, pair_hbm, left_for.at[1]),
    ]
    for move in moves:
        move.start()
    peers, share, _ = shares_ref.shape
    rows, _, channels = normal_ref.shape
    heads = share // rows
    total = jnp.sum(shares_ref[...].astype(f32).reshape(peers // GROUP, GROUP, share, LANES), axis=0)
    bias_w = aux_ref[8:16]
    mean_high, mean_low = split_sum(
        jnp.broadcast_to(jnp.mean(bias_w, axis=-1, keepdims=True), bias_w.shape)
    )
    exact = bias_w.astype(bf16)
    none = jnp.zeros(exact.shape, bf16)
    weights = jnp.concatenate(
        [
            jnp.concatenate([exact, mean_high], axis=1),
            jnp.concatenate([exact, mean_high], axis=1),
            jnp.concatenate([none, mean_low], axis=1),
        ],
        axis=0,
    )
    for i in range(rows):
        own = jnp.concatenate([total[t, i * heads : (i + 1) * heads] for t in range(GROUP)], axis=0)
        high, low = split_sum(own)
        both = dot_tn(jnp.concatenate([high, low, high], axis=0), weights)
        upstream, mean = both[:, :channels], both[:, channels:]
        normal = normal_ref[i]
        result[i] = inverse_ref[i] * (
            upstream - mean - normal * jnp.mean(upstream * normal, axis=-1, keepdims=True)
        )
        moves.append(pltpu.make_async_copy(result.at[i], out_hbm.at[i], left_for.at[2 + i]))
        moves[-1].start()
    for move in moves:
        move.wait()


def kernel_call(body, out_shape, in_specs=None, scratch=(), flops=0, moved=0, vmem_mib=12, out_specs=None, grid=()):
    vmem = pl.BlockSpec(memory_space=pltpu.VMEM)
    many = isinstance(out_shape, (list, tuple))
    return pl.pallas_call(
        body,
        grid=grid,
        out_shape=out_shape,
        in_specs=in_specs,
        out_specs=out_specs or ([vmem] * len(out_shape) if many else vmem),
        scratch_shapes=list(scratch),
        compiler_params=pltpu.CompilerParams(vmem_limit_bytes=vmem_mib * 1024 * 1024),
        cost_estimate=pl.CostEstimate(flops=flops, bytes_accessed=moved, transcendentals=0),
    )


def on_device_paired(
    alignment_rows,
    pair_state,
    update_cotangent,
    sequence_mask,
    residue_mask,
    left_weight,
    right_weight,
    outer_weight,
    bias_weight,
    query_weight,
    key_weight,
    value_weight,
    gate_weight,
    output_weight,
):
    sequence_wise, residues, channel_count = alignment_rows.shape
    rows_here, _, pair_channels = pair_state.shape
    head_count = bias_weight.shape[1]
    peers = lax.axis_size("row")
    factor = left_weight.shape[1]
    lines = peers // GROUP
    vmem = pl.BlockSpec(memory_space=pltpu.VMEM)
    smem = pl.BlockSpec(memory_space=pltpu.SMEM)
    token_rows = sequence_wise * residues
    columns_each = residues // GROUP
    block_rows = sequence_wise * 12
    flat_rows = alignment_rows.reshape(token_rows, channel_count)
    shape = jax.ShapeDtypeStruct

    pieces = [
        pl.BlockSpec((token_rows // PIECES, channel_count), lambda step, at=at: (at, 0)) for at in range(PIECES)
    ]
    send, aux, normed = kernel_call(
        factors_kernel,
        [
            shape((lines, GROUP, block_rows, LANES), bf16),
            shape((16, LANES), f32),
            shape((token_rows, channel_count), bf16),
        ],
        [smem] * 2 + [vmem] * 5 + pieces,
        [pltpu.VMEM((residues + 4 * GROUP, LANES), f32)],
        flops=2 * token_rows * channel_count * LANES,
        moved=1 << 20,
        vmem_mib=60,
        grid=(1,),
    )(
        sequence_mask,
        residue_mask,
        sequence_mask.reshape(1, -1),
        residue_mask.reshape(1, -1),
        bias_weight.T,
        left_weight.T,
        right_weight.T,
        *[flat_rows] * PIECES,
    )
    received = lax.all_to_all(
        send.reshape(peers, block_rows, LANES), "row", split_axis=0, concat_axis=0, tiled=True
    )

    group_heads = head_count // GROUP
    head_rows = group_heads * residues
    scale = (channel_count // head_count) ** (-0.5)
    normed, *weights = lax.optimization_barrier((normed, query_weight, key_weight, value_weight, gate_weight))
    joined = jnp.concatenate(weights, axis=1)
    joined, pair_rows = lax.optimization_barrier((joined, pair_state))
    own = lax.axis_index("row") % GROUP
    pair_blocks = [
        lax.dynamic_slice_in_dim(pair_rows, (own ^ step) * columns_each, columns_each, 1) for step in range(GROUP)
    ]
    part_shape = shape((rows_here, columns_each, pair_channels), bf16)
    gate, aux, own_block, *blocks = kernel_call(
        projections_kernel,
        [shape((GROUP, residues, LANES), f32), shape((16, LANES), f32), part_shape]
        + [shape((2 * sequence_wise, residues, LANES), bf16)] * GROUP,
        [vmem] * 6,
        [pltpu.VMEM((GROUP, 2 * sequence_wise, residues, LANES), bf16)],
        flops=10 * token_rows * channel_count * channel_count,
        moved=1 << 21,
    )(
        normed,
        update_cotangent.reshape(token_rows, channel_count),
        joined,
        output_weight,
        aux,
        pair_blocks[0],
    )

    def trade(parts):
        return parts[:1] + [
            lax.ppermute(parts[d], "row", [(i, i ^ d) for i in range(peers)]) for d in range(1, GROUP)
        ]

    pair_blocks = [own_block] + trade(pair_blocks)[1:]
    blocks = trade(blocks)
    weight_t = (
        outer_weight.reshape(factor, 4, 8, pair_channels)
        .transpose(1, 3, 2, 0)
        .reshape(4, pair_channels, 8 * factor)
    )
    share_rows = 4 * group_heads
    send_bias, *updated = kernel_call(
        pair_kernel,
        [shape((lines, GROUP, share_rows, LANES), bf16)] + [part_shape] * GROUP,
        [vmem] * (3 + GROUP),
        [
            pltpu.VMEM(((peers + 1) * block_rows, LANES), f32),
            pltpu.VMEM((4, peers * sequence_wise, 8 * LANES), bf16),
            pltpu.VMEM((peers * sequence_wise, 4 * LANES), f32),
            pltpu.VMEM((4, 8 * factor, 4 * LANES), bf16),
            pltpu.VMEM((GROUP, rows_here, columns_each, pair_channels), bf16),
            pltpu.VMEM((GROUP, rows_here, columns_each, pair_channels), bf16),
        ],
        flops=1 << 28,
        moved=1 << 20,
    )(received, weight_t, aux, *pair_blocks)
    bias_all = lax.all_to_all(
        send_bias.reshape(peers, share_rows, LANES), "row", split_axis=0, concat_axis=0, tiled=True
    )

    placed = kernel_call(
        place_kernel,
        shape((group_heads, residues + 16, LANES), f32),
        [vmem] * 2,
        [pltpu.VMEM((head_rows + 16 * group_heads, LANES), f32)],
        flops=1 << 22,
        moved=1 << 18,
    )(bias_all, aux)
    send_grad, weights, values = kernel_call(
        lambda *refs: bias_gradient_kernel(scale, *refs),
        [
            shape((peers, rows_here * group_heads, LANES), bf16),
            shape((GROUP * sequence_wise, head_rows, residues), bf16),
            shape((GROUP * sequence_wise, residues, LANES), bf16),
        ],
        [vmem] * (1 + GROUP),
        [pltpu.VMEM((head_rows + 16 * group_heads, LANES), f32)],
        flops=1 << 28,
        moved=1 << 22,
    )(*blocks, placed)
    shares = lax.all_to_all(send_grad, "row", split_axis=0, concat_axis=0, tiled=True)
    attended = kernel_call(
        attended_kernel,
        [shape((2, residues, LANES), bf16)] * GROUP,
        [vmem] * (2 + GROUP),
        flops=1 << 28,
        moved=1 << 21,
    )(weights, values, *updated)
    update, pair_updated, normal, inverse = kernel_call(
        output_kernel,
        [
            shape((token_rows, channel_count), bf16),
            shape((rows_here, residues, pair_channels), bf16),
            shape((rows_here, residues, pair_channels), f32),
            shape((rows_here, residues, pair_channels), f32),
        ],
        [vmem] * (2 + GROUP),
        flops=2 * token_rows * channel_count * channel_count,
        moved=1 << 20,
    )(gate, output_weight, *trade(list(attended)))
    update, pair_updated, pair_gradient = kernel_call(
        gradient_kernel,
        [
            shape((token_rows, channel_count), bf16),
            shape((rows_here, residues, pair_channels), bf16),
            shape((rows_here, residues, pair_channels), f32),
        ],
        [vmem] * 6,
        [pltpu.VMEM((rows_here, residues, pair_channels), f32), pltpu.SemaphoreType.DMA((2 + rows_here,))],
        flops=1 << 24,
        moved=1 << 20,
        out_specs=[pl.BlockSpec(memory_space=pltpu.HBM)] * 3,
    )(shares, aux, normal, inverse, update, pair_updated)
    return (update.reshape(alignment_rows.shape), pair_updated, pair_gradient)


def on_device(*arguments):
    rows, pair, left, bias = arguments[0], arguments[1], arguments[5], arguments[8]
    peers = lax.axis_size("row")
    fits = (
        lax.axis_size("col") == 1
        and peers == 32
        and rows.shape == (2, 128, 256)
        and pair.shape == (4, 128, 128)
        and left.shape[1] == 32
        and bias.shape[1] == 8
    )
    return (on_device_paired if fits else on_device_general)(*arguments)


def solution(mesh):
    placed = (
        P(("grp", "row"), "col", None),
        P(("grp", "row"), "col", None),
        P(("grp", "row"), "col", None),
        P("grp"),
        P("grp"),
        P(),
        P(),
        P(),
        P(),
        P(),
        P(),
        P(),
        P(),
        P(),
    )
    return jax.shard_map(
        on_device,
        mesh=mesh,
        in_specs=placed,
        out_specs=(
            P(("grp", "row"), "col", None),
            P(("grp", "row"), "col", None),
            P(("grp", "row"), "col", None),
        ),
        check_vma=False,
    )
```

```python
import jax
import jax.numpy as jnp
from jax import lax
from jax.experimental import pallas as pl
from jax.experimental.pallas import tpu as pltpu
from jax.sharding import PartitionSpec as P

norm_eps = 1e-05
mask_fill = 1000000000.0


def layer_normalize(values):
    values = values.astype(jnp.float32)
    center = values - jnp.mean(values, axis=-1, keepdims=True)
    spread = jnp.mean(center * center, axis=-1, keepdims=True)
    return center * lax.rsqrt(spread + norm_eps)


def norm_backward(values, upstream):
    values = values.astype(jnp.float32)
    center = values - jnp.mean(values, axis=-1, keepdims=True)
    inverse = lax.rsqrt(jnp.mean(center * center, axis=-1, keepdims=True) + norm_eps)
    normal_part = center * inverse
    return inverse * (
        upstream
        - jnp.mean(upstream, axis=-1, keepdims=True)
        - normal_part * jnp.mean(upstream * normal_part, axis=-1, keepdims=True)
    )


def spread_all(shard):
    copies = jnp.broadcast_to(shard[None], (lax.axis_size("row"),) + shard.shape)
    gathered = lax.all_to_all(copies, "row", split_axis=0, concat_axis=0, tiled=True)
    return gathered.reshape((-1,) + shard.shape[1:])


def attend_partial(
    projected_queries, projected_keys, projected_values, bias_all, key_mask, score_scale
):
    scores = jnp.einsum(
        "ihd,jhd->ihj", projected_queries, projected_keys, preferred_element_type=jnp.float32
    )
    scores = scores * score_scale + bias_all.astype(jnp.float32) + key_mask
    maxima = jnp.max(scores, axis=-1)
    weights = jnp.exp(scores - maxima[..., None])
    totals = jnp.sum(weights, axis=-1)
    summed = jnp.einsum(
        "ihj,jhd->ihd",
        weights.astype(jnp.bfloat16),
        projected_values,
        preferred_element_type=jnp.float32,
    )
    return (maxima, totals, summed.reshape(summed.shape[0], -1))


def on_device_general(
    alignment_rows,
    pair_state,
    update_cotangent,
    sequence_mask,
    residue_mask,
    left_weight,
    right_weight,
    outer_weight,
    bias_weight,
    query_weight,
    key_weight,
    value_weight,
    gate_weight,
    output_weight,
):
    sequence_wise, residue_half, channel_count = alignment_rows.shape
    rows_here = pair_state.shape[0]
    residues = residue_mask.shape[0]
    head_count = bias_weight.shape[1]
    head_dim = channel_count // head_count
    score_scale = head_dim ** (-0.5)
    row_index = lax.axis_index("row")
    col_index = lax.axis_index("col")
    complete_alignment, complete_cotangent = (
        lax.all_gather(alignment_rows, "col", axis=1, tiled=True),
        lax.all_gather(update_cotangent, "col", axis=1, tiled=True),
    )
    seq_live = sequence_mask.astype(jnp.float32)
    res_live = residue_mask.astype(jnp.float32)
    own_seq = lax.dynamic_slice_in_dim(seq_live, row_index * sequence_wise, sequence_wise)
    own_cols = lax.dynamic_slice_in_dim(res_live, col_index * residue_half, residue_half)
    own_rows = lax.dynamic_slice_in_dim(res_live, row_index * rows_here, rows_here)
    normalized_input = layer_normalize(complete_alignment).astype(jnp.bfloat16)
    flat_rows = normalized_input.reshape(-1, channel_count)
    normed_half = lax.dynamic_slice_in_dim(
        normalized_input, col_index * residue_half, residue_half, 1
    )
    half_rows = normed_half.reshape(-1, channel_count)
    left_proj = jnp.dot(flat_rows, left_weight, preferred_element_type=jnp.float32).reshape(
        sequence_wise, residues, -1
    )
    left_proj = (left_proj * (own_seq[:, None] * res_live[None, :])[..., None]).astype(jnp.bfloat16)
    right_proj = jnp.dot(half_rows, right_weight, preferred_element_type=jnp.float32).reshape(
        sequence_wise, residue_half, -1
    )
    right_proj = (right_proj * (own_seq[:, None] * own_cols[None, :])[..., None]).astype(
        jnp.bfloat16
    )
    left_tile = lax.all_to_all(left_proj, "row", split_axis=1, concat_axis=0, tiled=True)
    right_all = spread_all(right_proj)
    outer_width = left_tile.shape[2]
    outer_sum = lax.dot_general(
        left_tile.reshape(left_tile.shape[0], -1),
        right_all.reshape(right_all.shape[0], -1),
        (((0,), (0,)), ((), ())),
        preferred_element_type=jnp.float32,
    )
    outer_half = outer_sum.astype(jnp.bfloat16).reshape(
        rows_here, outer_width, residue_half, outer_width
    )
    opm_update = jnp.einsum(
        "ipjq,pqz->ijz", outer_half, outer_weight, preferred_element_type=jnp.float32
    )
    divisor = jnp.maximum(jnp.sum(seq_live) * own_rows[:, None] * own_cols[None, :], 1.0)
    pair_updated = (pair_state.astype(jnp.float32) + opm_update / divisor[..., None]).astype(
        jnp.bfloat16
    )
    pair_normed = layer_normalize(pair_updated).astype(jnp.bfloat16)
    bias_tile = jnp.einsum(
        "ijz,zh->ihj", pair_normed, bias_weight, preferred_element_type=jnp.float32
    ).astype(jnp.bfloat16)
    projected_queries = (
        jnp.dot(flat_rows, query_weight, preferred_element_type=jnp.float32)
        .astype(jnp.bfloat16)
        .reshape(sequence_wise, residues, head_count, head_dim)
    )
    gate_activations = jax.nn.sigmoid(
        jnp.dot(flat_rows, gate_weight, preferred_element_type=jnp.float32)
    ).reshape(sequence_wise, residues, channel_count)
    key_live = (res_live - 1.0) * mask_fill
    half_live = lax.dynamic_slice_in_dim(key_live, col_index * residue_half, residue_half)
    bias_cols = lax.all_gather(bias_tile, "col", axis=2, tiled=True)
    bias_all = spread_all(bias_cols)
    key_count = bias_all.shape[2]
    projected_keys = (
        jnp.dot(flat_rows, key_weight, preferred_element_type=jnp.float32)
        .astype(jnp.bfloat16)
        .reshape(sequence_wise, key_count, head_count, head_dim)
    )
    projected_values = (
        jnp.dot(flat_rows, value_weight, preferred_element_type=jnp.float32)
        .astype(jnp.bfloat16)
        .reshape(sequence_wise, key_count, head_count, head_dim)
    )
    maxima, totals, summed = lax.map(
        lambda inputs: attend_partial(
            inputs[0], inputs[1], inputs[2], bias_all, key_live, score_scale
        ),
        (projected_queries, projected_keys, projected_values),
    )
    attended = summed / jnp.repeat(totals, head_dim, axis=-1)
    gated = gate_activations * attended
    gated_own = lax.dynamic_slice_in_dim(gated, col_index * residue_half, residue_half, 1).astype(
        jnp.bfloat16
    )
    alignment_update = (
        jnp.dot(
            gated_own.reshape(-1, channel_count), output_weight, preferred_element_type=jnp.float32
        )
        .astype(jnp.bfloat16)
        .reshape(sequence_wise, residue_half, channel_count)
    )
    d_gated = lax.dot_general(
        complete_cotangent.reshape(-1, channel_count),
        output_weight,
        (((1,), (1,)), ((), ())),
        preferred_element_type=jnp.float32,
    ).reshape(sequence_wise, residues, channel_count)
    d_attended = d_gated * gate_activations
    delta_sum = jnp.sum(
        (d_attended * attended).reshape(sequence_wise, residues, head_count, head_dim), axis=-1
    )
    d_rounded = d_attended.astype(jnp.bfloat16).reshape(
        sequence_wise, residues, head_count, head_dim
    )
    log_total = maxima + jnp.log(totals)
    keys_half = lax.dynamic_slice_in_dim(projected_keys, col_index * residue_half, residue_half, 1)
    values_half = lax.dynamic_slice_in_dim(
        projected_values, col_index * residue_half, residue_half, 1
    )
    bias_half = lax.dynamic_slice_in_dim(bias_all, col_index * residue_half, residue_half, 2)
    bias_rows = bias_half.astype(jnp.float32)

    def single_sequence(running, sequence_items):
        query_rows, d_rows, total_rows, delta_rows, keys_one, values_one = sequence_items
        scores = jnp.einsum(
            "ihd,jhd->ihj", query_rows, keys_one, preferred_element_type=jnp.float32
        )
        scores = scores * score_scale + bias_rows + half_live
        probs = jnp.exp(scores - total_rows[..., None])
        d_weights = jnp.einsum(
            "ihd,jhd->ihj", d_rows, values_one, preferred_element_type=jnp.float32
        )
        return (running + probs * (d_weights - delta_rows[..., None]), None)

    sequence_items = (projected_queries, d_rounded, log_total, delta_sum, keys_half, values_half)
    initial_value = jnp.zeros(
        (rows_here * lax.axis_size("row"), head_count, residue_half), jnp.float32
    )
    result, unused = lax.scan(single_sequence, initial_value, sequence_items)
    shares = lax.all_to_all(
        result.astype(jnp.bfloat16).reshape((-1,) + (rows_here,) + result.shape[1:]),
        "row",
        split_axis=0,
        concat_axis=0,
        tiled=True,
    )
    bias_gradient = jnp.sum(shares.astype(jnp.float32), axis=0)
    d_normed = jnp.einsum(
        "ihj,zh->ijz",
        bias_gradient,
        bias_weight.astype(jnp.float32),
        precision=lax.Precision.HIGHEST,
    )
    pair_gradient = norm_backward(pair_updated, d_normed)
    return (alignment_update, pair_updated, pair_gradient)


LANES = 128
GROUP = 4
PIECES = 4
f32 = jnp.float32
bf16 = jnp.bfloat16


def dot_nn(a, b):
    return lax.dot_general(a, b, (((1,), (0,)), ((), ())), preferred_element_type=f32)


def dot_nt(a, b):
    return lax.dot_general(a, b, (((1,), (1,)), ((), ())), preferred_element_type=f32)


def dot_tn(a, b):
    return lax.dot_general(a, b, (((0,), (0,)), ((), ())), preferred_element_type=f32)


def lane_index(rows):
    return lax.broadcasted_iota(jnp.int32, (rows, LANES), 1)


def swap_groups(parts):
    lane = lane_index(parts[0].shape[0])
    low, even = lane < 64, lane % 64 < 32
    parts = [
        jnp.where(low, parts[0], pltpu.roll(parts[2], 64, 1)),
        jnp.where(low, parts[1], pltpu.roll(parts[3], 64, 1)),
        jnp.where(low, pltpu.roll(parts[0], 64, 1), parts[2]),
        jnp.where(low, pltpu.roll(parts[1], 64, 1), parts[3]),
    ]
    return [
        jnp.where(even, parts[0], pltpu.roll(parts[1], 32, 1)),
        jnp.where(even, pltpu.roll(parts[0], 96, 1), parts[1]),
        jnp.where(even, parts[2], pltpu.roll(parts[3], 32, 1)),
        jnp.where(even, pltpu.roll(parts[2], 96, 1), parts[3]),
    ]


def factors_kernel(
    seq_smem_ref, res_smem_ref, seq_ref, res_ref, bias_w_ref, left_ref, right_ref, *refs
):
    row_refs, (send_ref, aux_ref, normed_ref, left_scr) = refs[:PIECES], refs[PIECES:]
    lines = send_ref.shape[0]
    seqs = send_ref.shape[2] // 12
    residues = res_ref.shape[1]
    me = lax.axis_index("row")
    normed = jnp.concatenate([layer_normalize(rows[...]).astype(bf16) for rows in row_refs], axis=0)
    normed_ref[...] = normed
    live = res_ref[...].astype(f32)
    live_rows = jnp.broadcast_to(live, (residues, residues)).T
    right_t = right_ref[...]
    left_wide = jnp.concatenate([left_ref[...]] * 4, axis=0)
    lane_group = lane_index(lines) // 32
    quarters = []
    tail = []
    for s in range(seqs):
        seq_live = seq_smem_ref[me * seqs + s].astype(f32)
        own = normed[s * residues : (s + 1) * residues]
        factor = dot_nt(right_t, own) * (live * seq_live)
        quarters.append(swap_groups([factor[a * 8 : (a + 1) * 8] for a in range(4)]))
        left_scr[:residues] = dot_nt(own, left_wide) * (live_rows * seq_live)
        for a in range(4):
            row = jnp.zeros((lines, LANES), f32)
            for b in range(4):
                part = left_scr[pl.ds(4 * a + b, lines, stride=4 * GROUP), :]
                row = jnp.where(lane_group == b, part, row)
            tail.append(row)
    tail = jnp.stack(tail, axis=1).astype(bf16)
    right_rows = 8 * seqs
    for t in range(GROUP):
        block = jnp.concatenate([own[t] for own in quarters], axis=0).astype(bf16)
        send_ref[:, t, :right_rows, :] = jnp.broadcast_to(block[None], (lines, right_rows, LANES))
        send_ref[:, t, right_rows:, :] = tail
    aux_ref[0:4] = tile_inverse(res_smem_ref, res_ref, seq_ref)
    aux_ref[4:8] = jnp.broadcast_to((live - 1.0) * mask_fill, (4, LANES))
    aux_ref[8:16] = bias_w_ref[...].astype(f32)


def side_by_side(first, second, at):
    low = lane_index(first.shape[0]) < 64
    span = slice(at // 2 * LANES, at // 2 * LANES + LANES)
    first, second = first[:, span], second[:, span]
    if at % 2 == 0:
        return jnp.where(low, first, pltpu.roll(second, 64, 1))
    return jnp.where(low, pltpu.roll(first, 64, 1), second)


def partner(step):
    return lax.bitwise_xor(lax.rem(lax.axis_index("row"), GROUP), step)


def tile_inverse(res_smem_ref, res_ref, seq_ref):
    own = partner(0)
    rows = lax.div(lax.axis_index("row"), GROUP) * 16
    lane = lane_index(1)
    live = res_ref[...].astype(f32)
    columns = jnp.zeros((1, LANES), f32)
    for t in range(GROUP):
        turned = live if t == 0 else pltpu.roll(live, LANES - 32 * t, 1)
        columns = jnp.where(own == t, turned, columns)
    columns = jnp.where(lane < 32, columns, 0.0)
    columns = columns + pltpu.roll(columns, 32, 1)
    columns = columns + pltpu.roll(columns, 64, 1)
    total = jnp.sum(seq_ref[...].astype(f32), axis=-1, keepdims=True)
    lines = []
    for b in range(4):
        line = jnp.zeros((1, LANES), f32)
        for a in range(4):
            line = jnp.where(lane // 32 == a, res_smem_ref[rows + 4 * a + b].astype(f32), line)
        lines.append(1.0 / jnp.maximum(total * line * columns, 1.0))
    return jnp.concatenate(lines, axis=0)


def projections_kernel(
    normed_ref, cot_ref, weights_ref, wg_ref, wo_ref, aux_ref, pair_ref, gate_ref, aux_out_ref, pair_out_ref, *rest
):
    block_refs, every = rest[:GROUP], rest[GROUP]
    aux_out_ref[...] = aux_ref[...]
    pair_out_ref[...] = pair_ref[...]
    normed = normed_ref[...]
    tokens = normed.shape[0]
    residues = gate_ref.shape[1]
    seqs = tokens // residues
    channels = normed.shape[1]
    queries, keys, values = [
        dot_nn(normed, weights_ref[:, at * channels : (at + 1) * channels]) for at in range(3)
    ]
    gate = jax.nn.sigmoid(dot_nn(normed, wg_ref[...]))
    d_attended = dot_nt(cot_ref[...], wo_ref[...]) * gate
    for t in range(GROUP):
        rows = side_by_side(queries, d_attended, t).astype(bf16)
        columns = side_by_side(keys, values, t).astype(bf16)
        gate_ref[t] = side_by_side(gate[:residues], gate[residues:], t)
        for s in range(seqs):
            every[t, s] = rows[s * residues : (s + 1) * residues]
            every[t, seqs + s] = columns[s * residues : (s + 1) * residues]
    for step in range(GROUP):
        block_refs[step][...] = every[partner(step)]


def pair_kernel(recv_ref, weight_ref, aux_ref, *refs):
    pair_refs, send_ref, updated_refs = refs[:GROUP], refs[GROUP], refs[GROUP + 1 : 2 * GROUP + 1]
    flat, rbuf, lbuf, obuf, state, after = refs[2 * GROUP + 1 :]
    peers, block_rows, _ = recv_ref.shape
    seqs = block_rows // 12
    for step in range(GROUP):
        state[partner(step)] = pair_refs[step][...]
    before = [
        jnp.concatenate([state[a, b] for a in range(GROUP)], axis=0).astype(f32).T for b in range(4)
    ]
    flat[: peers * block_rows] = recv_ref[...].astype(f32).reshape(peers * block_rows, LANES)
    for s in range(seqs):
        for g in range(8):
            part = flat[pl.ds(s * 8 + g, peers, stride=block_rows), :]
            for a in range(4):
                turned = part if a == 0 else pltpu.roll(part, 32 * a, 1)
                rbuf[a, s * peers : (s + 1) * peers, g * LANES : (g + 1) * LANES] = turned.astype(bf16)
        for a in range(4):
            part = flat[pl.ds(8 * seqs + 4 * s + a, peers, stride=block_rows), :]
            lbuf[s * peers : (s + 1) * peers, a * LANES : (a + 1) * LANES] = part
    left_t = lbuf[...].T.astype(bf16)
    outer = [dot_nn(left_t[a * LANES : (a + 1) * LANES], rbuf[a]).astype(bf16) for a in range(4)]
    lane_group = lane_index(LANES) // 32
    sums = None
    for q in range(4):
        for g in range(8):
            span = slice(g * LANES, (g + 1) * LANES)
            picked = outer[3][:, span]
            for a in range(3):
                picked = jnp.where(lane_group == (q + a) % 4, outer[a][:, span], picked)
            for b in range(4):
                obuf[q, g * 32 : (g + 1) * 32, b * LANES : (b + 1) * LANES] = picked[b * 32 : (b + 1) * 32]
        part = dot_nn(weight_ref[q], obuf[q])
        if q:
            part = jnp.concatenate(
                [pltpu.roll(part[:, b * LANES : (b + 1) * LANES], LANES - 32 * q, 1) for b in range(4)], axis=1
            )
        sums = part if sums is None else sums + part
    bias_w = aux_ref[8:16].astype(bf16)
    blocks = []
    for b in range(4):
        update = sums[:, b * LANES : (b + 1) * LANES] * aux_ref[b : b + 1, :]
        updated = (before[b] + update).astype(bf16)
        values = updated.astype(f32)
        center = values - jnp.mean(values, axis=0, keepdims=True)
        spread = jnp.mean(center * center, axis=0, keepdims=True)
        line = dot_nn(bias_w, (center * lax.rsqrt(spread + norm_eps)).astype(bf16))
        blocks.append(pltpu.roll(line, partner(0) * 32, 1))
        values = values.T.astype(bf16)
        for a in range(GROUP):
            after[a, b] = values[a * 32 : (a + 1) * 32]
    lines, _, share, _ = send_ref.shape
    heads = share // 4
    for t in range(GROUP):
        block = jnp.concatenate([rows[t * heads : (t + 1) * heads] for rows in blocks], axis=0).astype(bf16)
        send_ref[:, t] = jnp.broadcast_to(block[None], (lines, share, LANES))
    for step in range(GROUP):
        updated_refs[step][...] = after[partner(step)]


def place_bias(flat, heads, h, bias):
    lines = bias.shape[0] // 16 - 1
    lane_group = lane_index(lines) // 32
    for b in range(4):
        rows = [flat[pl.ds((4 * t + b) * heads + h, lines, stride=16 * heads), :] for t in range(GROUP)]
        for a in range(4):
            picked = rows[3]
            for t in range(3):
                picked = jnp.where(lane_group == (a + t) % 4, rows[t], picked)
            if a:
                picked = pltpu.roll(picked, LANES - 32 * a, 1)
            bias[pl.ds(4 * a + b, lines, stride=16), :] = picked


def place_kernel(bias_ref, mask_ref, placed, flat):
    heads = placed.shape[0]
    rows = bias_ref.shape[0] * bias_ref.shape[1]
    flat[:rows] = bias_ref[...].reshape(rows, LANES).astype(f32)
    for h in range(heads):
        place_bias(flat, heads, h, placed.at[h])
    placed[0, placed.shape[1] - 16 : placed.shape[1] - 12] = mask_ref[4:8]


def bias_gradient_kernel(scale, *refs):
    block_refs, (placed, send_ref, weights_ref, value_ref, grads) = refs[:GROUP], refs[GROUP:]
    sequences, rows, residues = weights_ref.shape
    heads = rows // residues
    seqs = sequences // GROUP
    ones = jnp.ones((residues, LANES), bf16)
    part_of = lane_index(residues) // 32
    key_mask = placed[0, residues : residues + 1]
    totals = [jnp.zeros((residues, residues), f32) for _ in range(heads)]
    for step, block in enumerate(block_refs):
        for s in range(seqs):
            at = step * seqs + s
            columns = block[seqs + s]
            value_ref[at] = jnp.where(part_of < heads, jnp.ones((), bf16), columns)
            wide = jnp.concatenate(
                [jnp.where(part_of == g, block[s], jnp.zeros((), bf16)) for g in range(2 * heads)], axis=0
            )
            both = dot_nt(wide, columns)
            for h in range(heads):
                own = slice(h * residues, (h + 1) * residues)
                scores = both[own] * scale + placed[h, :residues] + key_mask
                weights = jnp.exp(scores - jnp.max(scores, axis=-1, keepdims=True))
                rounded = weights.astype(bf16)
                weights_ref[at, own, :] = rounded
                flow = both[(heads + h) * residues : (heads + h + 1) * residues]
                inverse = 1.0 / dot_nn(rounded, ones)
                delta = dot_nn((weights * flow).astype(bf16), ones) * inverse
                totals[h] = totals[h] + weights * inverse * (flow - delta)
    for h in range(heads):
        grads[pl.ds(h, residues, stride=heads), :] = totals[h]
    send_ref[...] = grads[:rows].astype(bf16).reshape(send_ref.shape)


def attended_kernel(weights_ref, value_ref, *refs):
    part_refs, out_refs = refs[:GROUP], refs[GROUP:]
    sequences, _, residues = weights_ref.shape
    seqs = sequences // GROUP
    lane = lane_index(residues)
    for step in range(GROUP):
        attended = []
        for s in range(seqs):
            mixed = dot_nn(weights_ref[step * seqs + s], value_ref[step * seqs + s])
            picked = jnp.where(lane < 96, mixed[:residues], mixed[residues:])
            totals = jnp.where(lane < 32, mixed[:residues], mixed[residues:])
            attended.append(picked / pltpu.roll(totals, 64, 1))
        out_refs[step][0] = jnp.where(lane < 64, pltpu.roll(attended[0], 64, 1), attended[1]).astype(bf16)
        out_refs[step][1] = part_refs[step][...].reshape(residues, LANES)


def output_kernel(gate_ref, wo_ref, *refs):
    in_refs, (out_ref, pair_ref, normal_ref, inverse_ref) = refs[:GROUP], refs[GROUP:]
    residues = gate_ref.shape[1]
    rows = pair_ref.shape[0]
    columns_each = residues // GROUP
    low = lane_index(residues) < 64
    zero = jnp.zeros((), bf16)
    sums = [jnp.zeros((residues, out_ref.shape[1]), f32) for _ in range(2)]
    for step in range(GROUP):
        at = partner(step)
        gated = (gate_ref[at] * in_refs[step][0].astype(f32)).astype(bf16)
        weight = wo_ref[pl.ds(pl.multiple_of(at * 64, 64), 64), :]
        weight = jnp.concatenate([weight, weight], axis=0)
        sums[0] = sums[0] + dot_nn(jnp.where(low, gated, zero), weight)
        sums[1] = sums[1] + dot_nn(jnp.where(low, zero, gated), weight)
        columns = pl.ds(pl.multiple_of(at * columns_each, columns_each), columns_each)
        pair_ref[:, columns, :] = in_refs[step][1].reshape(rows, columns_each, LANES)
        values = in_refs[step][1].astype(f32)
        center = values - jnp.mean(values, axis=-1, keepdims=True)
        inverse = lax.rsqrt(jnp.mean(center * center, axis=-1, keepdims=True) + norm_eps)
        normal_ref[:, columns, :] = (center * inverse).reshape(rows, columns_each, LANES)
        inverse_ref[:, columns, :] = jnp.broadcast_to(inverse, values.shape).reshape(rows, columns_each, LANES)
    for s in range(2):
        out_ref[s * residues : (s + 1) * residues, :] = sums[s].astype(bf16)


def split_sum(values):
    high = values.astype(bf16)
    return high, (values - high.astype(f32)).astype(bf16)


def gradient_kernel(
    shares_ref, aux_ref, normal_ref, inverse_ref, update_ref, pair_ref, update_hbm, pair_hbm, out_hbm, result, left_for
):
    moves = [
        pltpu.make_async_copy(update_ref, update_hbm, left_for.at[0]),
        pltpu.make_async_copy(pair_ref, pair_hbm, left_for.at[1]),
    ]
    for move in moves:
        move.start()
    peers, share, _ = shares_ref.shape
    rows, _, channels = normal_ref.shape
    heads = share // rows
    total = jnp.sum(shares_ref[...].astype(f32).reshape(peers // GROUP, GROUP, share, LANES), axis=0)
    bias_w = aux_ref[8:16]
    mean_high, mean_low = split_sum(
        jnp.broadcast_to(jnp.mean(bias_w, axis=-1, keepdims=True), bias_w.shape)
    )
    exact = bias_w.astype(bf16)
    none = jnp.zeros(exact.shape, bf16)
    weights = jnp.concatenate(
        [
            jnp.concatenate([exact, mean_high], axis=1),
            jnp.concatenate([exact, mean_high], axis=1),
            jnp.concatenate([none, mean_low], axis=1),
        ],
        axis=0,
    )
    for i in range(rows):
        own = jnp.concatenate([total[t, i * heads : (i + 1) * heads] for t in range(GROUP)], axis=0)
        high, low = split_sum(own)
        both = dot_tn(jnp.concatenate([high, low, high], axis=0), weights)
        upstream, mean = both[:, :channels], both[:, channels:]
        normal = normal_ref[i]
        result[i] = inverse_ref[i] * (
            upstream - mean - normal * jnp.mean(upstream * normal, axis=-1, keepdims=True)
        )
        moves.append(pltpu.make_async_copy(result.at[i], out_hbm.at[i], left_for.at[2 + i]))
        moves[-1].start()
    for move in moves:
        move.wait()


def kernel_call(body, out_shape, in_specs=None, scratch=(), flops=0, moved=0, vmem_mib=12, out_specs=None, grid=()):
    vmem = pl.BlockSpec(memory_space=pltpu.VMEM)
    many = isinstance(out_shape, (list, tuple))
    return pl.pallas_call(
        body,
        grid=grid,
        out_shape=out_shape,
        in_specs=in_specs,
        out_specs=out_specs or ([vmem] * len(out_shape) if many else vmem),
        scratch_shapes=list(scratch),
        compiler_params=pltpu.CompilerParams(vmem_limit_bytes=vmem_mib * 1024 * 1024),
        cost_estimate=pl.CostEstimate(flops=flops, bytes_accessed=moved, transcendentals=0),
    )


def on_device_paired(
    alignment_rows,
    pair_state,
    update_cotangent,
    sequence_mask,
    residue_mask,
    left_weight,
    right_weight,
    outer_weight,
    bias_weight,
    query_weight,
    key_weight,
    value_weight,
    gate_weight,
    output_weight,
):
    sequence_wise, residues, channel_count = alignment_rows.shape
    rows_here, _, pair_channels = pair_state.shape
    head_count = bias_weight.shape[1]
    peers = lax.axis_size("row")
    factor = left_weight.shape[1]
    lines = peers // GROUP
    vmem = pl.BlockSpec(memory_space=pltpu.VMEM)
    smem = pl.BlockSpec(memory_space=pltpu.SMEM)
    token_rows = sequence_wise * residues
    columns_each = residues // GROUP
    block_rows = sequence_wise * 12
    flat_rows = alignment_rows.reshape(token_rows, channel_count)
    shape = jax.ShapeDtypeStruct

    pieces = [
        pl.BlockSpec((token_rows // PIECES, channel_count), lambda step, at=at: (at, 0)) for at in range(PIECES)
    ]
    send, aux, normed = kernel_call(
        factors_kernel,
        [
            shape((lines, GROUP, block_rows, LANES), bf16),
            shape((16, LANES), f32),
            shape((token_rows, channel_count), bf16),
        ],
        [smem] * 2 + [vmem] * 5 + pieces,
        [pltpu.VMEM((residues + 4 * GROUP, LANES), f32)],
        flops=2 * token_rows * channel_count * LANES,
        moved=1 << 20,
        vmem_mib=60,
        grid=(1,),
    )(
        sequence_mask,
        residue_mask,
        sequence_mask.reshape(1, -1),
        residue_mask.reshape(1, -1),
        bias_weight.T,
        left_weight.T,
        right_weight.T,
        *[flat_rows] * PIECES,
    )
    received = lax.all_to_all(
        send.reshape(peers, block_rows, LANES), "row", split_axis=0, concat_axis=0, tiled=True
    )

    group_heads = head_count // GROUP
    head_rows = group_heads * residues
    scale = (channel_count // head_count) ** (-0.5)
    normed, *weights = lax.optimization_barrier((normed, query_weight, key_weight, value_weight))
    joined = jnp.concatenate(weights, axis=1)
    joined, pair_rows = lax.optimization_barrier((joined, pair_state))
    own = lax.axis_index("row") % GROUP
    pair_blocks = [
        lax.dynamic_slice_in_dim(pair_rows, (own ^ step) * columns_each, columns_each, 1) for step in range(GROUP)
    ]
    part_shape = shape((rows_here, columns_each, pair_channels), bf16)
    gate, aux, own_block, *blocks = kernel_call(
        projections_kernel,
        [shape((GROUP, residues, LANES), f32), shape((16, LANES), f32), part_shape]
        + [shape((2 * sequence_wise, residues, LANES), bf16)] * GROUP,
        [vmem] * 7,
        [pltpu.VMEM((GROUP, 2 * sequence_wise, residues, LANES), bf16)],
        flops=10 * token_rows * channel_count * channel_count,
        moved=1 << 21,
    )(
        normed,
        update_cotangent.reshape(token_rows, channel_count),
        joined,
        gate_weight,
        output_weight,
        aux,
        pair_blocks[0],
    )

    def trade(parts):
        return parts[:1] + [
            lax.ppermute(parts[d], "row", [(i, i ^ d) for i in range(peers)]) for d in range(1, GROUP)
        ]

    pair_blocks = [own_block] + trade(pair_blocks)[1:]
    blocks = trade(blocks)
    weight_t = (
        outer_weight.reshape(factor, 4, 8, pair_channels)
        .transpose(1, 3, 2, 0)
        .reshape(4, pair_channels, 8 * factor)
    )
    share_rows = 4 * group_heads
    send_bias, *updated = kernel_call(
        pair_kernel,
        [shape((lines, GROUP, share_rows, LANES), bf16)] + [part_shape] * GROUP,
        [vmem] * (3 + GROUP),
        [
            pltpu.VMEM(((peers + 1) * block_rows, LANES), f32),
            pltpu.VMEM((4, peers * sequence_wise, 8 * LANES), bf16),
            pltpu.VMEM((peers * sequence_wise, 4 * LANES), f32),
            pltpu.VMEM((4, 8 * factor, 4 * LANES), bf16),
            pltpu.VMEM((GROUP, rows_here, columns_each, pair_channels), bf16),
            pltpu.VMEM((GROUP, rows_here, columns_each, pair_channels), bf16),
        ],
        flops=1 << 28,
        moved=1 << 20,
    )(received, weight_t, aux, *pair_blocks)
    bias_all = lax.all_to_all(
        send_bias.reshape(peers, share_rows, LANES), "row", split_axis=0, concat_axis=0, tiled=True
    )

    placed = kernel_call(
        place_kernel,
        shape((group_heads, residues + 16, LANES), f32),
        [vmem] * 2,
        [pltpu.VMEM((head_rows + 16 * group_heads, LANES), f32)],
        flops=1 << 22,
        moved=1 << 18,
    )(bias_all, aux)
    send_grad, weights, values = kernel_call(
        lambda *refs: bias_gradient_kernel(scale, *refs),
        [
            shape((peers, rows_here * group_heads, LANES), bf16),
            shape((GROUP * sequence_wise, head_rows, residues), bf16),
            shape((GROUP * sequence_wise, residues, LANES), bf16),
        ],
        [vmem] * (1 + GROUP),
        [pltpu.VMEM((head_rows + 16 * group_heads, LANES), f32)],
        flops=1 << 28,
        moved=1 << 22,
    )(*blocks, placed)
    shares = lax.all_to_all(send_grad, "row", split_axis=0, concat_axis=0, tiled=True)
    attended = kernel_call(
        attended_kernel,
        [shape((2, residues, LANES), bf16)] * GROUP,
        [vmem] * (2 + GROUP),
        flops=1 << 28,
        moved=1 << 21,
    )(weights, values, *updated)
    update, pair_updated, normal, inverse = kernel_call(
        output_kernel,
        [
            shape((token_rows, channel_count), bf16),
            shape((rows_here, residues, pair_channels), bf16),
            shape((rows_here, residues, pair_channels), f32),
            shape((rows_here, residues, pair_channels), f32),
        ],
        [vmem] * (2 + GROUP),
        flops=2 * token_rows * channel_count * channel_count,
        moved=1 << 20,
    )(gate, output_weight, *trade(list(attended)))
    update, pair_updated, pair_gradient = kernel_call(
        gradient_kernel,
        [
            shape((token_rows, channel_count), bf16),
            shape((rows_here, residues, pair_channels), bf16),
            shape((rows_here, residues, pair_channels), f32),
        ],
        [vmem] * 6,
        [pltpu.VMEM((rows_here, residues, pair_channels), f32), pltpu.SemaphoreType.DMA((2 + rows_here,))],
        flops=1 << 24,
        moved=1 << 20,
        out_specs=[pl.BlockSpec(memory_space=pltpu.HBM)] * 3,
    )(shares, aux, normal, inverse, update, pair_updated)
    return (update.reshape(alignment_rows.shape), pair_updated, pair_gradient)


def on_device(*arguments):
    rows, pair, left, bias = arguments[0], arguments[1], arguments[5], arguments[8]
    peers = lax.axis_size("row")
    fits = (
        lax.axis_size("col") == 1
        and peers == 32
        and rows.shape == (2, 128, 256)
        and pair.shape == (4, 128, 128)
        and left.shape[1] == 32
        and bias.shape[1] == 8
    )
    return (on_device_paired if fits else on_device_general)(*arguments)


def solution(mesh):
    placed = (
        P(("grp", "row"), "col", None),
        P(("grp", "row"), "col", None),
        P(("grp", "row"), "col", None),
        P("grp"),
        P("grp"),
        P(),
        P(),
        P(),
        P(),
        P(),
        P(),
        P(),
        P(),
        P(),
    )
    return jax.shard_map(
        on_device,
        mesh=mesh,
        in_specs=placed,
        out_specs=(
            P(("grp", "row"), "col", None),
            P(("grp", "row"), "col", None),
            P(("grp", "row"), "col", None),
        ),
        check_vma=False,
    )
```

```python
import jax
import jax.numpy as jnp
from jax import lax
from jax.experimental import pallas as pl
from jax.experimental.pallas import tpu as pltpu
from jax.sharding import PartitionSpec as P

norm_eps = 1e-05
mask_fill = 1000000000.0


def layer_normalize(values):
    values = values.astype(jnp.float32)
    center = values - jnp.mean(values, axis=-1, keepdims=True)
    spread = jnp.mean(center * center, axis=-1, keepdims=True)
    return center * lax.rsqrt(spread + norm_eps)


def norm_backward(values, upstream):
    values = values.astype(jnp.float32)
    center = values - jnp.mean(values, axis=-1, keepdims=True)
    inverse = lax.rsqrt(jnp.mean(center * center, axis=-1, keepdims=True) + norm_eps)
    normal_part = center * inverse
    return inverse * (
        upstream
        - jnp.mean(upstream, axis=-1, keepdims=True)
        - normal_part * jnp.mean(upstream * normal_part, axis=-1, keepdims=True)
    )


def spread_all(shard):
    copies = jnp.broadcast_to(shard[None], (lax.axis_size("row"),) + shard.shape)
    gathered = lax.all_to_all(copies, "row", split_axis=0, concat_axis=0, tiled=True)
    return gathered.reshape((-1,) + shard.shape[1:])


def attend_partial(
    projected_queries, projected_keys, projected_values, bias_all, key_mask, score_scale
):
    scores = jnp.einsum(
        "ihd,jhd->ihj", projected_queries, projected_keys, preferred_element_type=jnp.float32
    )
    scores = scores * score_scale + bias_all.astype(jnp.float32) + key_mask
    maxima = jnp.max(scores, axis=-1)
    weights = jnp.exp(scores - maxima[..., None])
    totals = jnp.sum(weights, axis=-1)
    summed = jnp.einsum(
        "ihj,jhd->ihd",
        weights.astype(jnp.bfloat16),
        projected_values,
        preferred_element_type=jnp.float32,
    )
    return (maxima, totals, summed.reshape(summed.shape[0], -1))


def on_device_general(
    alignment_rows,
    pair_state,
    update_cotangent,
    sequence_mask,
    residue_mask,
    left_weight,
    right_weight,
    outer_weight,
    bias_weight,
    query_weight,
    key_weight,
    value_weight,
    gate_weight,
    output_weight,
):
    sequence_wise, residue_half, channel_count = alignment_rows.shape
    rows_here = pair_state.shape[0]
    residues = residue_mask.shape[0]
    head_count = bias_weight.shape[1]
    head_dim = channel_count // head_count
    score_scale = head_dim ** (-0.5)
    row_index = lax.axis_index("row")
    col_index = lax.axis_index("col")
    complete_alignment, complete_cotangent = (
        lax.all_gather(alignment_rows, "col", axis=1, tiled=True),
        lax.all_gather(update_cotangent, "col", axis=1, tiled=True),
    )
    seq_live = sequence_mask.astype(jnp.float32)
    res_live = residue_mask.astype(jnp.float32)
    own_seq = lax.dynamic_slice_in_dim(seq_live, row_index * sequence_wise, sequence_wise)
    own_cols = lax.dynamic_slice_in_dim(res_live, col_index * residue_half, residue_half)
    own_rows = lax.dynamic_slice_in_dim(res_live, row_index * rows_here, rows_here)
    normalized_input = layer_normalize(complete_alignment).astype(jnp.bfloat16)
    flat_rows = normalized_input.reshape(-1, channel_count)
    normed_half = lax.dynamic_slice_in_dim(
        normalized_input, col_index * residue_half, residue_half, 1
    )
    half_rows = normed_half.reshape(-1, channel_count)
    left_proj = jnp.dot(flat_rows, left_weight, preferred_element_type=jnp.float32).reshape(
        sequence_wise, residues, -1
    )
    left_proj = (left_proj * (own_seq[:, None] * res_live[None, :])[..., None]).astype(jnp.bfloat16)
    right_proj = jnp.dot(half_rows, right_weight, preferred_element_type=jnp.float32).reshape(
        sequence_wise, residue_half, -1
    )
    right_proj = (right_proj * (own_seq[:, None] * own_cols[None, :])[..., None]).astype(
        jnp.bfloat16
    )
    left_tile = lax.all_to_all(left_proj, "row", split_axis=1, concat_axis=0, tiled=True)
    right_all = spread_all(right_proj)
    outer_width = left_tile.shape[2]
    outer_sum = lax.dot_general(
        left_tile.reshape(left_tile.shape[0], -1),
        right_all.reshape(right_all.shape[0], -1),
        (((0,), (0,)), ((), ())),
        preferred_element_type=jnp.float32,
    )
    outer_half = outer_sum.astype(jnp.bfloat16).reshape(
        rows_here, outer_width, residue_half, outer_width
    )
    opm_update = jnp.einsum(
        "ipjq,pqz->ijz", outer_half, outer_weight, preferred_element_type=jnp.float32
    )
    divisor = jnp.maximum(jnp.sum(seq_live) * own_rows[:, None] * own_cols[None, :], 1.0)
    pair_updated = (pair_state.astype(jnp.float32) + opm_update / divisor[..., None]).astype(
        jnp.bfloat16
    )
    pair_normed = layer_normalize(pair_updated).astype(jnp.bfloat16)
    bias_tile = jnp.einsum(
        "ijz,zh->ihj", pair_normed, bias_weight, preferred_element_type=jnp.float32
    ).astype(jnp.bfloat16)
    projected_queries = (
        jnp.dot(flat_rows, query_weight, preferred_element_type=jnp.float32)
        .astype(jnp.bfloat16)
        .reshape(sequence_wise, residues, head_count, head_dim)
    )
    gate_activations = jax.nn.sigmoid(
        jnp.dot(flat_rows, gate_weight, preferred_element_type=jnp.float32)
    ).reshape(sequence_wise, residues, channel_count)
    key_live = (res_live - 1.0) * mask_fill
    half_live = lax.dynamic_slice_in_dim(key_live, col_index * residue_half, residue_half)
    bias_cols = lax.all_gather(bias_tile, "col", axis=2, tiled=True)
    bias_all = spread_all(bias_cols)
    key_count = bias_all.shape[2]
    projected_keys = (
        jnp.dot(flat_rows, key_weight, preferred_element_type=jnp.float32)
        .astype(jnp.bfloat16)
        .reshape(sequence_wise, key_count, head_count, head_dim)
    )
    projected_values = (
        jnp.dot(flat_rows, value_weight, preferred_element_type=jnp.float32)
        .astype(jnp.bfloat16)
        .reshape(sequence_wise, key_count, head_count, head_dim)
    )
    maxima, totals, summed = lax.map(
        lambda inputs: attend_partial(
            inputs[0], inputs[1], inputs[2], bias_all, key_live, score_scale
        ),
        (projected_queries, projected_keys, projected_values),
    )
    attended = summed / jnp.repeat(totals, head_dim, axis=-1)
    gated = gate_activations * attended
    gated_own = lax.dynamic_slice_in_dim(gated, col_index * residue_half, residue_half, 1).astype(
        jnp.bfloat16
    )
    alignment_update = (
        jnp.dot(
            gated_own.reshape(-1, channel_count), output_weight, preferred_element_type=jnp.float32
        )
        .astype(jnp.bfloat16)
        .reshape(sequence_wise, residue_half, channel_count)
    )
    d_gated = lax.dot_general(
        complete_cotangent.reshape(-1, channel_count),
        output_weight,
        (((1,), (1,)), ((), ())),
        preferred_element_type=jnp.float32,
    ).reshape(sequence_wise, residues, channel_count)
    d_attended = d_gated * gate_activations
    delta_sum = jnp.sum(
        (d_attended * attended).reshape(sequence_wise, residues, head_count, head_dim), axis=-1
    )
    d_rounded = d_attended.astype(jnp.bfloat16).reshape(
        sequence_wise, residues, head_count, head_dim
    )
    log_total = maxima + jnp.log(totals)
    keys_half = lax.dynamic_slice_in_dim(projected_keys, col_index * residue_half, residue_half, 1)
    values_half = lax.dynamic_slice_in_dim(
        projected_values, col_index * residue_half, residue_half, 1
    )
    bias_half = lax.dynamic_slice_in_dim(bias_all, col_index * residue_half, residue_half, 2)
    bias_rows = bias_half.astype(jnp.float32)

    def single_sequence(running, sequence_items):
        query_rows, d_rows, total_rows, delta_rows, keys_one, values_one = sequence_items
        scores = jnp.einsum(
            "ihd,jhd->ihj", query_rows, keys_one, preferred_element_type=jnp.float32
        )
        scores = scores * score_scale + bias_rows + half_live
        probs = jnp.exp(scores - total_rows[..., None])
        d_weights = jnp.einsum(
            "ihd,jhd->ihj", d_rows, values_one, preferred_element_type=jnp.float32
        )
        return (running + probs * (d_weights - delta_rows[..., None]), None)

    sequence_items = (projected_queries, d_rounded, log_total, delta_sum, keys_half, values_half)
    initial_value = jnp.zeros(
        (rows_here * lax.axis_size("row"), head_count, residue_half), jnp.float32
    )
    result, unused = lax.scan(single_sequence, initial_value, sequence_items)
    shares = lax.all_to_all(
        result.astype(jnp.bfloat16).reshape((-1,) + (rows_here,) + result.shape[1:]),
        "row",
        split_axis=0,
        concat_axis=0,
        tiled=True,
    )
    bias_gradient = jnp.sum(shares.astype(jnp.float32), axis=0)
    d_normed = jnp.einsum(
        "ihj,zh->ijz",
        bias_gradient,
        bias_weight.astype(jnp.float32),
        precision=lax.Precision.HIGHEST,
    )
    pair_gradient = norm_backward(pair_updated, d_normed)
    return (alignment_update, pair_updated, pair_gradient)


LANES = 128
GROUP = 4
PIECES = 4
f32 = jnp.float32
bf16 = jnp.bfloat16


def dot_nn(a, b):
    return lax.dot_general(a, b, (((1,), (0,)), ((), ())), preferred_element_type=f32)


def dot_nt(a, b):
    return lax.dot_general(a, b, (((1,), (1,)), ((), ())), preferred_element_type=f32)


def dot_tn(a, b):
    return lax.dot_general(a, b, (((0,), (0,)), ((), ())), preferred_element_type=f32)


def lane_index(rows):
    return lax.broadcasted_iota(jnp.int32, (rows, LANES), 1)


def swap_groups(parts):
    lane = lane_index(parts[0].shape[0])
    low, even = lane < 64, lane % 64 < 32
    parts = [
        jnp.where(low, parts[0], pltpu.roll(parts[2], 64, 1)),
        jnp.where(low, parts[1], pltpu.roll(parts[3], 64, 1)),
        jnp.where(low, pltpu.roll(parts[0], 64, 1), parts[2]),
        jnp.where(low, pltpu.roll(parts[1], 64, 1), parts[3]),
    ]
    return [
        jnp.where(even, parts[0], pltpu.roll(parts[1], 32, 1)),
        jnp.where(even, pltpu.roll(parts[0], 96, 1), parts[1]),
        jnp.where(even, parts[2], pltpu.roll(parts[3], 32, 1)),
        jnp.where(even, pltpu.roll(parts[2], 96, 1), parts[3]),
    ]


def factors_kernel(
    seq_smem_ref, res_smem_ref, seq_ref, res_ref, bias_w_ref, left_ref, right_ref, *refs
):
    row_refs, (send_ref, aux_ref, normed_ref, left_scr) = refs[:PIECES], refs[PIECES:]
    lines = send_ref.shape[0]
    seqs = send_ref.shape[2] // 12
    residues = res_ref.shape[1]
    me = lax.axis_index("row")
    normed = jnp.concatenate([layer_normalize(rows[...]).astype(bf16) for rows in row_refs], axis=0)
    normed_ref[...] = normed
    live = res_ref[...].astype(f32)
    live_rows = jnp.broadcast_to(live, (residues, residues)).T
    right_t = right_ref[...]
    left_wide = jnp.concatenate([left_ref[...]] * 4, axis=0)
    lane_group = lane_index(lines) // 32
    quarters = []
    tail = []
    for s in range(seqs):
        seq_live = seq_smem_ref[me * seqs + s].astype(f32)
        own = normed[s * residues : (s + 1) * residues]
        factor = dot_nt(right_t, own) * (live * seq_live)
        quarters.append(swap_groups([factor[a * 8 : (a + 1) * 8] for a in range(4)]))
        left_scr[:residues] = dot_nt(own, left_wide) * (live_rows * seq_live)
        for a in range(4):
            row = jnp.zeros((lines, LANES), f32)
            for b in range(4):
                part = left_scr[pl.ds(4 * a + b, lines, stride=4 * GROUP), :]
                row = jnp.where(lane_group == b, part, row)
            tail.append(row)
    tail = jnp.stack(tail, axis=1).astype(bf16)
    right_rows = 8 * seqs
    for t in range(GROUP):
        block = jnp.concatenate([own[t] for own in quarters], axis=0).astype(bf16)
        send_ref[:, t, :right_rows, :] = jnp.broadcast_to(block[None], (lines, right_rows, LANES))
        send_ref[:, t, right_rows:, :] = tail
    aux_ref[0:4] = tile_inverse(res_smem_ref, res_ref, seq_ref)
    aux_ref[4:8] = jnp.broadcast_to((live - 1.0) * mask_fill, (4, LANES))
    aux_ref[8:16] = bias_w_ref[...].astype(f32)


def side_by_side(first, second, at):
    low = lane_index(first.shape[0]) < 64
    span = slice(at // 2 * LANES, at // 2 * LANES + LANES)
    first, second = first[:, span], second[:, span]
    if at % 2 == 0:
        return jnp.where(low, first, pltpu.roll(second, 64, 1))
    return jnp.where(low, pltpu.roll(first, 64, 1), second)


def partner(step):
    return lax.bitwise_xor(lax.rem(lax.axis_index("row"), GROUP), step)


def tile_inverse(res_smem_ref, res_ref, seq_ref):
    own = partner(0)
    rows = lax.div(lax.axis_index("row"), GROUP) * 16
    lane = lane_index(1)
    live = res_ref[...].astype(f32)
    columns = jnp.zeros((1, LANES), f32)
    for t in range(GROUP):
        turned = live if t == 0 else pltpu.roll(live, LANES - 32 * t, 1)
        columns = jnp.where(own == t, turned, columns)
    columns = jnp.where(lane < 32, columns, 0.0)
    columns = columns + pltpu.roll(columns, 32, 1)
    columns = columns + pltpu.roll(columns, 64, 1)
    total = jnp.sum(seq_ref[...].astype(f32), axis=-1, keepdims=True)
    lines = []
    for b in range(4):
        line = jnp.zeros((1, LANES), f32)
        for a in range(4):
            line = jnp.where(lane // 32 == a, res_smem_ref[rows + 4 * a + b].astype(f32), line)
        lines.append(1.0 / jnp.maximum(total * line * columns, 1.0))
    return jnp.concatenate(lines, axis=0)


def projections_kernel(
    normed_ref, cot_ref, weights_ref, wg_ref, wo_ref, aux_ref, pair_ref, gate_ref, aux_out_ref, pair_out_ref, *rest
):
    block_refs, every = rest[:GROUP], rest[GROUP]
    aux_out_ref[...] = aux_ref[...]
    pair_out_ref[...] = pair_ref[...]
    normed = normed_ref[...]
    tokens = normed.shape[0]
    residues = gate_ref.shape[1]
    seqs = tokens // residues
    channels = normed.shape[1]
    queries, keys, values = [
        dot_nn(normed, weights_ref[:, at * channels : (at + 1) * channels]) for at in range(3)
    ]
    gate = jax.nn.sigmoid(dot_nn(normed, wg_ref[...]))
    d_attended = dot_nt(cot_ref[...], wo_ref[...]) * gate
    for t in range(GROUP):
        rows = side_by_side(queries, d_attended, t).astype(bf16)
        columns = side_by_side(keys, values, t).astype(bf16)
        gate_ref[t] = side_by_side(gate[:residues], gate[residues:], t)
        for s in range(seqs):
            every[t, s] = rows[s * residues : (s + 1) * residues]
            every[t, seqs + s] = columns[s * residues : (s + 1) * residues]
    for step in range(GROUP):
        block_refs[step][...] = every[partner(step)]


def pair_kernel(recv_ref, weight_ref, aux_ref, *refs):
    pair_refs, send_ref, updated_refs = refs[:GROUP], refs[GROUP], refs[GROUP + 1 : 2 * GROUP + 1]
    flat, rbuf, lbuf, obuf, state, after = refs[2 * GROUP + 1 :]
    peers, block_rows, _ = recv_ref.shape
    seqs = block_rows // 12
    for step in range(GROUP):
        state[partner(step)] = pair_refs[step][...]
    before = [
        jnp.concatenate([state[a, b] for a in range(GROUP)], axis=0).astype(f32).T for b in range(4)
    ]
    flat[: peers * block_rows] = recv_ref[...].astype(f32).reshape(peers * block_rows, LANES)
    for s in range(seqs):
        for g in range(8):
            part = flat[pl.ds(s * 8 + g, peers, stride=block_rows), :]
            for a in range(4):
                turned = part if a == 0 else pltpu.roll(part, 32 * a, 1)
                rbuf[a, s * peers : (s + 1) * peers, g * LANES : (g + 1) * LANES] = turned.astype(bf16)
        for a in range(4):
            part = flat[pl.ds(8 * seqs + 4 * s + a, peers, stride=block_rows), :]
            lbuf[s * peers : (s + 1) * peers, a * LANES : (a + 1) * LANES] = part
    left_t = lbuf[...].T.astype(bf16)
    outer = [dot_nn(left_t[a * LANES : (a + 1) * LANES], rbuf[a]).astype(bf16) for a in range(4)]
    lane_group = lane_index(LANES) // 32
    sums = None
    for q in range(4):
        for g in range(8):
            span = slice(g * LANES, (g + 1) * LANES)
            picked = outer[3][:, span]
            for a in range(3):
                picked = jnp.where(lane_group == (q + a) % 4, outer[a][:, span], picked)
            for b in range(4):
                obuf[q, g * 32 : (g + 1) * 32, b * LANES : (b + 1) * LANES] = picked[b * 32 : (b + 1) * 32]
        part = dot_tn(weight_ref[q], obuf[q])
        if q:
            part = jnp.concatenate(
                [pltpu.roll(part[:, b * LANES : (b + 1) * LANES], LANES - 32 * q, 1) for b in range(4)], axis=1
            )
        sums = part if sums is None else sums + part
    bias_w = aux_ref[8:16].astype(bf16)
    blocks = []
    for b in range(4):
        update = sums[:, b * LANES : (b + 1) * LANES] * aux_ref[b : b + 1, :]
        updated = (before[b] + update).astype(bf16)
        values = updated.astype(f32)
        center = values - jnp.mean(values, axis=0, keepdims=True)
        spread = jnp.mean(center * center, axis=0, keepdims=True)
        line = dot_nn(bias_w, (center * lax.rsqrt(spread + norm_eps)).astype(bf16))
        blocks.append(pltpu.roll(line, partner(0) * 32, 1))
        values = values.T.astype(bf16)
        for a in range(GROUP):
            after[a, b] = values[a * 32 : (a + 1) * 32]
    lines, _, share, _ = send_ref.shape
    heads = share // 4
    for t in range(GROUP):
        block = jnp.concatenate([rows[t * heads : (t + 1) * heads] for rows in blocks], axis=0).astype(bf16)
        send_ref[:, t] = jnp.broadcast_to(block[None], (lines, share, LANES))
    for step in range(GROUP):
        updated_refs[step][...] = after[partner(step)]


def place_bias(flat, heads, h, bias):
    lines = bias.shape[0] // 16 - 1
    lane_group = lane_index(lines) // 32
    for b in range(4):
        rows = [flat[pl.ds((4 * t + b) * heads + h, lines, stride=16 * heads), :] for t in range(GROUP)]
        for a in range(4):
            picked = rows[3]
            for t in range(3):
                picked = jnp.where(lane_group == (a + t) % 4, rows[t], picked)
            if a:
                picked = pltpu.roll(picked, LANES - 32 * a, 1)
            bias[pl.ds(4 * a + b, lines, stride=16), :] = picked


def place_kernel(bias_ref, mask_ref, placed, flat):
    heads = placed.shape[0]
    rows = bias_ref.shape[0] * bias_ref.shape[1]
    flat[:rows] = bias_ref[...].reshape(rows, LANES).astype(f32)
    for h in range(heads):
        place_bias(flat, heads, h, placed.at[h])
    placed[0, placed.shape[1] - 16 : placed.shape[1] - 12] = mask_ref[4:8]


def bias_gradient_kernel(scale, *refs):
    block_refs, (placed, send_ref, weights_ref, value_ref, grads) = refs[:GROUP], refs[GROUP:]
    sequences, rows, residues = weights_ref.shape
    heads = rows // residues
    seqs = sequences // GROUP
    ones = jnp.ones((residues, LANES), bf16)
    part_of = lane_index(residues) // 32
    key_mask = placed[0, residues : residues + 1]
    totals = [jnp.zeros((residues, residues), f32) for _ in range(heads)]
    for step, block in enumerate(block_refs):
        for s in range(seqs):
            at = step * seqs + s
            columns = block[seqs + s]
            value_ref[at] = jnp.where(part_of < heads, jnp.ones((), bf16), columns)
            wide = jnp.concatenate(
                [jnp.where(part_of == g, block[s], jnp.zeros((), bf16)) for g in range(2 * heads)], axis=0
            )
            both = dot_nt(wide, columns)
            for h in range(heads):
                own = slice(h * residues, (h + 1) * residues)
                scores = both[own] * scale + placed[h, :residues] + key_mask
                weights = jnp.exp(scores - jnp.max(scores, axis=-1, keepdims=True))
                rounded = weights.astype(bf16)
                weights_ref[at, own, :] = rounded
                flow = both[(heads + h) * residues : (heads + h + 1) * residues]
                inverse = 1.0 / dot_nn(rounded, ones)
                delta = dot_nn((weights * flow).astype(bf16), ones) * inverse
                totals[h] = totals[h] + weights * inverse * (flow - delta)
    for h in range(heads):
        grads[pl.ds(h, residues, stride=heads), :] = totals[h]
    send_ref[...] = grads[:rows].astype(bf16).reshape(send_ref.shape)


def attended_kernel(weights_ref, value_ref, *refs):
    part_refs, out_refs = refs[:GROUP], refs[GROUP:]
    sequences, _, residues = weights_ref.shape
    seqs = sequences // GROUP
    lane = lane_index(residues)
    for step in range(GROUP):
        attended = []
        for s in range(seqs):
            mixed = dot_nn(weights_ref[step * seqs + s], value_ref[step * seqs + s])
            picked = jnp.where(lane < 96, mixed[:residues], mixed[residues:])
            totals = jnp.where(lane < 32, mixed[:residues], mixed[residues:])
            attended.append(picked / pltpu.roll(totals, 64, 1))
        out_refs[step][0] = jnp.where(lane < 64, pltpu.roll(attended[0], 64, 1), attended[1]).astype(bf16)
        out_refs[step][1] = part_refs[step][...].reshape(residues, LANES)


def output_kernel(gate_ref, wo_ref, *refs):
    in_refs, (out_ref, pair_ref, normal_ref, inverse_ref) = refs[:GROUP], refs[GROUP:]
    residues = gate_ref.shape[1]
    rows = pair_ref.shape[0]
    columns_each = residues // GROUP
    low = lane_index(residues) < 64
    zero = jnp.zeros((), bf16)
    sums = [jnp.zeros((residues, out_ref.shape[1]), f32) for _ in range(2)]
    for step in range(GROUP):
        at = partner(step)
        gated = (gate_ref[at] * in_refs[step][0].astype(f32)).astype(bf16)
        weight = wo_ref[pl.ds(pl.multiple_of(at * 64, 64), 64), :]
        weight = jnp.concatenate([weight, weight], axis=0)
        sums[0] = sums[0] + dot_nn(jnp.where(low, gated, zero), weight)
        sums[1] = sums[1] + dot_nn(jnp.where(low, zero, gated), weight)
        columns = pl.ds(pl.multiple_of(at * columns_each, columns_each), columns_each)
        pair_ref[:, columns, :] = in_refs[step][1].reshape(rows, columns_each, LANES)
        values = in_refs[step][1].astype(f32)
        center = values - jnp.mean(values, axis=-1, keepdims=True)
        inverse = lax.rsqrt(jnp.mean(center * center, axis=-1, keepdims=True) + norm_eps)
        normal_ref[:, columns, :] = (center * inverse).reshape(rows, columns_each, LANES)
        inverse_ref[:, columns, :] = jnp.broadcast_to(inverse, values.shape).reshape(rows, columns_each, LANES)
    for s in range(2):
        out_ref[s * residues : (s + 1) * residues, :] = sums[s].astype(bf16)


def split_sum(values):
    high = values.astype(bf16)
    return high, (values - high.astype(f32)).astype(bf16)


def gradient_kernel(
    shares_ref, aux_ref, normal_ref, inverse_ref, update_ref, pair_ref, update_hbm, pair_hbm, out_hbm, result, left_for
):
    moves = [
        pltpu.make_async_copy(update_ref, update_hbm, left_for.at[0]),
        pltpu.make_async_copy(pair_ref, pair_hbm, left_for.at[1]),
    ]
    for move in moves:
        move.start()
    peers, share, _ = shares_ref.shape
    rows, _, channels = normal_ref.shape
    heads = share // rows
    total = jnp.sum(shares_ref[...].astype(f32).reshape(peers // GROUP, GROUP, share, LANES), axis=0)
    bias_w = aux_ref[8:16]
    mean_high, mean_low = split_sum(
        jnp.broadcast_to(jnp.mean(bias_w, axis=-1, keepdims=True), bias_w.shape)
    )
    exact = bias_w.astype(bf16)
    none = jnp.zeros(exact.shape, bf16)
    weights = jnp.concatenate(
        [
            jnp.concatenate([exact, mean_high], axis=1),
            jnp.concatenate([exact, mean_high], axis=1),
            jnp.concatenate([none, mean_low], axis=1),
        ],
        axis=0,
    )
    for i in range(rows):
        own = jnp.concatenate([total[t, i * heads : (i + 1) * heads] for t in range(GROUP)], axis=0)
        high, low = split_sum(own)
        both = dot_tn(jnp.concatenate([high, low, high], axis=0), weights)
        upstream, mean = both[:, :channels], both[:, channels:]
        normal = normal_ref[i]
        result[i] = inverse_ref[i] * (
            upstream - mean - normal * jnp.mean(upstream * normal, axis=-1, keepdims=True)
        )
        moves.append(pltpu.make_async_copy(result.at[i], out_hbm.at[i], left_for.at[2 + i]))
        moves[-1].start()
    for move in moves:
        move.wait()


def kernel_call(body, out_shape, in_specs=None, scratch=(), flops=0, moved=0, vmem_mib=12, out_specs=None, grid=()):
    vmem = pl.BlockSpec(memory_space=pltpu.VMEM)
    many = isinstance(out_shape, (list, tuple))
    return pl.pallas_call(
        body,
        grid=grid,
        out_shape=out_shape,
        in_specs=in_specs,
        out_specs=out_specs or ([vmem] * len(out_shape) if many else vmem),
        scratch_shapes=list(scratch),
        compiler_params=pltpu.CompilerParams(vmem_limit_bytes=vmem_mib * 1024 * 1024),
        cost_estimate=pl.CostEstimate(flops=flops, bytes_accessed=moved, transcendentals=0),
    )


def on_device_paired(
    alignment_rows,
    pair_state,
    update_cotangent,
    sequence_mask,
    residue_mask,
    left_weight,
    right_weight,
    outer_weight,
    bias_weight,
    query_weight,
    key_weight,
    value_weight,
    gate_weight,
    output_weight,
):
    sequence_wise, residues, channel_count = alignment_rows.shape
    rows_here, _, pair_channels = pair_state.shape
    head_count = bias_weight.shape[1]
    peers = lax.axis_size("row")
    factor = left_weight.shape[1]
    lines = peers // GROUP
    vmem = pl.BlockSpec(memory_space=pltpu.VMEM)
    smem = pl.BlockSpec(memory_space=pltpu.SMEM)
    token_rows = sequence_wise * residues
    columns_each = residues // GROUP
    block_rows = sequence_wise * 12
    flat_rows = alignment_rows.reshape(token_rows, channel_count)
    shape = jax.ShapeDtypeStruct

    pieces = [
        pl.BlockSpec((token_rows // PIECES, channel_count), lambda step, at=at: (at, 0)) for at in range(PIECES)
    ]
    send, aux, normed = kernel_call(
        factors_kernel,
        [
            shape((lines, GROUP, block_rows, LANES), bf16),
            shape((16, LANES), f32),
            shape((token_rows, channel_count), bf16),
        ],
        [smem] * 2 + [vmem] * 5 + pieces,
        [pltpu.VMEM((residues + 4 * GROUP, LANES), f32)],
        flops=2 * token_rows * channel_count * LANES,
        moved=1 << 20,
        vmem_mib=60,
        grid=(1,),
    )(
        sequence_mask,
        residue_mask,
        sequence_mask.reshape(1, -1),
        residue_mask.reshape(1, -1),
        bias_weight.T,
        left_weight.T,
        right_weight.T,
        *[flat_rows] * PIECES,
    )
    received = lax.all_to_all(
        send.reshape(peers, block_rows, LANES), "row", split_axis=0, concat_axis=0, tiled=True
    )

    group_heads = head_count // GROUP
    head_rows = group_heads * residues
    scale = (channel_count // head_count) ** (-0.5)
    normed, *weights = lax.optimization_barrier((normed, query_weight, key_weight, value_weight))
    joined = jnp.concatenate(weights, axis=1)
    joined, pair_rows = lax.optimization_barrier((joined, pair_state))
    own = lax.axis_index("row") % GROUP
    pair_blocks = [
        lax.dynamic_slice_in_dim(pair_rows, (own ^ step) * columns_each, columns_each, 1) for step in range(GROUP)
    ]
    part_shape = shape((rows_here, columns_each, pair_channels), bf16)
    gate, aux, own_block, *blocks = kernel_call(
        projections_kernel,
        [shape((GROUP, residues, LANES), f32), shape((16, LANES), f32), part_shape]
        + [shape((2 * sequence_wise, residues, LANES), bf16)] * GROUP,
        [vmem] * 7,
        [pltpu.VMEM((GROUP, 2 * sequence_wise, residues, LANES), bf16)],
        flops=10 * token_rows * channel_count * channel_count,
        moved=1 << 21,
    )(
        normed,
        update_cotangent.reshape(token_rows, channel_count),
        joined,
        gate_weight,
        output_weight,
        aux,
        pair_blocks[0],
    )

    def trade(parts):
        return parts[:1] + [
            lax.ppermute(parts[d], "row", [(i, i ^ d) for i in range(peers)]) for d in range(1, GROUP)
        ]

    pair_blocks = [own_block] + trade(pair_blocks)[1:]
    blocks = trade(blocks)
    weight_t = (
        outer_weight.reshape(factor, 4, 8, pair_channels)
        .transpose(1, 2, 0, 3)
        .reshape(4, 8 * factor, pair_channels)
    )
    share_rows = 4 * group_heads
    send_bias, *updated = kernel_call(
        pair_kernel,
        [shape((lines, GROUP, share_rows, LANES), bf16)] + [part_shape] * GROUP,
        [vmem] * (3 + GROUP),
        [
            pltpu.VMEM(((peers + 1) * block_rows, LANES), f32),
            pltpu.VMEM((4, peers * sequence_wise, 8 * LANES), bf16),
            pltpu.VMEM((peers * sequence_wise, 4 * LANES), f32),
            pltpu.VMEM((4, 8 * factor, 4 * LANES), bf16),
            pltpu.VMEM((GROUP, rows_here, columns_each, pair_channels), bf16),
            pltpu.VMEM((GROUP, rows_here, columns_each, pair_channels), bf16),
        ],
        flops=1 << 28,
        moved=1 << 20,
    )(received, weight_t, aux, *pair_blocks)
    bias_all = lax.all_to_all(
        send_bias.reshape(peers, share_rows, LANES), "row", split_axis=0, concat_axis=0, tiled=True
    )

    placed = kernel_call(
        place_kernel,
        shape((group_heads, residues + 16, LANES), f32),
        [vmem] * 2,
        [pltpu.VMEM((head_rows + 16 * group_heads, LANES), f32)],
        flops=1 << 22,
        moved=1 << 18,
    )(bias_all, aux)
    send_grad, weights, values = kernel_call(
        lambda *refs: bias_gradient_kernel(scale, *refs),
        [
            shape((peers, rows_here * group_heads, LANES), bf16),
            shape((GROUP * sequence_wise, head_rows, residues), bf16),
            shape((GROUP * sequence_wise, residues, LANES), bf16),
        ],
        [vmem] * (1 + GROUP),
        [pltpu.VMEM((head_rows + 16 * group_heads, LANES), f32)],
        flops=1 << 28,
        moved=1 << 22,
    )(*blocks, placed)
    shares = lax.all_to_all(send_grad, "row", split_axis=0, concat_axis=0, tiled=True)
    attended = kernel_call(
        attended_kernel,
        [shape((2, residues, LANES), bf16)] * GROUP,
        [vmem] * (2 + GROUP),
        flops=1 << 28,
        moved=1 << 21,
    )(weights, values, *updated)
    update, pair_updated, normal, inverse = kernel_call(
        output_kernel,
        [
            shape((token_rows, channel_count), bf16),
            shape((rows_here, residues, pair_channels), bf16),
            shape((rows_here, residues, pair_channels), f32),
            shape((rows_here, residues, pair_channels), f32),
        ],
        [vmem] * (2 + GROUP),
        flops=2 * token_rows * channel_count * channel_count,
        moved=1 << 20,
    )(gate, output_weight, *trade(list(attended)))
    update, pair_updated, pair_gradient = kernel_call(
        gradient_kernel,
        [
            shape((token_rows, channel_count), bf16),
            shape((rows_here, residues, pair_channels), bf16),
            shape((rows_here, residues, pair_channels), f32),
        ],
        [vmem] * 6,
        [pltpu.VMEM((rows_here, residues, pair_channels), f32), pltpu.SemaphoreType.DMA((2 + rows_here,))],
        flops=1 << 24,
        moved=1 << 20,
        out_specs=[pl.BlockSpec(memory_space=pltpu.HBM)] * 3,
    )(shares, aux, normal, inverse, update, pair_updated)
    return (update.reshape(alignment_rows.shape), pair_updated, pair_gradient)


def on_device(*arguments):
    rows, pair, left, bias = arguments[0], arguments[1], arguments[5], arguments[8]
    peers = lax.axis_size("row")
    fits = (
        lax.axis_size("col") == 1
        and peers == 32
        and rows.shape == (2, 128, 256)
        and pair.shape == (4, 128, 128)
        and left.shape[1] == 32
        and bias.shape[1] == 8
    )
    return (on_device_paired if fits else on_device_general)(*arguments)


def solution(mesh):
    placed = (
        P(("grp", "row"), "col", None),
        P(("grp", "row"), "col", None),
        P(("grp", "row"), "col", None),
        P("grp"),
        P("grp"),
        P(),
        P(),
        P(),
        P(),
        P(),
        P(),
        P(),
        P(),
        P(),
    )
    return jax.shard_map(
        on_device,
        mesh=mesh,
        in_specs=placed,
        out_specs=(
            P(("grp", "row"), "col", None),
            P(("grp", "row"), "col", None),
            P(("grp", "row"), "col", None),
        ),
        check_vma=False,
    )
```

```python
import jax
import jax.numpy as jnp
from jax import lax
from jax.experimental import pallas as pl
from jax.experimental.pallas import tpu as pltpu
from jax.sharding import PartitionSpec as P

norm_eps = 1e-05
mask_fill = 1000000000.0


def layer_normalize(values):
    values = values.astype(jnp.float32)
    center = values - jnp.mean(values, axis=-1, keepdims=True)
    spread = jnp.mean(center * center, axis=-1, keepdims=True)
    return center * lax.rsqrt(spread + norm_eps)


def norm_backward(values, upstream):
    values = values.astype(jnp.float32)
    center = values - jnp.mean(values, axis=-1, keepdims=True)
    inverse = lax.rsqrt(jnp.mean(center * center, axis=-1, keepdims=True) + norm_eps)
    normal_part = center * inverse
    return inverse * (
        upstream
        - jnp.mean(upstream, axis=-1, keepdims=True)
        - normal_part * jnp.mean(upstream * normal_part, axis=-1, keepdims=True)
    )


def spread_all(shard):
    copies = jnp.broadcast_to(shard[None], (lax.axis_size("row"),) + shard.shape)
    gathered = lax.all_to_all(copies, "row", split_axis=0, concat_axis=0, tiled=True)
    return gathered.reshape((-1,) + shard.shape[1:])


def attend_partial(
    projected_queries, projected_keys, projected_values, bias_all, key_mask, score_scale
):
    scores = jnp.einsum(
        "ihd,jhd->ihj", projected_queries, projected_keys, preferred_element_type=jnp.float32
    )
    scores = scores * score_scale + bias_all.astype(jnp.float32) + key_mask
    maxima = jnp.max(scores, axis=-1)
    weights = jnp.exp(scores - maxima[..., None])
    totals = jnp.sum(weights, axis=-1)
    summed = jnp.einsum(
        "ihj,jhd->ihd",
        weights.astype(jnp.bfloat16),
        projected_values,
        preferred_element_type=jnp.float32,
    )
    return (maxima, totals, summed.reshape(summed.shape[0], -1))


def on_device_general(
    alignment_rows,
    pair_state,
    update_cotangent,
    sequence_mask,
    residue_mask,
    left_weight,
    right_weight,
    outer_weight,
    bias_weight,
    query_weight,
    key_weight,
    value_weight,
    gate_weight,
    output_weight,
):
    sequence_wise, residue_half, channel_count = alignment_rows.shape
    rows_here = pair_state.shape[0]
    residues = residue_mask.shape[0]
    head_count = bias_weight.shape[1]
    head_dim = channel_count // head_count
    score_scale = head_dim ** (-0.5)
    row_index = lax.axis_index("row")
    col_index = lax.axis_index("col")
    complete_alignment, complete_cotangent = (
        lax.all_gather(alignment_rows, "col", axis=1, tiled=True),
        lax.all_gather(update_cotangent, "col", axis=1, tiled=True),
    )
    seq_live = sequence_mask.astype(jnp.float32)
    res_live = residue_mask.astype(jnp.float32)
    own_seq = lax.dynamic_slice_in_dim(seq_live, row_index * sequence_wise, sequence_wise)
    own_cols = lax.dynamic_slice_in_dim(res_live, col_index * residue_half, residue_half)
    own_rows = lax.dynamic_slice_in_dim(res_live, row_index * rows_here, rows_here)
    normalized_input = layer_normalize(complete_alignment).astype(jnp.bfloat16)
    flat_rows = normalized_input.reshape(-1, channel_count)
    normed_half = lax.dynamic_slice_in_dim(
        normalized_input, col_index * residue_half, residue_half, 1
    )
    half_rows = normed_half.reshape(-1, channel_count)
    left_proj = jnp.dot(flat_rows, left_weight, preferred_element_type=jnp.float32).reshape(
        sequence_wise, residues, -1
    )
    left_proj = (left_proj * (own_seq[:, None] * res_live[None, :])[..., None]).astype(jnp.bfloat16)
    right_proj = jnp.dot(half_rows, right_weight, preferred_element_type=jnp.float32).reshape(
        sequence_wise, residue_half, -1
    )
    right_proj = (right_proj * (own_seq[:, None] * own_cols[None, :])[..., None]).astype(
        jnp.bfloat16
    )
    left_tile = lax.all_to_all(left_proj, "row", split_axis=1, concat_axis=0, tiled=True)
    right_all = spread_all(right_proj)
    outer_width = left_tile.shape[2]
    outer_sum = lax.dot_general(
        left_tile.reshape(left_tile.shape[0], -1),
        right_all.reshape(right_all.shape[0], -1),
        (((0,), (0,)), ((), ())),
        preferred_element_type=jnp.float32,
    )
    outer_half = outer_sum.astype(jnp.bfloat16).reshape(
        rows_here, outer_width, residue_half, outer_width
    )
    opm_update = jnp.einsum(
        "ipjq,pqz->ijz", outer_half, outer_weight, preferred_element_type=jnp.float32
    )
    divisor = jnp.maximum(jnp.sum(seq_live) * own_rows[:, None] * own_cols[None, :], 1.0)
    pair_updated = (pair_state.astype(jnp.float32) + opm_update / divisor[..., None]).astype(
        jnp.bfloat16
    )
    pair_normed = layer_normalize(pair_updated).astype(jnp.bfloat16)
    bias_tile = jnp.einsum(
        "ijz,zh->ihj", pair_normed, bias_weight, preferred_element_type=jnp.float32
    ).astype(jnp.bfloat16)
    projected_queries = (
        jnp.dot(flat_rows, query_weight, preferred_element_type=jnp.float32)
        .astype(jnp.bfloat16)
        .reshape(sequence_wise, residues, head_count, head_dim)
    )
    gate_activations = jax.nn.sigmoid(
        jnp.dot(flat_rows, gate_weight, preferred_element_type=jnp.float32)
    ).reshape(sequence_wise, residues, channel_count)
    key_live = (res_live - 1.0) * mask_fill
    half_live = lax.dynamic_slice_in_dim(key_live, col_index * residue_half, residue_half)
    bias_cols = lax.all_gather(bias_tile, "col", axis=2, tiled=True)
    bias_all = spread_all(bias_cols)
    key_count = bias_all.shape[2]
    projected_keys = (
        jnp.dot(flat_rows, key_weight, preferred_element_type=jnp.float32)
        .astype(jnp.bfloat16)
        .reshape(sequence_wise, key_count, head_count, head_dim)
    )
    projected_values = (
        jnp.dot(flat_rows, value_weight, preferred_element_type=jnp.float32)
        .astype(jnp.bfloat16)
        .reshape(sequence_wise, key_count, head_count, head_dim)
    )
    maxima, totals, summed = lax.map(
        lambda inputs: attend_partial(
            inputs[0], inputs[1], inputs[2], bias_all, key_live, score_scale
        ),
        (projected_queries, projected_keys, projected_values),
    )
    attended = summed / jnp.repeat(totals, head_dim, axis=-1)
    gated = gate_activations * attended
    gated_own = lax.dynamic_slice_in_dim(gated, col_index * residue_half, residue_half, 1).astype(
        jnp.bfloat16
    )
    alignment_update = (
        jnp.dot(
            gated_own.reshape(-1, channel_count), output_weight, preferred_element_type=jnp.float32
        )
        .astype(jnp.bfloat16)
        .reshape(sequence_wise, residue_half, channel_count)
    )
    d_gated = lax.dot_general(
        complete_cotangent.reshape(-1, channel_count),
        output_weight,
        (((1,), (1,)), ((), ())),
        preferred_element_type=jnp.float32,
    ).reshape(sequence_wise, residues, channel_count)
    d_attended = d_gated * gate_activations
    delta_sum = jnp.sum(
        (d_attended * attended).reshape(sequence_wise, residues, head_count, head_dim), axis=-1
    )
    d_rounded = d_attended.astype(jnp.bfloat16).reshape(
        sequence_wise, residues, head_count, head_dim
    )
    log_total = maxima + jnp.log(totals)
    keys_half = lax.dynamic_slice_in_dim(projected_keys, col_index * residue_half, residue_half, 1)
    values_half = lax.dynamic_slice_in_dim(
        projected_values, col_index * residue_half, residue_half, 1
    )
    bias_half = lax.dynamic_slice_in_dim(bias_all, col_index * residue_half, residue_half, 2)
    bias_rows = bias_half.astype(jnp.float32)

    def single_sequence(running, sequence_items):
        query_rows, d_rows, total_rows, delta_rows, keys_one, values_one = sequence_items
        scores = jnp.einsum(
            "ihd,jhd->ihj", query_rows, keys_one, preferred_element_type=jnp.float32
        )
        scores = scores * score_scale + bias_rows + half_live
        probs = jnp.exp(scores - total_rows[..., None])
        d_weights = jnp.einsum(
            "ihd,jhd->ihj", d_rows, values_one, preferred_element_type=jnp.float32
        )
        return (running + probs * (d_weights - delta_rows[..., None]), None)

    sequence_items = (projected_queries, d_rounded, log_total, delta_sum, keys_half, values_half)
    initial_value = jnp.zeros(
        (rows_here * lax.axis_size("row"), head_count, residue_half), jnp.float32
    )
    result, unused = lax.scan(single_sequence, initial_value, sequence_items)
    shares = lax.all_to_all(
        result.astype(jnp.bfloat16).reshape((-1,) + (rows_here,) + result.shape[1:]),
        "row",
        split_axis=0,
        concat_axis=0,
        tiled=True,
    )
    bias_gradient = jnp.sum(shares.astype(jnp.float32), axis=0)
    d_normed = jnp.einsum(
        "ihj,zh->ijz",
        bias_gradient,
        bias_weight.astype(jnp.float32),
        precision=lax.Precision.HIGHEST,
    )
    pair_gradient = norm_backward(pair_updated, d_normed)
    return (alignment_update, pair_updated, pair_gradient)


LANES = 128
GROUP = 4
PIECES = 4
f32 = jnp.float32
bf16 = jnp.bfloat16


def dot_nn(a, b):
    return lax.dot_general(a, b, (((1,), (0,)), ((), ())), preferred_element_type=f32)


def dot_nt(a, b):
    return lax.dot_general(a, b, (((1,), (1,)), ((), ())), preferred_element_type=f32)


def dot_tn(a, b):
    return lax.dot_general(a, b, (((0,), (0,)), ((), ())), preferred_element_type=f32)


def lane_index(rows):
    return lax.broadcasted_iota(jnp.int32, (rows, LANES), 1)


def swap_groups(parts):
    lane = lane_index(parts[0].shape[0])
    low, even = lane < 64, lane % 64 < 32
    parts = [
        jnp.where(low, parts[0], pltpu.roll(parts[2], 64, 1)),
        jnp.where(low, parts[1], pltpu.roll(parts[3], 64, 1)),
        jnp.where(low, pltpu.roll(parts[0], 64, 1), parts[2]),
        jnp.where(low, pltpu.roll(parts[1], 64, 1), parts[3]),
    ]
    return [
        jnp.where(even, parts[0], pltpu.roll(parts[1], 32, 1)),
        jnp.where(even, pltpu.roll(parts[0], 96, 1), parts[1]),
        jnp.where(even, parts[2], pltpu.roll(parts[3], 32, 1)),
        jnp.where(even, pltpu.roll(parts[2], 96, 1), parts[3]),
    ]


def factors_kernel(
    seq_smem_ref, res_smem_ref, seq_ref, res_ref, bias_w_ref, left_ref, right_ref, *refs
):
    row_refs, (send_ref, aux_ref, normed_ref, left_scr) = refs[:PIECES], refs[PIECES:]
    lines = send_ref.shape[0]
    seqs = send_ref.shape[2] // 12
    residues = res_ref.shape[1]
    me = lax.axis_index("row")
    normed = jnp.concatenate([layer_normalize(rows[...]).astype(bf16) for rows in row_refs], axis=0)
    normed_ref[...] = normed
    live = res_ref[...].astype(f32)
    live_rows = jnp.broadcast_to(live, (residues, residues)).T
    right_t = right_ref[...]
    left_wide = jnp.concatenate([left_ref[...]] * 4, axis=0)
    lane_group = lane_index(lines) // 32
    quarters = []
    tail = []
    for s in range(seqs):
        seq_live = seq_smem_ref[me * seqs + s].astype(f32)
        own = normed[s * residues : (s + 1) * residues]
        factor = dot_nt(right_t, own) * (live * seq_live)
        quarters.append(swap_groups([factor[a * 8 : (a + 1) * 8] for a in range(4)]))
        left_scr[:residues] = dot_nt(own, left_wide) * (live_rows * seq_live)
        for a in range(4):
            row = jnp.zeros((lines, LANES), f32)
            for b in range(4):
                part = left_scr[pl.ds(4 * a + b, lines, stride=4 * GROUP), :]
                row = jnp.where(lane_group == b, part, row)
            tail.append(row)
    tail = jnp.stack(tail, axis=1).astype(bf16)
    right_rows = 8 * seqs
    for t in range(GROUP):
        block = jnp.concatenate([own[t] for own in quarters], axis=0).astype(bf16)
        send_ref[:, t, :right_rows, :] = jnp.broadcast_to(block[None], (lines, right_rows, LANES))
        send_ref[:, t, right_rows:, :] = tail
    aux_ref[0:4] = tile_inverse(res_smem_ref, res_ref, seq_ref)
    aux_ref[4:8] = jnp.broadcast_to((live - 1.0) * mask_fill, (4, LANES))
    aux_ref[8:16] = bias_w_ref[...].astype(f32)


def side_by_side(first, second, at):
    low = lane_index(first.shape[0]) < 64
    span = slice(at // 2 * LANES, at // 2 * LANES + LANES)
    first, second = first[:, span], second[:, span]
    if at % 2 == 0:
        return jnp.where(low, first, pltpu.roll(second, 64, 1))
    return jnp.where(low, pltpu.roll(first, 64, 1), second)


def partner(step):
    return lax.bitwise_xor(lax.rem(lax.axis_index("row"), GROUP), step)


def tile_inverse(res_smem_ref, res_ref, seq_ref):
    own = partner(0)
    rows = lax.div(lax.axis_index("row"), GROUP) * 16
    lane = lane_index(1)
    live = res_ref[...].astype(f32)
    columns = jnp.zeros((1, LANES), f32)
    for t in range(GROUP):
        turned = live if t == 0 else pltpu.roll(live, LANES - 32 * t, 1)
        columns = jnp.where(own == t, turned, columns)
    columns = jnp.where(lane < 32, columns, 0.0)
    columns = columns + pltpu.roll(columns, 32, 1)
    columns = columns + pltpu.roll(columns, 64, 1)
    total = jnp.sum(seq_ref[...].astype(f32), axis=-1, keepdims=True)
    lines = []
    for b in range(4):
        line = jnp.zeros((1, LANES), f32)
        for a in range(4):
            line = jnp.where(lane // 32 == a, res_smem_ref[rows + 4 * a + b].astype(f32), line)
        lines.append(1.0 / jnp.maximum(total * line * columns, 1.0))
    return jnp.concatenate(lines, axis=0)


def projections_kernel(
    normed_ref, cot_ref, weights_ref, wg_ref, wo_ref, aux_ref, pair_ref, gate_ref, aux_out_ref, pair_out_ref, *rest
):
    block_refs, every = rest[:GROUP], rest[GROUP]
    aux_out_ref[...] = aux_ref[...]
    pair_out_ref[...] = pair_ref[...]
    normed = normed_ref[...]
    tokens = normed.shape[0]
    residues = gate_ref.shape[1]
    seqs = tokens // residues
    channels = normed.shape[1]
    queries, keys, values = [
        dot_nn(normed, weights_ref[:, at * channels : (at + 1) * channels]) for at in range(3)
    ]
    gate = jax.nn.sigmoid(dot_nn(normed, wg_ref[...]))
    d_attended = dot_nt(cot_ref[...], wo_ref[...]) * gate
    for t in range(GROUP):
        rows = side_by_side(queries, d_attended, t).astype(bf16)
        columns = side_by_side(keys, values, t).astype(bf16)
        gate_ref[t] = side_by_side(gate[:residues], gate[residues:], t)
        for s in range(seqs):
            every[t, s] = rows[s * residues : (s + 1) * residues]
            every[t, seqs + s] = columns[s * residues : (s + 1) * residues]
    for step in range(GROUP):
        block_refs[step][...] = every[partner(step)]


def pair_kernel(recv_ref, weight_ref, aux_ref, *refs):
    pair_refs, send_ref, updated_refs = refs[:GROUP], refs[GROUP], refs[GROUP + 1 : 2 * GROUP + 1]
    flat, rbuf, lbuf, obuf, state, after = refs[2 * GROUP + 1 :]
    peers, block_rows, _ = recv_ref.shape
    seqs = block_rows // 12
    for step in range(GROUP):
        state[partner(step)] = pair_refs[step][...]
    before = [
        jnp.concatenate([state[a, b] for a in range(GROUP)], axis=0).astype(f32).T for b in range(4)
    ]
    flat[: peers * block_rows] = recv_ref[...].astype(f32).reshape(peers * block_rows, LANES)
    for s in range(seqs):
        for g in range(8):
            part = flat[pl.ds(s * 8 + g, peers, stride=block_rows), :]
            for a in range(4):
                turned = part if a == 0 else pltpu.roll(part, 32 * a, 1)
                rbuf[a, s * peers : (s + 1) * peers, g * LANES : (g + 1) * LANES] = turned.astype(bf16)
        for a in range(4):
            part = flat[pl.ds(8 * seqs + 4 * s + a, peers, stride=block_rows), :]
            lbuf[s * peers : (s + 1) * peers, a * LANES : (a + 1) * LANES] = part
    left_t = lbuf[...].T.astype(bf16)
    outer = [dot_nn(left_t[a * LANES : (a + 1) * LANES], rbuf[a]).astype(bf16) for a in range(4)]
    lane_group = lane_index(LANES) // 32
    sums = None
    for q in range(4):
        for g in range(8):
            span = slice(g * LANES, (g + 1) * LANES)
            picked = outer[3][:, span]
            for a in range(3):
                picked = jnp.where(lane_group == (q + a) % 4, outer[a][:, span], picked)
            for b in range(4):
                obuf[q, g * 32 : (g + 1) * 32, b * LANES : (b + 1) * LANES] = picked[b * 32 : (b + 1) * 32]
        part = dot_tn(weight_ref[q], obuf[q])
        if q:
            part = jnp.concatenate(
                [pltpu.roll(part[:, b * LANES : (b + 1) * LANES], LANES - 32 * q, 1) for b in range(4)], axis=1
            )
        sums = part if sums is None else sums + part
    bias_w = aux_ref[8:16].astype(bf16)
    blocks = []
    for b in range(4):
        update = sums[:, b * LANES : (b + 1) * LANES] * aux_ref[b : b + 1, :]
        updated = (before[b] + update).astype(bf16)
        values = updated.astype(f32)
        center = values - jnp.mean(values, axis=0, keepdims=True)
        spread = jnp.mean(center * center, axis=0, keepdims=True)
        line = dot_nn(bias_w, (center * lax.rsqrt(spread + norm_eps)).astype(bf16))
        blocks.append(pltpu.roll(line, partner(0) * 32, 1))
        values = values.T.astype(bf16)
        for a in range(GROUP):
            after[a, b] = values[a * 32 : (a + 1) * 32]
    lines, _, share, _ = send_ref.shape
    heads = share // 4
    for t in range(GROUP):
        block = jnp.concatenate([rows[t * heads : (t + 1) * heads] for rows in blocks], axis=0).astype(bf16)
        send_ref[:, t] = jnp.broadcast_to(block[None], (lines, share, LANES))
    for step in range(GROUP):
        updated_refs[step][...] = after[partner(step)]


def place_bias(flat, heads, h, bias):
    lines = bias.shape[0] // 16 - 1
    lane_group = lane_index(lines) // 32
    for b in range(4):
        rows = [flat[pl.ds((4 * t + b) * heads + h, lines, stride=16 * heads), :] for t in range(GROUP)]
        for a in range(4):
            picked = rows[3]
            for t in range(3):
                picked = jnp.where(lane_group == (a + t) % 4, rows[t], picked)
            if a:
                picked = pltpu.roll(picked, LANES - 32 * a, 1)
            bias[pl.ds(4 * a + b, lines, stride=16), :] = picked


def place_kernel(bias_ref, mask_ref, placed, flat):
    heads = placed.shape[0]
    rows = bias_ref.shape[0] * bias_ref.shape[1]
    flat[:rows] = bias_ref[...].reshape(rows, LANES).astype(f32)
    for h in range(heads):
        place_bias(flat, heads, h, placed.at[h])
    placed[0, placed.shape[1] - 16 : placed.shape[1] - 12] = mask_ref[4:8]


def bias_gradient_kernel(scale, *refs):
    block_refs, (placed, send_ref, weights_ref, value_ref, grads) = refs[:GROUP], refs[GROUP:]
    sequences, rows, residues = weights_ref.shape
    heads = rows // residues
    seqs = sequences // GROUP
    ones = jnp.ones((residues, LANES), bf16)
    part_of = lane_index(residues) // 32
    key_mask = placed[0, residues : residues + 1]
    totals = [jnp.zeros((residues, residues), f32) for _ in range(heads)]
    for step, block in enumerate(block_refs):
        for s in range(seqs):
            at = step * seqs + s
            columns = block[seqs + s]
            value_ref[at] = jnp.where(part_of < heads, jnp.ones((), bf16), columns)
            wide = jnp.concatenate(
                [jnp.where(part_of == g, block[s], jnp.zeros((), bf16)) for g in range(2 * heads)], axis=0
            )
            both = dot_nt(wide, columns)
            for h in range(heads):
                own = slice(h * residues, (h + 1) * residues)
                scores = both[own] * scale + placed[h, :residues] + key_mask
                weights = jnp.exp(scores - jnp.max(scores, axis=-1, keepdims=True))
                rounded = weights.astype(bf16)
                weights_ref[at, own, :] = rounded
                flow = both[(heads + h) * residues : (heads + h + 1) * residues]
                inverse = 1.0 / dot_nn(rounded, ones)
                delta = dot_nn((weights * flow).astype(bf16), ones) * inverse
                totals[h] = totals[h] + weights * inverse * (flow - delta)
    for h in range(heads):
        grads[pl.ds(h, residues, stride=heads), :] = totals[h]
    send_ref[...] = grads[:rows].astype(bf16).reshape(send_ref.shape)


def attended_kernel(weights_ref, value_ref, *refs):
    part_refs, out_refs = refs[:GROUP], refs[GROUP:]
    sequences, _, residues = weights_ref.shape
    seqs = sequences // GROUP
    lane = lane_index(residues)
    for step in range(GROUP):
        attended = []
        for s in range(seqs):
            mixed = dot_nn(weights_ref[step * seqs + s], value_ref[step * seqs + s])
            picked = jnp.where(lane < 96, mixed[:residues], mixed[residues:])
            totals = jnp.where(lane < 32, mixed[:residues], mixed[residues:])
            attended.append(picked / pltpu.roll(totals, 64, 1))
        out_refs[step][0] = jnp.where(lane < 64, pltpu.roll(attended[0], 64, 1), attended[1]).astype(bf16)
        out_refs[step][1] = part_refs[step][...].reshape(residues, LANES)


def output_kernel(aux_ref, gate_ref, wo_ref, *refs):
    in_refs, (out_ref, pair_ref, normal_ref, inverse_ref, both_ref) = refs[:GROUP], refs[GROUP:]
    bias_w = aux_ref[8:16]
    mean_high, mean_low = split_sum(
        jnp.broadcast_to(jnp.mean(bias_w, axis=-1, keepdims=True), bias_w.shape)
    )
    exact = bias_w.astype(bf16)
    none = jnp.zeros(exact.shape, bf16)
    both_ref[...] = jnp.concatenate(
        [
            jnp.concatenate([exact, mean_high], axis=1),
            jnp.concatenate([exact, mean_high], axis=1),
            jnp.concatenate([none, mean_low], axis=1),
        ],
        axis=0,
    )
    residues = gate_ref.shape[1]
    rows = pair_ref.shape[0]
    columns_each = residues // GROUP
    low = lane_index(residues) < 64
    zero = jnp.zeros((), bf16)
    sums = [jnp.zeros((residues, out_ref.shape[1]), f32) for _ in range(2)]
    for step in range(GROUP):
        at = partner(step)
        gated = (gate_ref[at] * in_refs[step][0].astype(f32)).astype(bf16)
        weight = wo_ref[pl.ds(pl.multiple_of(at * 64, 64), 64), :]
        weight = jnp.concatenate([weight, weight], axis=0)
        sums[0] = sums[0] + dot_nn(jnp.where(low, gated, zero), weight)
        sums[1] = sums[1] + dot_nn(jnp.where(low, zero, gated), weight)
        columns = pl.ds(pl.multiple_of(at * columns_each, columns_each), columns_each)
        pair_ref[:, columns, :] = in_refs[step][1].reshape(rows, columns_each, LANES)
        values = in_refs[step][1].astype(f32)
        center = values - jnp.mean(values, axis=-1, keepdims=True)
        inverse = lax.rsqrt(jnp.mean(center * center, axis=-1, keepdims=True) + norm_eps)
        normal_ref[:, columns, :] = (center * inverse).reshape(rows, columns_each, LANES)
        inverse_ref[:, columns, :] = jnp.broadcast_to(inverse, values.shape).reshape(rows, columns_each, LANES)
    for s in range(2):
        out_ref[s * residues : (s + 1) * residues, :] = sums[s].astype(bf16)


def split_sum(values):
    high = values.astype(bf16)
    return high, (values - high.astype(f32)).astype(bf16)


def gradient_kernel(
    shares_ref, both_ref, normal_ref, inverse_ref, update_ref, pair_ref, update_hbm, pair_hbm, out_hbm, result, left_for
):
    moves = [
        pltpu.make_async_copy(update_ref, update_hbm, left_for.at[0]),
        pltpu.make_async_copy(pair_ref, pair_hbm, left_for.at[1]),
    ]
    for move in moves:
        move.start()
    peers, share, _ = shares_ref.shape
    rows, _, channels = normal_ref.shape
    heads = share // rows
    total = jnp.sum(shares_ref[...].astype(f32).reshape(peers // GROUP, GROUP, share, LANES), axis=0)
    weights = both_ref[...]
    for i in range(rows):
        own = jnp.concatenate([total[t, i * heads : (i + 1) * heads] for t in range(GROUP)], axis=0)
        high, low = split_sum(own)
        both = dot_tn(jnp.concatenate([high, low, high], axis=0), weights)
        upstream, mean = both[:, :channels], both[:, channels:]
        normal = normal_ref[i]
        result[i] = inverse_ref[i] * (
            upstream - mean - normal * jnp.mean(upstream * normal, axis=-1, keepdims=True)
        )
        moves.append(pltpu.make_async_copy(result.at[i], out_hbm.at[i], left_for.at[2 + i]))
        moves[-1].start()
    for move in moves:
        move.wait()


def kernel_call(body, out_shape, in_specs=None, scratch=(), flops=0, moved=0, vmem_mib=12, out_specs=None, grid=()):
    vmem = pl.BlockSpec(memory_space=pltpu.VMEM)
    many = isinstance(out_shape, (list, tuple))
    return pl.pallas_call(
        body,
        grid=grid,
        out_shape=out_shape,
        in_specs=in_specs,
        out_specs=out_specs or ([vmem] * len(out_shape) if many else vmem),
        scratch_shapes=list(scratch),
        compiler_params=pltpu.CompilerParams(vmem_limit_bytes=vmem_mib * 1024 * 1024),
        cost_estimate=pl.CostEstimate(flops=flops, bytes_accessed=moved, transcendentals=0),
    )


def on_device_paired(
    alignment_rows,
    pair_state,
    update_cotangent,
    sequence_mask,
    residue_mask,
    left_weight,
    right_weight,
    outer_weight,
    bias_weight,
    query_weight,
    key_weight,
    value_weight,
    gate_weight,
    output_weight,
):
    sequence_wise, residues, channel_count = alignment_rows.shape
    rows_here, _, pair_channels = pair_state.shape
    head_count = bias_weight.shape[1]
    peers = lax.axis_size("row")
    factor = left_weight.shape[1]
    lines = peers // GROUP
    vmem = pl.BlockSpec(memory_space=pltpu.VMEM)
    smem = pl.BlockSpec(memory_space=pltpu.SMEM)
    token_rows = sequence_wise * residues
    columns_each = residues // GROUP
    block_rows = sequence_wise * 12
    flat_rows = alignment_rows.reshape(token_rows, channel_count)
    shape = jax.ShapeDtypeStruct

    pieces = [
        pl.BlockSpec((token_rows // PIECES, channel_count), lambda step, at=at: (at, 0)) for at in range(PIECES)
    ]
    send, aux, normed = kernel_call(
        factors_kernel,
        [
            shape((lines, GROUP, block_rows, LANES), bf16),
            shape((16, LANES), f32),
            shape((token_rows, channel_count), bf16),
        ],
        [smem] * 2 + [vmem] * 5 + pieces,
        [pltpu.VMEM((residues + 4 * GROUP, LANES), f32)],
        flops=2 * token_rows * channel_count * LANES,
        moved=1 << 20,
        vmem_mib=60,
        grid=(1,),
    )(
        sequence_mask,
        residue_mask,
        sequence_mask.reshape(1, -1),
        residue_mask.reshape(1, -1),
        bias_weight.T,
        left_weight.T,
        right_weight.T,
        *[flat_rows] * PIECES,
    )
    received = lax.all_to_all(
        send.reshape(peers, block_rows, LANES), "row", split_axis=0, concat_axis=0, tiled=True
    )

    group_heads = head_count // GROUP
    head_rows = group_heads * residues
    scale = (channel_count // head_count) ** (-0.5)
    normed, *weights = lax.optimization_barrier((normed, query_weight, key_weight, value_weight))
    joined = jnp.concatenate(weights, axis=1)
    joined, pair_rows = lax.optimization_barrier((joined, pair_state))
    own = lax.axis_index("row") % GROUP
    pair_blocks = [
        lax.dynamic_slice_in_dim(pair_rows, (own ^ step) * columns_each, columns_each, 1) for step in range(GROUP)
    ]
    part_shape = shape((rows_here, columns_each, pair_channels), bf16)
    gate, aux, own_block, *blocks = kernel_call(
        projections_kernel,
        [shape((GROUP, residues, LANES), f32), shape((16, LANES), f32), part_shape]
        + [shape((2 * sequence_wise, residues, LANES), bf16)] * GROUP,
        [vmem] * 7,
        [pltpu.VMEM((GROUP, 2 * sequence_wise, residues, LANES), bf16)],
        flops=10 * token_rows * channel_count * channel_count,
        moved=1 << 21,
    )(
        normed,
        update_cotangent.reshape(token_rows, channel_count),
        joined,
        gate_weight,
        output_weight,
        aux,
        pair_blocks[0],
    )

    def trade(parts):
        return parts[:1] + [
            lax.ppermute(parts[d], "row", [(i, i ^ d) for i in range(peers)]) for d in range(1, GROUP)
        ]

    pair_blocks = [own_block] + trade(pair_blocks)[1:]
    blocks = trade(blocks)
    weight_t = (
        outer_weight.reshape(factor, 4, 8, pair_channels)
        .transpose(1, 2, 0, 3)
        .reshape(4, 8 * factor, pair_channels)
    )
    share_rows = 4 * group_heads
    send_bias, *updated = kernel_call(
        pair_kernel,
        [shape((lines, GROUP, share_rows, LANES), bf16)] + [part_shape] * GROUP,
        [vmem] * (3 + GROUP),
        [
            pltpu.VMEM(((peers + 1) * block_rows, LANES), f32),
            pltpu.VMEM((4, peers * sequence_wise, 8 * LANES), bf16),
            pltpu.VMEM((peers * sequence_wise, 4 * LANES), f32),
            pltpu.VMEM((4, 8 * factor, 4 * LANES), bf16),
            pltpu.VMEM((GROUP, rows_here, columns_each, pair_channels), bf16),
            pltpu.VMEM((GROUP, rows_here, columns_each, pair_channels), bf16),
        ],
        flops=1 << 28,
        moved=1 << 20,
    )(received, weight_t, aux, *pair_blocks)
    bias_all = lax.all_to_all(
        send_bias.reshape(peers, share_rows, LANES), "row", split_axis=0, concat_axis=0, tiled=True
    )

    placed = kernel_call(
        place_kernel,
        shape((group_heads, residues + 16, LANES), f32),
        [vmem] * 2,
        [pltpu.VMEM((head_rows + 16 * group_heads, LANES), f32)],
        flops=1 << 22,
        moved=1 << 18,
    )(bias_all, aux)
    send_grad, weights, values = kernel_call(
        lambda *refs: bias_gradient_kernel(scale, *refs),
        [
            shape((peers, rows_here * group_heads, LANES), bf16),
            shape((GROUP * sequence_wise, head_rows, residues), bf16),
            shape((GROUP * sequence_wise, residues, LANES), bf16),
        ],
        [vmem] * (1 + GROUP),
        [pltpu.VMEM((head_rows + 16 * group_heads, LANES), f32)],
        flops=1 << 28,
        moved=1 << 22,
    )(*blocks, placed)
    shares = lax.all_to_all(send_grad, "row", split_axis=0, concat_axis=0, tiled=True)
    attended = kernel_call(
        attended_kernel,
        [shape((2, residues, LANES), bf16)] * GROUP,
        [vmem] * (2 + GROUP),
        flops=1 << 28,
        moved=1 << 21,
    )(weights, values, *updated)
    update, pair_updated, normal, inverse, both = kernel_call(
        output_kernel,
        [
            shape((token_rows, channel_count), bf16),
            shape((rows_here, residues, pair_channels), bf16),
            shape((rows_here, residues, pair_channels), f32),
            shape((rows_here, residues, pair_channels), f32),
            shape((3 * head_count, 2 * pair_channels), bf16),
        ],
        [vmem] * (3 + GROUP),
        flops=2 * token_rows * channel_count * channel_count,
        moved=1 << 20,
    )(aux, gate, output_weight, *trade(list(attended)))
    update, pair_updated, pair_gradient = kernel_call(
        gradient_kernel,
        [
            shape((token_rows, channel_count), bf16),
            shape((rows_here, residues, pair_channels), bf16),
            shape((rows_here, residues, pair_channels), f32),
        ],
        [vmem] * 6,
        [pltpu.VMEM((rows_here, residues, pair_channels), f32), pltpu.SemaphoreType.DMA((2 + rows_here,))],
        flops=1 << 24,
        moved=1 << 20,
        out_specs=[pl.BlockSpec(memory_space=pltpu.HBM)] * 3,
    )(shares, both, normal, inverse, update, pair_updated)
    return (update.reshape(alignment_rows.shape), pair_updated, pair_gradient)


def on_device(*arguments):
    rows, pair, left, bias = arguments[0], arguments[1], arguments[5], arguments[8]
    peers = lax.axis_size("row")
    fits = (
        lax.axis_size("col") == 1
        and peers == 32
        and rows.shape == (2, 128, 256)
        and pair.shape == (4, 128, 128)
        and left.shape[1] == 32
        and bias.shape[1] == 8
    )
    return (on_device_paired if fits else on_device_general)(*arguments)


def solution(mesh):
    placed = (
        P(("grp", "row"), "col", None),
        P(("grp", "row"), "col", None),
        P(("grp", "row"), "col", None),
        P("grp"),
        P("grp"),
        P(),
        P(),
        P(),
        P(),
        P(),
        P(),
        P(),
        P(),
        P(),
    )
    return jax.shard_map(
        on_device,
        mesh=mesh,
        in_specs=placed,
        out_specs=(
            P(("grp", "row"), "col", None),
            P(("grp", "row"), "col", None),
            P(("grp", "row"), "col", None),
        ),
        check_vma=False,
    )
```

```python
import jax
import jax.numpy as jnp
from jax import lax
from jax.experimental import pallas as pl
from jax.experimental.pallas import tpu as pltpu
from jax.sharding import PartitionSpec as P

norm_eps = 1e-05
mask_fill = 1000000000.0


def layer_normalize(values):
    values = values.astype(jnp.float32)
    center = values - jnp.mean(values, axis=-1, keepdims=True)
    spread = jnp.mean(center * center, axis=-1, keepdims=True)
    return center * lax.rsqrt(spread + norm_eps)


def norm_backward(values, upstream):
    values = values.astype(jnp.float32)
    center = values - jnp.mean(values, axis=-1, keepdims=True)
    inverse = lax.rsqrt(jnp.mean(center * center, axis=-1, keepdims=True) + norm_eps)
    normal_part = center * inverse
    return inverse * (
        upstream
        - jnp.mean(upstream, axis=-1, keepdims=True)
        - normal_part * jnp.mean(upstream * normal_part, axis=-1, keepdims=True)
    )


def spread_all(shard):
    copies = jnp.broadcast_to(shard[None], (lax.axis_size("row"),) + shard.shape)
    gathered = lax.all_to_all(copies, "row", split_axis=0, concat_axis=0, tiled=True)
    return gathered.reshape((-1,) + shard.shape[1:])


def attend_partial(
    projected_queries, projected_keys, projected_values, bias_all, key_mask, score_scale
):
    scores = jnp.einsum(
        "ihd,jhd->ihj", projected_queries, projected_keys, preferred_element_type=jnp.float32
    )
    scores = scores * score_scale + bias_all.astype(jnp.float32) + key_mask
    maxima = jnp.max(scores, axis=-1)
    weights = jnp.exp(scores - maxima[..., None])
    totals = jnp.sum(weights, axis=-1)
    summed = jnp.einsum(
        "ihj,jhd->ihd",
        weights.astype(jnp.bfloat16),
        projected_values,
        preferred_element_type=jnp.float32,
    )
    return (maxima, totals, summed.reshape(summed.shape[0], -1))


def on_device_general(
    alignment_rows,
    pair_state,
    update_cotangent,
    sequence_mask,
    residue_mask,
    left_weight,
    right_weight,
    outer_weight,
    bias_weight,
    query_weight,
    key_weight,
    value_weight,
    gate_weight,
    output_weight,
):
    sequence_wise, residue_half, channel_count = alignment_rows.shape
    rows_here = pair_state.shape[0]
    residues = residue_mask.shape[0]
    head_count = bias_weight.shape[1]
    head_dim = channel_count // head_count
    score_scale = head_dim ** (-0.5)
    row_index = lax.axis_index("row")
    col_index = lax.axis_index("col")
    complete_alignment, complete_cotangent = (
        lax.all_gather(alignment_rows, "col", axis=1, tiled=True),
        lax.all_gather(update_cotangent, "col", axis=1, tiled=True),
    )
    seq_live = sequence_mask.astype(jnp.float32)
    res_live = residue_mask.astype(jnp.float32)
    own_seq = lax.dynamic_slice_in_dim(seq_live, row_index * sequence_wise, sequence_wise)
    own_cols = lax.dynamic_slice_in_dim(res_live, col_index * residue_half, residue_half)
    own_rows = lax.dynamic_slice_in_dim(res_live, row_index * rows_here, rows_here)
    normalized_input = layer_normalize(complete_alignment).astype(jnp.bfloat16)
    flat_rows = normalized_input.reshape(-1, channel_count)
    normed_half = lax.dynamic_slice_in_dim(
        normalized_input, col_index * residue_half, residue_half, 1
    )
    half_rows = normed_half.reshape(-1, channel_count)
    left_proj = jnp.dot(flat_rows, left_weight, preferred_element_type=jnp.float32).reshape(
        sequence_wise, residues, -1
    )
    left_proj = (left_proj * (own_seq[:, None] * res_live[None, :])[..., None]).astype(jnp.bfloat16)
    right_proj = jnp.dot(half_rows, right_weight, preferred_element_type=jnp.float32).reshape(
        sequence_wise, residue_half, -1
    )
    right_proj = (right_proj * (own_seq[:, None] * own_cols[None, :])[..., None]).astype(
        jnp.bfloat16
    )
    left_tile = lax.all_to_all(left_proj, "row", split_axis=1, concat_axis=0, tiled=True)
    right_all = spread_all(right_proj)
    outer_width = left_tile.shape[2]
    outer_sum = lax.dot_general(
        left_tile.reshape(left_tile.shape[0], -1),
        right_all.reshape(right_all.shape[0], -1),
        (((0,), (0,)), ((), ())),
        preferred_element_type=jnp.float32,
    )
    outer_half = outer_sum.astype(jnp.bfloat16).reshape(
        rows_here, outer_width, residue_half, outer_width
    )
    opm_update = jnp.einsum(
        "ipjq,pqz->ijz", outer_half, outer_weight, preferred_element_type=jnp.float32
    )
    divisor = jnp.maximum(jnp.sum(seq_live) * own_rows[:, None] * own_cols[None, :], 1.0)
    pair_updated = (pair_state.astype(jnp.float32) + opm_update / divisor[..., None]).astype(
        jnp.bfloat16
    )
    pair_normed = layer_normalize(pair_updated).astype(jnp.bfloat16)
    bias_tile = jnp.einsum(
        "ijz,zh->ihj", pair_normed, bias_weight, preferred_element_type=jnp.float32
    ).astype(jnp.bfloat16)
    projected_queries = (
        jnp.dot(flat_rows, query_weight, preferred_element_type=jnp.float32)
        .astype(jnp.bfloat16)
        .reshape(sequence_wise, residues, head_count, head_dim)
    )
    gate_activations = jax.nn.sigmoid(
        jnp.dot(flat_rows, gate_weight, preferred_element_type=jnp.float32)
    ).reshape(sequence_wise, residues, channel_count)
    key_live = (res_live - 1.0) * mask_fill
    half_live = lax.dynamic_slice_in_dim(key_live, col_index * residue_half, residue_half)
    bias_cols = lax.all_gather(bias_tile, "col", axis=2, tiled=True)
    bias_all = spread_all(bias_cols)
    key_count = bias_all.shape[2]
    projected_keys = (
        jnp.dot(flat_rows, key_weight, preferred_element_type=jnp.float32)
        .astype(jnp.bfloat16)
        .reshape(sequence_wise, key_count, head_count, head_dim)
    )
    projected_values = (
        jnp.dot(flat_rows, value_weight, preferred_element_type=jnp.float32)
        .astype(jnp.bfloat16)
        .reshape(sequence_wise, key_count, head_count, head_dim)
    )
    maxima, totals, summed = lax.map(
        lambda inputs: attend_partial(
            inputs[0], inputs[1], inputs[2], bias_all, key_live, score_scale
        ),
        (projected_queries, projected_keys, projected_values),
    )
    attended = summed / jnp.repeat(totals, head_dim, axis=-1)
    gated = gate_activations * attended
    gated_own = lax.dynamic_slice_in_dim(gated, col_index * residue_half, residue_half, 1).astype(
        jnp.bfloat16
    )
    alignment_update = (
        jnp.dot(
            gated_own.reshape(-1, channel_count), output_weight, preferred_element_type=jnp.float32
        )
        .astype(jnp.bfloat16)
        .reshape(sequence_wise, residue_half, channel_count)
    )
    d_gated = lax.dot_general(
        complete_cotangent.reshape(-1, channel_count),
        output_weight,
        (((1,), (1,)), ((), ())),
        preferred_element_type=jnp.float32,
    ).reshape(sequence_wise, residues, channel_count)
    d_attended = d_gated * gate_activations
    delta_sum = jnp.sum(
        (d_attended * attended).reshape(sequence_wise, residues, head_count, head_dim), axis=-1
    )
    d_rounded = d_attended.astype(jnp.bfloat16).reshape(
        sequence_wise, residues, head_count, head_dim
    )
    log_total = maxima + jnp.log(totals)
    keys_half = lax.dynamic_slice_in_dim(projected_keys, col_index * residue_half, residue_half, 1)
    values_half = lax.dynamic_slice_in_dim(
        projected_values, col_index * residue_half, residue_half, 1
    )
    bias_half = lax.dynamic_slice_in_dim(bias_all, col_index * residue_half, residue_half, 2)
    bias_rows = bias_half.astype(jnp.float32)

    def single_sequence(running, sequence_items):
        query_rows, d_rows, total_rows, delta_rows, keys_one, values_one = sequence_items
        scores = jnp.einsum(
            "ihd,jhd->ihj", query_rows, keys_one, preferred_element_type=jnp.float32
        )
        scores = scores * score_scale + bias_rows + half_live
        probs = jnp.exp(scores - total_rows[..., None])
        d_weights = jnp.einsum(
            "ihd,jhd->ihj", d_rows, values_one, preferred_element_type=jnp.float32
        )
        return (running + probs * (d_weights - delta_rows[..., None]), None)

    sequence_items = (projected_queries, d_rounded, log_total, delta_sum, keys_half, values_half)
    initial_value = jnp.zeros(
        (rows_here * lax.axis_size("row"), head_count, residue_half), jnp.float32
    )
    result, unused = lax.scan(single_sequence, initial_value, sequence_items)
    shares = lax.all_to_all(
        result.astype(jnp.bfloat16).reshape((-1,) + (rows_here,) + result.shape[1:]),
        "row",
        split_axis=0,
        concat_axis=0,
        tiled=True,
    )
    bias_gradient = jnp.sum(shares.astype(jnp.float32), axis=0)
    d_normed = jnp.einsum(
        "ihj,zh->ijz",
        bias_gradient,
        bias_weight.astype(jnp.float32),
        precision=lax.Precision.HIGHEST,
    )
    pair_gradient = norm_backward(pair_updated, d_normed)
    return (alignment_update, pair_updated, pair_gradient)


LANES = 128
GROUP = 4
PIECES = 4
f32 = jnp.float32
bf16 = jnp.bfloat16


def dot_nn(a, b):
    return lax.dot_general(a, b, (((1,), (0,)), ((), ())), preferred_element_type=f32)


def dot_nt(a, b):
    return lax.dot_general(a, b, (((1,), (1,)), ((), ())), preferred_element_type=f32)


def dot_tn(a, b):
    return lax.dot_general(a, b, (((0,), (0,)), ((), ())), preferred_element_type=f32)


def lane_index(rows):
    return lax.broadcasted_iota(jnp.int32, (rows, LANES), 1)


def swap_groups(parts):
    lane = lane_index(parts[0].shape[0])
    low, even = lane < 64, lane % 64 < 32
    parts = [
        jnp.where(low, parts[0], pltpu.roll(parts[2], 64, 1)),
        jnp.where(low, parts[1], pltpu.roll(parts[3], 64, 1)),
        jnp.where(low, pltpu.roll(parts[0], 64, 1), parts[2]),
        jnp.where(low, pltpu.roll(parts[1], 64, 1), parts[3]),
    ]
    return [
        jnp.where(even, parts[0], pltpu.roll(parts[1], 32, 1)),
        jnp.where(even, pltpu.roll(parts[0], 96, 1), parts[1]),
        jnp.where(even, parts[2], pltpu.roll(parts[3], 32, 1)),
        jnp.where(even, pltpu.roll(parts[2], 96, 1), parts[3]),
    ]


def factors_kernel(
    seq_smem_ref, res_smem_ref, seq_ref, res_ref, bias_w_ref, left_ref, right_ref, *refs
):
    row_refs, (send_ref, aux_ref, normed_ref, left_scr) = refs[:PIECES], refs[PIECES:]
    lines = send_ref.shape[0]
    seqs = send_ref.shape[2] // 12
    residues = res_ref.shape[1]
    me = lax.axis_index("row")
    normed = jnp.concatenate([layer_normalize(rows[...]).astype(bf16) for rows in row_refs], axis=0)
    normed_ref[...] = normed
    live = res_ref[...].astype(f32)
    live_rows = jnp.broadcast_to(live, (residues, residues)).T
    right_t = right_ref[...]
    left_wide = jnp.concatenate([left_ref[...]] * 4, axis=0)
    lane_group = lane_index(lines) // 32
    quarters = []
    tail = []
    for s in range(seqs):
        seq_live = seq_smem_ref[me * seqs + s].astype(f32)
        own = normed[s * residues : (s + 1) * residues]
        factor = dot_nt(right_t, own) * (live * seq_live)
        quarters.append(swap_groups([factor[a * 8 : (a + 1) * 8] for a in range(4)]))
        left_scr[s, :residues] = dot_nt(own, left_wide) * (live_rows * seq_live)
        for a in range(4):
            row = jnp.zeros((lines, LANES), f32)
            for b in range(4):
                part = left_scr[s, pl.ds(4 * a + b, lines, stride=4 * GROUP), :]
                row = jnp.where(lane_group == b, part, row)
            tail.append(row)
    tail = jnp.stack(tail, axis=1).astype(bf16)
    right_rows = 8 * seqs
    for t in range(GROUP):
        block = jnp.concatenate([own[t] for own in quarters], axis=0).astype(bf16)
        send_ref[:, t, :right_rows, :] = jnp.broadcast_to(block[None], (lines, right_rows, LANES))
        send_ref[:, t, right_rows:, :] = tail
    aux_ref[0:4] = tile_inverse(res_smem_ref, res_ref, seq_ref)
    aux_ref[4:8] = jnp.broadcast_to((live - 1.0) * mask_fill, (4, LANES))
    aux_ref[8:16] = bias_w_ref[...].astype(f32)


def side_by_side(first, second, at):
    low = lane_index(first.shape[0]) < 64
    span = slice(at // 2 * LANES, at // 2 * LANES + LANES)
    first, second = first[:, span], second[:, span]
    if at % 2 == 0:
        return jnp.where(low, first, pltpu.roll(second, 64, 1))
    return jnp.where(low, pltpu.roll(first, 64, 1), second)


def partner(step):
    return lax.bitwise_xor(lax.rem(lax.axis_index("row"), GROUP), step)


def tile_inverse(res_smem_ref, res_ref, seq_ref):
    own = partner(0)
    rows = lax.div(lax.axis_index("row"), GROUP) * 16
    lane = lane_index(1)
    live = res_ref[...].astype(f32)
    columns = jnp.zeros((1, LANES), f32)
    for t in range(GROUP):
        turned = live if t == 0 else pltpu.roll(live, LANES - 32 * t, 1)
        columns = jnp.where(own == t, turned, columns)
    columns = jnp.where(lane < 32, columns, 0.0)
    columns = columns + pltpu.roll(columns, 32, 1)
    columns = columns + pltpu.roll(columns, 64, 1)
    total = jnp.sum(seq_ref[...].astype(f32), axis=-1, keepdims=True)
    lines = []
    for b in range(4):
        line = jnp.zeros((1, LANES), f32)
        for a in range(4):
            line = jnp.where(lane // 32 == a, res_smem_ref[rows + 4 * a + b].astype(f32), line)
        lines.append(1.0 / jnp.maximum(total * line * columns, 1.0))
    return jnp.concatenate(lines, axis=0)


def projections_kernel(
    normed_ref, cot_ref, weights_ref, wg_ref, wo_ref, aux_ref, pair_ref, gate_ref, aux_out_ref, pair_out_ref, *rest
):
    block_refs, every = rest[:GROUP], rest[GROUP]
    aux_out_ref[...] = aux_ref[...]
    pair_out_ref[...] = pair_ref[...]
    normed = normed_ref[...]
    tokens = normed.shape[0]
    residues = gate_ref.shape[1]
    seqs = tokens // residues
    channels = normed.shape[1]
    queries, keys, values = [
        dot_nn(normed, weights_ref[:, at * channels : (at + 1) * channels]) for at in range(3)
    ]
    gate = jax.nn.sigmoid(dot_nn(normed, wg_ref[...]))
    d_attended = dot_nt(cot_ref[...], wo_ref[...]) * gate
    for t in range(GROUP):
        rows = side_by_side(queries, d_attended, t).astype(bf16)
        columns = side_by_side(keys, values, t).astype(bf16)
        gate_ref[t] = side_by_side(gate[:residues], gate[residues:], t)
        for s in range(seqs):
            every[t, s] = rows[s * residues : (s + 1) * residues]
            every[t, seqs + s] = columns[s * residues : (s + 1) * residues]
    for step in range(GROUP):
        block_refs[step][...] = every[partner(step)]


def pair_kernel(recv_ref, weight_ref, aux_ref, *refs):
    pair_refs, send_ref, updated_refs = refs[:GROUP], refs[GROUP], refs[GROUP + 1 : 2 * GROUP + 1]
    flat, rbuf, lbuf, obuf, state, after = refs[2 * GROUP + 1 :]
    peers, block_rows, _ = recv_ref.shape
    seqs = block_rows // 12
    for step in range(GROUP):
        state[partner(step)] = pair_refs[step][...]
    before = [
        jnp.concatenate([state[a, b] for a in range(GROUP)], axis=0).astype(f32).T for b in range(4)
    ]
    flat[: peers * block_rows] = recv_ref[...].astype(f32).reshape(peers * block_rows, LANES)
    for s in range(seqs):
        for g in range(8):
            part = flat[pl.ds(s * 8 + g, peers, stride=block_rows), :]
            for a in range(4):
                turned = part if a == 0 else pltpu.roll(part, 32 * a, 1)
                rbuf[a, s * peers : (s + 1) * peers, g * LANES : (g + 1) * LANES] = turned.astype(bf16)
        for a in range(4):
            part = flat[pl.ds(8 * seqs + 4 * s + a, peers, stride=block_rows), :]
            lbuf[s * peers : (s + 1) * peers, a * LANES : (a + 1) * LANES] = part
    left_t = lbuf[...].T.astype(bf16)
    outer = [dot_nn(left_t[a * LANES : (a + 1) * LANES], rbuf[a]).astype(bf16) for a in range(4)]
    lane_group = lane_index(LANES) // 32
    sums = None
    for q in range(4):
        for g in range(8):
            span = slice(g * LANES, (g + 1) * LANES)
            picked = outer[3][:, span]
            for a in range(3):
                picked = jnp.where(lane_group == (q + a) % 4, outer[a][:, span], picked)
            for b in range(4):
                obuf[q, g * 32 : (g + 1) * 32, b * LANES : (b + 1) * LANES] = picked[b * 32 : (b + 1) * 32]
        part = dot_tn(weight_ref[q], obuf[q])
        if q:
            part = jnp.concatenate(
                [pltpu.roll(part[:, b * LANES : (b + 1) * LANES], LANES - 32 * q, 1) for b in range(4)], axis=1
            )
        sums = part if sums is None else sums + part
    bias_w = aux_ref[8:16].astype(bf16)
    blocks = []
    for b in range(4):
        update = sums[:, b * LANES : (b + 1) * LANES] * aux_ref[b : b + 1, :]
        updated = (before[b] + update).astype(bf16)
        values = updated.astype(f32)
        center = values - jnp.mean(values, axis=0, keepdims=True)
        spread = jnp.mean(center * center, axis=0, keepdims=True)
        line = dot_nn(bias_w, (center * lax.rsqrt(spread + norm_eps)).astype(bf16))
        blocks.append(pltpu.roll(line, partner(0) * 32, 1))
        values = values.T.astype(bf16)
        for a in range(GROUP):
            after[a, b] = values[a * 32 : (a + 1) * 32]
    lines, _, share, _ = send_ref.shape
    heads = share // 4
    for t in range(GROUP):
        block = jnp.concatenate([rows[t * heads : (t + 1) * heads] for rows in blocks], axis=0).astype(bf16)
        send_ref[:, t] = jnp.broadcast_to(block[None], (lines, share, LANES))
    for step in range(GROUP):
        updated_refs[step][...] = after[partner(step)]


def place_bias(flat, heads, h, bias):
    lines = bias.shape[0] // 16 - 1
    lane_group = lane_index(lines) // 32
    for b in range(4):
        rows = [flat[pl.ds((4 * t + b) * heads + h, lines, stride=16 * heads), :] for t in range(GROUP)]
        for a in range(4):
            picked = rows[3]
            for t in range(3):
                picked = jnp.where(lane_group == (a + t) % 4, rows[t], picked)
            if a:
                picked = pltpu.roll(picked, LANES - 32 * a, 1)
            bias[pl.ds(4 * a + b, lines, stride=16), :] = picked


def place_kernel(bias_ref, mask_ref, placed, flat):
    heads = placed.shape[0]
    rows = bias_ref.shape[0] * bias_ref.shape[1]
    flat[:rows] = bias_ref[...].reshape(rows, LANES).astype(f32)
    for h in range(heads):
        place_bias(flat, heads, h, placed.at[h])
    placed[0, placed.shape[1] - 16 : placed.shape[1] - 12] = mask_ref[4:8]


def bias_gradient_kernel(scale, *refs):
    block_refs, (placed, send_ref, weights_ref, value_ref, grads) = refs[:GROUP], refs[GROUP:]
    sequences, rows, residues = weights_ref.shape
    heads = rows // residues
    seqs = sequences // GROUP
    ones = jnp.ones((residues, LANES), bf16)
    part_of = lane_index(residues) // 32
    key_mask = placed[0, residues : residues + 1]
    totals = [jnp.zeros((residues, residues), f32) for _ in range(heads)]
    for step, block in enumerate(block_refs):
        for s in range(seqs):
            at = step * seqs + s
            columns = block[seqs + s]
            value_ref[at] = jnp.where(part_of < heads, jnp.ones((), bf16), columns)
            wide = jnp.concatenate(
                [jnp.where(part_of == g, block[s], jnp.zeros((), bf16)) for g in range(2 * heads)], axis=0
            )
            both = dot_nt(wide, columns)
            for h in range(heads):
                own = slice(h * residues, (h + 1) * residues)
                scores = both[own] * scale + placed[h, :residues] + key_mask
                weights = jnp.exp(scores - jnp.max(scores, axis=-1, keepdims=True))
                rounded = weights.astype(bf16)
                weights_ref[at, own, :] = rounded
                flow = both[(heads + h) * residues : (heads + h + 1) * residues]
                inverse = 1.0 / dot_nn(rounded, ones)
                delta = dot_nn((weights * flow).astype(bf16), ones) * inverse
                totals[h] = totals[h] + weights * inverse * (flow - delta)
    for h in range(heads):
        grads[pl.ds(h, residues, stride=heads), :] = totals[h]
    send_ref[...] = grads[:rows].astype(bf16).reshape(send_ref.shape)


def attended_kernel(weights_ref, value_ref, *refs):
    part_refs, out_refs = refs[:GROUP], refs[GROUP:]
    sequences, _, residues = weights_ref.shape
    seqs = sequences // GROUP
    lane = lane_index(residues)
    for step in range(GROUP):
        attended = []
        for s in range(seqs):
            mixed = dot_nn(weights_ref[step * seqs + s], value_ref[step * seqs + s])
            picked = jnp.where(lane < 96, mixed[:residues], mixed[residues:])
            totals = jnp.where(lane < 32, mixed[:residues], mixed[residues:])
            attended.append(picked / pltpu.roll(totals, 64, 1))
        out_refs[step][0] = jnp.where(lane < 64, pltpu.roll(attended[0], 64, 1), attended[1]).astype(bf16)
        out_refs[step][1] = part_refs[step][...].reshape(residues, LANES)


def output_kernel(gate_ref, wo_ref, *refs):
    in_refs, (out_ref, pair_ref, normal_ref, inverse_ref) = refs[:GROUP], refs[GROUP:]
    residues = gate_ref.shape[1]
    rows = pair_ref.shape[0]
    columns_each = residues // GROUP
    low = lane_index(residues) < 64
    zero = jnp.zeros((), bf16)
    sums = [jnp.zeros((residues, out_ref.shape[1]), f32) for _ in range(2)]
    for step in range(GROUP):
        at = partner(step)
        gated = (gate_ref[at] * in_refs[step][0].astype(f32)).astype(bf16)
        weight = wo_ref[pl.ds(pl.multiple_of(at * 64, 64), 64), :]
        weight = jnp.concatenate([weight, weight], axis=0)
        sums[0] = sums[0] + dot_nn(jnp.where(low, gated, zero), weight)
        sums[1] = sums[1] + dot_nn(jnp.where(low, zero, gated), weight)
        columns = pl.ds(pl.multiple_of(at * columns_each, columns_each), columns_each)
        pair_ref[:, columns, :] = in_refs[step][1].reshape(rows, columns_each, LANES)
        values = in_refs[step][1].astype(f32)
        center = values - jnp.mean(values, axis=-1, keepdims=True)
        inverse = lax.rsqrt(jnp.mean(center * center, axis=-1, keepdims=True) + norm_eps)
        normal_ref[:, columns, :] = (center * inverse).reshape(rows, columns_each, LANES)
        inverse_ref[:, columns, :] = jnp.broadcast_to(inverse, values.shape).reshape(rows, columns_each, LANES)
    for s in range(2):
        out_ref[s * residues : (s + 1) * residues, :] = sums[s].astype(bf16)


def split_sum(values):
    high = values.astype(bf16)
    return high, (values - high.astype(f32)).astype(bf16)


def gradient_kernel(
    shares_ref, aux_ref, normal_ref, inverse_ref, update_ref, pair_ref, update_hbm, pair_hbm, out_hbm, result, left_for
):
    moves = [
        pltpu.make_async_copy(update_ref, update_hbm, left_for.at[0]),
        pltpu.make_async_copy(pair_ref, pair_hbm, left_for.at[1]),
    ]
    for move in moves:
        move.start()
    peers, share, _ = shares_ref.shape
    rows, _, channels = normal_ref.shape
    heads = share // rows
    total = jnp.sum(shares_ref[...].astype(f32).reshape(peers // GROUP, GROUP, share, LANES), axis=0)
    bias_w = aux_ref[8:16]
    mean_high, mean_low = split_sum(
        jnp.broadcast_to(jnp.mean(bias_w, axis=-1, keepdims=True), bias_w.shape)
    )
    exact = bias_w.astype(bf16)
    none = jnp.zeros(exact.shape, bf16)
    weights = jnp.concatenate(
        [
            jnp.concatenate([exact, mean_high], axis=1),
            jnp.concatenate([exact, mean_high], axis=1),
            jnp.concatenate([none, mean_low], axis=1),
        ],
        axis=0,
    )
    for i in range(rows):
        own = jnp.concatenate([total[t, i * heads : (i + 1) * heads] for t in range(GROUP)], axis=0)
        high, low = split_sum(own)
        both = dot_tn(jnp.concatenate([high, low, high], axis=0), weights)
        upstream, mean = both[:, :channels], both[:, channels:]
        normal = normal_ref[i]
        result[i] = inverse_ref[i] * (
            upstream - mean - normal * jnp.mean(upstream * normal, axis=-1, keepdims=True)
        )
        moves.append(pltpu.make_async_copy(result.at[i], out_hbm.at[i], left_for.at[2 + i]))
        moves[-1].start()
    for move in moves:
        move.wait()


def kernel_call(body, out_shape, in_specs=None, scratch=(), flops=0, moved=0, vmem_mib=12, out_specs=None, grid=()):
    vmem = pl.BlockSpec(memory_space=pltpu.VMEM)
    many = isinstance(out_shape, (list, tuple))
    return pl.pallas_call(
        body,
        grid=grid,
        out_shape=out_shape,
        in_specs=in_specs,
        out_specs=out_specs or ([vmem] * len(out_shape) if many else vmem),
        scratch_shapes=list(scratch),
        compiler_params=pltpu.CompilerParams(vmem_limit_bytes=vmem_mib * 1024 * 1024),
        cost_estimate=pl.CostEstimate(flops=flops, bytes_accessed=moved, transcendentals=0),
    )


def on_device_paired(
    alignment_rows,
    pair_state,
    update_cotangent,
    sequence_mask,
    residue_mask,
    left_weight,
    right_weight,
    outer_weight,
    bias_weight,
    query_weight,
    key_weight,
    value_weight,
    gate_weight,
    output_weight,
):
    sequence_wise, residues, channel_count = alignment_rows.shape
    rows_here, _, pair_channels = pair_state.shape
    head_count = bias_weight.shape[1]
    peers = lax.axis_size("row")
    factor = left_weight.shape[1]
    lines = peers // GROUP
    vmem = pl.BlockSpec(memory_space=pltpu.VMEM)
    smem = pl.BlockSpec(memory_space=pltpu.SMEM)
    token_rows = sequence_wise * residues
    columns_each = residues // GROUP
    block_rows = sequence_wise * 12
    flat_rows = alignment_rows.reshape(token_rows, channel_count)
    shape = jax.ShapeDtypeStruct

    pieces = [
        pl.BlockSpec((token_rows // PIECES, channel_count), lambda step, at=at: (at, 0)) for at in range(PIECES)
    ]
    send, aux, normed = kernel_call(
        factors_kernel,
        [
            shape((lines, GROUP, block_rows, LANES), bf16),
            shape((16, LANES), f32),
            shape((token_rows, channel_count), bf16),
        ],
        [smem] * 2 + [vmem] * 5 + pieces,
        [pltpu.VMEM((sequence_wise, residues + 4 * GROUP, LANES), f32)],
        flops=2 * token_rows * channel_count * LANES,
        moved=1 << 20,
        vmem_mib=60,
        grid=(1,),
    )(
        sequence_mask,
        residue_mask,
        sequence_mask.reshape(1, -1),
        residue_mask.reshape(1, -1),
        bias_weight.T,
        left_weight.T,
        right_weight.T,
        *[flat_rows] * PIECES,
    )
    received = lax.all_to_all(
        send.reshape(peers, block_rows, LANES), "row", split_axis=0, concat_axis=0, tiled=True
    )

    group_heads = head_count // GROUP
    head_rows = group_heads * residues
    scale = (channel_count // head_count) ** (-0.5)
    normed, *weights = lax.optimization_barrier((normed, query_weight, key_weight, value_weight))
    joined = jnp.concatenate(weights, axis=1)
    joined, pair_rows = lax.optimization_barrier((joined, pair_state))
    own = lax.axis_index("row") % GROUP
    pair_blocks = [
        lax.dynamic_slice_in_dim(pair_rows, (own ^ step) * columns_each, columns_each, 1) for step in range(GROUP)
    ]
    part_shape = shape((rows_here, columns_each, pair_channels), bf16)
    gate, aux, own_block, *blocks = kernel_call(
        projections_kernel,
        [shape((GROUP, residues, LANES), f32), shape((16, LANES), f32), part_shape]
        + [shape((2 * sequence_wise, residues, LANES), bf16)] * GROUP,
        [vmem] * 7,
        [pltpu.VMEM((GROUP, 2 * sequence_wise, residues, LANES), bf16)],
        flops=10 * token_rows * channel_count * channel_count,
        moved=1 << 21,
    )(
        normed,
        update_cotangent.reshape(token_rows, channel_count),
        joined,
        gate_weight,
        output_weight,
        aux,
        pair_blocks[0],
    )

    def trade(parts):
        return parts[:1] + [
            lax.ppermute(parts[d], "row", [(i, i ^ d) for i in range(peers)]) for d in range(1, GROUP)
        ]

    pair_blocks = [own_block] + trade(pair_blocks)[1:]
    blocks = trade(blocks)
    weight_t = (
        outer_weight.reshape(factor, 4, 8, pair_channels)
        .transpose(1, 2, 0, 3)
        .reshape(4, 8 * factor, pair_channels)
    )
    share_rows = 4 * group_heads
    send_bias, *updated = kernel_call(
        pair_kernel,
        [shape((lines, GROUP, share_rows, LANES), bf16)] + [part_shape] * GROUP,
        [vmem] * (3 + GROUP),
        [
            pltpu.VMEM(((peers + 1) * block_rows, LANES), f32),
            pltpu.VMEM((4, peers * sequence_wise, 8 * LANES), bf16),
            pltpu.VMEM((peers * sequence_wise, 4 * LANES), f32),
            pltpu.VMEM((4, 8 * factor, 4 * LANES), bf16),
            pltpu.VMEM((GROUP, rows_here, columns_each, pair_channels), bf16),
            pltpu.VMEM((GROUP, rows_here, columns_each, pair_channels), bf16),
        ],
        flops=1 << 28,
        moved=1 << 20,
    )(received, weight_t, aux, *pair_blocks)
    bias_all = lax.all_to_all(
        send_bias.reshape(peers, share_rows, LANES), "row", split_axis=0, concat_axis=0, tiled=True
    )

    placed = kernel_call(
        place_kernel,
        shape((group_heads, residues + 16, LANES), f32),
        [vmem] * 2,
        [pltpu.VMEM((head_rows + 16 * group_heads, LANES), f32)],
        flops=1 << 22,
        moved=1 << 18,
    )(bias_all, aux)
    send_grad, weights, values = kernel_call(
        lambda *refs: bias_gradient_kernel(scale, *refs),
        [
            shape((peers, rows_here * group_heads, LANES), bf16),
            shape((GROUP * sequence_wise, head_rows, residues), bf16),
            shape((GROUP * sequence_wise, residues, LANES), bf16),
        ],
        [vmem] * (1 + GROUP),
        [pltpu.VMEM((head_rows + 16 * group_heads, LANES), f32)],
        flops=1 << 28,
        moved=1 << 22,
    )(*blocks, placed)
    shares = lax.all_to_all(send_grad, "row", split_axis=0, concat_axis=0, tiled=True)
    attended = kernel_call(
        attended_kernel,
        [shape((2, residues, LANES), bf16)] * GROUP,
        [vmem] * (2 + GROUP),
        flops=1 << 28,
        moved=1 << 21,
    )(weights, values, *updated)
    update, pair_updated, normal, inverse = kernel_call(
        output_kernel,
        [
            shape((token_rows, channel_count), bf16),
            shape((rows_here, residues, pair_channels), bf16),
            shape((rows_here, residues, pair_channels), f32),
            shape((rows_here, residues, pair_channels), f32),
        ],
        [vmem] * (2 + GROUP),
        flops=2 * token_rows * channel_count * channel_count,
        moved=1 << 20,
    )(gate, output_weight, *trade(list(attended)))
    update, pair_updated, pair_gradient = kernel_call(
        gradient_kernel,
        [
            shape((token_rows, channel_count), bf16),
            shape((rows_here, residues, pair_channels), bf16),
            shape((rows_here, residues, pair_channels), f32),
        ],
        [vmem] * 6,
        [pltpu.VMEM((rows_here, residues, pair_channels), f32), pltpu.SemaphoreType.DMA((2 + rows_here,))],
        flops=1 << 24,
        moved=1 << 20,
        out_specs=[pl.BlockSpec(memory_space=pltpu.HBM)] * 3,
    )(shares, aux, normal, inverse, update, pair_updated)
    return (update.reshape(alignment_rows.shape), pair_updated, pair_gradient)


def on_device(*arguments):
    rows, pair, left, bias = arguments[0], arguments[1], arguments[5], arguments[8]
    peers = lax.axis_size("row")
    fits = (
        lax.axis_size("col") == 1
        and peers == 32
        and rows.shape == (2, 128, 256)
        and pair.shape == (4, 128, 128)
        and left.shape[1] == 32
        and bias.shape[1] == 8
    )
    return (on_device_paired if fits else on_device_general)(*arguments)


def solution(mesh):
    placed = (
        P(("grp", "row"), "col", None),
        P(("grp", "row"), "col", None),
        P(("grp", "row"), "col", None),
        P("grp"),
        P("grp"),
        P(),
        P(),
        P(),
        P(),
        P(),
        P(),
        P(),
        P(),
        P(),
    )
    return jax.shard_map(
        on_device,
        mesh=mesh,
        in_specs=placed,
        out_specs=(
            P(("grp", "row"), "col", None),
            P(("grp", "row"), "col", None),
            P(("grp", "row"), "col", None),
        ),
        check_vma=False,
    )
```

```python
import jax
import jax.numpy as jnp
from jax import lax
from jax.experimental import pallas as pl
from jax.experimental.pallas import tpu as pltpu
from jax.sharding import PartitionSpec as P

norm_eps = 1e-05
mask_fill = 1000000000.0


def layer_normalize(values):
    values = values.astype(jnp.float32)
    center = values - jnp.mean(values, axis=-1, keepdims=True)
    spread = jnp.mean(center * center, axis=-1, keepdims=True)
    return center * lax.rsqrt(spread + norm_eps)


def norm_backward(values, upstream):
    values = values.astype(jnp.float32)
    center = values - jnp.mean(values, axis=-1, keepdims=True)
    inverse = lax.rsqrt(jnp.mean(center * center, axis=-1, keepdims=True) + norm_eps)
    normal_part = center * inverse
    return inverse * (
        upstream
        - jnp.mean(upstream, axis=-1, keepdims=True)
        - normal_part * jnp.mean(upstream * normal_part, axis=-1, keepdims=True)
    )


def spread_all(shard):
    copies = jnp.broadcast_to(shard[None], (lax.axis_size("row"),) + shard.shape)
    gathered = lax.all_to_all(copies, "row", split_axis=0, concat_axis=0, tiled=True)
    return gathered.reshape((-1,) + shard.shape[1:])


def attend_partial(
    projected_queries, projected_keys, projected_values, bias_all, key_mask, score_scale
):
    scores = jnp.einsum(
        "ihd,jhd->ihj", projected_queries, projected_keys, preferred_element_type=jnp.float32
    )
    scores = scores * score_scale + bias_all.astype(jnp.float32) + key_mask
    maxima = jnp.max(scores, axis=-1)
    weights = jnp.exp(scores - maxima[..., None])
    totals = jnp.sum(weights, axis=-1)
    summed = jnp.einsum(
        "ihj,jhd->ihd",
        weights.astype(jnp.bfloat16),
        projected_values,
        preferred_element_type=jnp.float32,
    )
    return (maxima, totals, summed.reshape(summed.shape[0], -1))


def on_device_general(
    alignment_rows,
    pair_state,
    update_cotangent,
    sequence_mask,
    residue_mask,
    left_weight,
    right_weight,
    outer_weight,
    bias_weight,
    query_weight,
    key_weight,
    value_weight,
    gate_weight,
    output_weight,
):
    sequence_wise, residue_half, channel_count = alignment_rows.shape
    rows_here = pair_state.shape[0]
    residues = residue_mask.shape[0]
    head_count = bias_weight.shape[1]
    head_dim = channel_count // head_count
    score_scale = head_dim ** (-0.5)
    row_index = lax.axis_index("row")
    col_index = lax.axis_index("col")
    complete_alignment, complete_cotangent = (
        lax.all_gather(alignment_rows, "col", axis=1, tiled=True),
        lax.all_gather(update_cotangent, "col", axis=1, tiled=True),
    )
    seq_live = sequence_mask.astype(jnp.float32)
    res_live = residue_mask.astype(jnp.float32)
    own_seq = lax.dynamic_slice_in_dim(seq_live, row_index * sequence_wise, sequence_wise)
    own_cols = lax.dynamic_slice_in_dim(res_live, col_index * residue_half, residue_half)
    own_rows = lax.dynamic_slice_in_dim(res_live, row_index * rows_here, rows_here)
    normalized_input = layer_normalize(complete_alignment).astype(jnp.bfloat16)
    flat_rows = normalized_input.reshape(-1, channel_count)
    normed_half = lax.dynamic_slice_in_dim(
        normalized_input, col_index * residue_half, residue_half, 1
    )
    half_rows = normed_half.reshape(-1, channel_count)
    left_proj = jnp.dot(flat_rows, left_weight, preferred_element_type=jnp.float32).reshape(
        sequence_wise, residues, -1
    )
    left_proj = (left_proj * (own_seq[:, None] * res_live[None, :])[..., None]).astype(jnp.bfloat16)
    right_proj = jnp.dot(half_rows, right_weight, preferred_element_type=jnp.float32).reshape(
        sequence_wise, residue_half, -1
    )
    right_proj = (right_proj * (own_seq[:, None] * own_cols[None, :])[..., None]).astype(
        jnp.bfloat16
    )
    left_tile = lax.all_to_all(left_proj, "row", split_axis=1, concat_axis=0, tiled=True)
    right_all = spread_all(right_proj)
    outer_width = left_tile.shape[2]
    outer_sum = lax.dot_general(
        left_tile.reshape(left_tile.shape[0], -1),
        right_all.reshape(right_all.shape[0], -1),
        (((0,), (0,)), ((), ())),
        preferred_element_type=jnp.float32,
    )
    outer_half = outer_sum.astype(jnp.bfloat16).reshape(
        rows_here, outer_width, residue_half, outer_width
    )
    opm_update = jnp.einsum(
        "ipjq,pqz->ijz", outer_half, outer_weight, preferred_element_type=jnp.float32
    )
    divisor = jnp.maximum(jnp.sum(seq_live) * own_rows[:, None] * own_cols[None, :], 1.0)
    pair_updated = (pair_state.astype(jnp.float32) + opm_update / divisor[..., None]).astype(
        jnp.bfloat16
    )
    pair_normed = layer_normalize(pair_updated).astype(jnp.bfloat16)
    bias_tile = jnp.einsum(
        "ijz,zh->ihj", pair_normed, bias_weight, preferred_element_type=jnp.float32
    ).astype(jnp.bfloat16)
    projected_queries = (
        jnp.dot(flat_rows, query_weight, preferred_element_type=jnp.float32)
        .astype(jnp.bfloat16)
        .reshape(sequence_wise, residues, head_count, head_dim)
    )
    gate_activations = jax.nn.sigmoid(
        jnp.dot(flat_rows, gate_weight, preferred_element_type=jnp.float32)
    ).reshape(sequence_wise, residues, channel_count)
    key_live = (res_live - 1.0) * mask_fill
    half_live = lax.dynamic_slice_in_dim(key_live, col_index * residue_half, residue_half)
    bias_cols = lax.all_gather(bias_tile, "col", axis=2, tiled=True)
    bias_all = spread_all(bias_cols)
    key_count = bias_all.shape[2]
    projected_keys = (
        jnp.dot(flat_rows, key_weight, preferred_element_type=jnp.float32)
        .astype(jnp.bfloat16)
        .reshape(sequence_wise, key_count, head_count, head_dim)
    )
    projected_values = (
        jnp.dot(flat_rows, value_weight, preferred_element_type=jnp.float32)
        .astype(jnp.bfloat16)
        .reshape(sequence_wise, key_count, head_count, head_dim)
    )
    maxima, totals, summed = lax.map(
        lambda inputs: attend_partial(
            inputs[0], inputs[1], inputs[2], bias_all, key_live, score_scale
        ),
        (projected_queries, projected_keys, projected_values),
    )
    attended = summed / jnp.repeat(totals, head_dim, axis=-1)
    gated = gate_activations * attended
    gated_own = lax.dynamic_slice_in_dim(gated, col_index * residue_half, residue_half, 1).astype(
        jnp.bfloat16
    )
    alignment_update = (
        jnp.dot(
            gated_own.reshape(-1, channel_count), output_weight, preferred_element_type=jnp.float32
        )
        .astype(jnp.bfloat16)
        .reshape(sequence_wise, residue_half, channel_count)
    )
    d_gated = lax.dot_general(
        complete_cotangent.reshape(-1, channel_count),
        output_weight,
        (((1,), (1,)), ((), ())),
        preferred_element_type=jnp.float32,
    ).reshape(sequence_wise, residues, channel_count)
    d_attended = d_gated * gate_activations
    delta_sum = jnp.sum(
        (d_attended * attended).reshape(sequence_wise, residues, head_count, head_dim), axis=-1
    )
    d_rounded = d_attended.astype(jnp.bfloat16).reshape(
        sequence_wise, residues, head_count, head_dim
    )
    log_total = maxima + jnp.log(totals)
    keys_half = lax.dynamic_slice_in_dim(projected_keys, col_index * residue_half, residue_half, 1)
    values_half = lax.dynamic_slice_in_dim(
        projected_values, col_index * residue_half, residue_half, 1
    )
    bias_half = lax.dynamic_slice_in_dim(bias_all, col_index * residue_half, residue_half, 2)
    bias_rows = bias_half.astype(jnp.float32)

    def single_sequence(running, sequence_items):
        query_rows, d_rows, total_rows, delta_rows, keys_one, values_one = sequence_items
        scores = jnp.einsum(
            "ihd,jhd->ihj", query_rows, keys_one, preferred_element_type=jnp.float32
        )
        scores = scores * score_scale + bias_rows + half_live
        probs = jnp.exp(scores - total_rows[..., None])
        d_weights = jnp.einsum(
            "ihd,jhd->ihj", d_rows, values_one, preferred_element_type=jnp.float32
        )
        return (running + probs * (d_weights - delta_rows[..., None]), None)

    sequence_items = (projected_queries, d_rounded, log_total, delta_sum, keys_half, values_half)
    initial_value = jnp.zeros(
        (rows_here * lax.axis_size("row"), head_count, residue_half), jnp.float32
    )
    result, unused = lax.scan(single_sequence, initial_value, sequence_items)
    shares = lax.all_to_all(
        result.astype(jnp.bfloat16).reshape((-1,) + (rows_here,) + result.shape[1:]),
        "row",
        split_axis=0,
        concat_axis=0,
        tiled=True,
    )
    bias_gradient = jnp.sum(shares.astype(jnp.float32), axis=0)
    d_normed = jnp.einsum(
        "ihj,zh->ijz",
        bias_gradient,
        bias_weight.astype(jnp.float32),
        precision=lax.Precision.HIGHEST,
    )
    pair_gradient = norm_backward(pair_updated, d_normed)
    return (alignment_update, pair_updated, pair_gradient)


LANES = 128
GROUP = 4
PIECES = 4
f32 = jnp.float32
bf16 = jnp.bfloat16


def dot_nn(a, b):
    return lax.dot_general(a, b, (((1,), (0,)), ((), ())), preferred_element_type=f32)


def dot_nt(a, b):
    return lax.dot_general(a, b, (((1,), (1,)), ((), ())), preferred_element_type=f32)


def dot_tn(a, b):
    return lax.dot_general(a, b, (((0,), (0,)), ((), ())), preferred_element_type=f32)


def lane_index(rows):
    return lax.broadcasted_iota(jnp.int32, (rows, LANES), 1)


def swap_groups(parts):
    lane = lane_index(parts[0].shape[0])
    low, even = lane < 64, lane % 64 < 32
    parts = [
        jnp.where(low, parts[0], pltpu.roll(parts[2], 64, 1)),
        jnp.where(low, parts[1], pltpu.roll(parts[3], 64, 1)),
        jnp.where(low, pltpu.roll(parts[0], 64, 1), parts[2]),
        jnp.where(low, pltpu.roll(parts[1], 64, 1), parts[3]),
    ]
    return [
        jnp.where(even, parts[0], pltpu.roll(parts[1], 32, 1)),
        jnp.where(even, pltpu.roll(parts[0], 96, 1), parts[1]),
        jnp.where(even, parts[2], pltpu.roll(parts[3], 32, 1)),
        jnp.where(even, pltpu.roll(parts[2], 96, 1), parts[3]),
    ]


def factors_kernel(
    seq_smem_ref, res_smem_ref, seq_ref, res_ref, bias_w_ref, left_ref, right_ref, *refs
):
    row_refs, (send_ref, aux_ref, normed_ref, left_scr) = refs[:PIECES], refs[PIECES:]
    lines = send_ref.shape[0]
    seqs = send_ref.shape[2] // 12
    residues = res_ref.shape[1]
    me = lax.axis_index("row")
    normed = jnp.concatenate([layer_normalize(rows[...]).astype(bf16) for rows in row_refs], axis=0)
    normed_ref[...] = normed
    live = res_ref[...].astype(f32)
    live_rows = jnp.broadcast_to(live, (residues, residues)).T
    right_t = right_ref[...]
    left_wide = jnp.concatenate([left_ref[...]] * 4, axis=0)
    lane_group = lane_index(lines) // 32
    quarters = []
    tail = []
    for s in range(seqs):
        seq_live = seq_smem_ref[me * seqs + s].astype(f32)
        own = normed[s * residues : (s + 1) * residues]
        factor = dot_nt(right_t, own) * (live * seq_live)
        quarters.append(swap_groups([factor[a * 8 : (a + 1) * 8] for a in range(4)]))
        left_scr[:residues] = dot_nt(own, left_wide) * (live_rows * seq_live)
        for a in range(4):
            row = jnp.zeros((lines, LANES), f32)
            for b in range(4):
                part = left_scr[pl.ds(4 * a + b, lines, stride=4 * GROUP), :]
                row = jnp.where(lane_group == b, part, row)
            tail.append(row)
    tail = jnp.stack(tail, axis=1).astype(bf16)
    right_rows = 8 * seqs
    for t in range(GROUP):
        block = jnp.concatenate([own[t] for own in quarters], axis=0).astype(bf16)
        send_ref[:, t, :right_rows, :] = jnp.broadcast_to(block[None], (lines, right_rows, LANES))
        send_ref[:, t, right_rows:, :] = tail
    aux_ref[0:4] = tile_inverse(res_smem_ref, res_ref, seq_ref)
    aux_ref[4:8] = jnp.broadcast_to((live - 1.0) * mask_fill, (4, LANES))
    aux_ref[8:16] = bias_w_ref[...].astype(f32)


def side_by_side(first, second, at):
    low = lane_index(first.shape[0]) < 64
    span = slice(at // 2 * LANES, at // 2 * LANES + LANES)
    first, second = first[:, span], second[:, span]
    if at % 2 == 0:
        return jnp.where(low, first, pltpu.roll(second, 64, 1))
    return jnp.where(low, pltpu.roll(first, 64, 1), second)


def partner(step):
    return lax.bitwise_xor(lax.rem(lax.axis_index("row"), GROUP), step)


def tile_inverse(res_smem_ref, res_ref, seq_ref):
    own = partner(0)
    rows = lax.div(lax.axis_index("row"), GROUP) * 16
    lane = lane_index(1)
    live = res_ref[...].astype(f32)
    columns = jnp.zeros((1, LANES), f32)
    for t in range(GROUP):
        turned = live if t == 0 else pltpu.roll(live, LANES - 32 * t, 1)
        columns = jnp.where(own == t, turned, columns)
    columns = jnp.where(lane < 32, columns, 0.0)
    columns = columns + pltpu.roll(columns, 32, 1)
    columns = columns + pltpu.roll(columns, 64, 1)
    total = jnp.sum(seq_ref[...].astype(f32), axis=-1, keepdims=True)
    lines = []
    for b in range(4):
        line = jnp.zeros((1, LANES), f32)
        for a in range(4):
            line = jnp.where(lane // 32 == a, res_smem_ref[rows + 4 * a + b].astype(f32), line)
        lines.append(1.0 / jnp.maximum(total * line * columns, 1.0))
    return jnp.concatenate(lines, axis=0)


def projections_kernel(
    normed_ref, cot_ref, weights_ref, wg_ref, wo_ref, aux_ref, pair_ref, gate_ref, aux_out_ref, pair_out_ref, *rest
):
    block_refs, every = rest[:GROUP], rest[GROUP]
    aux_out_ref[...] = aux_ref[...]
    pair_out_ref[...] = pair_ref[...]
    normed = normed_ref[...]
    tokens = normed.shape[0]
    residues = gate_ref.shape[1]
    seqs = tokens // residues
    channels = normed.shape[1]
    queries, keys, values = [
        dot_nn(normed, weights_ref[:, at * channels : (at + 1) * channels]) for at in range(3)
    ]
    gate = jax.nn.sigmoid(dot_nn(normed, wg_ref[...]))
    d_attended = dot_nt(cot_ref[...], wo_ref[...]) * gate
    for t in range(GROUP):
        rows = side_by_side(queries, d_attended, t).astype(bf16)
        columns = side_by_side(keys, values, t).astype(bf16)
        gate_ref[t] = side_by_side(gate[:residues], gate[residues:], t)
        for s in range(seqs):
            every[t, s] = rows[s * residues : (s + 1) * residues]
            every[t, seqs + s] = columns[s * residues : (s + 1) * residues]
    for step in range(GROUP):
        block_refs[step][...] = every[partner(step)]


def pair_kernel(recv_ref, weight_ref, aux_ref, *refs):
    pair_refs, send_ref, updated_refs = refs[:GROUP], refs[GROUP], refs[GROUP + 1 : 2 * GROUP + 1]
    flat, rbuf, lbuf, obuf, state, after = refs[2 * GROUP + 1 :]
    peers, block_rows, _ = recv_ref.shape
    seqs = block_rows // 12
    for step in range(GROUP):
        state[partner(step)] = pair_refs[step][...]
    before = [
        jnp.concatenate([state[a, b] for a in range(GROUP)], axis=0).astype(f32).T for b in range(4)
    ]
    flat[: peers * block_rows] = recv_ref[...].astype(f32).reshape(peers * block_rows, LANES)
    for s in range(seqs):
        for g in range(8):
            part = flat[pl.ds(s * 8 + g, peers, stride=block_rows), :]
            for a in range(4):
                turned = part if a == 0 else pltpu.roll(part, 32 * a, 1)
                rbuf[a, s * peers : (s + 1) * peers, g * LANES : (g + 1) * LANES] = turned.astype(bf16)
        for a in range(4):
            part = flat[pl.ds(8 * seqs + 4 * s + a, peers, stride=block_rows), :]
            lbuf[s * peers : (s + 1) * peers, a * LANES : (a + 1) * LANES] = part
    left_t = lbuf[...].T.astype(bf16)
    outer = [dot_nn(left_t[a * LANES : (a + 1) * LANES], rbuf[a]).astype(bf16) for a in range(4)]
    low, even = lane_index(LANES) < 64, lane_index(LANES) % 64 < 32
    sums = None
    for q in range(4):
        for g in range(8):
            span = slice(g * LANES, (g + 1) * LANES)
            turned = [outer[(group - q) % 4][:, span] for group in range(4)]
            picked = jnp.where(
                low, jnp.where(even, turned[0], turned[1]), jnp.where(even, turned[2], turned[3])
            )
            for b in range(4):
                obuf[q, g * 32 : (g + 1) * 32, b * LANES : (b + 1) * LANES] = picked[b * 32 : (b + 1) * 32]
        part = dot_tn(weight_ref[q], obuf[q])
        if q:
            part = jnp.concatenate(
                [pltpu.roll(part[:, b * LANES : (b + 1) * LANES], LANES - 32 * q, 1) for b in range(4)], axis=1
            )
        sums = part if sums is None else sums + part
    bias_w = aux_ref[8:16].astype(bf16)
    blocks = []
    for b in range(4):
        update = sums[:, b * LANES : (b + 1) * LANES] * aux_ref[b : b + 1, :]
        updated = (before[b] + update).astype(bf16)
        values = updated.astype(f32)
        center = values - jnp.mean(values, axis=0, keepdims=True)
        spread = jnp.mean(center * center, axis=0, keepdims=True)
        line = dot_nn(bias_w, (center * lax.rsqrt(spread + norm_eps)).astype(bf16))
        blocks.append(pltpu.roll(line, partner(0) * 32, 1))
        values = values.T.astype(bf16)
        for a in range(GROUP):
            after[a, b] = values[a * 32 : (a + 1) * 32]
    lines, _, share, _ = send_ref.shape
    heads = share // 4
    for t in range(GROUP):
        block = jnp.concatenate([rows[t * heads : (t + 1) * heads] for rows in blocks], axis=0).astype(bf16)
        send_ref[:, t] = jnp.broadcast_to(block[None], (lines, share, LANES))
    for step in range(GROUP):
        updated_refs[step][...] = after[partner(step)]


def place_bias(flat, heads, h, bias):
    lines = bias.shape[0] // 16 - 1
    lane_group = lane_index(lines) // 32
    for b in range(4):
        rows = [flat[pl.ds((4 * t + b) * heads + h, lines, stride=16 * heads), :] for t in range(GROUP)]
        for a in range(4):
            picked = rows[3]
            for t in range(3):
                picked = jnp.where(lane_group == (a + t) % 4, rows[t], picked)
            if a:
                picked = pltpu.roll(picked, LANES - 32 * a, 1)
            bias[pl.ds(4 * a + b, lines, stride=16), :] = picked


def place_kernel(bias_ref, mask_ref, placed, flat):
    heads = placed.shape[0]
    rows = bias_ref.shape[0] * bias_ref.shape[1]
    flat[:rows] = bias_ref[...].reshape(rows, LANES).astype(f32)
    for h in range(heads):
        place_bias(flat, heads, h, placed.at[h])
    placed[0, placed.shape[1] - 16 : placed.shape[1] - 12] = mask_ref[4:8]


def bias_gradient_kernel(scale, *refs):
    block_refs, (placed, send_ref, weights_ref, value_ref, grads) = refs[:GROUP], refs[GROUP:]
    sequences, rows, residues = weights_ref.shape
    heads = rows // residues
    seqs = sequences // GROUP
    ones = jnp.ones((residues, LANES), bf16)
    part_of = lane_index(residues) // 32
    key_mask = placed[0, residues : residues + 1]
    totals = [jnp.zeros((residues, residues), f32) for _ in range(heads)]
    for step, block in enumerate(block_refs):
        for s in range(seqs):
            at = step * seqs + s
            columns = block[seqs + s]
            value_ref[at] = jnp.where(part_of < heads, jnp.ones((), bf16), columns)
            wide = jnp.concatenate(
                [jnp.where(part_of == g, block[s], jnp.zeros((), bf16)) for g in range(2 * heads)], axis=0
            )
            both = dot_nt(wide, columns)
            for h in range(heads):
                own = slice(h * residues, (h + 1) * residues)
                scores = both[own] * scale + placed[h, :residues] + key_mask
                weights = jnp.exp(scores - jnp.max(scores, axis=-1, keepdims=True))
                rounded = weights.astype(bf16)
                weights_ref[at, own, :] = rounded
                flow = both[(heads + h) * residues : (heads + h + 1) * residues]
                inverse = 1.0 / dot_nn(rounded, ones)
                delta = dot_nn((weights * flow).astype(bf16), ones) * inverse
                totals[h] = totals[h] + weights * inverse * (flow - delta)
    for h in range(heads):
        grads[pl.ds(h, residues, stride=heads), :] = totals[h]
    send_ref[...] = grads[:rows].astype(bf16).reshape(send_ref.shape)


def attended_kernel(weights_ref, value_ref, *refs):
    part_refs, out_refs = refs[:GROUP], refs[GROUP:]
    sequences, _, residues = weights_ref.shape
    seqs = sequences // GROUP
    lane = lane_index(residues)
    for step in range(GROUP):
        attended = []
        for s in range(seqs):
            mixed = dot_nn(weights_ref[step * seqs + s], value_ref[step * seqs + s])
            picked = jnp.where(lane < 96, mixed[:residues], mixed[residues:])
            totals = jnp.where(lane < 32, mixed[:residues], mixed[residues:])
            attended.append(picked / pltpu.roll(totals, 64, 1))
        out_refs[step][0] = jnp.where(lane < 64, pltpu.roll(attended[0], 64, 1), attended[1]).astype(bf16)
        out_refs[step][1] = part_refs[step][...].reshape(residues, LANES)


def output_kernel(gate_ref, wo_ref, *refs):
    in_refs, (out_ref, pair_ref, normal_ref, inverse_ref) = refs[:GROUP], refs[GROUP:]
    residues = gate_ref.shape[1]
    rows = pair_ref.shape[0]
    columns_each = residues // GROUP
    low = lane_index(residues) < 64
    zero = jnp.zeros((), bf16)
    sums = [jnp.zeros((residues, out_ref.shape[1]), f32) for _ in range(2)]
    for step in range(GROUP):
        at = partner(step)
        gated = (gate_ref[at] * in_refs[step][0].astype(f32)).astype(bf16)
        weight = wo_ref[pl.ds(pl.multiple_of(at * 64, 64), 64), :]
        weight = jnp.concatenate([weight, weight], axis=0)
        sums[0] = sums[0] + dot_nn(jnp.where(low, gated, zero), weight)
        sums[1] = sums[1] + dot_nn(jnp.where(low, zero, gated), weight)
        columns = pl.ds(pl.multiple_of(at * columns_each, columns_each), columns_each)
        pair_ref[:, columns, :] = in_refs[step][1].reshape(rows, columns_each, LANES)
        values = in_refs[step][1].astype(f32)
        center = values - jnp.mean(values, axis=-1, keepdims=True)
        inverse = lax.rsqrt(jnp.mean(center * center, axis=-1, keepdims=True) + norm_eps)
        normal_ref[:, columns, :] = (center * inverse).reshape(rows, columns_each, LANES)
        inverse_ref[:, columns, :] = jnp.broadcast_to(inverse, values.shape).reshape(rows, columns_each, LANES)
    for s in range(2):
        out_ref[s * residues : (s + 1) * residues, :] = sums[s].astype(bf16)


def split_sum(values):
    high = values.astype(bf16)
    return high, (values - high.astype(f32)).astype(bf16)


def gradient_kernel(
    shares_ref, aux_ref, normal_ref, inverse_ref, update_ref, pair_ref, update_hbm, pair_hbm, out_hbm, result, left_for
):
    moves = [
        pltpu.make_async_copy(update_ref, update_hbm, left_for.at[0]),
        pltpu.make_async_copy(pair_ref, pair_hbm, left_for.at[1]),
    ]
    for move in moves:
        move.start()
    peers, share, _ = shares_ref.shape
    rows, _, channels = normal_ref.shape
    heads = share // rows
    total = jnp.sum(shares_ref[...].astype(f32).reshape(peers // GROUP, GROUP, share, LANES), axis=0)
    bias_w = aux_ref[8:16]
    mean_high, mean_low = split_sum(
        jnp.broadcast_to(jnp.mean(bias_w, axis=-1, keepdims=True), bias_w.shape)
    )
    exact = bias_w.astype(bf16)
    none = jnp.zeros(exact.shape, bf16)
    weights = jnp.concatenate(
        [
            jnp.concatenate([exact, mean_high], axis=1),
            jnp.concatenate([exact, mean_high], axis=1),
            jnp.concatenate([none, mean_low], axis=1),
        ],
        axis=0,
    )
    for i in range(rows):
        own = jnp.concatenate([total[t, i * heads : (i + 1) * heads] for t in range(GROUP)], axis=0)
        high, low = split_sum(own)
        both = dot_tn(jnp.concatenate([high, low, high], axis=0), weights)
        upstream, mean = both[:, :channels], both[:, channels:]
        normal = normal_ref[i]
        result[i] = inverse_ref[i] * (
            upstream - mean - normal * jnp.mean(upstream * normal, axis=-1, keepdims=True)
        )
        moves.append(pltpu.make_async_copy(result.at[i], out_hbm.at[i], left_for.at[2 + i]))
        moves[-1].start()
    for move in moves:
        move.wait()


def kernel_call(body, out_shape, in_specs=None, scratch=(), flops=0, moved=0, vmem_mib=12, out_specs=None, grid=()):
    vmem = pl.BlockSpec(memory_space=pltpu.VMEM)
    many = isinstance(out_shape, (list, tuple))
    return pl.pallas_call(
        body,
        grid=grid,
        out_shape=out_shape,
        in_specs=in_specs,
        out_specs=out_specs or ([vmem] * len(out_shape) if many else vmem),
        scratch_shapes=list(scratch),
        compiler_params=pltpu.CompilerParams(vmem_limit_bytes=vmem_mib * 1024 * 1024),
        cost_estimate=pl.CostEstimate(flops=flops, bytes_accessed=moved, transcendentals=0),
    )


def on_device_paired(
    alignment_rows,
    pair_state,
    update_cotangent,
    sequence_mask,
    residue_mask,
    left_weight,
    right_weight,
    outer_weight,
    bias_weight,
    query_weight,
    key_weight,
    value_weight,
    gate_weight,
    output_weight,
):
    sequence_wise, residues, channel_count = alignment_rows.shape
    rows_here, _, pair_channels = pair_state.shape
    head_count = bias_weight.shape[1]
    peers = lax.axis_size("row")
    factor = left_weight.shape[1]
    lines = peers // GROUP
    vmem = pl.BlockSpec(memory_space=pltpu.VMEM)
    smem = pl.BlockSpec(memory_space=pltpu.SMEM)
    token_rows = sequence_wise * residues
    columns_each = residues // GROUP
    block_rows = sequence_wise * 12
    flat_rows = alignment_rows.reshape(token_rows, channel_count)
    shape = jax.ShapeDtypeStruct

    pieces = [
        pl.BlockSpec((token_rows // PIECES, channel_count), lambda step, at=at: (at, 0)) for at in range(PIECES)
    ]
    send, aux, normed = kernel_call(
        factors_kernel,
        [
            shape((lines, GROUP, block_rows, LANES), bf16),
            shape((16, LANES), f32),
            shape((token_rows, channel_count), bf16),
        ],
        [smem] * 2 + [vmem] * 5 + pieces,
        [pltpu.VMEM((residues + 4 * GROUP, LANES), f32)],
        flops=2 * token_rows * channel_count * LANES,
        moved=1 << 20,
        vmem_mib=60,
        grid=(1,),
    )(
        sequence_mask,
        residue_mask,
        sequence_mask.reshape(1, -1),
        residue_mask.reshape(1, -1),
        bias_weight.T,
        left_weight.T,
        right_weight.T,
        *[flat_rows] * PIECES,
    )
    received = lax.all_to_all(
        send.reshape(peers, block_rows, LANES), "row", split_axis=0, concat_axis=0, tiled=True
    )

    group_heads = head_count // GROUP
    head_rows = group_heads * residues
    scale = (channel_count // head_count) ** (-0.5)
    normed, *weights = lax.optimization_barrier((normed, query_weight, key_weight, value_weight))
    joined = jnp.concatenate(weights, axis=1)
    joined, pair_rows = lax.optimization_barrier((joined, pair_state))
    own = lax.axis_index("row") % GROUP
    pair_blocks = [
        lax.dynamic_slice_in_dim(pair_rows, (own ^ step) * columns_each, columns_each, 1) for step in range(GROUP)
    ]
    part_shape = shape((rows_here, columns_each, pair_channels), bf16)
    gate, aux, own_block, *blocks = kernel_call(
        projections_kernel,
        [shape((GROUP, residues, LANES), f32), shape((16, LANES), f32), part_shape]
        + [shape((2 * sequence_wise, residues, LANES), bf16)] * GROUP,
        [vmem] * 7,
        [pltpu.VMEM((GROUP, 2 * sequence_wise, residues, LANES), bf16)],
        flops=10 * token_rows * channel_count * channel_count,
        moved=1 << 21,
    )(
        normed,
        update_cotangent.reshape(token_rows, channel_count),
        joined,
        gate_weight,
        output_weight,
        aux,
        pair_blocks[0],
    )

    def trade(parts):
        return parts[:1] + [
            lax.ppermute(parts[d], "row", [(i, i ^ d) for i in range(peers)]) for d in range(1, GROUP)
        ]

    pair_blocks = [own_block] + trade(pair_blocks)[1:]
    blocks = trade(blocks)
    weight_t = (
        outer_weight.reshape(factor, 4, 8, pair_channels)
        .transpose(1, 2, 0, 3)
        .reshape(4, 8 * factor, pair_channels)
    )
    share_rows = 4 * group_heads
    send_bias, *updated = kernel_call(
        pair_kernel,
        [shape((lines, GROUP, share_rows, LANES), bf16)] + [part_shape] * GROUP,
        [vmem] * (3 + GROUP),
        [
            pltpu.VMEM(((peers + 1) * block_rows, LANES), f32),
            pltpu.VMEM((4, peers * sequence_wise, 8 * LANES), bf16),
            pltpu.VMEM((peers * sequence_wise, 4 * LANES), f32),
            pltpu.VMEM((4, 8 * factor, 4 * LANES), bf16),
            pltpu.VMEM((GROUP, rows_here, columns_each, pair_channels), bf16),
            pltpu.VMEM((GROUP, rows_here, columns_each, pair_channels), bf16),
        ],
        flops=1 << 28,
        moved=1 << 20,
    )(received, weight_t, aux, *pair_blocks)
    bias_all = lax.all_to_all(
        send_bias.reshape(peers, share_rows, LANES), "row", split_axis=0, concat_axis=0, tiled=True
    )

    placed = kernel_call(
        place_kernel,
        shape((group_heads, residues + 16, LANES), f32),
        [vmem] * 2,
        [pltpu.VMEM((head_rows + 16 * group_heads, LANES), f32)],
        flops=1 << 22,
        moved=1 << 18,
    )(bias_all, aux)
    send_grad, weights, values = kernel_call(
        lambda *refs: bias_gradient_kernel(scale, *refs),
        [
            shape((peers, rows_here * group_heads, LANES), bf16),
            shape((GROUP * sequence_wise, head_rows, residues), bf16),
            shape((GROUP * sequence_wise, residues, LANES), bf16),
        ],
        [vmem] * (1 + GROUP),
        [pltpu.VMEM((head_rows + 16 * group_heads, LANES), f32)],
        flops=1 << 28,
        moved=1 << 22,
    )(*blocks, placed)
    shares = lax.all_to_all(send_grad, "row", split_axis=0, concat_axis=0, tiled=True)
    attended = kernel_call(
        attended_kernel,
        [shape((2, residues, LANES), bf16)] * GROUP,
        [vmem] * (2 + GROUP),
        flops=1 << 28,
        moved=1 << 21,
    )(weights, values, *updated)
    update, pair_updated, normal, inverse = kernel_call(
        output_kernel,
        [
            shape((token_rows, channel_count), bf16),
            shape((rows_here, residues, pair_channels), bf16),
            shape((rows_here, residues, pair_channels), f32),
            shape((rows_here, residues, pair_channels), f32),
        ],
        [vmem] * (2 + GROUP),
        flops=2 * token_rows * channel_count * channel_count,
        moved=1 << 20,
    )(gate, output_weight, *trade(list(attended)))
    update, pair_updated, pair_gradient = kernel_call(
        gradient_kernel,
        [
            shape((token_rows, channel_count), bf16),
            shape((rows_here, residues, pair_channels), bf16),
            shape((rows_here, residues, pair_channels), f32),
        ],
        [vmem] * 6,
        [pltpu.VMEM((rows_here, residues, pair_channels), f32), pltpu.SemaphoreType.DMA((2 + rows_here,))],
        flops=1 << 24,
        moved=1 << 20,
        out_specs=[pl.BlockSpec(memory_space=pltpu.HBM)] * 3,
    )(shares, aux, normal, inverse, update, pair_updated)
    return (update.reshape(alignment_rows.shape), pair_updated, pair_gradient)


def on_device(*arguments):
    rows, pair, left, bias = arguments[0], arguments[1], arguments[5], arguments[8]
    peers = lax.axis_size("row")
    fits = (
        lax.axis_size("col") == 1
        and peers == 32
        and rows.shape == (2, 128, 256)
        and pair.shape == (4, 128, 128)
        and left.shape[1] == 32
        and bias.shape[1] == 8
    )
    return (on_device_paired if fits else on_device_general)(*arguments)


def solution(mesh):
    placed = (
        P(("grp", "row"), "col", None),
        P(("grp", "row"), "col", None),
        P(("grp", "row"), "col", None),
        P("grp"),
        P("grp"),
        P(),
        P(),
        P(),
        P(),
        P(),
        P(),
        P(),
        P(),
        P(),
    )
    return jax.shard_map(
        on_device,
        mesh=mesh,
        in_specs=placed,
        out_specs=(
            P(("grp", "row"), "col", None),
            P(("grp", "row"), "col", None),
            P(("grp", "row"), "col", None),
        ),
        check_vma=False,
    )
```
